32 devices in a mesh: groups: 2 (over y), expert: 4 (over z), dp: 4 (over x, core).
Axes of the slice: x: 2, y: 2, z: 4, core: 2. Of those that a mesh axis runs over, the one named last changes fastest.
Arguments:
- tokens: bfloat16 [4096, 4096], P(('groups', 'expert'), 'dp'), parts along dimension 0, may hold values from -6 to 6
- router_weight: bfloat16 [4096, 4], P('dp'), may hold values from -0.09375 to 0.09375
- gate_weight: bfloat16 [4, 4096, 1024], P('expert', None, 'dp'), may hold values from -0.09375 to 0.09375
- up_weight: bfloat16 [4, 4096, 1024], P('expert', None, 'dp'), may hold values from -0.09375 to 0.09375
- down_weight: bfloat16 [4, 1024, 4096], P('expert', None, 'dp'), may hold values from -0.1875 to 0.1875
- picks: int32 [8, 512], P('groups'), parts along dimension 0, may hold values from 0 to 2047, as said below
Outputs:
- combined: bfloat16 [4096, 4096], P(('groups', 'expert'), 'dp'), parts along dimension 0
The draws below stay inside these ranges and needn't reach their ends.
There are 2 independent parts, one for each index of `groups`. The reference program is written for one: setup_inputs(seed, part) draws one part's arguments, and reference() takes and returns one part's arrays. A program takes and returns all parts, laid end to end along the dimension named above; an argument that names none is the same for every part. Nothing has to cross between parts.
Inputs may be any that keep to these rules, and one draw needn't show every extreme that they name: Each row of picks holds 512 distinct token indices; at most 256 of a row lie among one index of expert's 512 consecutive tokens, and exactly 256 do in one such block for every row.
All inputs are finite; a program needn't handle non-finite values.
Results may differ from the reference program's by a relative error of at most 0.0059.
Values may be sent and summed in bfloat16 or wider, within the bound.
No kernel may reach another device: no remote copies, remote signals or barrier semaphores. Data moves between devices by JAX's collectives and lax.ppermute only.
A program may use at most 64 MiB of HBM per device.

```python
import jax
import jax.numpy as jnp
from jax import lax

D = 4096
FF = 1024
CAP = 512
TOK_DEV = 512
EXPERTS = 4
TOKENS = 2048
MOST = 256
N_EXPERT = 4


def draw_picks(key, part):
    key = jax.random.fold_in(key, 11)
    key_hot, key_blocks, key_order = jax.random.split(key, 3)
    remainder = CAP - MOST
    position = jnp.arange(CAP, dtype=jnp.int32)
    after_hot = position - MOST
    safe_after = jnp.maximum(after_hot, 0)
    offset_steps = 1 + (N_EXPERT - 1) * (3 * remainder * safe_after + safe_after * safe_after) // (4 * remainder * remainder)
    offset_steps = jnp.where(after_hot < 0, 0, offset_steps)
    same_source = offset_steps[:, None] == offset_steps[None, :]
    earlier = position[None, :] < position[:, None]
    block_rank = jnp.sum((same_source & earlier).astype(jnp.int32), axis=1)
    hot_source = jax.random.randint(key_hot, (EXPERTS,), 0, N_EXPERT)
    owner = (hot_source[:, None] + offset_steps[None, :]) % N_EXPERT
    block_keys = jax.random.split(key_blocks, EXPERTS * N_EXPERT)
    shuffles = jax.vmap(lambda one_key: jax.random.permutation(one_key, TOK_DEV))(block_keys)
    shuffles = shuffles.reshape(EXPERTS, N_EXPERT, TOK_DEV).astype(jnp.int32)
    expert_ids = jnp.arange(EXPERTS, dtype=jnp.int32)
    inblock = shuffles[expert_ids[:, None], owner, block_rank[None, :]]
    token_ids = owner * TOK_DEV + inblock
    order_keys = jax.random.split(key_order, EXPERTS)
    list_order = jax.vmap(lambda one_key: jax.random.permutation(one_key, CAP))(order_keys).astype(jnp.int32)
    return jnp.take_along_axis(token_ids, list_order, axis=1).astype(jnp.int32)


def block_scale(key, extent, cuts, smallest, largest):
    def one(dim, parts):
        draws = jax.random.uniform(jax.random.fold_in(jax.random.fold_in(key, 6), dim), (parts,), jnp.float32, smallest / len(cuts), largest / len(cuts))
        return jnp.repeat(jnp.exp(draws), extent[dim] // parts).reshape((-1,) + (1,) * (len(extent) - dim - 1))

    gain = one(*cuts[0])
    for cut in cuts[1:]:
        gain = gain * one(*cut)
    return gain


def noise(key, extent, scale, most, shards=(), held_as=jnp.bfloat16):
    drawn = jax.random.normal(key, extent, jnp.float32) * scale
    if len(shards) > 0:
        drawn = block_scale(key, extent, shards, -0.22, 0.18) * drawn
    return jnp.clip(drawn, min=-most, max=most).astype(held_as)


def setup_inputs(seed: int = 0, part: int = 0) -> dict:
    keys = jax.random.split(jax.random.key(seed), 7)
    part_keys = jax.random.split(jax.random.fold_in(keys[6], part), 7)
    return {
        "tokens": noise(part_keys[0], (TOKENS, D), 1.0, 6.0, ((0, 4), (1, 4))),
        "router_weight": noise(keys[1], (D, EXPERTS), D ** -0.5, 0.09375, ((0, 4),)),
        "gate_weight": noise(keys[2], (EXPERTS, D, FF), D ** -0.5, 0.09375, ((0, 4), (2, 4))),
        "up_weight": noise(keys[3], (EXPERTS, D, FF), D ** -0.5, 0.09375, ((0, 4), (2, 4))),
        "down_weight": noise(keys[4], (EXPERTS, FF, D), FF ** -0.5, 0.1875, ((0, 4), (2, 4))),
        "picks": draw_picks(jax.random.fold_in(jax.random.fold_in(keys[6], part), 71), part),
    }


def scaled_scores(kernel):
    row_scale = jnp.ones((kernel.shape[0],), jnp.float32)
    column_scale = jnp.ones((kernel.shape[1],), jnp.float32)
    for sweep_index in range(3):
        column_scale = 1.0 / jnp.sum(kernel * row_scale[:, None], axis=0)
        row_scale = 1.0 / jnp.sum(kernel * column_scale[None, :], axis=1)
    return row_scale[:, None] * kernel * column_scale[None, :]


def reference(tokens, router_weight, gate_weight, up_weight, down_weight, picks):
    logits = jnp.dot(tokens, router_weight, preferred_element_type=jnp.float32)
    scores = scaled_scores(jnp.exp(logits))
    expert_ids = jnp.arange(EXPERTS, dtype=jnp.int32)
    picked = scores[picks, expert_ids[:, None]]
    token_total = jnp.zeros((TOKENS,), jnp.float32).at[picks].add(picked)
    weights = (picked / jnp.maximum(token_total[picks], 1.0 / EXPERTS)).astype(jnp.bfloat16)

    def one_expert(total, expert_index):
        chosen = picks[expert_index]
        row_block = tokens[chosen]
        gate = jnp.dot(row_block, gate_weight[expert_index], preferred_element_type=jnp.float32)
        upward = jnp.dot(row_block, up_weight[expert_index], preferred_element_type=jnp.float32)
        hidden = (jax.nn.silu(gate) * upward).astype(jnp.bfloat16)
        expert_out = jnp.dot(hidden, down_weight[expert_index], preferred_element_type=jnp.float32).astype(jnp.bfloat16)
        term = weights[expert_index][:, None].astype(jnp.float32) * expert_out.astype(jnp.float32)
        return total.at[chosen].add(term), None

    start_total = jnp.zeros((TOKENS, D), jnp.float32)
    total, unused = lax.scan(one_expert, start_total, expert_ids)
    return total.astype(jnp.bfloat16)
```

```python
import functools

import jax
import jax.numpy as jnp
from jax import lax
from jax.experimental import pallas as pl
from jax.experimental.pallas import tpu as pltpu
from jax.sharding import PartitionSpec as P

BATCHES = 2
F32 = jnp.float32
BF16 = jnp.bfloat16
I32 = jnp.int32
VMEM_LIMIT = 48 * 1024 * 1024


def whole(count):
    return [pl.BlockSpec(memory_space=pltpu.VMEM)] * count


def smem():
    return pl.BlockSpec(memory_space=pltpu.SMEM)


def params():
    return pltpu.CompilerParams(vmem_limit_bytes=VMEM_LIMIT)


def dot(a, b):
    return jnp.dot(a, b, preferred_element_type=F32)


def pack_kernel(experts, depth, place_ref, picks_ref, tokens_ref, code_ref, *sends):
    me = place_ref[0]
    rows, width = tokens_ref.shape
    capacity = picks_ref.shape[1]
    strips = rows // 128
    lanes = lax.broadcasted_iota(I32, (128, capacity), 0)
    strip_ids = lax.broadcasted_iota(I32, (8, capacity), 0)
    upper = (lax.broadcasted_iota(I32, (128, 128), 0) < lax.broadcasted_iota(I32, (128, 128), 1)).astype(BF16)
    before = (lax.broadcasted_iota(I32, (8, 8), 1) < lax.broadcasted_iota(I32, (8, 8), 0)).astype(BF16)
    slot_ids = lax.broadcasted_iota(I32, (BATCHES * depth, rows), 0)
    ones = jnp.ones((128, 128), BF16)
    for shift in range(experts):
        expert = lax.rem(me + shift, experts)
        chosen = picks_ref[pl.ds(expert, 1), :]
        local = chosen - me * rows
        start = jnp.sum((local < 0).astype(F32)).astype(I32)
        strip = lax.shift_right_arithmetic(local, 7)
        place = jnp.bitwise_and(local, 127)
        high = (strip == strip_ids).astype(BF16)
        high = jnp.where(strip_ids < strips, high, jnp.zeros_like(high))
        low = (place == lanes).astype(BF16)
        mask = lax.dot_general(high, low, (((1,), (1,)), ((), ())), preferred_element_type=F32)
        mask16 = mask.astype(BF16)
        totals = dot(mask16, ones)
        rank = (dot(mask16, upper) + dot(before, totals.astype(BF16))).astype(I32)
        batch = lax.rem(rank + start, BATCHES)
        slot = batch * depth + lax.div(rank, BATCHES)
        code = jnp.where(mask > 0.5, slot, -1)
        row = jnp.concatenate([code[i : i + 1] for i in range(strips)], axis=1)
        code_ref[pl.ds(shift, 1), :] = row
        selector = (slot_ids == row).astype(F32).astype(BF16)
        packed = dot(selector, tokens_ref[...]).astype(BF16)
        for k in range(BATCHES):
            sends[k * experts + shift][...] = packed[k * depth : (k + 1) * depth]


def pack_rows(place, picks, tokens, experts, depth):
    rows, width = tokens.shape
    out = pl.pallas_call(
        functools.partial(pack_kernel, experts, depth),
        out_shape=[jax.ShapeDtypeStruct((experts, rows), I32)]
        + [jax.ShapeDtypeStruct((depth, width), BF16)] * (BATCHES * experts),
        in_specs=[smem()] + whole(2),
        out_specs=whole(1 + BATCHES * experts),
        compiler_params=params(),
    )(place, picks, tokens)
    code, sends = out[0], out[1:]
    return code, [sends[k * experts : (k + 1) * experts] for k in range(BATCHES)]


def compact_kernel(experts, k, offset_ref, count_ref, *refs):
    blocks, out_ref = refs[:experts], refs[experts]
    depth = blocks[0].shape[0]
    size = out_ref.shape[0]
    row = lax.broadcasted_iota(I32, (size, depth), 0)
    lane = lax.broadcasted_iota(I32, (size, depth), 1)
    parts = [
        ((row - offset_ref[k, i] == lane) & (lane < count_ref[k, i])).astype(F32).astype(BF16)
        for i in range(experts)
    ]
    out_ref[...] = dot(
        jnp.concatenate(parts, axis=1), jnp.concatenate([b[...] for b in blocks], axis=0)
    ).astype(BF16)


def compact(offsets, counts, k, blocks, size):
    experts = len(blocks)
    return pl.pallas_call(
        functools.partial(compact_kernel, experts, k),
        out_shape=jax.ShapeDtypeStruct((size, blocks[0].shape[1]), BF16),
        in_specs=[smem(), smem()] + whole(experts),
        out_specs=whole(1)[0],
        compiler_params=params(),
    )(offsets, counts, *blocks)


def hidden_kernel(parts, order_ref, gate_ref, up_ref, *refs):
    xs, out_ref, gate_sum, up_sum = refs[:parts], refs[parts], refs[parts + 1], refs[parts + 2]
    step = pl.program_id(0)
    for i in range(parts):

        @pl.when(step == i)
        def _():
            gate = dot(xs[i][...], gate_ref[0])
            up = dot(xs[i][...], up_ref[0])
            if i > 0:
                gate = gate + gate_sum[...]
                up = up + up_sum[...]
            if i < parts - 1:
                gate_sum[...] = gate
                up_sum[...] = up
            else:
                out_ref[...] = (gate * jax.nn.sigmoid(gate) * up).astype(BF16)


def hidden_units(order, gate_weight, up_weight, xs):
    parts = len(xs)
    size, width = xs[0].shape
    units = gate_weight.shape[2]
    weight_spec = pl.BlockSpec((1, width, units), lambda i, order: (0, order[i], 0))
    return pl.pallas_call(
        functools.partial(hidden_kernel, parts),
        grid_spec=pltpu.PrefetchScalarGridSpec(
            num_scalar_prefetch=1,
            grid=(parts,),
            in_specs=[weight_spec, weight_spec] + [pl.BlockSpec((size, width), lambda i, order: (0, 0))] * parts,
            out_specs=pl.BlockSpec((size, units), lambda i, order: (0, 0)),
            scratch_shapes=[pltpu.VMEM((size, units), F32)] * 2,
        ),
        out_shape=jax.ShapeDtypeStruct((size, units), BF16),
        compiler_params=params(),
    )(order, gate_weight, up_weight, *xs)


def down_kernel(parts, experts, k, order_ref, offset_ref, count_ref, down_ref, *refs):
    hs, outs = refs[:parts], refs[parts : parts + experts]
    size, units = hs[0].shape
    depth = outs[0].shape[0]
    total = None
    for i in range(parts):
        first = pl.multiple_of(order_ref[i] * units, units)
        term = dot(hs[i][...], down_ref[0, pl.ds(first, units), :])
        total = term if total is None else total + term
    result = total.astype(BF16)
    row = lax.broadcasted_iota(I32, (depth, size), 0)
    lane = lax.broadcasted_iota(I32, (depth, size), 1)
    for i in range(experts):
        pick = ((lane - offset_ref[k, i] == row) & (row < count_ref[k, i])).astype(F32).astype(BF16)
        outs[i][...] = dot(pick, result).astype(BF16)


def down_rows(order, offsets, counts, k, down_weight, hs, experts, depth):
    parts = len(hs)
    width = down_weight.shape[2]
    return pl.pallas_call(
        functools.partial(down_kernel, parts, experts, k),
        out_shape=[jax.ShapeDtypeStruct((depth, width), BF16)] * experts,
        in_specs=[smem()] * 3 + whole(1 + parts),
        out_specs=whole(experts),
        compiler_params=params(),
    )(order, offsets, counts, down_weight, *hs)


def weight_kernel(experts, place_ref, own_ref, logits_ref, code_ref, out_ref, score_ref):
    me = place_ref[0]
    kernel = jnp.exp(logits_ref[...])
    row_scale = jnp.ones((kernel.shape[0], 1, kernel.shape[2]), F32)
    for sweep in range(3):
        column = jnp.sum(jnp.sum(kernel * row_scale, axis=0, keepdims=True), axis=2, keepdims=True)
        column_scale = 1.0 / column
        row_scale = 1.0 / jnp.sum(kernel * column_scale, axis=1, keepdims=True)
    own = jnp.exp(own_ref[...])
    column_scale = column_scale[0]
    own_scale = 1.0 / jnp.sum(own * column_scale, axis=0, keepdims=True)
    score_ref[...] = own_scale * own * column_scale
    picked = []
    for shift in range(experts):
        score = score_ref[pl.ds(lax.rem(me + shift, experts), 1), :]
        picked.append(jnp.where(code_ref[pl.ds(shift, 1), :] >= 0, score, 0.0))
    total = picked[0]
    for one in picked[1:]:
        total = total + one
    total = jnp.maximum(total, 1.0 / experts)
    for shift in range(experts):
        out_ref[pl.ds(shift, 1), :] = picked[shift] / total


def slot_weights(place, own, logits, code):
    experts, rows = own.shape
    return pl.pallas_call(
        functools.partial(weight_kernel, experts),
        out_shape=jax.ShapeDtypeStruct((experts, rows), F32),
        in_specs=[smem()] + whole(3),
        out_specs=whole(1)[0],
        scratch_shapes=[pltpu.VMEM((experts, rows), F32)],
        compiler_params=params(),
    )(place, own, logits, code)


def combine_kernel(experts, k, last, code_ref, weight_ref, *refs):
    blocks = refs[:experts]
    out_ref = refs[-1]
    depth = blocks[0].shape[0]
    rows = code_ref.shape[1]
    slot_ids = lax.broadcasted_iota(I32, (depth, rows), 0) + k * depth
    parts = [
        jnp.where(slot_ids == code_ref[pl.ds(i, 1), :], weight_ref[pl.ds(i, 1), :], 0.0).astype(BF16)
        for i in range(experts)
    ]
    total = lax.dot_general(
        jnp.concatenate(parts, axis=0),
        jnp.concatenate([b[...] for b in blocks], axis=0),
        (((0,), (0,)), ((), ())),
        preferred_element_type=F32,
    )
    if k > 0:
        total = total + refs[experts][...]
    out_ref[...] = total.astype(out_ref.dtype)


def combine(code, weights, k, blocks, so_far):
    experts = len(blocks)
    last = k == BATCHES - 1
    more = [] if so_far is None else [so_far]
    return pl.pallas_call(
        functools.partial(combine_kernel, experts, k, last),
        out_shape=jax.ShapeDtypeStruct((code.shape[1], blocks[0].shape[1]), BF16 if last else F32),
        in_specs=whole(2 + experts + len(more)),
        out_specs=whole(1)[0],
        compiler_params=params(),
    )(code, weights, *blocks, *more)


def shards(tokens, router_weight, gate_weight, up_weight, down_weight, picks):
    experts = lax.axis_size("expert")
    width_parts = lax.axis_size("dp")
    me = lax.axis_index("expert")
    part = lax.axis_index("dp")
    rows = tokens.shape[0]
    capacity = picks.shape[1]
    depth = 2 * capacity // experts // BATCHES
    size = capacity // BATCHES
    place = me.astype(I32).reshape(1)

    def along_expert(x, shift):
        return lax.ppermute(x, "expert", [(i, (i + shift) % experts) for i in range(experts)])

    def swap(x, bit):
        return lax.ppermute(x, "dp", [(i, i ^ bit) for i in range(width_parts)])

    bits = []
    bit = width_parts // 2
    while bit:
        bits.append(bit)
        bit //= 2
    masks = [0]
    for bit in bits:
        masks = masks + [m ^ bit for m in masks]
    order = jnp.stack([part ^ m for m in masks]).astype(I32)

    def all_parts(x):
        held = [x]
        for bit in bits:
            held = held + [swap(h, bit) for h in held]
        return held

    code, sends = pack_rows(place, picks, tokens, experts, depth)
    own_picks = lax.dynamic_slice_in_dim(picks, me, 1, axis=0)
    sources = lax.rem(me - jnp.arange(experts, dtype=I32) + experts, experts)
    start = jnp.sum((own_picks < (sources * rows)[:, None]).astype(I32), axis=1)
    stop = jnp.sum((own_picks < ((sources + 1) * rows)[:, None]).astype(I32), axis=1)
    ids = jnp.arange(BATCHES, dtype=I32)[:, None]
    offsets = (start[None, :] + (BATCHES - 1) - ids) // BATCHES
    counts = (stop[None, :] + (BATCHES - 1) - ids) // BATCHES - offsets

    arrived = [
        [sends[k][0]] + [along_expert(sends[k][shift], shift) for shift in range(1, experts)]
        for k in range(BATCHES)
    ]

    logits = lax.dot_general(
        router_weight, tokens, (((0,), (1,)), ((), ())), preferred_element_type=F32
    )
    for bit in bits:
        logits = logits + swap(logits, bit)
    gathered = jnp.stack([logits] + [along_expert(logits, shift) for shift in range(1, experts)])
    weights = slot_weights(place, logits, gathered, code)

    total = None
    for k in range(BATCHES):
        block = compact(offsets, counts, k, arrived[k], size)
        hidden = hidden_units(order, gate_weight, up_weight, all_parts(block))
        results = down_rows(order, offsets, counts, k, down_weight, all_parts(hidden), experts, depth)
        returned = [results[0]] + [along_expert(results[shift], -shift) for shift in range(1, experts)]
        total = combine(code, weights, k, returned, total)
    return total


def solution(mesh):
    return jax.shard_map(
        shards,
        mesh=mesh,
        in_specs=(
            P(("groups", "expert"), "dp"),
            P("dp", None),
            P("expert", None, "dp"),
            P("expert", None, "dp"),
            P("expert", None, "dp"),
            P("groups", None),
        ),
        out_specs=P(("groups", "expert"), "dp"),
        check_vma=False,
    )
```

```python
import functools

import jax
import jax.numpy as jnp
from jax import lax
from jax.experimental import pallas as pl
from jax.experimental.pallas import tpu as pltpu
from jax.sharding import PartitionSpec as P

BATCHES = 2
F32 = jnp.float32
BF16 = jnp.bfloat16
I32 = jnp.int32
VMEM_LIMIT = 24 * 1024 * 1024


def whole(count):
    return [pl.BlockSpec(memory_space=pltpu.VMEM)] * count


def apart(count):
    return [pl.BlockSpec(memory_space=pl.ANY)] * count


def smem():
    return pl.BlockSpec(memory_space=pltpu.SMEM)


def params():
    return pltpu.CompilerParams(vmem_limit_bytes=VMEM_LIMIT)


def dot(a, b):
    return jnp.dot(a, b, preferred_element_type=F32)


def start_all(sources, targets, sems):
    copies = [pltpu.make_async_copy(a, b, sems.at[i]) for i, (a, b) in enumerate(zip(sources, targets))]
    for copy in copies:
        copy.start()
    return copies


def code_kernel(experts, depth, place_ref, picks_ref, router_ref, tokens_ref, code_ref, logits_ref, *refs):
    sends = refs[:experts]
    held, staged, in_sems, out_sems = refs[experts:]
    load = start_all([tokens_ref], [held], in_sems)[0]
    me = place_ref[0]
    rows, width = held.shape
    capacity = picks_ref.shape[1]
    strips = rows // 128
    lanes = lax.broadcasted_iota(I32, (128, capacity), 0)
    strip_ids = lax.broadcasted_iota(I32, (8, capacity), 0)
    upper = (lax.broadcasted_iota(I32, (128, 128), 0) < lax.broadcasted_iota(I32, (128, 128), 1)).astype(BF16)
    before = (lax.broadcasted_iota(I32, (8, 8), 1) < lax.broadcasted_iota(I32, (8, 8), 0)).astype(BF16)
    ones = jnp.ones((128, 128), BF16)
    code_rows = []
    for shift in range(experts):
        expert = lax.rem(me + shift, experts)
        chosen = picks_ref[pl.ds(expert, 1), :]
        local = chosen - me * rows
        start = jnp.sum((local < 0).astype(F32)).astype(I32)
        strip = lax.shift_right_arithmetic(local, 7)
        place = jnp.bitwise_and(local, 127)
        high = (strip == strip_ids).astype(BF16)
        high = jnp.where(strip_ids < strips, high, jnp.zeros_like(high))
        low = (place == lanes).astype(BF16)
        mask = lax.dot_general(high, low, (((1,), (1,)), ((), ())), preferred_element_type=F32)
        mask16 = mask.astype(BF16)
        totals = dot(mask16, ones)
        rank = (dot(mask16, upper) + dot(before, totals.astype(BF16))).astype(I32)
        batch = lax.rem(rank + start, BATCHES)
        slot = batch * depth + lax.div(rank, BATCHES)
        code = jnp.where(mask > 0.5, slot, -1)
        row = jnp.concatenate([code[i : i + 1] for i in range(strips)], axis=1)
        code_ref[pl.ds(shift, 1), :] = row
        code_rows.append(row)
    load.wait()
    logits_ref[...] = lax.dot_general(
        router_ref[...], held[...], (((1,), (1,)), ((), ())), preferred_element_type=F32
    )
    pack(0, depth, code_rows, held, staged, sends, out_sems)


def pack(k, depth, code_rows, held, staged, sends, sems):
    slot_ids = lax.broadcasted_iota(I32, (depth, held.shape[0]), 0) + k * depth
    copies = []
    for shift in list(range(1, len(sends))) + [0]:
        selector = (slot_ids == code_rows[shift]).astype(F32).astype(BF16)
        staged[shift] = dot(selector, held[...]).astype(BF16)
        copy = pltpu.make_async_copy(staged.at[shift], sends[shift], sems.at[shift])
        copy.start()
        copies.append(copy)
    for copy in copies:
        copy.wait()


def first_batch(place, picks, router, tokens, depth):
    rows, width = tokens.shape
    experts = picks.shape[0]
    out = pl.pallas_call(
        functools.partial(code_kernel, experts, depth),
        out_shape=[jax.ShapeDtypeStruct((experts, rows), I32), jax.ShapeDtypeStruct((experts, rows), F32)]
        + [jax.ShapeDtypeStruct((depth, width), BF16)] * experts,
        in_specs=[smem()] + whole(2) + apart(1),
        out_specs=whole(2) + apart(experts),
        scratch_shapes=[
            pltpu.VMEM((rows, width), BF16),
            pltpu.VMEM((experts, depth, width), BF16),
            pltpu.SemaphoreType.DMA((1,)),
            pltpu.SemaphoreType.DMA((experts,)),
        ],
        compiler_params=params(),
    )(place, picks, router, tokens)
    return out[0], out[1], out[2:]


def pack_kernel(experts, depth, k, code_ref, tokens_ref, *refs):
    sends = refs[:experts]
    held, staged, in_sems, out_sems = refs[experts:]
    start_all([tokens_ref], [held], in_sems)[0].wait()
    code_rows = [code_ref[pl.ds(shift, 1), :] for shift in range(experts)]
    pack(k, depth, code_rows, held, staged, sends, out_sems)


def later_batch(code, tokens, k, depth):
    rows, width = tokens.shape
    experts = code.shape[0]
    return pl.pallas_call(
        functools.partial(pack_kernel, experts, depth, k),
        out_shape=[jax.ShapeDtypeStruct((depth, width), BF16)] * experts,
        in_specs=whole(1) + apart(1),
        out_specs=apart(experts),
        scratch_shapes=[
            pltpu.VMEM((rows, width), BF16),
            pltpu.VMEM((experts, depth, width), BF16),
            pltpu.SemaphoreType.DMA((1,)),
            pltpu.SemaphoreType.DMA((experts,)),
        ],
        compiler_params=params(),
    )(code, tokens)


def compact_kernel(experts, k, offset_ref, count_ref, *refs):
    blocks, out_ref = refs[:experts], refs[experts]
    held, sems = refs[experts + 1 :]
    depth = blocks[0].shape[0]
    size = out_ref.shape[0]
    loads = start_all(blocks, [held.at[pl.ds(i * depth, depth)] for i in range(experts)], sems)
    row = lax.broadcasted_iota(I32, (size, depth), 0)
    lane = lax.broadcasted_iota(I32, (size, depth), 1)
    parts = [
        ((row - offset_ref[k, i] == lane) & (lane < count_ref[k, i])).astype(F32).astype(BF16)
        for i in range(experts)
    ]
    selector = jnp.concatenate(parts, axis=1)
    for load in loads:
        load.wait()
    out_ref[...] = dot(selector, held[...]).astype(BF16)


def compact(offsets, counts, k, blocks, size):
    experts = len(blocks)
    depth, width = blocks[0].shape
    return pl.pallas_call(
        functools.partial(compact_kernel, experts, k),
        out_shape=jax.ShapeDtypeStruct((size, width), BF16),
        in_specs=[smem(), smem()] + apart(experts),
        out_specs=whole(1)[0],
        scratch_shapes=[pltpu.VMEM((experts * depth, width), BF16), pltpu.SemaphoreType.DMA((experts,))],
        compiler_params=params(),
    )(offsets, counts, *blocks)


def hidden_kernel(parts, order_ref, gate_ref, up_ref, *refs):
    xs, out_ref = refs[:parts], refs[parts]
    gate_held, up_held, x_held, sems = refs[parts + 1 :]
    width = xs[0].shape[1]
    loads = []
    for i in range(parts):
        first = pl.multiple_of(order_ref[i] * width, width)
        copies = [
            pltpu.make_async_copy(xs[i], x_held.at[i], sems.at[3 * i]),
            pltpu.make_async_copy(gate_ref.at[0, pl.ds(first, width), :], gate_held.at[i], sems.at[3 * i + 1]),
            pltpu.make_async_copy(up_ref.at[0, pl.ds(first, width), :], up_held.at[i], sems.at[3 * i + 2]),
        ]
        for copy in copies:
            copy.start()
        loads.append(copies)
    gate = up = None
    for i in range(parts):
        for copy in loads[i]:
            copy.wait()
        x = x_held[i]
        gate_term = dot(x, gate_held[i])
        up_term = dot(x, up_held[i])
        gate = gate_term if gate is None else gate + gate_term
        up = up_term if up is None else up + up_term
    out_ref[...] = (gate * jax.nn.sigmoid(gate) * up).astype(BF16)


def hidden_units(order, gate_weight, up_weight, xs):
    parts = len(xs)
    size, width = xs[0].shape
    units = gate_weight.shape[2]
    return pl.pallas_call(
        functools.partial(hidden_kernel, parts),
        out_shape=jax.ShapeDtypeStruct((size, units), BF16),
        in_specs=[smem()] + apart(2 + parts),
        out_specs=whole(1)[0],
        scratch_shapes=[
            pltpu.VMEM((parts, width, units), BF16),
            pltpu.VMEM((parts, width, units), BF16),
            pltpu.VMEM((parts, size, width), BF16),
            pltpu.SemaphoreType.DMA((3 * parts,)),
        ],
        compiler_params=params(),
    )(order, gate_weight, up_weight, *xs)


def down_kernel(parts, experts, k, order_ref, offset_ref, count_ref, down_ref, *refs):
    hs, outs = refs[:parts], refs[parts : parts + experts]
    down_held, h_held, staged, in_sems, out_sems = refs[parts + experts :]
    size, units = hs[0].shape
    depth = outs[0].shape[0]
    loads = []
    for i in range(parts):
        first = pl.multiple_of(order_ref[i] * units, units)
        copies = [
            pltpu.make_async_copy(hs[i], h_held.at[i], in_sems.at[2 * i]),
            pltpu.make_async_copy(down_ref.at[0, pl.ds(first, units), :], down_held.at[i], in_sems.at[2 * i + 1]),
        ]
        for copy in copies:
            copy.start()
        loads.append(copies)
    row = lax.broadcasted_iota(I32, (depth, size), 0)
    lane = lax.broadcasted_iota(I32, (depth, size), 1)
    total = None
    for i in range(parts):
        for copy in loads[i]:
            copy.wait()
        term = dot(h_held[i], down_held[i])
        total = term if total is None else total + term
    result = total.astype(BF16)
    copies = []
    for i in list(range(1, experts)) + [0]:
        pick = ((lane - offset_ref[k, i] == row) & (row < count_ref[k, i])).astype(F32).astype(BF16)
        staged[i] = dot(pick, result).astype(BF16)
        copy = pltpu.make_async_copy(staged.at[i], outs[i], out_sems.at[i])
        copy.start()
        copies.append(copy)
    for copy in copies:
        copy.wait()


def down_rows(order, offsets, counts, k, down_weight, hs, experts, depth):
    parts = len(hs)
    size, units = hs[0].shape
    width = down_weight.shape[2]
    return pl.pallas_call(
        functools.partial(down_kernel, parts, experts, k),
        out_shape=[jax.ShapeDtypeStruct((depth, width), BF16)] * experts,
        in_specs=[smem()] * 3 + apart(1 + parts),
        out_specs=apart(experts),
        scratch_shapes=[
            pltpu.VMEM((parts, units, width), BF16),
            pltpu.VMEM((parts, size, units), BF16),
            pltpu.VMEM((experts, depth, width), BF16),
            pltpu.SemaphoreType.DMA((2 * parts,)),
            pltpu.SemaphoreType.DMA((experts,)),
        ],
        compiler_params=params(),
    )(order, offsets, counts, down_weight, *hs)


def weight_kernel(experts, place_ref, own_ref, logits_ref, code_ref, out_ref, score_ref):
    me = place_ref[0]
    kernel = jnp.exp(logits_ref[...])
    row_scale = jnp.ones((kernel.shape[0], 1, kernel.shape[2]), F32)
    for sweep in range(3):
        column = jnp.sum(jnp.sum(kernel * row_scale, axis=0, keepdims=True), axis=2, keepdims=True)
        column_scale = 1.0 / column
        row_scale = 1.0 / jnp.sum(kernel * column_scale, axis=1, keepdims=True)
    own = jnp.exp(own_ref[...])
    column_scale = column_scale[0]
    own_scale = 1.0 / jnp.sum(own * column_scale, axis=0, keepdims=True)
    score_ref[...] = own_scale * own * column_scale
    picked = []
    for shift in range(experts):
        score = score_ref[pl.ds(lax.rem(me + shift, experts), 1), :]
        picked.append(jnp.where(code_ref[pl.ds(shift, 1), :] >= 0, score, 0.0))
    total = picked[0]
    for one in picked[1:]:
        total = total + one
    total = jnp.maximum(total, 1.0 / experts)
    for shift in range(experts):
        out_ref[pl.ds(shift, 1), :] = picked[shift] / total


def slot_weights(place, own, logits, code):
    experts, rows = own.shape
    return pl.pallas_call(
        functools.partial(weight_kernel, experts),
        out_shape=jax.ShapeDtypeStruct((experts, rows), F32),
        in_specs=[smem()] + whole(3),
        out_specs=whole(1)[0],
        scratch_shapes=[pltpu.VMEM((experts, rows), F32)],
        compiler_params=params(),
    )(place, own, logits, code)


def combine_kernel(experts, k, code_ref, weight_ref, *refs):
    count = experts + (k > 0)
    blocks, out_ref = refs[:count], refs[count]
    held, sems = refs[count + 1], refs[count + 2]
    depth = blocks[0].shape[0]
    rows = code_ref.shape[1]
    targets = [held.at[pl.ds(i * depth, depth)] for i in range(experts)]
    if k > 0:
        targets.append(refs[count + 3])
    loads = start_all(blocks, targets, sems)
    slot_ids = lax.broadcasted_iota(I32, (depth, rows), 0) + k * depth
    parts = [
        jnp.where(slot_ids == code_ref[pl.ds(i, 1), :], weight_ref[pl.ds(i, 1), :], 0.0).astype(BF16)
        for i in range(experts)
    ]
    spread = jnp.concatenate(parts, axis=0)
    for load in loads:
        load.wait()
    total = lax.dot_general(spread, held[...], (((0,), (0,)), ((), ())), preferred_element_type=F32)
    if k > 0:
        total = total + refs[count + 3][...]
    out_ref[...] = total.astype(out_ref.dtype)


def combine(code, weights, k, blocks, so_far):
    experts = len(blocks)
    depth, width = blocks[0].shape
    rows = code.shape[1]
    last = k == BATCHES - 1
    more = [] if so_far is None else [so_far]
    return pl.pallas_call(
        functools.partial(combine_kernel, experts, k),
        out_shape=jax.ShapeDtypeStruct((rows, width), BF16 if last else F32),
        in_specs=whole(2) + apart(experts + len(more)),
        out_specs=whole(1)[0],
        scratch_shapes=[
            pltpu.VMEM((experts * depth, width), BF16),
            pltpu.SemaphoreType.DMA((experts + len(more),)),
        ]
        + [pltpu.VMEM((rows, width), F32)] * len(more),
        compiler_params=params(),
    )(code, weights, *blocks, *more)


def after(value, *first):
    return lax.optimization_barrier((value, first))[0]


def shards(tokens, router_weight, gate_weight, up_weight, down_weight, picks):
    experts = lax.axis_size("expert")
    width_parts = lax.axis_size("dp")
    me = lax.axis_index("expert")
    part = lax.axis_index("dp")
    rows = tokens.shape[0]
    capacity = picks.shape[1]
    depth = 2 * capacity // experts // BATCHES
    size = capacity // BATCHES
    place = me.astype(I32).reshape(1)

    def along_expert(x, shift):
        return lax.ppermute(x, "expert", [(i, (i + shift) % experts) for i in range(experts)])

    def swap(x, bit):
        return lax.ppermute(x, "dp", [(i, i ^ bit) for i in range(width_parts)])

    bits = []
    bit = width_parts // 2
    while bit:
        bits.append(bit)
        bit //= 2
    masks = [0]
    for bit in bits:
        masks = masks + [m ^ bit for m in masks]
    order = jnp.stack([part ^ m for m in masks]).astype(I32)

    def all_parts(x):
        held = [x]
        for bit in bits:
            held = held + [swap(h, bit) for h in held]
        return held

    code, logits, sends = first_batch(place, picks, router_weight.T, tokens, depth)
    gathered = jnp.stack([logits] + [along_expert(logits, shift) for shift in range(1, experts)])
    sends = [[sends[0]] + [after(block, logits) for block in sends[1:]]]
    arrived = [[sends[0][0]] + [along_expert(sends[0][shift], shift) for shift in range(1, experts)]]
    for k in range(1, BATCHES):
        blocks = later_batch(code, tokens, k, depth)
        arrived.append(
            [blocks[0]]
            + [along_expert(after(blocks[shift], arrived[k - 1][shift]), shift) for shift in range(1, experts)]
        )
    for bit in bits:
        gathered = gathered + swap(gathered, bit)
    weights = slot_weights(place, gathered[0], gathered, code)

    own_picks = lax.dynamic_slice_in_dim(picks, me, 1, axis=0)
    sources = lax.rem(me - jnp.arange(experts, dtype=I32) + experts, experts)
    start = jnp.sum((own_picks < (sources * rows)[:, None]).astype(I32), axis=1)
    stop = jnp.sum((own_picks < ((sources + 1) * rows)[:, None]).astype(I32), axis=1)
    ids = jnp.arange(BATCHES, dtype=I32)[:, None]
    offsets = (start[None, :] + (BATCHES - 1) - ids) // BATCHES
    counts = (stop[None, :] + (BATCHES - 1) - ids) // BATCHES - offsets
    offsets, counts, order = after((offsets, counts, order), code)

    total = None
    results = []
    for k in range(BATCHES):
        if k == 0:
            blocks = after(arrived[0], weights)
        else:
            blocks = after(arrived[k], results)
        block = compact(offsets, counts, k, blocks, size)
        hidden = hidden_units(order, gate_weight, up_weight, all_parts(block))
        results = down_rows(order, offsets, counts, k, down_weight, all_parts(hidden), experts, depth)
        returned = [results[0]] + [along_expert(results[shift], -shift) for shift in range(1, experts)]
        total = combine(code, weights, k, returned, total)
    return total


def solution(mesh):
    return jax.shard_map(
        shards,
        mesh=mesh,
        in_specs=(
            P(("groups", "expert"), "dp"),
            P("dp", None),
            P("expert", None, "dp"),
            P("expert", None, "dp"),
            P("expert", None, "dp"),
            P("groups", None),
        ),
        out_specs=P(("groups", "expert"), "dp"),
        check_vma=False,
    )
```

```python
import functools

import jax
import jax.numpy as jnp
from jax import lax
from jax.experimental import pallas as pl
from jax.experimental.pallas import tpu as pltpu
from jax.sharding import PartitionSpec as P

BATCHES = 2
F32 = jnp.float32
BF16 = jnp.bfloat16
I32 = jnp.int32
VMEM_LIMIT = 24 * 1024 * 1024
COST = pl.CostEstimate(flops=1024, bytes_accessed=1024, transcendentals=0)


def whole(count):
    return [pl.BlockSpec(memory_space=pltpu.VMEM)] * count


def apart(count):
    return [pl.BlockSpec(memory_space=pl.ANY)] * count


def smem():
    return pl.BlockSpec(memory_space=pltpu.SMEM)


def params():
    return pltpu.CompilerParams(vmem_limit_bytes=VMEM_LIMIT)


def dot(a, b):
    return jnp.dot(a, b, preferred_element_type=F32)


def start_all(sources, targets, sems):
    copies = [pltpu.make_async_copy(a, b, sems.at[i]) for i, (a, b) in enumerate(zip(sources, targets))]
    for copy in copies:
        copy.start()
    return copies


def code_kernel(experts, depth, place_ref, picks_ref, router_ref, tokens_ref, code_ref, logits_ref, *refs):
    sends = refs[:experts]
    held, staged, in_sems, out_sems = refs[experts:]
    load = start_all([tokens_ref], [held], in_sems)[0]
    me = place_ref[0]
    rows, width = held.shape
    capacity = picks_ref.shape[1]
    strips = rows // 128
    lanes = lax.broadcasted_iota(I32, (128, capacity), 0)
    strip_ids = lax.broadcasted_iota(I32, (8, capacity), 0)
    upper = (lax.broadcasted_iota(I32, (128, 128), 0) < lax.broadcasted_iota(I32, (128, 128), 1)).astype(BF16)
    before = (lax.broadcasted_iota(I32, (8, 8), 1) < lax.broadcasted_iota(I32, (8, 8), 0)).astype(BF16)
    ones = jnp.ones((128, 128), BF16)
    code_rows = []
    for shift in range(experts):
        expert = lax.rem(me + shift, experts)
        chosen = picks_ref[pl.ds(expert, 1), :]
        local = chosen - me * rows
        start = jnp.sum((local < 0).astype(F32)).astype(I32)
        strip = lax.shift_right_arithmetic(local, 7)
        place = jnp.bitwise_and(local, 127)
        high = (strip == strip_ids).astype(BF16)
        high = jnp.where(strip_ids < strips, high, jnp.zeros_like(high))
        low = (place == lanes).astype(BF16)
        mask = lax.dot_general(high, low, (((1,), (1,)), ((), ())), preferred_element_type=F32)
        mask16 = mask.astype(BF16)
        totals = dot(mask16, ones)
        rank = (dot(mask16, upper) + dot(before, totals.astype(BF16))).astype(I32)
        batch = lax.rem(rank + start, BATCHES)
        slot = batch * depth + lax.div(rank, BATCHES)
        code = jnp.where(mask > 0.5, slot, -1)
        row = jnp.concatenate([code[i : i + 1] for i in range(strips)], axis=1)
        code_ref[pl.ds(shift, 1), :] = row
        code_rows.append(row)
    load.wait()
    logits_ref[...] = lax.dot_general(
        router_ref[...], held[...], (((1,), (1,)), ((), ())), preferred_element_type=F32
    )
    pack(0, depth, code_rows, held, staged, sends, out_sems)


def pack(k, depth, code_rows, held, staged, sends, sems):
    slot_ids = lax.broadcasted_iota(I32, (depth, held.shape[0]), 0) + k * depth
    copies = []
    for shift in list(range(1, len(sends))) + [0]:
        selector = (slot_ids == code_rows[shift]).astype(F32).astype(BF16)
        staged[shift] = dot(selector, held[...]).astype(BF16)
        copy = pltpu.make_async_copy(staged.at[shift], sends[shift], sems.at[shift])
        copy.start()
        copies.append(copy)
    for copy in copies:
        copy.wait()


def first_batch(place, picks, router, tokens, depth):
    rows, width = tokens.shape
    experts = picks.shape[0]
    out = pl.pallas_call(
        functools.partial(code_kernel, experts, depth),
        out_shape=[jax.ShapeDtypeStruct((experts, rows), I32), jax.ShapeDtypeStruct((experts, rows), F32)]
        + [jax.ShapeDtypeStruct((depth, width), BF16)] * experts,
        in_specs=[smem()] + whole(2) + apart(1),
        out_specs=whole(2) + apart(experts),
        scratch_shapes=[
            pltpu.VMEM((rows, width), BF16),
            pltpu.VMEM((experts, depth, width), BF16),
            pltpu.SemaphoreType.DMA((1,)),
            pltpu.SemaphoreType.DMA((experts,)),
        ],
        compiler_params=params(),
        cost_estimate=COST,
    )(place, picks, router, tokens)
    return out[0], out[1], out[2:]


def pack_kernel(experts, depth, k, code_ref, tokens_ref, *refs):
    sends = refs[:experts]
    held, staged, in_sems, out_sems = refs[experts:]
    start_all([tokens_ref], [held], in_sems)[0].wait()
    code_rows = [code_ref[pl.ds(shift, 1), :] for shift in range(experts)]
    pack(k, depth, code_rows, held, staged, sends, out_sems)


def later_batch(code, tokens, k, depth):
    rows, width = tokens.shape
    experts = code.shape[0]
    return pl.pallas_call(
        functools.partial(pack_kernel, experts, depth, k),
        out_shape=[jax.ShapeDtypeStruct((depth, width), BF16)] * experts,
        in_specs=whole(1) + apart(1),
        out_specs=apart(experts),
        scratch_shapes=[
            pltpu.VMEM((rows, width), BF16),
            pltpu.VMEM((experts, depth, width), BF16),
            pltpu.SemaphoreType.DMA((1,)),
            pltpu.SemaphoreType.DMA((experts,)),
        ],
        compiler_params=params(),
        cost_estimate=COST,
    )(code, tokens)


def compact_kernel(experts, k, offset_ref, count_ref, *refs):
    blocks, out_ref = refs[:experts], refs[experts]
    held, sems = refs[experts + 1 :]
    depth = blocks[0].shape[0]
    size = out_ref.shape[0]
    loads = start_all(blocks, [held.at[pl.ds(i * depth, depth)] for i in range(experts)], sems)
    row = lax.broadcasted_iota(I32, (size, depth), 0)
    lane = lax.broadcasted_iota(I32, (size, depth), 1)
    parts = [
        ((row - offset_ref[k, i] == lane) & (lane < count_ref[k, i])).astype(F32).astype(BF16)
        for i in range(experts)
    ]
    selector = jnp.concatenate(parts, axis=1)
    for load in loads:
        load.wait()
    out_ref[...] = dot(selector, held[...]).astype(BF16)


def compact(offsets, counts, k, blocks, size):
    experts = len(blocks)
    depth, width = blocks[0].shape
    return pl.pallas_call(
        functools.partial(compact_kernel, experts, k),
        out_shape=jax.ShapeDtypeStruct((size, width), BF16),
        in_specs=[smem(), smem()] + apart(experts),
        out_specs=whole(1)[0],
        scratch_shapes=[pltpu.VMEM((experts * depth, width), BF16), pltpu.SemaphoreType.DMA((experts,))],
        compiler_params=params(),
        cost_estimate=COST,
    )(offsets, counts, *blocks)


def hidden_kernel(parts, order_ref, gate_ref, up_ref, *refs):
    xs, out_ref = refs[:parts], refs[parts]
    gate_held, up_held, x_held, sems = refs[parts + 1 :]
    width = xs[0].shape[1]
    loads = []
    for i in range(parts):
        first = pl.multiple_of(order_ref[i] * width, width)
        copies = [
            pltpu.make_async_copy(xs[i], x_held.at[i], sems.at[3 * i]),
            pltpu.make_async_copy(gate_ref.at[0, pl.ds(first, width), :], gate_held.at[i], sems.at[3 * i + 1]),
            pltpu.make_async_copy(up_ref.at[0, pl.ds(first, width), :], up_held.at[i], sems.at[3 * i + 2]),
        ]
        for copy in copies:
            copy.start()
        loads.append(copies)
    gate = up = None
    for i in range(parts):
        for copy in loads[i]:
            copy.wait()
        x = x_held[i]
        gate_term = dot(x, gate_held[i])
        up_term = dot(x, up_held[i])
        gate = gate_term if gate is None else gate + gate_term
        up = up_term if up is None else up + up_term
    out_ref[...] = (gate * jax.nn.sigmoid(gate) * up).astype(BF16)


def hidden_units(order, gate_weight, up_weight, xs):
    parts = len(xs)
    size, width = xs[0].shape
    units = gate_weight.shape[2]
    return pl.pallas_call(
        functools.partial(hidden_kernel, parts),
        out_shape=jax.ShapeDtypeStruct((size, units), BF16),
        in_specs=[smem()] + apart(2 + parts),
        out_specs=whole(1)[0],
        scratch_shapes=[
            pltpu.VMEM((parts, width, units), BF16),
            pltpu.VMEM((parts, width, units), BF16),
            pltpu.VMEM((parts, size, width), BF16),
            pltpu.SemaphoreType.DMA((3 * parts,)),
        ],
        compiler_params=params(),
        cost_estimate=COST,
    )(order, gate_weight, up_weight, *xs)


def down_kernel(parts, experts, k, order_ref, offset_ref, count_ref, down_ref, *refs):
    hs, outs = refs[:parts], refs[parts : parts + experts]
    down_held, h_held, staged, in_sems, out_sems = refs[parts + experts :]
    size, units = hs[0].shape
    depth = outs[0].shape[0]
    loads = []
    for i in range(parts):
        first = pl.multiple_of(order_ref[i] * units, units)
        copies = [
            pltpu.make_async_copy(hs[i], h_held.at[i], in_sems.at[2 * i]),
            pltpu.make_async_copy(down_ref.at[0, pl.ds(first, units), :], down_held.at[i], in_sems.at[2 * i + 1]),
        ]
        for copy in copies:
            copy.start()
        loads.append(copies)
    row = lax.broadcasted_iota(I32, (depth, size), 0)
    lane = lax.broadcasted_iota(I32, (depth, size), 1)
    total = None
    for i in range(parts):
        for copy in loads[i]:
            copy.wait()
        term = dot(h_held[i], down_held[i])
        total = term if total is None else total + term
    result = total.astype(BF16)
    copies = []
    for i in list(range(1, experts)) + [0]:
        pick = ((lane - offset_ref[k, i] == row) & (row < count_ref[k, i])).astype(F32).astype(BF16)
        staged[i] = dot(pick, result).astype(BF16)
        copy = pltpu.make_async_copy(staged.at[i], outs[i], out_sems.at[i])
        copy.start()
        copies.append(copy)
    for copy in copies:
        copy.wait()


def down_rows(order, offsets, counts, k, down_weight, hs, experts, depth):
    parts = len(hs)
    size, units = hs[0].shape
    width = down_weight.shape[2]
    return pl.pallas_call(
        functools.partial(down_kernel, parts, experts, k),
        out_shape=[jax.ShapeDtypeStruct((depth, width), BF16)] * experts,
        in_specs=[smem()] * 3 + apart(1 + parts),
        out_specs=apart(experts),
        scratch_shapes=[
            pltpu.VMEM((parts, units, width), BF16),
            pltpu.VMEM((parts, size, units), BF16),
            pltpu.VMEM((experts, depth, width), BF16),
            pltpu.SemaphoreType.DMA((2 * parts,)),
            pltpu.SemaphoreType.DMA((experts,)),
        ],
        compiler_params=params(),
        cost_estimate=COST,
    )(order, offsets, counts, down_weight, *hs)


def weight_kernel(experts, place_ref, own_ref, logits_ref, code_ref, out_ref, score_ref):
    me = place_ref[0]
    kernel = jnp.exp(logits_ref[...])
    row_scale = jnp.ones((kernel.shape[0], 1, kernel.shape[2]), F32)
    for sweep in range(3):
        column = jnp.sum(jnp.sum(kernel * row_scale, axis=0, keepdims=True), axis=2, keepdims=True)
        column_scale = 1.0 / column
        row_scale = 1.0 / jnp.sum(kernel * column_scale, axis=1, keepdims=True)
    own = jnp.exp(own_ref[...])
    column_scale = column_scale[0]
    own_scale = 1.0 / jnp.sum(own * column_scale, axis=0, keepdims=True)
    score_ref[...] = own_scale * own * column_scale
    picked = []
    for shift in range(experts):
        score = score_ref[pl.ds(lax.rem(me + shift, experts), 1), :]
        picked.append(jnp.where(code_ref[pl.ds(shift, 1), :] >= 0, score, 0.0))
    total = picked[0]
    for one in picked[1:]:
        total = total + one
    total = jnp.maximum(total, 1.0 / experts)
    for shift in range(experts):
        out_ref[pl.ds(shift, 1), :] = picked[shift] / total


def slot_weights(place, own, logits, code):
    experts, rows = own.shape
    return pl.pallas_call(
        functools.partial(weight_kernel, experts),
        out_shape=jax.ShapeDtypeStruct((experts, rows), F32),
        in_specs=[smem()] + whole(3),
        out_specs=whole(1)[0],
        scratch_shapes=[pltpu.VMEM((experts, rows), F32)],
        compiler_params=params(),
        cost_estimate=COST,
    )(place, own, logits, code)


def combine_kernel(experts, k, code_ref, weight_ref, *refs):
    count = experts + (k > 0)
    blocks, out_ref = refs[:count], refs[count]
    held, sems = refs[count + 1], refs[count + 2]
    depth = blocks[0].shape[0]
    rows = code_ref.shape[1]
    targets = [held.at[pl.ds(i * depth, depth)] for i in range(experts)]
    if k > 0:
        targets.append(refs[count + 3])
    loads = start_all(blocks, targets, sems)
    slot_ids = lax.broadcasted_iota(I32, (depth, rows), 0) + k * depth
    parts = [
        jnp.where(slot_ids == code_ref[pl.ds(i, 1), :], weight_ref[pl.ds(i, 1), :], 0.0).astype(BF16)
        for i in range(experts)
    ]
    spread = jnp.concatenate(parts, axis=0)
    for load in loads:
        load.wait()
    total = lax.dot_general(spread, held[...], (((0,), (0,)), ((), ())), preferred_element_type=F32)
    if k > 0:
        total = total + refs[count + 3][...]
    out_ref[...] = total.astype(out_ref.dtype)


def combine(code, weights, k, blocks, so_far):
    experts = len(blocks)
    depth, width = blocks[0].shape
    rows = code.shape[1]
    last = k == BATCHES - 1
    more = [] if so_far is None else [so_far]
    return pl.pallas_call(
        functools.partial(combine_kernel, experts, k),
        out_shape=jax.ShapeDtypeStruct((rows, width), BF16 if last else F32),
        in_specs=whole(2) + apart(experts + len(more)),
        out_specs=whole(1)[0],
        scratch_shapes=[
            pltpu.VMEM((experts * depth, width), BF16),
            pltpu.SemaphoreType.DMA((experts + len(more),)),
        ]
        + [pltpu.VMEM((rows, width), F32)] * len(more),
        compiler_params=params(),
        cost_estimate=COST,
    )(code, weights, *blocks, *more)


def after(value, *first):
    return lax.optimization_barrier((value, first))[0]


def shards(tokens, router_weight, gate_weight, up_weight, down_weight, picks):
    experts = lax.axis_size("expert")
    width_parts = lax.axis_size("dp")
    me = lax.axis_index("expert")
    part = lax.axis_index("dp")
    rows = tokens.shape[0]
    capacity = picks.shape[1]
    depth = 2 * capacity // experts // BATCHES
    size = capacity // BATCHES
    place = me.astype(I32).reshape(1)

    def along_expert(x, shift):
        return lax.ppermute(x, "expert", [(i, (i + shift) % experts) for i in range(experts)])

    def swap(x, bit):
        return lax.ppermute(x, "dp", [(i, i ^ bit) for i in range(width_parts)])

    bits = []
    bit = width_parts // 2
    while bit:
        bits.append(bit)
        bit //= 2
    masks = [0]
    for bit in bits:
        masks = masks + [m ^ bit for m in masks]
    order = jnp.stack([part ^ m for m in masks]).astype(I32)

    def all_parts(x):
        held = [x]
        for bit in bits:
            held = held + [swap(h, bit) for h in held]
        return held

    code, logits, first = first_batch(place, picks, router_weight.T, tokens, depth)
    later = [later_batch(code, tokens, k, depth) for k in range(1, BATCHES)]
    gathered = jnp.stack([logits] + [along_expert(logits, shift) for shift in range(1, experts)])
    first = [first[0]] + [after(block, logits) for block in first[1:]]
    arrived = [[first[0]] + [along_expert(first[shift], shift) for shift in range(1, experts)]]
    gathered = after(gathered, later)
    for bit in bits:
        gathered = gathered + swap(gathered, bit)
    weights = slot_weights(place, gathered[0], gathered, code)

    own_picks = lax.dynamic_slice_in_dim(picks, me, 1, axis=0)
    sources = lax.rem(me - jnp.arange(experts, dtype=I32) + experts, experts)
    start = jnp.sum((own_picks < (sources * rows)[:, None]).astype(I32), axis=1)
    stop = jnp.sum((own_picks < ((sources + 1) * rows)[:, None]).astype(I32), axis=1)
    ids = jnp.arange(BATCHES, dtype=I32)[:, None]
    offsets = (start[None, :] + (BATCHES - 1) - ids) // BATCHES
    counts = (stop[None, :] + (BATCHES - 1) - ids) // BATCHES - offsets
    offsets, counts, order = after((offsets, counts, order), code)

    def expert_rows(k, blocks):
        block = compact(offsets, counts, k, blocks, size)
        hidden = hidden_units(order, gate_weight, up_weight, all_parts(block))
        return tuple(down_rows(order, offsets, counts, k, down_weight, all_parts(hidden), experts, depth))

    def no_rows(k, blocks):
        return tuple(jnp.zeros_like(block) for block in blocks)

    waiting = []
    results = weights
    for k in range(BATCHES):
        moving = later[k] if k < BATCHES - 1 else None
        blocks, moving = after((arrived[k], moving), results, arrived[k])
        if moving is not None:
            arrived.append([moving[0]] + [along_expert(moving[shift], shift) for shift in range(1, experts)])
        results = lax.cond(
            jnp.sum(counts[k]) > 0, functools.partial(expert_rows, k), functools.partial(no_rows, k), list(blocks)
        )
        waiting.append([results[0]] + [along_expert(results[shift], -shift) for shift in range(1, experts)])
    total = None
    for k in range(BATCHES):
        blocks = waiting[k] if k == BATCHES - 1 else after(waiting[k], results)
        total = combine(code, weights, k, blocks, total)
    return total


def solution(mesh):
    return jax.shard_map(
        shards,
        mesh=mesh,
        in_specs=(
            P(("groups", "expert"), "dp"),
            P("dp", None),
            P("expert", None, "dp"),
            P("expert", None, "dp"),
            P("expert", None, "dp"),
            P("groups", None),
        ),
        out_specs=P(("groups", "expert"), "dp"),
        check_vma=False,
    )
```

```python
import functools

import jax
import jax.numpy as jnp
from jax import lax
from jax.experimental import pallas as pl
from jax.experimental.pallas import tpu as pltpu
from jax.sharding import PartitionSpec as P

BATCHES = 2
F32 = jnp.float32
BF16 = jnp.bfloat16
I32 = jnp.int32
VMEM_LIMIT = 24 * 1024 * 1024
COST = pl.CostEstimate(flops=1024, bytes_accessed=1024, transcendentals=0)


def whole(count):
    return [pl.BlockSpec(memory_space=pltpu.VMEM)] * count


def apart(count):
    return [pl.BlockSpec(memory_space=pl.ANY)] * count


def smem():
    return pl.BlockSpec(memory_space=pltpu.SMEM)


def params(limit=VMEM_LIMIT):
    return pltpu.CompilerParams(vmem_limit_bytes=limit)


def dot(a, b):
    return jnp.dot(a, b, preferred_element_type=F32)


def start_all(sources, targets, sems):
    copies = [pltpu.make_async_copy(a, b, sems.at[i]) for i, (a, b) in enumerate(zip(sources, targets))]
    for copy in copies:
        copy.start()
    return copies


def code_kernel(experts, depth, place_ref, picks_in, router_in, tokens_ref, code_ref, logits_ref, *refs):
    sends = refs[:experts]
    picks_ref, router_ref, held, staged, in_sems, out_sems = refs[experts:]
    picks_load, router_load, load = start_all(
        [picks_in, router_in, tokens_ref], [picks_ref, router_ref, held], in_sems
    )
    me = place_ref[0]
    rows, width = held.shape
    capacity = picks_ref.shape[1]
    strips = rows // 128
    lanes = lax.broadcasted_iota(I32, (128, capacity), 0)
    strip_ids = lax.broadcasted_iota(I32, (8, capacity), 0)
    upper = (lax.broadcasted_iota(I32, (128, 128), 0) < lax.broadcasted_iota(I32, (128, 128), 1)).astype(BF16)
    before = (lax.broadcasted_iota(I32, (8, 8), 1) < lax.broadcasted_iota(I32, (8, 8), 0)).astype(BF16)
    ones = jnp.ones((128, 128), BF16)
    picks_load.wait()
    code_rows = []
    for shift in range(experts):
        expert = lax.rem(me + shift, experts)
        chosen = picks_ref[pl.ds(expert, 1), :]
        local = chosen - me * rows
        start = jnp.sum((local < 0).astype(F32)).astype(I32)
        strip = lax.shift_right_arithmetic(local, 7)
        place = jnp.bitwise_and(local, 127)
        high = (strip == strip_ids).astype(BF16)
        high = jnp.where(strip_ids < strips, high, jnp.zeros_like(high))
        low = (place == lanes).astype(BF16)
        mask = lax.dot_general(high, low, (((1,), (1,)), ((), ())), preferred_element_type=F32)
        mask16 = mask.astype(BF16)
        totals = dot(mask16, ones)
        rank = (dot(mask16, upper) + dot(before, totals.astype(BF16))).astype(I32)
        batch = lax.rem(rank + start, BATCHES)
        slot = batch * depth + lax.div(rank, BATCHES)
        code = jnp.where(mask > 0.5, slot, -1)
        row = jnp.concatenate([code[i : i + 1] for i in range(strips)], axis=1)
        code_ref[pl.ds(shift, 1), :] = row
        code_rows.append(row)
    router_load.wait()
    load.wait()
    logits_ref[...] = lax.dot_general(
        router_ref[...], held[...], (((1,), (1,)), ((), ())), preferred_element_type=F32
    )
    pack(0, depth, code_rows, held, staged, sends, out_sems)


def pack(k, depth, code_rows, held, staged, sends, sems):
    slot_ids = lax.broadcasted_iota(I32, (depth, held.shape[0]), 0) + k * depth
    copies = []
    for shift in list(range(1, len(sends))) + [0]:
        selector = (slot_ids == code_rows[shift]).astype(F32).astype(BF16)
        staged[shift] = dot(selector, held[...]).astype(BF16)
        copy = pltpu.make_async_copy(staged.at[shift], sends[shift], sems.at[shift])
        copy.start()
        copies.append(copy)
    for copy in copies:
        copy.wait()


def first_batch(place, picks, router, tokens, depth):
    rows, width = tokens.shape
    experts = picks.shape[0]
    out = pl.pallas_call(
        functools.partial(code_kernel, experts, depth),
        out_shape=[jax.ShapeDtypeStruct((experts, rows), I32), jax.ShapeDtypeStruct((experts, rows), F32)]
        + [jax.ShapeDtypeStruct((depth, width), BF16)] * experts,
        in_specs=[smem()] + apart(3),
        out_specs=whole(2) + apart(experts),
        scratch_shapes=[
            pltpu.VMEM(picks.shape, I32),
            pltpu.VMEM(router.shape, BF16),
            pltpu.VMEM((rows, width), BF16),
            pltpu.VMEM((experts, depth, width), BF16),
            pltpu.SemaphoreType.DMA((3,)),
            pltpu.SemaphoreType.DMA((experts,)),
        ],
        compiler_params=params(60 * 1024 * 1024),
        cost_estimate=COST,
    )(place, picks, router, tokens)
    return out[0], out[1], out[2:]


def pack_kernel(experts, depth, k, code_ref, tokens_ref, *refs):
    sends = refs[:experts]
    held, staged, in_sems, out_sems = refs[experts:]
    start_all([tokens_ref], [held], in_sems)[0].wait()
    code_rows = [code_ref[pl.ds(shift, 1), :] for shift in range(experts)]
    pack(k, depth, code_rows, held, staged, sends, out_sems)


def later_batch(code, tokens, k, depth):
    rows, width = tokens.shape
    experts = code.shape[0]
    return pl.pallas_call(
        functools.partial(pack_kernel, experts, depth, k),
        out_shape=[jax.ShapeDtypeStruct((depth, width), BF16)] * experts,
        in_specs=whole(1) + apart(1),
        out_specs=apart(experts),
        scratch_shapes=[
            pltpu.VMEM((rows, width), BF16),
            pltpu.VMEM((experts, depth, width), BF16),
            pltpu.SemaphoreType.DMA((1,)),
            pltpu.SemaphoreType.DMA((experts,)),
        ],
        compiler_params=params(),
        cost_estimate=COST,
    )(code, tokens)


def compact_kernel(experts, k, offset_ref, count_ref, *refs):
    blocks, out_ref = refs[:experts], refs[experts]
    held, sems = refs[experts + 1 :]
    depth = blocks[0].shape[0]
    size = out_ref.shape[0]
    loads = start_all(blocks, [held.at[pl.ds(i * depth, depth)] for i in range(experts)], sems)
    row = lax.broadcasted_iota(I32, (size, depth), 0)
    lane = lax.broadcasted_iota(I32, (size, depth), 1)
    parts = [
        ((row - offset_ref[k, i] == lane) & (lane < count_ref[k, i])).astype(F32).astype(BF16)
        for i in range(experts)
    ]
    selector = jnp.concatenate(parts, axis=1)
    for load in loads:
        load.wait()
    out_ref[...] = dot(selector, held[...]).astype(BF16)


def compact(offsets, counts, k, blocks, size):
    experts = len(blocks)
    depth, width = blocks[0].shape
    return pl.pallas_call(
        functools.partial(compact_kernel, experts, k),
        out_shape=jax.ShapeDtypeStruct((size, width), BF16),
        in_specs=[smem(), smem()] + apart(experts),
        out_specs=whole(1)[0],
        scratch_shapes=[pltpu.VMEM((experts * depth, width), BF16), pltpu.SemaphoreType.DMA((experts,))],
        compiler_params=params(),
        cost_estimate=COST,
    )(offsets, counts, *blocks)


def gate_up_kernel(parts, places, last, order_ref, gate_ref, up_ref, *refs):
    xs, refs = refs[:parts], refs[parts:]
    if last:
        gate_before, up_before, out_ref, *refs = refs
    else:
        gate_out, up_out, *refs = refs
    gate_held, up_held, x_held, sems = refs
    width = xs[0].shape[1]
    loads = []
    for i in range(parts):
        first = pl.multiple_of(order_ref[places[i]] * width, width)
        copies = [
            pltpu.make_async_copy(xs[i], x_held.at[i], sems.at[3 * i]),
            pltpu.make_async_copy(gate_ref.at[0, pl.ds(first, width), :], gate_held.at[i], sems.at[3 * i + 1]),
            pltpu.make_async_copy(up_ref.at[0, pl.ds(first, width), :], up_held.at[i], sems.at[3 * i + 2]),
        ]
        for copy in copies:
            copy.start()
        loads.append(copies)
    gate, up = (gate_before[...], up_before[...]) if last else (None, None)
    for i in range(parts):
        for copy in loads[i]:
            copy.wait()
        x = x_held[i]
        gate_term = dot(x, gate_held[i])
        up_term = dot(x, up_held[i])
        gate = gate_term if gate is None else gate + gate_term
        up = up_term if up is None else up + up_term
    if last:
        out_ref[...] = (gate * jax.nn.sigmoid(gate) * up).astype(BF16)
    else:
        gate_out[...] = gate
        up_out[...] = up


def gate_up(order, places, gate_weight, up_weight, xs, before):
    parts = len(xs)
    size, width = xs[0].shape
    units = gate_weight.shape[2]
    last = before is not None
    sums = [jax.ShapeDtypeStruct((size, units), F32)] * 2
    return pl.pallas_call(
        functools.partial(gate_up_kernel, parts, places, last),
        out_shape=jax.ShapeDtypeStruct((size, units), BF16) if last else sums,
        in_specs=[smem()] + apart(2 + parts) + (whole(2) if last else []),
        out_specs=whole(1)[0] if last else whole(2),
        scratch_shapes=[
            pltpu.VMEM((parts, width, units), BF16),
            pltpu.VMEM((parts, width, units), BF16),
            pltpu.VMEM((parts, size, width), BF16),
            pltpu.SemaphoreType.DMA((3 * parts,)),
        ],
        compiler_params=params(),
        cost_estimate=COST,
    )(order, gate_weight, up_weight, *xs, *(before or []))


def down_sum(places, order_ref, down_ref, hs, down_held, h_held, sems, total):
    units = hs[0].shape[1]
    loads = []
    for i in range(len(hs)):
        first = pl.multiple_of(order_ref[places[i]] * units, units)
        copies = [
            pltpu.make_async_copy(hs[i], h_held.at[i], sems.at[2 * i]),
            pltpu.make_async_copy(down_ref.at[0, pl.ds(first, units), :], down_held.at[i], sems.at[2 * i + 1]),
        ]
        for copy in copies:
            copy.start()
        loads.append(copies)
    for i in range(len(hs)):
        for copy in loads[i]:
            copy.wait()
        term = dot(h_held[i], down_held[i])
        total = term if total is None else total + term
    return total


def down_first_kernel(parts, places, order_ref, down_ref, *refs):
    hs, out_ref = refs[:parts], refs[parts]
    out_ref[...] = down_sum(places, order_ref, down_ref, hs, *refs[parts + 1 :], None)


def down_last_kernel(parts, places, experts, k, order_ref, offset_ref, count_ref, down_ref, *refs):
    hs, before, outs = refs[:parts], refs[parts], refs[parts + 1 : parts + 1 + experts]
    down_held, h_held, in_sems, staged, out_sems = refs[parts + 1 + experts :]
    size = hs[0].shape[0]
    depth = outs[0].shape[0]
    total = down_sum(places, order_ref, down_ref, hs, down_held, h_held, in_sems, before[...])
    result = total.astype(BF16)
    row = lax.broadcasted_iota(I32, (depth, size), 0)
    lane = lax.broadcasted_iota(I32, (depth, size), 1)
    copies = []
    for i in list(range(1, experts)) + [0]:
        pick = ((lane - offset_ref[k, i] == row) & (row < count_ref[k, i])).astype(F32).astype(BF16)
        staged[i] = dot(pick, result).astype(BF16)
        copy = pltpu.make_async_copy(staged.at[i], outs[i], out_sems.at[i])
        copy.start()
        copies.append(copy)
    for copy in copies:
        copy.wait()


def down_scratch(parts, size, units, width):
    return [
        pltpu.VMEM((parts, units, width), BF16),
        pltpu.VMEM((parts, size, units), BF16),
        pltpu.SemaphoreType.DMA((2 * parts,)),
    ]


def down_first(order, places, down_weight, hs):
    parts = len(hs)
    size, units = hs[0].shape
    width = down_weight.shape[2]
    return pl.pallas_call(
        functools.partial(down_first_kernel, parts, places),
        out_shape=jax.ShapeDtypeStruct((size, width), F32),
        in_specs=[smem()] + apart(1 + parts),
        out_specs=whole(1)[0],
        scratch_shapes=down_scratch(parts, size, units, width),
        compiler_params=params(),
        cost_estimate=COST,
    )(order, down_weight, *hs)


def down_last(order, places, offsets, counts, k, down_weight, hs, before, experts, depth):
    parts = len(hs)
    size, units = hs[0].shape
    width = down_weight.shape[2]
    return pl.pallas_call(
        functools.partial(down_last_kernel, parts, places, experts, k),
        out_shape=[jax.ShapeDtypeStruct((depth, width), BF16)] * experts,
        in_specs=[smem()] * 3 + apart(1 + parts) + whole(1),
        out_specs=apart(experts),
        scratch_shapes=down_scratch(parts, size, units, width)
        + [pltpu.VMEM((experts, depth, width), BF16), pltpu.SemaphoreType.DMA((experts,))],
        compiler_params=params(),
        cost_estimate=COST,
    )(order, offsets, counts, down_weight, *hs, before)


def weight_kernel(experts, place_ref, own_ref, logits_ref, code_ref, out_ref, score_ref):
    me = place_ref[0]
    kernel = jnp.exp(logits_ref[...])
    row_scale = jnp.ones((kernel.shape[0], 1, kernel.shape[2]), F32)
    for sweep in range(3):
        column = jnp.sum(jnp.sum(kernel * row_scale, axis=0, keepdims=True), axis=2, keepdims=True)
        column_scale = 1.0 / column
        row_scale = 1.0 / jnp.sum(kernel * column_scale, axis=1, keepdims=True)
    own = jnp.exp(own_ref[...])
    column_scale = column_scale[0]
    own_scale = 1.0 / jnp.sum(own * column_scale, axis=0, keepdims=True)
    score_ref[...] = own_scale * own * column_scale
    picked = []
    for shift in range(experts):
        score = score_ref[pl.ds(lax.rem(me + shift, experts), 1), :]
        picked.append(jnp.where(code_ref[pl.ds(shift, 1), :] >= 0, score, 0.0))
    total = picked[0]
    for one in picked[1:]:
        total = total + one
    total = jnp.maximum(total, 1.0 / experts)
    for shift in range(experts):
        out_ref[pl.ds(shift, 1), :] = picked[shift] / total


def slot_weights(place, own, logits, code):
    experts, rows = own.shape
    return pl.pallas_call(
        functools.partial(weight_kernel, experts),
        out_shape=jax.ShapeDtypeStruct((experts, rows), F32),
        in_specs=[smem()] + whole(3),
        out_specs=whole(1)[0],
        scratch_shapes=[pltpu.VMEM((experts, rows), F32)],
        compiler_params=params(),
        cost_estimate=COST,
    )(place, own, logits, code)


def combine_kernel(experts, k, code_ref, weight_ref, *refs):
    count = experts + (k > 0)
    blocks, out_ref = refs[:count], refs[count]
    held, sems = refs[count + 1], refs[count + 2]
    depth = blocks[0].shape[0]
    rows = code_ref.shape[1]
    targets = [held.at[pl.ds(i * depth, depth)] for i in range(experts)]
    if k > 0:
        targets.append(refs[count + 3])
    loads = start_all(blocks, targets, sems)
    slot_ids = lax.broadcasted_iota(I32, (depth, rows), 0) + k * depth
    parts = [
        jnp.where(slot_ids == code_ref[pl.ds(i, 1), :], weight_ref[pl.ds(i, 1), :], 0.0).astype(BF16)
        for i in range(experts)
    ]
    spread = jnp.concatenate(parts, axis=0)
    for load in loads:
        load.wait()
    total = lax.dot_general(spread, held[...], (((0,), (0,)), ((), ())), preferred_element_type=F32)
    if k > 0:
        total = total + refs[count + 3][...]
    out_ref[...] = total.astype(out_ref.dtype)


def combine(code, weights, k, blocks, so_far):
    experts = len(blocks)
    depth, width = blocks[0].shape
    rows = code.shape[1]
    last = k == BATCHES - 1
    more = [] if so_far is None else [so_far]
    return pl.pallas_call(
        functools.partial(combine_kernel, experts, k),
        out_shape=jax.ShapeDtypeStruct((rows, width), BF16 if last else F32),
        in_specs=whole(2) + apart(experts + len(more)),
        out_specs=whole(1)[0],
        scratch_shapes=[
            pltpu.VMEM((experts * depth, width), BF16),
            pltpu.SemaphoreType.DMA((experts + len(more),)),
        ]
        + [pltpu.VMEM((rows, width), F32)] * len(more),
        compiler_params=params(),
        cost_estimate=COST,
    )(code, weights, *blocks, *more)


def after(value, *first):
    return lax.optimization_barrier((value, first))[0]


def shards(tokens, router_weight, gate_weight, up_weight, down_weight, picks):
    experts = lax.axis_size("expert")
    width_parts = lax.axis_size("dp")
    me = lax.axis_index("expert")
    part = lax.axis_index("dp")
    rows = tokens.shape[0]
    capacity = picks.shape[1]
    depth = 2 * capacity // experts // BATCHES
    size = capacity // BATCHES
    place = me.astype(I32).reshape(1)

    def along_expert(x, shift):
        return lax.ppermute(x, "expert", [(i, (i + shift) % experts) for i in range(experts)])

    def swap(x, bit):
        return lax.ppermute(x, "dp", [(i, i ^ bit) for i in range(width_parts)])

    bits = []
    bit = width_parts // 2
    while bit:
        bits.append(bit)
        bit //= 2
    near = [0]
    for bit in bits[1:]:
        near = near + [m ^ bit for m in near]
    masks = near + [m ^ bits[0] for m in near]
    places = range(len(masks))
    near_places, far_places = places[: len(near)], places[len(near) :]
    order = jnp.stack([part ^ m for m in masks]).astype(I32)

    def swap_expert(x, bit):
        return lax.ppermute(x, "expert", [(i, i ^ bit) for i in range(experts)])

    expert_bits = [1 << i for i in range(experts.bit_length() - 1)]

    def spread(x):
        held = [x]
        for bit in bits[1:]:
            held = held + [swap(h, bit) for h in held]
        return held

    def both_parts(x):
        far = swap(x, bits[0])
        return spread(x), spread(far)

    code, logits, first = first_batch(place, picks, router_weight.T, tokens, depth)
    own_picks = lax.dynamic_slice_in_dim(picks, me, 1, axis=0)
    sources = lax.rem(me - jnp.arange(experts, dtype=I32) + experts, experts)
    start = jnp.sum((own_picks < (sources * rows)[:, None]).astype(I32), axis=1)
    stop = jnp.sum((own_picks < ((sources + 1) * rows)[:, None]).astype(I32), axis=1)
    ids = jnp.arange(BATCHES, dtype=I32)[:, None]
    offsets = (start[None, :] + (BATCHES - 1) - ids) // BATCHES
    counts = (stop[None, :] + (BATCHES - 1) - ids) // BATCHES - offsets

    present = [jnp.sum(counts[k]) > 0 for k in range(BATCHES)]

    def beside_first(logits):
        later = [tuple(later_batch(code, tokens, k, depth)) for k in range(1, BATCHES)]
        for bit in bits:
            logits = logits + swap(logits, bit)
        gathered = logits[None]
        for bit in expert_bits[:-1]:
            gathered = jnp.concatenate([gathered, swap_expert(gathered, bit)])
        return later, logits, gathered

    def nothing_first(logits):
        return jax.tree.map(lambda x: jnp.zeros(x.shape, x.dtype), jax.eval_shape(beside_first, logits))

    arrived = [[first[0]] + [along_expert(first[shift], shift) for shift in range(1, experts)]]
    later, logits, gathered = lax.cond(present[0], beside_first, nothing_first, logits)

    def expert_rows(k, blocks):
        block = compact(offsets, counts, k, blocks, size)
        near, far = both_parts(block)
        sums = gate_up(order, near_places, gate_weight, up_weight, near, None)
        hidden = gate_up(order, far_places, gate_weight, up_weight, far, sums)
        near, far = both_parts(hidden)
        partial = down_first(order, near_places, down_weight, near)
        return tuple(
            down_last(order, far_places, offsets, counts, k, down_weight, far, partial, experts, depth)
        )

    def no_rows(k, blocks):
        return tuple(jnp.zeros_like(block) for block in blocks)

    waiting = []
    results = gathered
    for k in range(BATCHES):
        moving = later[k] if k < BATCHES - 1 else None
        blocks, moving = after((arrived[k], moving), results, arrived[k])
        if moving is not None:
            arrived.append([moving[0]] + [along_expert(moving[shift], shift) for shift in range(1, experts)])
        if k == 0:
            gathered = after(gathered, blocks)
            gathered = jnp.concatenate([gathered, swap_expert(gathered, expert_bits[-1])])
        results = lax.cond(
            present[k], functools.partial(expert_rows, k), functools.partial(no_rows, k), list(blocks)
        )
        if moving is not None:
            results, arrived[k + 1] = lax.optimization_barrier((results, arrived[k + 1]))
        if k == 0:
            results = after(results, gathered)
        else:
            results, waiting[k - 1] = lax.optimization_barrier((results, waiting[k - 1]))
        waiting.append([results[0]] + [along_expert(results[shift], -shift) for shift in range(1, experts)])
    weights = slot_weights(place, logits, after(gathered, results), code)
    total = None
    for k in range(BATCHES):
        total = combine(code, weights, k, waiting[k], total)
    return total


def solution(mesh):
    return jax.shard_map(
        shards,
        mesh=mesh,
        in_specs=(
            P(("groups", "expert"), "dp"),
            P("dp", None),
            P("expert", None, "dp"),
            P("expert", None, "dp"),
            P("expert", None, "dp"),
            P("groups", None),
        ),
        out_specs=P(("groups", "expert"), "dp"),
        check_vma=False,
    )
```

```python
import functools

import jax
import jax.numpy as jnp
from jax import lax
from jax.experimental import pallas as pl
from jax.experimental.pallas import tpu as pltpu
from jax.sharding import PartitionSpec as P

BATCHES = 2
F32 = jnp.float32
BF16 = jnp.bfloat16
I32 = jnp.int32
VMEM_LIMIT = 24 * 1024 * 1024
COST = pl.CostEstimate(flops=1024, bytes_accessed=1024, transcendentals=0)


def whole(count):
    return [pl.BlockSpec(memory_space=pltpu.VMEM)] * count


def apart(count):
    return [pl.BlockSpec(memory_space=pl.ANY)] * count


def smem():
    return pl.BlockSpec(memory_space=pltpu.SMEM)


def params(limit=VMEM_LIMIT):
    return pltpu.CompilerParams(vmem_limit_bytes=limit)


def dot(a, b):
    return jnp.dot(a, b, preferred_element_type=F32)


def start_all(sources, targets, sems):
    copies = [pltpu.make_async_copy(a, b, sems.at[i]) for i, (a, b) in enumerate(zip(sources, targets))]
    for copy in copies:
        copy.start()
    return copies


def code_kernel(experts, depth, place_ref, picks_in, router_in, tokens_ref, code_ref, logits_ref, *refs):
    sends = refs[:experts]
    picks_ref, router_ref, held, staged, in_sems, out_sems = refs[experts:]
    picks_load, router_load, load = start_all(
        [picks_in, router_in, tokens_ref], [picks_ref, router_ref, held], in_sems
    )
    me = place_ref[0]
    rows, width = held.shape
    capacity = picks_ref.shape[1]
    strips = rows // 128
    lanes = lax.broadcasted_iota(I32, (128, capacity), 0)
    strip_ids = lax.broadcasted_iota(I32, (8, capacity), 0)
    upper = (lax.broadcasted_iota(I32, (128, 128), 0) < lax.broadcasted_iota(I32, (128, 128), 1)).astype(BF16)
    before = (lax.broadcasted_iota(I32, (8, 8), 1) < lax.broadcasted_iota(I32, (8, 8), 0)).astype(BF16)
    ones = jnp.ones((128, 128), BF16)
    picks_load.wait()
    code_rows = []
    for shift in range(experts):
        expert = lax.rem(me + shift, experts)
        chosen = picks_ref[pl.ds(expert, 1), :]
        local = chosen - me * rows
        start = jnp.sum((local < 0).astype(F32)).astype(I32)
        strip = lax.shift_right_arithmetic(local, 7)
        place = jnp.bitwise_and(local, 127)
        high = (strip == strip_ids).astype(BF16)
        high = jnp.where(strip_ids < strips, high, jnp.zeros_like(high))
        low = (place == lanes).astype(BF16)
        mask = lax.dot_general(high, low, (((1,), (1,)), ((), ())), preferred_element_type=F32)
        mask16 = mask.astype(BF16)
        totals = dot(mask16, ones)
        rank = (dot(mask16, upper) + dot(before, totals.astype(BF16))).astype(I32)
        batch = lax.rem(rank + start, BATCHES)
        slot = batch * depth + lax.div(rank, BATCHES)
        code = jnp.where(mask > 0.5, slot, -1)
        row = jnp.concatenate([code[i : i + 1] for i in range(strips)], axis=1)
        code_ref[pl.ds(shift, 1), :] = row
        code_rows.append(row)
    router_load.wait()
    load.wait()
    logits_ref[...] = lax.dot_general(
        router_ref[...], held[...], (((1,), (1,)), ((), ())), preferred_element_type=F32
    )
    pack(0, depth, code_rows, held, staged, sends, out_sems)


def pack(k, depth, code_rows, held, staged, sends, sems):
    slot_ids = lax.broadcasted_iota(I32, (depth, held.shape[0]), 0) + k * depth
    copies = []
    for shift in list(range(1, len(sends))) + [0]:
        selector = (slot_ids == code_rows[shift]).astype(F32).astype(BF16)
        staged[shift] = dot(selector, held[...]).astype(BF16)
        copy = pltpu.make_async_copy(staged.at[shift], sends[shift], sems.at[shift])
        copy.start()
        copies.append(copy)
    for copy in copies:
        copy.wait()


def first_batch(place, picks, router, tokens, depth):
    rows, width = tokens.shape
    experts = picks.shape[0]
    out = pl.pallas_call(
        functools.partial(code_kernel, experts, depth),
        out_shape=[jax.ShapeDtypeStruct((experts, rows), I32), jax.ShapeDtypeStruct((experts, rows), F32)]
        + [jax.ShapeDtypeStruct((depth, width), BF16)] * experts,
        in_specs=[smem()] + apart(3),
        out_specs=whole(2) + apart(experts),
        scratch_shapes=[
            pltpu.VMEM(picks.shape, I32),
            pltpu.VMEM(router.shape, BF16),
            pltpu.VMEM((rows, width), BF16),
            pltpu.VMEM((experts, depth, width), BF16),
            pltpu.SemaphoreType.DMA((3,)),
            pltpu.SemaphoreType.DMA((experts,)),
        ],
        compiler_params=params(60 * 1024 * 1024),
        cost_estimate=COST,
    )(place, picks, router, tokens)
    return out[0], out[1], out[2:]


def pack_kernel(experts, depth, k, code_ref, tokens_ref, *refs):
    sends = refs[:experts]
    held, staged, in_sems, out_sems = refs[experts:]
    start_all([tokens_ref], [held], in_sems)[0].wait()
    code_rows = [code_ref[pl.ds(shift, 1), :] for shift in range(experts)]
    pack(k, depth, code_rows, held, staged, sends, out_sems)


def later_batch(code, tokens, k, depth):
    rows, width = tokens.shape
    experts = code.shape[0]
    return pl.pallas_call(
        functools.partial(pack_kernel, experts, depth, k),
        out_shape=[jax.ShapeDtypeStruct((depth, width), BF16)] * experts,
        in_specs=whole(1) + apart(1),
        out_specs=apart(experts),
        scratch_shapes=[
            pltpu.VMEM((rows, width), BF16),
            pltpu.VMEM((experts, depth, width), BF16),
            pltpu.SemaphoreType.DMA((1,)),
            pltpu.SemaphoreType.DMA((experts,)),
        ],
        compiler_params=params(),
        cost_estimate=COST,
    )(code, tokens)


def compact_kernel(experts, k, offset_ref, count_ref, *refs):
    blocks, out_ref = refs[:experts], refs[experts]
    held, sems = refs[experts + 1 :]
    depth = blocks[0].shape[0]
    size = out_ref.shape[0]
    loads = start_all(blocks, [held.at[pl.ds(i * depth, depth)] for i in range(experts)], sems)
    row = lax.broadcasted_iota(I32, (size, depth), 0)
    lane = lax.broadcasted_iota(I32, (size, depth), 1)
    parts = [
        ((row - offset_ref[k, i] == lane) & (lane < count_ref[k, i])).astype(F32).astype(BF16)
        for i in range(experts)
    ]
    selector = jnp.concatenate(parts, axis=1)
    for load in loads:
        load.wait()
    out_ref[...] = dot(selector, held[...]).astype(BF16)


def compact(offsets, counts, k, blocks, size):
    experts = len(blocks)
    depth, width = blocks[0].shape
    return pl.pallas_call(
        functools.partial(compact_kernel, experts, k),
        out_shape=jax.ShapeDtypeStruct((size, width), BF16),
        in_specs=[smem(), smem()] + apart(experts),
        out_specs=whole(1)[0],
        scratch_shapes=[pltpu.VMEM((experts * depth, width), BF16), pltpu.SemaphoreType.DMA((experts,))],
        compiler_params=params(),
        cost_estimate=COST,
    )(offsets, counts, *blocks)


def gate_up_kernel(parts, places, last, order_ref, gate_ref, up_ref, *refs):
    xs, refs = refs[:parts], refs[parts:]
    if last:
        gate_before, up_before, out_ref, *refs = refs
    else:
        gate_out, up_out, *refs = refs
    gate_held, up_held, x_held, sems = refs
    width = xs[0].shape[1]
    loads = []
    for i in range(parts):
        first = pl.multiple_of(order_ref[places[i]] * width, width)
        copies = [
            pltpu.make_async_copy(xs[i], x_held.at[i], sems.at[3 * i]),
            pltpu.make_async_copy(gate_ref.at[0, pl.ds(first, width), :], gate_held.at[i], sems.at[3 * i + 1]),
            pltpu.make_async_copy(up_ref.at[0, pl.ds(first, width), :], up_held.at[i], sems.at[3 * i + 2]),
        ]
        for copy in copies:
            copy.start()
        loads.append(copies)
    gate, up = (gate_before[...], up_before[...]) if last else (None, None)
    for i in range(parts):
        for copy in loads[i]:
            copy.wait()
        x = x_held[i]
        gate_term = dot(x, gate_held[i])
        up_term = dot(x, up_held[i])
        gate = gate_term if gate is None else gate + gate_term
        up = up_term if up is None else up + up_term
    if last:
        out_ref[...] = (gate * jax.nn.sigmoid(gate) * up).astype(BF16)
    else:
        gate_out[...] = gate
        up_out[...] = up


def gate_up(order, places, gate_weight, up_weight, xs, before):
    parts = len(xs)
    size, width = xs[0].shape
    units = gate_weight.shape[2]
    last = before is not None
    sums = [jax.ShapeDtypeStruct((size, units), F32)] * 2
    return pl.pallas_call(
        functools.partial(gate_up_kernel, parts, places, last),
        out_shape=jax.ShapeDtypeStruct((size, units), BF16) if last else sums,
        in_specs=[smem()] + apart(2 + parts) + (whole(2) if last else []),
        out_specs=whole(1)[0] if last else whole(2),
        scratch_shapes=[
            pltpu.VMEM((parts, width, units), BF16),
            pltpu.VMEM((parts, width, units), BF16),
            pltpu.VMEM((parts, size, width), BF16),
            pltpu.SemaphoreType.DMA((3 * parts,)),
        ],
        compiler_params=params(),
        cost_estimate=COST,
    )(order, gate_weight, up_weight, *xs, *(before or []))


def down_sum(places, order_ref, down_ref, hs, down_held, h_held, sems, total):
    units = hs[0].shape[1]
    loads = []
    for i in range(len(hs)):
        first = pl.multiple_of(order_ref[places[i]] * units, units)
        copies = [
            pltpu.make_async_copy(hs[i], h_held.at[i], sems.at[2 * i]),
            pltpu.make_async_copy(down_ref.at[0, pl.ds(first, units), :], down_held.at[i], sems.at[2 * i + 1]),
        ]
        for copy in copies:
            copy.start()
        loads.append(copies)
    for i in range(len(hs)):
        for copy in loads[i]:
            copy.wait()
        term = dot(h_held[i], down_held[i])
        total = term if total is None else total + term
    return total


def down_first_kernel(parts, places, order_ref, down_ref, *refs):
    hs, out_ref = refs[:parts], refs[parts]
    out_ref[...] = down_sum(places, order_ref, down_ref, hs, *refs[parts + 1 :], None)


def down_last_kernel(parts, places, experts, k, order_ref, offset_ref, count_ref, down_ref, *refs):
    hs, before, outs = refs[:parts], refs[parts], refs[parts + 1 : parts + 1 + experts]
    down_held, h_held, in_sems, staged, out_sems = refs[parts + 1 + experts :]
    size = hs[0].shape[0]
    depth = outs[0].shape[0]
    total = down_sum(places, order_ref, down_ref, hs, down_held, h_held, in_sems, before[...])
    result = total.astype(BF16)
    row = lax.broadcasted_iota(I32, (depth, size), 0)
    lane = lax.broadcasted_iota(I32, (depth, size), 1)
    copies = []
    for i in list(range(1, experts)) + [0]:
        pick = ((lane - offset_ref[k, i] == row) & (row < count_ref[k, i])).astype(F32).astype(BF16)
        staged[i] = dot(pick, result).astype(BF16)
        copy = pltpu.make_async_copy(staged.at[i], outs[i], out_sems.at[i])
        copy.start()
        copies.append(copy)
    for copy in copies:
        copy.wait()


def down_scratch(parts, size, units, width):
    return [
        pltpu.VMEM((parts, units, width), BF16),
        pltpu.VMEM((parts, size, units), BF16),
        pltpu.SemaphoreType.DMA((2 * parts,)),
    ]


def down_first(order, places, down_weight, hs):
    parts = len(hs)
    size, units = hs[0].shape
    width = down_weight.shape[2]
    return pl.pallas_call(
        functools.partial(down_first_kernel, parts, places),
        out_shape=jax.ShapeDtypeStruct((size, width), F32),
        in_specs=[smem()] + apart(1 + parts),
        out_specs=whole(1)[0],
        scratch_shapes=down_scratch(parts, size, units, width),
        compiler_params=params(),
        cost_estimate=COST,
    )(order, down_weight, *hs)


def down_last(order, places, offsets, counts, k, down_weight, hs, before, experts, depth):
    parts = len(hs)
    size, units = hs[0].shape
    width = down_weight.shape[2]
    return pl.pallas_call(
        functools.partial(down_last_kernel, parts, places, experts, k),
        out_shape=[jax.ShapeDtypeStruct((depth, width), BF16)] * experts,
        in_specs=[smem()] * 3 + apart(1 + parts) + whole(1),
        out_specs=apart(experts),
        scratch_shapes=down_scratch(parts, size, units, width)
        + [pltpu.VMEM((experts, depth, width), BF16), pltpu.SemaphoreType.DMA((experts,))],
        compiler_params=params(),
        cost_estimate=COST,
    )(order, offsets, counts, down_weight, *hs, before)


def weight_kernel(experts, place_ref, own_ref, logits_ref, code_ref, out_ref, score_ref):
    me = place_ref[0]
    kernel = jnp.exp(logits_ref[...])
    row_scale = jnp.ones((kernel.shape[0], 1, kernel.shape[2]), F32)
    for sweep in range(3):
        column = jnp.sum(jnp.sum(kernel * row_scale, axis=0, keepdims=True), axis=2, keepdims=True)
        column_scale = 1.0 / column
        row_scale = 1.0 / jnp.sum(kernel * column_scale, axis=1, keepdims=True)
    own = jnp.exp(own_ref[...])
    column_scale = column_scale[0]
    own_scale = 1.0 / jnp.sum(own * column_scale, axis=0, keepdims=True)
    score_ref[...] = own_scale * own * column_scale
    picked = []
    for shift in range(experts):
        score = score_ref[pl.ds(lax.rem(me + shift, experts), 1), :]
        picked.append(jnp.where(code_ref[pl.ds(shift, 1), :] >= 0, score, 0.0))
    total = picked[0]
    for one in picked[1:]:
        total = total + one
    total = jnp.maximum(total, 1.0 / experts)
    for shift in range(experts):
        out_ref[pl.ds(shift, 1), :] = picked[shift] / total


def slot_weights(place, own, logits, code):
    experts, rows = own.shape
    return pl.pallas_call(
        functools.partial(weight_kernel, experts),
        out_shape=jax.ShapeDtypeStruct((experts, rows), F32),
        in_specs=[smem()] + whole(3),
        out_specs=whole(1)[0],
        scratch_shapes=[pltpu.VMEM((experts, rows), F32)],
        compiler_params=params(),
        cost_estimate=COST,
    )(place, own, logits, code)


def combine_kernel(experts, k, code_ref, weight_ref, *refs):
    count = experts + (k > 0)
    blocks, out_ref = refs[:count], refs[count]
    held, sems = refs[count + 1], refs[count + 2]
    depth = blocks[0].shape[0]
    rows = code_ref.shape[1]
    targets = [held.at[pl.ds(i * depth, depth)] for i in range(experts)]
    if k > 0:
        targets.append(refs[count + 3])
    loads = start_all(blocks, targets, sems)
    slot_ids = lax.broadcasted_iota(I32, (depth, rows), 0) + k * depth
    parts = [
        jnp.where(slot_ids == code_ref[pl.ds(i, 1), :], weight_ref[pl.ds(i, 1), :], 0.0).astype(BF16)
        for i in range(experts)
    ]
    spread = jnp.concatenate(parts, axis=0)
    for load in loads:
        load.wait()
    total = lax.dot_general(spread, held[...], (((0,), (0,)), ((), ())), preferred_element_type=F32)
    if k > 0:
        total = total + refs[count + 3][...]
    out_ref[...] = total.astype(out_ref.dtype)


def combine(code, weights, k, blocks, so_far):
    experts = len(blocks)
    depth, width = blocks[0].shape
    rows = code.shape[1]
    last = k == BATCHES - 1
    more = [] if so_far is None else [so_far]
    return pl.pallas_call(
        functools.partial(combine_kernel, experts, k),
        out_shape=jax.ShapeDtypeStruct((rows, width), BF16 if last else F32),
        in_specs=whole(2) + apart(experts + len(more)),
        out_specs=whole(1)[0],
        scratch_shapes=[
            pltpu.VMEM((experts * depth, width), BF16),
            pltpu.SemaphoreType.DMA((experts + len(more),)),
        ]
        + [pltpu.VMEM((rows, width), F32)] * len(more),
        compiler_params=params(),
        cost_estimate=COST,
    )(code, weights, *blocks, *more)


def after(value, *first):
    return lax.optimization_barrier((value, first))[0]


def shards(tokens, router_weight, gate_weight, up_weight, down_weight, picks):
    experts = lax.axis_size("expert")
    width_parts = lax.axis_size("dp")
    me = lax.axis_index("expert")
    part = lax.axis_index("dp")
    rows = tokens.shape[0]
    capacity = picks.shape[1]
    depth = 2 * capacity // experts // BATCHES
    size = capacity // BATCHES
    place = me.astype(I32).reshape(1)

    def along_expert(x, shift):
        return lax.ppermute(x, "expert", [(i, (i + shift) % experts) for i in range(experts)])

    def swap(x, bit):
        return lax.ppermute(x, "dp", [(i, i ^ bit) for i in range(width_parts)])

    bits = []
    bit = width_parts // 2
    while bit:
        bits.append(bit)
        bit //= 2
    near = [0]
    for bit in bits[1:]:
        near = near + [m ^ bit for m in near]
    masks = near + [m ^ bits[0] for m in near]
    places = range(len(masks))
    near_places, far_places = places[: len(near)], places[len(near) :]
    order = jnp.stack([part ^ m for m in masks]).astype(I32)

    def swap_expert(x, bit):
        return lax.ppermute(x, "expert", [(i, i ^ bit) for i in range(experts)])

    expert_bits = [1 << i for i in range(experts.bit_length() - 1)]

    def spread(x):
        held = [x]
        for bit in bits[1:]:
            held = held + [swap(h, bit) for h in held]
        return held

    def both_parts(x):
        far = swap(x, bits[0])
        return spread(x), spread(far)

    code, logits, first = first_batch(place, picks, router_weight.T, tokens, depth)
    own_picks = lax.dynamic_slice_in_dim(picks, me, 1, axis=0)
    sources = lax.rem(me - jnp.arange(experts, dtype=I32) + experts, experts)
    start = jnp.sum((own_picks < (sources * rows)[:, None]).astype(I32), axis=1)
    stop = jnp.sum((own_picks < ((sources + 1) * rows)[:, None]).astype(I32), axis=1)
    ids = jnp.arange(BATCHES, dtype=I32)[:, None]
    offsets = (start[None, :] + (BATCHES - 1) - ids) // BATCHES
    counts = (stop[None, :] + (BATCHES - 1) - ids) // BATCHES - offsets

    present = [jnp.sum(counts[k]) > 0 for k in range(BATCHES)]

    def beside_first(logits):
        later = [tuple(later_batch(code, tokens, k, depth)) for k in range(1, BATCHES)]
        for bit in bits:
            logits = logits + swap(logits, bit)
        gathered = logits[None]
        for bit in expert_bits:
            gathered = jnp.concatenate([gathered, swap_expert(gathered, bit)])
        return later, logits, gathered

    def nothing_first(logits):
        return jax.tree.map(lambda x: jnp.zeros(x.shape, x.dtype), jax.eval_shape(beside_first, logits))

    arrived = [[first[0]] + [along_expert(first[shift], shift) for shift in range(1, experts)]]
    later, logits, gathered = lax.cond(present[0], beside_first, nothing_first, logits)

    def far_half(far, sums):
        far = spread(far)
        hidden = gate_up(order, far_places, gate_weight, up_weight, far, sums)
        far = swap(hidden, bits[0])
        partial = down_first(order, near_places, down_weight, spread(hidden))
        far, partial = lax.optimization_barrier((far, partial))
        return spread(far), partial

    def settle(k, far, partial):
        return tuple(
            down_last(order, far_places, offsets, counts, k, down_weight, far, partial, experts, depth)
        )

    def fenced(k, run, *operands):
        def skip(*operands):
            return jax.tree.map(lambda x: jnp.zeros(x.shape, x.dtype), jax.eval_shape(run, *operands))

        return lax.cond(present[k], run, skip, *operands)

    def send_back(results):
        return [results[0]] + [along_expert(results[shift], -shift) for shift in range(1, experts)]

    waiting = []
    far = partial = None
    moved = gathered
    for k in range(BATCHES):
        blocks = after(arrived[k], moved)
        if k < BATCHES - 1:
            moving = after(later[k], blocks)
            arrived.append([moving[0]] + [along_expert(moving[shift], shift) for shift in range(1, experts)])
        block = fenced(k, lambda *blocks: compact(offsets, counts, k, blocks, size), *blocks)
        across = swap(block, bits[0])
        near = spread(block)
        if k > 0:
            far, partial = after((far, partial), block)
            results = fenced(k, functools.partial(settle, k - 1), far, partial)
            if k > 1:
                results, waiting[k - 2] = lax.optimization_barrier((results, waiting[k - 2]))
            waiting.append(send_back(results))
            near = after(near, results)
        sums = fenced(k, lambda *near: gate_up(order, near_places, gate_weight, up_weight, near, None), *near)
        across, sums = lax.optimization_barrier((across, sums))
        far, partial = fenced(k, far_half, across, sums)
        moved = partial
    results = fenced(0, functools.partial(settle, BATCHES - 1), far, partial)
    results, waiting[-1] = lax.optimization_barrier((results, waiting[-1]))
    waiting.append(send_back(results))
    weights = slot_weights(place, logits, after(gathered, results), code)
    total = None
    for k in range(BATCHES):
        total = combine(code, weights, k, waiting[k], total)
    return total


def solution(mesh):
    return jax.shard_map(
        shards,
        mesh=mesh,
        in_specs=(
            P(("groups", "expert"), "dp"),
            P("dp", None),
            P("expert", None, "dp"),
            P("expert", None, "dp"),
            P("expert", None, "dp"),
            P("groups", None),
        ),
        out_specs=P(("groups", "expert"), "dp"),
        check_vma=False,
    )
```

```python
import functools

import jax
import jax.numpy as jnp
from jax import lax
from jax.experimental import pallas as pl
from jax.experimental.pallas import tpu as pltpu
from jax.sharding import PartitionSpec as P

BATCHES = 2
F32 = jnp.float32
BF16 = jnp.bfloat16
I32 = jnp.int32
VMEM_LIMIT = 16 * 1024 * 1024
COST = pl.CostEstimate(flops=1024, bytes_accessed=1024, transcendentals=0)


def whole(count):
    return [pl.BlockSpec(memory_space=pltpu.VMEM)] * count


def apart(count):
    return [pl.BlockSpec(memory_space=pl.ANY)] * count


def smem():
    return pl.BlockSpec(memory_space=pltpu.SMEM)


def params(limit=VMEM_LIMIT):
    return pltpu.CompilerParams(vmem_limit_bytes=limit)


def dot(a, b):
    return jnp.dot(a, b, preferred_element_type=F32)


def start_all(sources, targets, sems):
    copies = [pltpu.make_async_copy(a, b, sems.at[i]) for i, (a, b) in enumerate(zip(sources, targets))]
    for copy in copies:
        copy.start()
    return copies


def code_kernel(experts, depth, place_ref, picks_in, router_in, tokens_ref, code_ref, logits_ref, *refs):
    sends = refs[:experts]
    picks_ref, router_ref, held, staged, in_sems, out_sems = refs[experts:]
    picks_load, router_load, load = start_all(
        [picks_in, router_in, tokens_ref], [picks_ref, router_ref, held], in_sems
    )
    me = place_ref[0]
    rows, width = held.shape
    capacity = picks_ref.shape[1]
    strips = rows // 128
    lanes = lax.broadcasted_iota(I32, (128, capacity), 0)
    strip_ids = lax.broadcasted_iota(I32, (8, capacity), 0)
    upper = (lax.broadcasted_iota(I32, (128, 128), 0) < lax.broadcasted_iota(I32, (128, 128), 1)).astype(BF16)
    before = (lax.broadcasted_iota(I32, (8, 8), 1) < lax.broadcasted_iota(I32, (8, 8), 0)).astype(BF16)
    ones = jnp.ones((128, 128), BF16)
    picks_load.wait()
    code_rows = []
    for shift in range(experts):
        expert = lax.rem(me + shift, experts)
        chosen = picks_ref[pl.ds(expert, 1), :]
        local = chosen - me * rows
        start = jnp.sum((local < 0).astype(F32)).astype(I32)
        strip = lax.shift_right_arithmetic(local, 7)
        place = jnp.bitwise_and(local, 127)
        high = (strip == strip_ids).astype(BF16)
        high = jnp.where(strip_ids < strips, high, jnp.zeros_like(high))
        low = (place == lanes).astype(BF16)
        mask = lax.dot_general(high, low, (((1,), (1,)), ((), ())), preferred_element_type=F32)
        mask16 = mask.astype(BF16)
        totals = dot(mask16, ones)
        rank = (dot(mask16, upper) + dot(before, totals.astype(BF16))).astype(I32)
        batch = lax.rem(rank + start, BATCHES)
        slot = batch * depth + lax.div(rank, BATCHES)
        code = jnp.where(mask > 0.5, slot, -1)
        row = jnp.concatenate([code[i : i + 1] for i in range(strips)], axis=1)
        code_ref[pl.ds(shift, 1), :] = row
        code_rows.append(row)
    router_load.wait()
    load.wait()
    logits_ref[...] = lax.dot_general(
        router_ref[...], held[...], (((1,), (1,)), ((), ())), preferred_element_type=F32
    )
    pack(0, depth, code_rows, held, staged, sends, out_sems)


def pack(k, depth, code_rows, held, staged, sends, sems):
    slot_ids = lax.broadcasted_iota(I32, (depth, held.shape[0]), 0) + k * depth
    copies = []
    for shift in list(range(1, len(sends))) + [0]:
        selector = (slot_ids == code_rows[shift]).astype(F32).astype(BF16)
        staged[shift] = dot(selector, held[...]).astype(BF16)
        copy = pltpu.make_async_copy(staged.at[shift], sends[shift], sems.at[shift])
        copy.start()
        copies.append(copy)
    for copy in copies:
        copy.wait()


def first_batch(place, picks, router, tokens, depth):
    rows, width = tokens.shape
    experts = picks.shape[0]
    out = pl.pallas_call(
        functools.partial(code_kernel, experts, depth),
        out_shape=[jax.ShapeDtypeStruct((experts, rows), I32), jax.ShapeDtypeStruct((experts, rows), F32)]
        + [jax.ShapeDtypeStruct((depth, width), BF16)] * experts,
        in_specs=[smem()] + apart(3),
        out_specs=whole(2) + apart(experts),
        scratch_shapes=[
            pltpu.VMEM(picks.shape, I32),
            pltpu.VMEM(router.shape, BF16),
            pltpu.VMEM((rows, width), BF16),
            pltpu.VMEM((experts, depth, width), BF16),
            pltpu.SemaphoreType.DMA((3,)),
            pltpu.SemaphoreType.DMA((experts,)),
        ],
        compiler_params=params(60 * 1024 * 1024),
        cost_estimate=COST,
    )(place, picks, router, tokens)
    return out[0], out[1], out[2:]


def pack_kernel(experts, depth, k, code_ref, tokens_ref, *refs):
    sends = refs[:experts]
    held, staged, in_sems, out_sems = refs[experts:]
    start_all([tokens_ref], [held], in_sems)[0].wait()
    code_rows = [code_ref[pl.ds(shift, 1), :] for shift in range(experts)]
    pack(k, depth, code_rows, held, staged, sends, out_sems)


def later_batch(code, tokens, k, depth):
    rows, width = tokens.shape
    experts = code.shape[0]
    return pl.pallas_call(
        functools.partial(pack_kernel, experts, depth, k),
        out_shape=[jax.ShapeDtypeStruct((depth, width), BF16)] * experts,
        in_specs=whole(1) + apart(1),
        out_specs=apart(experts),
        scratch_shapes=[
            pltpu.VMEM((rows, width), BF16),
            pltpu.VMEM((experts, depth, width), BF16),
            pltpu.SemaphoreType.DMA((1,)),
            pltpu.SemaphoreType.DMA((experts,)),
        ],
        compiler_params=params(),
        cost_estimate=COST,
    )(code, tokens)


def compact_kernel(experts, k, offset_ref, count_ref, *refs):
    blocks, out_ref = refs[:experts], refs[experts]
    held, sems = refs[experts + 1 :]
    depth = blocks[0].shape[0]
    size = out_ref.shape[0]
    loads = start_all(blocks, [held.at[pl.ds(i * depth, depth)] for i in range(experts)], sems)
    row = lax.broadcasted_iota(I32, (size, depth), 0)
    lane = lax.broadcasted_iota(I32, (size, depth), 1)
    parts = [
        ((row - offset_ref[k, i] == lane) & (lane < count_ref[k, i])).astype(F32).astype(BF16)
        for i in range(experts)
    ]
    selector = jnp.concatenate(parts, axis=1)
    for load in loads:
        load.wait()
    out_ref[...] = dot(selector, held[...]).astype(BF16)


def compact(offsets, counts, k, blocks, size):
    experts = len(blocks)
    depth, width = blocks[0].shape
    return pl.pallas_call(
        functools.partial(compact_kernel, experts, k),
        out_shape=jax.ShapeDtypeStruct((size, width), BF16),
        in_specs=[smem(), smem()] + apart(experts),
        out_specs=whole(1)[0],
        scratch_shapes=[pltpu.VMEM((experts * depth, width), BF16), pltpu.SemaphoreType.DMA((experts,))],
        compiler_params=params(),
        cost_estimate=COST,
    )(offsets, counts, *blocks)


def gate_up_kernel(parts, places, last, order_ref, gate_ref, up_ref, *refs):
    xs, refs = refs[:parts], refs[parts:]
    if last:
        gate_before, up_before, out_ref, *refs = refs
    else:
        gate_out, up_out, *refs = refs
    x_held, sems = refs
    width = xs[0].shape[1]
    loads = start_all(xs, [x_held.at[i] for i in range(parts)], sems)
    gate, up = (gate_before[...], up_before[...]) if last else (None, None)
    for i in range(parts):
        first = pl.multiple_of(order_ref[places[i]] * width, width)
        loads[i].wait()
        x = x_held[i]
        gate_term = dot(x, gate_ref[0, pl.ds(first, width), :])
        up_term = dot(x, up_ref[0, pl.ds(first, width), :])
        gate = gate_term if gate is None else gate + gate_term
        up = up_term if up is None else up + up_term
    if last:
        out_ref[...] = (gate * jax.nn.sigmoid(gate) * up).astype(BF16)
    else:
        gate_out[...] = gate
        up_out[...] = up


def gate_up(order, places, gate_weight, up_weight, xs, before):
    parts = len(xs)
    size, width = xs[0].shape
    units = gate_weight.shape[2]
    last = before is not None
    sums = [jax.ShapeDtypeStruct((size, units), F32)] * 2
    return pl.pallas_call(
        functools.partial(gate_up_kernel, parts, places, last),
        out_shape=jax.ShapeDtypeStruct((size, units), BF16) if last else sums,
        in_specs=[smem()] + whole(2) + apart(parts) + (whole(2) if last else []),
        out_specs=whole(1)[0] if last else whole(2),
        scratch_shapes=[
            pltpu.VMEM((parts, size, width), BF16),
            pltpu.SemaphoreType.DMA((parts,)),
        ],
        compiler_params=params(),
        cost_estimate=COST,
    )(order, gate_weight, up_weight, *xs, *(before or []))


def down_sum(places, order_ref, down_ref, hs, h_held, sems, total):
    units = hs[0].shape[1]
    loads = start_all(hs, [h_held.at[i] for i in range(len(hs))], sems)
    for i in range(len(hs)):
        first = pl.multiple_of(order_ref[places[i]] * units, units)
        loads[i].wait()
        term = dot(h_held[i], down_ref[0, pl.ds(first, units), :])
        total = term if total is None else total + term
    return total


def down_first_kernel(parts, places, order_ref, down_ref, *refs):
    hs, out_ref = refs[:parts], refs[parts]
    out_ref[...] = down_sum(places, order_ref, down_ref, hs, *refs[parts + 1 :], None)


def down_last_kernel(parts, places, experts, k, order_ref, offset_ref, count_ref, down_ref, *refs):
    hs, before, outs = refs[:parts], refs[parts], refs[parts + 1 : parts + 1 + experts]
    h_held, in_sems, staged, out_sems = refs[parts + 1 + experts :]
    size = hs[0].shape[0]
    depth = outs[0].shape[0]
    total = down_sum(places, order_ref, down_ref, hs, h_held, in_sems, before[...])
    result = total.astype(BF16)
    row = lax.broadcasted_iota(I32, (depth, size), 0)
    lane = lax.broadcasted_iota(I32, (depth, size), 1)
    copies = []
    for i in list(range(1, experts)) + [0]:
        pick = ((lane - offset_ref[k, i] == row) & (row < count_ref[k, i])).astype(F32).astype(BF16)
        staged[i] = dot(pick, result).astype(BF16)
        copy = pltpu.make_async_copy(staged.at[i], outs[i], out_sems.at[i])
        copy.start()
        copies.append(copy)
    for copy in copies:
        copy.wait()


def down_scratch(parts, size, units):
    return [pltpu.VMEM((parts, size, units), BF16), pltpu.SemaphoreType.DMA((parts,))]


def down_first(order, places, down_weight, hs):
    parts = len(hs)
    size, units = hs[0].shape
    width = down_weight.shape[2]
    return pl.pallas_call(
        functools.partial(down_first_kernel, parts, places),
        out_shape=jax.ShapeDtypeStruct((size, width), F32),
        in_specs=[smem()] + whole(1) + apart(parts),
        out_specs=whole(1)[0],
        scratch_shapes=down_scratch(parts, size, units),
        compiler_params=params(),
        cost_estimate=COST,
    )(order, down_weight, *hs)


def down_last(order, places, offsets, counts, k, down_weight, hs, before, experts, depth):
    parts = len(hs)
    size, units = hs[0].shape
    width = down_weight.shape[2]
    return pl.pallas_call(
        functools.partial(down_last_kernel, parts, places, experts, k),
        out_shape=[jax.ShapeDtypeStruct((depth, width), BF16)] * experts,
        in_specs=[smem()] * 3 + whole(1) + apart(parts) + whole(1),
        out_specs=apart(experts),
        scratch_shapes=down_scratch(parts, size, units)
        + [pltpu.VMEM((experts, depth, width), BF16), pltpu.SemaphoreType.DMA((experts,))],
        compiler_params=params(),
        cost_estimate=COST,
    )(order, offsets, counts, down_weight, *hs, before)


def weight_kernel(experts, place_ref, own_ref, logits_ref, code_ref, out_ref, score_ref):
    me = place_ref[0]
    kernel = jnp.exp(logits_ref[...])
    row_scale = jnp.ones((kernel.shape[0], 1, kernel.shape[2]), F32)
    for sweep in range(3):
        column = jnp.sum(jnp.sum(kernel * row_scale, axis=0, keepdims=True), axis=2, keepdims=True)
        column_scale = 1.0 / column
        row_scale = 1.0 / jnp.sum(kernel * column_scale, axis=1, keepdims=True)
    own = jnp.exp(own_ref[...])
    column_scale = column_scale[0]
    own_scale = 1.0 / jnp.sum(own * column_scale, axis=0, keepdims=True)
    score_ref[...] = own_scale * own * column_scale
    picked = []
    for shift in range(experts):
        score = score_ref[pl.ds(lax.rem(me + shift, experts), 1), :]
        picked.append(jnp.where(code_ref[pl.ds(shift, 1), :] >= 0, score, 0.0))
    total = picked[0]
    for one in picked[1:]:
        total = total + one
    total = jnp.maximum(total, 1.0 / experts)
    for shift in range(experts):
        out_ref[pl.ds(shift, 1), :] = picked[shift] / total


def slot_weights(place, own, logits, code):
    experts, rows = own.shape
    return pl.pallas_call(
        functools.partial(weight_kernel, experts),
        out_shape=jax.ShapeDtypeStruct((experts, rows), F32),
        in_specs=[smem()] + whole(3),
        out_specs=whole(1)[0],
        scratch_shapes=[pltpu.VMEM((experts, rows), F32)],
        compiler_params=params(),
        cost_estimate=COST,
    )(place, own, logits, code)


def combine_kernel(experts, k, code_ref, weight_ref, *refs):
    count = experts + (k > 0)
    blocks, out_ref = refs[:count], refs[count]
    held, sems = refs[count + 1], refs[count + 2]
    depth = blocks[0].shape[0]
    rows = code_ref.shape[1]
    targets = [held.at[pl.ds(i * depth, depth)] for i in range(experts)]
    if k > 0:
        targets.append(refs[count + 3])
    loads = start_all(blocks, targets, sems)
    slot_ids = lax.broadcasted_iota(I32, (depth, rows), 0) + k * depth
    parts = [
        jnp.where(slot_ids == code_ref[pl.ds(i, 1), :], weight_ref[pl.ds(i, 1), :], 0.0).astype(BF16)
        for i in range(experts)
    ]
    spread = jnp.concatenate(parts, axis=0)
    for load in loads:
        load.wait()
    total = lax.dot_general(spread, held[...], (((0,), (0,)), ((), ())), preferred_element_type=F32)
    if k > 0:
        total = total + refs[count + 3][...]
    out_ref[...] = total.astype(out_ref.dtype)


def combine(code, weights, k, blocks, so_far):
    experts = len(blocks)
    depth, width = blocks[0].shape
    rows = code.shape[1]
    last = k == BATCHES - 1
    more = [] if so_far is None else [so_far]
    return pl.pallas_call(
        functools.partial(combine_kernel, experts, k),
        out_shape=jax.ShapeDtypeStruct((rows, width), BF16 if last else F32),
        in_specs=whole(2) + apart(experts + len(more)),
        out_specs=whole(1)[0],
        scratch_shapes=[
            pltpu.VMEM((experts * depth, width), BF16),
            pltpu.SemaphoreType.DMA((experts + len(more),)),
        ]
        + [pltpu.VMEM((rows, width), F32)] * len(more),
        compiler_params=params(),
        cost_estimate=COST,
    )(code, weights, *blocks, *more)


def after(value, *first):
    return lax.optimization_barrier((value, first))[0]


def shards(tokens, router_weight, gate_weight, up_weight, down_weight, picks):
    experts = lax.axis_size("expert")
    width_parts = lax.axis_size("dp")
    me = lax.axis_index("expert")
    part = lax.axis_index("dp")
    rows = tokens.shape[0]
    capacity = picks.shape[1]
    depth = 2 * capacity // experts // BATCHES
    size = capacity // BATCHES
    place = me.astype(I32).reshape(1)

    def along_expert(x, shift):
        return lax.ppermute(x, "expert", [(i, (i + shift) % experts) for i in range(experts)])

    def swap(x, bit):
        return lax.ppermute(x, "dp", [(i, i ^ bit) for i in range(width_parts)])

    bits = []
    bit = width_parts // 2
    while bit:
        bits.append(bit)
        bit //= 2
    near = [0]
    for bit in bits[1:]:
        near = near + [m ^ bit for m in near]
    masks = near + [m ^ bits[0] for m in near]
    places = range(len(masks))
    near_places, far_places = places[: len(near)], places[len(near) :]
    order = jnp.stack([part ^ m for m in masks]).astype(I32)

    def swap_expert(x, bit):
        return lax.ppermute(x, "expert", [(i, i ^ bit) for i in range(experts)])

    expert_bits = [1 << i for i in range(experts.bit_length() - 1)]

    def spread(x):
        held = [x]
        for bit in bits[1:]:
            held = held + [swap(h, bit) for h in held]
        return held

    def both_parts(x):
        far = swap(x, bits[0])
        return spread(x), spread(far)

    code, logits, first = first_batch(place, picks, router_weight.T, tokens, depth)
    own_picks = lax.dynamic_slice_in_dim(picks, me, 1, axis=0)
    sources = lax.rem(me - jnp.arange(experts, dtype=I32) + experts, experts)
    start = jnp.sum((own_picks < (sources * rows)[:, None]).astype(I32), axis=1)
    stop = jnp.sum((own_picks < ((sources + 1) * rows)[:, None]).astype(I32), axis=1)
    ids = jnp.arange(BATCHES, dtype=I32)[:, None]
    offsets = (start[None, :] + (BATCHES - 1) - ids) // BATCHES
    counts = (stop[None, :] + (BATCHES - 1) - ids) // BATCHES - offsets

    present = [jnp.sum(counts[k]) > 0 for k in range(BATCHES)]

    def beside_first(logits):
        later = [tuple(later_batch(code, tokens, k, depth)) for k in range(1, BATCHES)]
        for bit in bits:
            logits = logits + swap(logits, bit)
        gathered = logits[None]
        for bit in expert_bits:
            gathered = jnp.concatenate([gathered, swap_expert(gathered, bit)])
        return later, logits, gathered

    def nothing_first(logits):
        return jax.tree.map(lambda x: jnp.zeros(x.shape, x.dtype), jax.eval_shape(beside_first, logits))

    arrived = [[first[0]] + [along_expert(first[shift], shift) for shift in range(1, experts)]]
    later, logits, gathered = lax.cond(present[0], beside_first, nothing_first, logits)

    def far_half(far, sums):
        far = spread(far)
        hidden = gate_up(order, far_places, gate_weight, up_weight, far, sums)
        far = swap(hidden, bits[0])
        partial = down_first(order, near_places, down_weight, spread(hidden))
        far, partial = lax.optimization_barrier((far, partial))
        return spread(far), partial

    def whole_chain(*blocks):
        block = compact(offsets, counts, 0, blocks, size)
        across = swap(block, bits[0])
        sums = gate_up(order, near_places, gate_weight, up_weight, spread(block), None)
        across, sums = lax.optimization_barrier((across, sums))
        return far_half(across, sums)

    def settle(k, far, partial):
        return tuple(
            down_last(order, far_places, offsets, counts, k, down_weight, far, partial, experts, depth)
        )

    def fenced(k, run, *operands):
        def skip(*operands):
            return jax.tree.map(lambda x: jnp.zeros(x.shape, x.dtype), jax.eval_shape(run, *operands))

        return lax.cond(present[k], run, skip, *operands)

    def send_back(results):
        return [results[0]] + [along_expert(results[shift], -shift) for shift in range(1, experts)]

    waiting = []
    far = partial = None
    moved = gathered
    for k in range(BATCHES):
        blocks = after(arrived[k], moved)
        if k < BATCHES - 1:
            moving = after(later[k], blocks)
            arrived.append([moving[0]] + [along_expert(moving[shift], shift) for shift in range(1, experts)])
        if k == 0:
            far, partial = fenced(k, whole_chain, *blocks)
            moved = partial
            continue
        block = fenced(k, lambda *blocks: compact(offsets, counts, k, blocks, size), *blocks)
        across = swap(block, bits[0])
        near = spread(block)
        far, partial = after((far, partial), block)
        results = fenced(k, functools.partial(settle, k - 1), far, partial)
        if k > 1:
            results, waiting[k - 2] = lax.optimization_barrier((results, waiting[k - 2]))
        waiting.append(send_back(results))
        near = after(near, results)
        sums = fenced(k, lambda *near: gate_up(order, near_places, gate_weight, up_weight, near, None), *near)
        across, sums = lax.optimization_barrier((across, sums))
        far, partial = fenced(k, far_half, across, sums)
        moved = partial
    results = fenced(0, functools.partial(settle, BATCHES - 1), far, partial)
    results, waiting[-1] = lax.optimization_barrier((results, waiting[-1]))
    waiting.append(send_back(results))
    weights = slot_weights(place, logits, after(gathered, results), code)
    total = None
    for k in range(BATCHES):
        total = combine(code, weights, k, waiting[k], total)
    return total


def solution(mesh):
    return jax.shard_map(
        shards,
        mesh=mesh,
        in_specs=(
            P(("groups", "expert"), "dp"),
            P("dp", None),
            P("expert", None, "dp"),
            P("expert", None, "dp"),
            P("expert", None, "dp"),
            P("groups", None),
        ),
        out_specs=P(("groups", "expert"), "dp"),
        check_vma=False,
    )
```

```python
import functools

import jax
import jax.numpy as jnp
from jax import lax
from jax.experimental import pallas as pl
from jax.experimental.pallas import tpu as pltpu
from jax.sharding import PartitionSpec as P

BATCHES = 2
F32 = jnp.float32
BF16 = jnp.bfloat16
I32 = jnp.int32
VMEM_LIMIT = 16 * 1024 * 1024
COST = pl.CostEstimate(flops=1024, bytes_accessed=1024, transcendentals=0)


def whole(count):
    return [pl.BlockSpec(memory_space=pltpu.VMEM)] * count


def apart(count):
    return [pl.BlockSpec(memory_space=pl.ANY)] * count


def smem():
    return pl.BlockSpec(memory_space=pltpu.SMEM)


def params(limit=VMEM_LIMIT):
    return pltpu.CompilerParams(vmem_limit_bytes=limit)


def dot(a, b):
    return jnp.dot(a, b, preferred_element_type=F32)


def start_all(sources, targets, sems):
    copies = [pltpu.make_async_copy(a, b, sems.at[i]) for i, (a, b) in enumerate(zip(sources, targets))]
    for copy in copies:
        copy.start()
    return copies


def code_kernel(experts, depth, place_ref, picks_in, router_in, tokens_ref, code_ref, logits_ref, *refs):
    sends = refs[:experts]
    picks_ref, router_ref, held, staged, in_sems, out_sems = refs[experts:]
    picks_load, router_load, load = start_all(
        [picks_in, router_in, tokens_ref], [picks_ref, router_ref, held], in_sems
    )
    me = place_ref[0]
    rows, width = held.shape
    capacity = picks_ref.shape[1]
    strips = rows // 128
    lanes = lax.broadcasted_iota(I32, (128, capacity), 0)
    strip_ids = lax.broadcasted_iota(I32, (8, capacity), 0)
    upper = (lax.broadcasted_iota(I32, (128, 128), 0) < lax.broadcasted_iota(I32, (128, 128), 1)).astype(BF16)
    before = (lax.broadcasted_iota(I32, (8, 8), 1) < lax.broadcasted_iota(I32, (8, 8), 0)).astype(BF16)
    ones = jnp.ones((128, 128), BF16)
    picks_load.wait()
    code_rows = []
    for shift in range(experts):
        expert = lax.rem(me + shift, experts)
        chosen = picks_ref[pl.ds(expert, 1), :]
        local = chosen - me * rows
        start = jnp.sum((local < 0).astype(F32)).astype(I32)
        strip = lax.shift_right_arithmetic(local, 7)
        place = jnp.bitwise_and(local, 127)
        high = (strip == strip_ids).astype(BF16)
        high = jnp.where(strip_ids < strips, high, jnp.zeros_like(high))
        low = (place == lanes).astype(BF16)
        mask = lax.dot_general(high, low, (((1,), (1,)), ((), ())), preferred_element_type=F32)
        mask16 = mask.astype(BF16)
        totals = dot(mask16, ones)
        rank = (dot(mask16, upper) + dot(before, totals.astype(BF16))).astype(I32)
        batch = lax.rem(rank + start, BATCHES)
        slot = batch * depth + lax.div(rank, BATCHES)
        code = jnp.where(mask > 0.5, slot, -1)
        row = jnp.concatenate([code[i : i + 1] for i in range(strips)], axis=1)
        code_ref[pl.ds(shift, 1), :] = row
        code_rows.append(row)
    router_load.wait()
    load.wait()
    logits_ref[...] = lax.dot_general(
        router_ref[...], held[...], (((1,), (1,)), ((), ())), preferred_element_type=F32
    )
    pack(0, depth, code_rows, held, staged, sends, out_sems)


def pack(k, depth, code_rows, held, staged, sends, sems):
    slot_ids = lax.broadcasted_iota(I32, (depth, held.shape[0]), 0) + k * depth
    copies = []
    for shift in list(range(1, len(sends))) + [0]:
        selector = (slot_ids == code_rows[shift]).astype(F32).astype(BF16)
        staged[shift] = dot(selector, held[...]).astype(BF16)
        copy = pltpu.make_async_copy(staged.at[shift], sends[shift], sems.at[shift])
        copy.start()
        copies.append(copy)
    for copy in copies:
        copy.wait()


def first_batch(place, picks, router, tokens, depth):
    rows, width = tokens.shape
    experts = picks.shape[0]
    out = pl.pallas_call(
        functools.partial(code_kernel, experts, depth),
        out_shape=[jax.ShapeDtypeStruct((experts, rows), I32), jax.ShapeDtypeStruct((experts, rows), F32)]
        + [jax.ShapeDtypeStruct((depth, width), BF16)] * experts,
        in_specs=[smem()] + apart(3),
        out_specs=whole(2) + apart(experts),
        scratch_shapes=[
            pltpu.VMEM(picks.shape, I32),
            pltpu.VMEM(router.shape, BF16),
            pltpu.VMEM((rows, width), BF16),
            pltpu.VMEM((experts, depth, width), BF16),
            pltpu.SemaphoreType.DMA((3,)),
            pltpu.SemaphoreType.DMA((experts,)),
        ],
        compiler_params=params(60 * 1024 * 1024),
        cost_estimate=COST,
    )(place, picks, router, tokens)
    return out[0], out[1], out[2:]


def pack_kernel(experts, depth, k, code_ref, tokens_ref, *refs):
    sends = refs[:experts]
    held, staged, in_sems, out_sems = refs[experts:]
    start_all([tokens_ref], [held], in_sems)[0].wait()
    code_rows = [code_ref[pl.ds(shift, 1), :] for shift in range(experts)]
    pack(k, depth, code_rows, held, staged, sends, out_sems)


def later_batch(code, tokens, k, depth):
    rows, width = tokens.shape
    experts = code.shape[0]
    return pl.pallas_call(
        functools.partial(pack_kernel, experts, depth, k),
        out_shape=[jax.ShapeDtypeStruct((depth, width), BF16)] * experts,
        in_specs=whole(1) + apart(1),
        out_specs=apart(experts),
        scratch_shapes=[
            pltpu.VMEM((rows, width), BF16),
            pltpu.VMEM((experts, depth, width), BF16),
            pltpu.SemaphoreType.DMA((1,)),
            pltpu.SemaphoreType.DMA((experts,)),
        ],
        compiler_params=params(),
        cost_estimate=COST,
    )(code, tokens)


def compact_kernel(experts, k, offset_ref, count_ref, *refs):
    blocks, out_ref = refs[:experts], refs[experts]
    held, sems = refs[experts + 1 :]
    depth = blocks[0].shape[0]
    size = out_ref.shape[0]
    loads = start_all(blocks, [held.at[pl.ds(i * depth, depth)] for i in range(experts)], sems)
    row = lax.broadcasted_iota(I32, (size, depth), 0)
    lane = lax.broadcasted_iota(I32, (size, depth), 1)
    parts = [
        ((row - offset_ref[k, i] == lane) & (lane < count_ref[k, i])).astype(F32).astype(BF16)
        for i in range(experts)
    ]
    selector = jnp.concatenate(parts, axis=1)
    for load in loads:
        load.wait()
    out_ref[...] = dot(selector, held[...]).astype(BF16)


def compact(offsets, counts, k, blocks, size):
    experts = len(blocks)
    depth, width = blocks[0].shape
    return pl.pallas_call(
        functools.partial(compact_kernel, experts, k),
        out_shape=jax.ShapeDtypeStruct((size, width), BF16),
        in_specs=[smem(), smem()] + apart(experts),
        out_specs=whole(1)[0],
        scratch_shapes=[pltpu.VMEM((experts * depth, width), BF16), pltpu.SemaphoreType.DMA((experts,))],
        compiler_params=params(),
        cost_estimate=COST,
    )(offsets, counts, *blocks)


def gate_up_near_kernel(parts, near, far, order_ref, gate_ref, up_ref, *refs):
    xs, refs = refs[:parts], refs[parts:]
    gate_out, up_out, gate_far, up_far, gate_held, up_held, x_held, sems = refs
    width = xs[0].shape[1]

    def fetch(i, place, gate_to, up_to, base):
        first = pl.multiple_of(order_ref[place] * width, width)
        return start_all(
            [gate_ref.at[0, pl.ds(first, width), :], up_ref.at[0, pl.ds(first, width), :]],
            [gate_to.at[i], up_to.at[i]],
            sems.at[pl.ds(base, 2)],
        )

    x_loads = start_all(xs, [x_held.at[i] for i in range(parts)], sems.at[pl.ds(0, parts)])
    loads = [fetch(i, near[i], gate_held, up_held, parts + 2 * i) for i in range(parts)]
    late = [fetch(i, far[i], gate_far, up_far, 3 * parts + 2 * i) for i in range(len(far))]
    gate = up = None
    for i in range(parts):
        for copy in [x_loads[i]] + loads[i]:
            copy.wait()
        x = x_held[i]
        gate_term = dot(x, gate_held[i])
        up_term = dot(x, up_held[i])
        gate = gate_term if gate is None else gate + gate_term
        up = up_term if up is None else up + up_term
    gate_out[...] = gate
    up_out[...] = up
    for copies in late:
        for copy in copies:
            copy.wait()


def gate_up_near(order, near, far, gate_weight, up_weight, xs):
    parts = len(xs)
    size, width = xs[0].shape
    units = gate_weight.shape[2]
    held = jax.ShapeDtypeStruct((len(far), width, units), BF16)
    return pl.pallas_call(
        functools.partial(gate_up_near_kernel, parts, near, far),
        out_shape=[jax.ShapeDtypeStruct((size, units), F32)] * 2 + [held] * 2,
        in_specs=[smem()] + apart(2 + parts),
        out_specs=whole(4),
        scratch_shapes=[
            pltpu.VMEM((parts, width, units), BF16),
            pltpu.VMEM((parts, width, units), BF16),
            pltpu.VMEM((parts, size, width), BF16),
            pltpu.SemaphoreType.DMA((3 * parts + 2 * len(far),)),
        ],
        compiler_params=params(),
        cost_estimate=COST,
    )(order, gate_weight, up_weight, *xs)


def gate_up_far_kernel(parts, gate_before, up_before, gate_ref, up_ref, *refs):
    xs, out_ref = refs[:parts], refs[parts]
    gate, up = gate_before[...], up_before[...]
    for i in range(parts):
        x = xs[i][...]
        gate = gate + dot(x, gate_ref[i])
        up = up + dot(x, up_ref[i])
    out_ref[...] = (gate * jax.nn.sigmoid(gate) * up).astype(BF16)


def gate_up_far(xs, before):
    size, units = before[0].shape
    return pl.pallas_call(
        functools.partial(gate_up_far_kernel, len(xs)),
        out_shape=jax.ShapeDtypeStruct((size, units), BF16),
        in_specs=whole(4 + len(xs)),
        out_specs=whole(1)[0],
        compiler_params=params(),
        cost_estimate=COST,
    )(*before, *xs)


def down_sum(places, order_ref, down_ref, hs, h_held, sems, total):
    units = hs[0].shape[1]
    loads = start_all(hs, [h_held.at[i] for i in range(len(hs))], sems)
    for i in range(len(hs)):
        first = pl.multiple_of(order_ref[places[i]] * units, units)
        loads[i].wait()
        term = dot(h_held[i], down_ref[0, pl.ds(first, units), :])
        total = term if total is None else total + term
    return total


def down_first_kernel(parts, places, order_ref, down_ref, *refs):
    hs, out_ref = refs[:parts], refs[parts]
    out_ref[...] = down_sum(places, order_ref, down_ref, hs, *refs[parts + 1 :], None)


def down_last_kernel(parts, places, experts, k, order_ref, offset_ref, count_ref, down_ref, *refs):
    hs, before, outs = refs[:parts], refs[parts], refs[parts + 1 : parts + 1 + experts]
    h_held, in_sems, staged, out_sems = refs[parts + 1 + experts :]
    size = hs[0].shape[0]
    depth = outs[0].shape[0]
    total = down_sum(places, order_ref, down_ref, hs, h_held, in_sems, before[...])
    result = total.astype(BF16)
    row = lax.broadcasted_iota(I32, (depth, size), 0)
    lane = lax.broadcasted_iota(I32, (depth, size), 1)
    copies = []
    for i in list(range(1, experts)) + [0]:
        pick = ((lane - offset_ref[k, i] == row) & (row < count_ref[k, i])).astype(F32).astype(BF16)
        staged[i] = dot(pick, result).astype(BF16)
        copy = pltpu.make_async_copy(staged.at[i], outs[i], out_sems.at[i])
        copy.start()
        copies.append(copy)
    for copy in copies:
        copy.wait()


def down_scratch(parts, size, units):
    return [pltpu.VMEM((parts, size, units), BF16), pltpu.SemaphoreType.DMA((parts,))]


def down_first(order, places, down_weight, hs):
    parts = len(hs)
    size, units = hs[0].shape
    width = down_weight.shape[2]
    return pl.pallas_call(
        functools.partial(down_first_kernel, parts, places),
        out_shape=jax.ShapeDtypeStruct((size, width), F32),
        in_specs=[smem()] + whole(1) + apart(parts),
        out_specs=whole(1)[0],
        scratch_shapes=down_scratch(parts, size, units),
        compiler_params=params(),
        cost_estimate=COST,
    )(order, down_weight, *hs)


def down_last(order, places, offsets, counts, k, down_weight, hs, before, experts, depth):
    parts = len(hs)
    size, units = hs[0].shape
    width = down_weight.shape[2]
    return pl.pallas_call(
        functools.partial(down_last_kernel, parts, places, experts, k),
        out_shape=[jax.ShapeDtypeStruct((depth, width), BF16)] * experts,
        in_specs=[smem()] * 3 + whole(1) + apart(parts) + whole(1),
        out_specs=apart(experts),
        scratch_shapes=down_scratch(parts, size, units)
        + [pltpu.VMEM((experts, depth, width), BF16), pltpu.SemaphoreType.DMA((experts,))],
        compiler_params=params(),
        cost_estimate=COST,
    )(order, offsets, counts, down_weight, *hs, before)


def weight_kernel(experts, place_ref, own_ref, logits_ref, code_ref, out_ref, score_ref):
    me = place_ref[0]
    kernel = jnp.exp(logits_ref[...])
    row_scale = jnp.ones((kernel.shape[0], 1, kernel.shape[2]), F32)
    for sweep in range(3):
        column = jnp.sum(jnp.sum(kernel * row_scale, axis=0, keepdims=True), axis=2, keepdims=True)
        column_scale = 1.0 / column
        row_scale = 1.0 / jnp.sum(kernel * column_scale, axis=1, keepdims=True)
    own = jnp.exp(own_ref[...])
    column_scale = column_scale[0]
    own_scale = 1.0 / jnp.sum(own * column_scale, axis=0, keepdims=True)
    score_ref[...] = own_scale * own * column_scale
    picked = []
    for shift in range(experts):
        score = score_ref[pl.ds(lax.rem(me + shift, experts), 1), :]
        picked.append(jnp.where(code_ref[pl.ds(shift, 1), :] >= 0, score, 0.0))
    total = picked[0]
    for one in picked[1:]:
        total = total + one
    total = jnp.maximum(total, 1.0 / experts)
    for shift in range(experts):
        out_ref[pl.ds(shift, 1), :] = picked[shift] / total


def slot_weights(place, own, logits, code):
    experts, rows = own.shape
    return pl.pallas_call(
        functools.partial(weight_kernel, experts),
        out_shape=jax.ShapeDtypeStruct((experts, rows), F32),
        in_specs=[smem()] + whole(3),
        out_specs=whole(1)[0],
        scratch_shapes=[pltpu.VMEM((experts, rows), F32)],
        compiler_params=params(),
        cost_estimate=COST,
    )(place, own, logits, code)


def combine_kernel(experts, k, code_ref, weight_ref, *refs):
    count = experts + (k > 0)
    blocks, out_ref = refs[:count], refs[count]
    held, sems = refs[count + 1], refs[count + 2]
    depth = blocks[0].shape[0]
    rows = code_ref.shape[1]
    targets = [held.at[pl.ds(i * depth, depth)] for i in range(experts)]
    if k > 0:
        targets.append(refs[count + 3])
    loads = start_all(blocks, targets, sems)
    slot_ids = lax.broadcasted_iota(I32, (depth, rows), 0) + k * depth
    parts = [
        jnp.where(slot_ids == code_ref[pl.ds(i, 1), :], weight_ref[pl.ds(i, 1), :], 0.0).astype(BF16)
        for i in range(experts)
    ]
    spread = jnp.concatenate(parts, axis=0)
    for load in loads:
        load.wait()
    total = lax.dot_general(spread, held[...], (((0,), (0,)), ((), ())), preferred_element_type=F32)
    if k > 0:
        total = total + refs[count + 3][...]
    out_ref[...] = total.astype(out_ref.dtype)


def combine(code, weights, k, blocks, so_far):
    experts = len(blocks)
    depth, width = blocks[0].shape
    rows = code.shape[1]
    last = k == BATCHES - 1
    more = [] if so_far is None else [so_far]
    return pl.pallas_call(
        functools.partial(combine_kernel, experts, k),
        out_shape=jax.ShapeDtypeStruct((rows, width), BF16 if last else F32),
        in_specs=whole(2) + apart(experts + len(more)),
        out_specs=whole(1)[0],
        scratch_shapes=[
            pltpu.VMEM((experts * depth, width), BF16),
            pltpu.SemaphoreType.DMA((experts + len(more),)),
        ]
        + [pltpu.VMEM((rows, width), F32)] * len(more),
        compiler_params=params(),
        cost_estimate=COST,
    )(code, weights, *blocks, *more)


def after(value, *first):
    return lax.optimization_barrier((value, first))[0]


def shards(tokens, router_weight, gate_weight, up_weight, down_weight, picks):
    experts = lax.axis_size("expert")
    width_parts = lax.axis_size("dp")
    me = lax.axis_index("expert")
    part = lax.axis_index("dp")
    rows = tokens.shape[0]
    capacity = picks.shape[1]
    depth = 2 * capacity // experts // BATCHES
    size = capacity // BATCHES
    place = me.astype(I32).reshape(1)

    def along_expert(x, shift):
        return lax.ppermute(x, "expert", [(i, (i + shift) % experts) for i in range(experts)])

    def swap(x, bit):
        return lax.ppermute(x, "dp", [(i, i ^ bit) for i in range(width_parts)])

    bits = []
    bit = width_parts // 2
    while bit:
        bits.append(bit)
        bit //= 2
    near = [0]
    for bit in bits[1:]:
        near = near + [m ^ bit for m in near]
    masks = near + [m ^ bits[0] for m in near]
    places = range(len(masks))
    near_places, far_places = places[: len(near)], places[len(near) :]
    order = jnp.stack([part ^ m for m in masks]).astype(I32)

    def swap_expert(x, bit):
        return lax.ppermute(x, "expert", [(i, i ^ bit) for i in range(experts)])

    expert_bits = [1 << i for i in range(experts.bit_length() - 1)]

    def spread(x):
        held = [x]
        for bit in bits[1:]:
            held = held + [swap(h, bit) for h in held]
        return held

    def both_parts(x):
        far = swap(x, bits[0])
        return spread(x), spread(far)

    code, logits, first = first_batch(place, picks, router_weight.T, tokens, depth)
    own_picks = lax.dynamic_slice_in_dim(picks, me, 1, axis=0)
    sources = lax.rem(me - jnp.arange(experts, dtype=I32) + experts, experts)
    start = jnp.sum((own_picks < (sources * rows)[:, None]).astype(I32), axis=1)
    stop = jnp.sum((own_picks < ((sources + 1) * rows)[:, None]).astype(I32), axis=1)
    ids = jnp.arange(BATCHES, dtype=I32)[:, None]
    offsets = (start[None, :] + (BATCHES - 1) - ids) // BATCHES
    counts = (stop[None, :] + (BATCHES - 1) - ids) // BATCHES - offsets

    present = [jnp.sum(counts[k]) > 0 for k in range(BATCHES)]

    def beside_first(logits):
        later = [tuple(later_batch(code, tokens, k, depth)) for k in range(1, BATCHES)]
        for bit in bits:
            logits = logits + swap(logits, bit)
        gathered = logits[None]
        for bit in expert_bits:
            gathered = jnp.concatenate([gathered, swap_expert(gathered, bit)])
        return later, logits, gathered

    def nothing_first(logits):
        return jax.tree.map(lambda x: jnp.zeros(x.shape, x.dtype), jax.eval_shape(beside_first, logits))

    arrived = [[first[0]] + [along_expert(first[shift], shift) for shift in range(1, experts)]]
    later, logits, gathered = lax.cond(present[0], beside_first, nothing_first, logits)

    def far_half(far, sums):
        far = spread(far)
        hidden = gate_up_far(far, sums)
        far = swap(hidden, bits[0])
        partial = down_first(order, near_places, down_weight, spread(hidden))
        far, partial = lax.optimization_barrier((far, partial))
        return spread(far), partial

    def settle(k, far, partial):
        return tuple(
            down_last(order, far_places, offsets, counts, k, down_weight, far, partial, experts, depth)
        )

    def fenced(k, run, *operands):
        def skip(*operands):
            return jax.tree.map(lambda x: jnp.zeros(x.shape, x.dtype), jax.eval_shape(run, *operands))

        return lax.cond(present[k], run, skip, *operands)

    def send_back(results):
        return [results[0]] + [along_expert(results[shift], -shift) for shift in range(1, experts)]

    waiting = []
    far = partial = None
    moved = gathered
    for k in range(BATCHES):
        blocks = after(arrived[k], moved)
        if k < BATCHES - 1:
            moving = after(later[k], blocks)
            arrived.append([moving[0]] + [along_expert(moving[shift], shift) for shift in range(1, experts)])
        block = compact(offsets, counts, k, blocks, size)
        across = swap(block, bits[0])
        near = spread(block)
        if k > 0:
            far, partial = after((far, partial), block)
            results = settle(k - 1, far, partial)
            if k > 1:
                results, waiting[k - 2] = lax.optimization_barrier((results, waiting[k - 2]))
            waiting.append(send_back(results))
            near = after(near, results)
        sums = gate_up_near(order, near_places, far_places, gate_weight, up_weight, near)
        across, sums = lax.optimization_barrier((across, sums))
        far, partial = fenced(k, far_half, across, sums)
        moved = partial
    results = settle(BATCHES - 1, far, partial)
    results, waiting[-1] = lax.optimization_barrier((results, waiting[-1]))
    waiting.append(send_back(results))
    weights = slot_weights(place, logits, after(gathered, results), code)
    total = None
    for k in range(BATCHES):
        total = combine(code, weights, k, waiting[k], total)
    return total


def solution(mesh):
    return jax.shard_map(
        shards,
        mesh=mesh,
        in_specs=(
            P(("groups", "expert"), "dp"),
            P("dp", None),
            P("expert", None, "dp"),
            P("expert", None, "dp"),
            P("expert", None, "dp"),
            P("groups", None),
        ),
        out_specs=P(("groups", "expert"), "dp"),
        check_vma=False,
    )
```

```python
import functools

import jax
import jax.numpy as jnp
from jax import lax
from jax.experimental import pallas as pl
from jax.experimental.pallas import tpu as pltpu
from jax.sharding import PartitionSpec as P

BATCHES = 2
F32 = jnp.float32
BF16 = jnp.bfloat16
I32 = jnp.int32
VMEM_LIMIT = 16 * 1024 * 1024
COST = pl.CostEstimate(flops=1024, bytes_accessed=1024, transcendentals=0)


def whole(count):
    return [pl.BlockSpec(memory_space=pltpu.VMEM)] * count


def apart(count):
    return [pl.BlockSpec(memory_space=pl.ANY)] * count


def smem():
    return pl.BlockSpec(memory_space=pltpu.SMEM)


def params(limit=VMEM_LIMIT):
    return pltpu.CompilerParams(vmem_limit_bytes=limit)


def dot(a, b):
    return jnp.dot(a, b, preferred_element_type=F32)


def start_all(sources, targets, sems):
    copies = [pltpu.make_async_copy(a, b, sems.at[i]) for i, (a, b) in enumerate(zip(sources, targets))]
    for copy in copies:
        copy.start()
    return copies


def code_kernel(experts, depth, place_ref, picks_in, router_in, tokens_ref, code_ref, logits_ref, *refs):
    sends = refs[:experts]
    picks_ref, router_ref, held, staged, in_sems, out_sems = refs[experts:]
    picks_load, router_load, load = start_all(
        [picks_in, router_in, tokens_ref], [picks_ref, router_ref, held], in_sems
    )
    me = place_ref[0]
    rows, width = held.shape
    capacity = picks_ref.shape[1]
    strips = rows // 128
    lanes = lax.broadcasted_iota(I32, (128, capacity), 0)
    strip_ids = lax.broadcasted_iota(I32, (8, capacity), 0)
    upper = (lax.broadcasted_iota(I32, (128, 128), 0) < lax.broadcasted_iota(I32, (128, 128), 1)).astype(BF16)
    before = (lax.broadcasted_iota(I32, (8, 8), 1) < lax.broadcasted_iota(I32, (8, 8), 0)).astype(BF16)
    ones = jnp.ones((128, 128), BF16)
    picks_load.wait()
    code_rows = []
    for shift in range(experts):
        expert = lax.rem(me + shift, experts)
        chosen = picks_ref[pl.ds(expert, 1), :]
        local = chosen - me * rows
        start = jnp.sum((local < 0).astype(F32)).astype(I32)
        strip = lax.shift_right_arithmetic(local, 7)
        place = jnp.bitwise_and(local, 127)
        high = (strip == strip_ids).astype(BF16)
        high = jnp.where(strip_ids < strips, high, jnp.zeros_like(high))
        low = (place == lanes).astype(BF16)
        mask = lax.dot_general(high, low, (((1,), (1,)), ((), ())), preferred_element_type=F32)
        mask16 = mask.astype(BF16)
        totals = dot(mask16, ones)
        rank = (dot(mask16, upper) + dot(before, totals.astype(BF16))).astype(I32)
        batch = lax.rem(rank + start, BATCHES)
        slot = batch * depth + lax.div(rank, BATCHES)
        code = jnp.where(mask > 0.5, slot, -1)
        row = jnp.concatenate([code[i : i + 1] for i in range(strips)], axis=1)
        code_ref[pl.ds(shift, 1), :] = row
        code_rows.append(row)
    router_load.wait()
    load.wait()
    logits_ref[...] = lax.dot_general(
        router_ref[...], held[...], (((1,), (1,)), ((), ())), preferred_element_type=F32
    )
    pack(0, depth, code_rows, held, staged, sends, out_sems)


def pack(k, depth, code_rows, held, staged, sends, sems):
    slot_ids = lax.broadcasted_iota(I32, (depth, held.shape[0]), 0) + k * depth
    copies = []
    for shift in list(range(1, len(sends))) + [0]:
        selector = (slot_ids == code_rows[shift]).astype(F32).astype(BF16)
        staged[shift] = dot(selector, held[...]).astype(BF16)
        copy = pltpu.make_async_copy(staged.at[shift], sends[shift], sems.at[shift])
        copy.start()
        copies.append(copy)
    for copy in copies:
        copy.wait()


def first_batch(place, picks, router, tokens, depth):
    rows, width = tokens.shape
    experts = picks.shape[0]
    out = pl.pallas_call(
        functools.partial(code_kernel, experts, depth),
        out_shape=[jax.ShapeDtypeStruct((experts, rows), I32), jax.ShapeDtypeStruct((experts, rows), F32)]
        + [jax.ShapeDtypeStruct((depth, width), BF16)] * experts,
        in_specs=[smem()] + apart(3),
        out_specs=whole(2) + apart(experts),
        scratch_shapes=[
            pltpu.VMEM(picks.shape, I32),
            pltpu.VMEM(router.shape, BF16),
            pltpu.VMEM((rows, width), BF16),
            pltpu.VMEM((experts, depth, width), BF16),
            pltpu.SemaphoreType.DMA((3,)),
            pltpu.SemaphoreType.DMA((experts,)),
        ],
        compiler_params=params(60 * 1024 * 1024),
        cost_estimate=COST,
    )(place, picks, router, tokens)
    return out[0], out[1], out[2:]


def pack_kernel(experts, depth, k, code_ref, tokens_ref, *refs):
    sends = refs[:experts]
    held, staged, in_sems, out_sems = refs[experts:]
    start_all([tokens_ref], [held], in_sems)[0].wait()
    code_rows = [code_ref[pl.ds(shift, 1), :] for shift in range(experts)]
    pack(k, depth, code_rows, held, staged, sends, out_sems)


def later_batch(code, tokens, k, depth):
    rows, width = tokens.shape
    experts = code.shape[0]
    return pl.pallas_call(
        functools.partial(pack_kernel, experts, depth, k),
        out_shape=[jax.ShapeDtypeStruct((depth, width), BF16)] * experts,
        in_specs=whole(1) + apart(1),
        out_specs=apart(experts),
        scratch_shapes=[
            pltpu.VMEM((rows, width), BF16),
            pltpu.VMEM((experts, depth, width), BF16),
            pltpu.SemaphoreType.DMA((1,)),
            pltpu.SemaphoreType.DMA((experts,)),
        ],
        compiler_params=params(),
        cost_estimate=COST,
    )(code, tokens)


def compact_kernel(experts, k, offset_ref, count_ref, *refs):
    blocks, out_ref = refs[:experts], refs[experts]
    held, sems = refs[experts + 1 :]
    depth = blocks[0].shape[0]
    size = out_ref.shape[0]
    loads = start_all(blocks, [held.at[pl.ds(i * depth, depth)] for i in range(experts)], sems)
    row = lax.broadcasted_iota(I32, (size, depth), 0)
    lane = lax.broadcasted_iota(I32, (size, depth), 1)
    parts = [
        ((row - offset_ref[k, i] == lane) & (lane < count_ref[k, i])).astype(F32).astype(BF16)
        for i in range(experts)
    ]
    selector = jnp.concatenate(parts, axis=1)
    for load in loads:
        load.wait()
    out_ref[...] = dot(selector, held[...]).astype(BF16)


def compact(offsets, counts, k, blocks, size):
    experts = len(blocks)
    depth, width = blocks[0].shape
    return pl.pallas_call(
        functools.partial(compact_kernel, experts, k),
        out_shape=jax.ShapeDtypeStruct((size, width), BF16),
        in_specs=[smem(), smem()] + apart(experts),
        out_specs=whole(1)[0],
        scratch_shapes=[pltpu.VMEM((experts * depth, width), BF16), pltpu.SemaphoreType.DMA((experts,))],
        compiler_params=params(),
        cost_estimate=COST,
    )(offsets, counts, *blocks)


def gate_up_near_kernel(parts, near, far, order_ref, gate_ref, up_ref, *refs):
    xs, refs = refs[:parts], refs[parts:]
    gate_out, up_out, gate_far, up_far, gate_held, up_held, x_held, sems = refs
    width = xs[0].shape[1]

    def fetch(i, place, gate_to, up_to, base):
        first = pl.multiple_of(order_ref[place] * width, width)
        return start_all(
            [gate_ref.at[0, pl.ds(first, width), :], up_ref.at[0, pl.ds(first, width), :]],
            [gate_to.at[i], up_to.at[i]],
            sems.at[pl.ds(base, 2)],
        )

    x_loads = start_all(xs, [x_held.at[i] for i in range(parts)], sems.at[pl.ds(0, parts)])
    loads = [fetch(i, near[i], gate_held, up_held, parts + 2 * i) for i in range(parts)]
    late = [fetch(i, far[i], gate_far, up_far, 3 * parts + 2 * i) for i in range(len(far))]
    gate = up = None
    for i in range(parts):
        for copy in [x_loads[i]] + loads[i]:
            copy.wait()
        x = x_held[i]
        gate_term = dot(x, gate_held[i])
        up_term = dot(x, up_held[i])
        gate = gate_term if gate is None else gate + gate_term
        up = up_term if up is None else up + up_term
    gate_out[...] = gate
    up_out[...] = up
    for copies in late:
        for copy in copies:
            copy.wait()


def gate_up_near(order, near, far, gate_weight, up_weight, xs):
    parts = len(xs)
    size, width = xs[0].shape
    units = gate_weight.shape[2]
    held = jax.ShapeDtypeStruct((len(far), width, units), BF16)
    return pl.pallas_call(
        functools.partial(gate_up_near_kernel, parts, near, far),
        out_shape=[jax.ShapeDtypeStruct((size, units), F32)] * 2 + [held] * 2,
        in_specs=[smem()] + apart(2 + parts),
        out_specs=whole(4),
        scratch_shapes=[
            pltpu.VMEM((parts, width, units), BF16),
            pltpu.VMEM((parts, width, units), BF16),
            pltpu.VMEM((parts, size, width), BF16),
            pltpu.SemaphoreType.DMA((3 * parts + 2 * len(far),)),
        ],
        compiler_params=params(),
        cost_estimate=COST,
    )(order, gate_weight, up_weight, *xs)


def gate_up_far_kernel(parts, gate_before, up_before, gate_ref, up_ref, *refs):
    xs, out_ref = refs[:parts], refs[parts]
    gate, up = gate_before[...], up_before[...]
    for i in range(parts):
        x = xs[i][...]
        gate = gate + dot(x, gate_ref[i])
        up = up + dot(x, up_ref[i])
    out_ref[...] = (gate * jax.nn.sigmoid(gate) * up).astype(BF16)


def gate_up_far(xs, before):
    size, units = before[0].shape
    return pl.pallas_call(
        functools.partial(gate_up_far_kernel, len(xs)),
        out_shape=jax.ShapeDtypeStruct((size, units), BF16),
        in_specs=whole(4 + len(xs)),
        out_specs=whole(1)[0],
        compiler_params=params(),
        cost_estimate=COST,
    )(*before, *xs)


def down_first_kernel(parts, near, far, order_ref, down_ref, *refs):
    hs, (out_ref, far_ref, down_held, h_held, sems) = refs[:parts], refs[parts:]
    units = hs[0].shape[1]

    def fetch(i, place, target, sem):
        first = pl.multiple_of(order_ref[place] * units, units)
        copy = pltpu.make_async_copy(down_ref.at[0, pl.ds(first, units), :], target.at[i], sems.at[sem])
        copy.start()
        return copy

    h_loads = start_all(hs, [h_held.at[i] for i in range(parts)], sems.at[pl.ds(0, parts)])
    loads = [fetch(i, near[i], down_held, parts + i) for i in range(parts)]
    late = [fetch(i, far[i], far_ref, 2 * parts + i) for i in range(len(far))]
    total = None
    for i in range(parts):
        h_loads[i].wait()
        loads[i].wait()
        term = dot(h_held[i], down_held[i])
        total = term if total is None else total + term
    out_ref[...] = total
    for copy in late:
        copy.wait()


def down_first(order, near, far, down_weight, hs):
    parts = len(hs)
    size, units = hs[0].shape
    width = down_weight.shape[2]
    return pl.pallas_call(
        functools.partial(down_first_kernel, parts, near, far),
        out_shape=[
            jax.ShapeDtypeStruct((size, width), F32),
            jax.ShapeDtypeStruct((len(far), units, width), BF16),
        ],
        in_specs=[smem()] + apart(1 + parts),
        out_specs=whole(2),
        scratch_shapes=[
            pltpu.VMEM((parts, units, width), BF16),
            pltpu.VMEM((parts, size, units), BF16),
            pltpu.SemaphoreType.DMA((2 * parts + len(far),)),
        ],
        compiler_params=params(),
        cost_estimate=COST,
    )(order, down_weight, *hs)


def down_last_kernel(parts, experts, k, offset_ref, count_ref, before_ref, down_ref, *refs):
    hs, outs = refs[:parts], refs[parts : parts + experts]
    h_held, sems = refs[parts + experts :]
    loads = start_all(hs, [h_held.at[i] for i in range(parts)], sems)
    size = hs[0].shape[0]
    depth = outs[0].shape[0]
    row = lax.broadcasted_iota(I32, (depth, size), 0)
    lane = lax.broadcasted_iota(I32, (depth, size), 1)
    picks = [
        ((lane - offset_ref[k, i] == row) & (row < count_ref[k, i])).astype(F32).astype(BF16)
        for i in range(experts)
    ]
    total = before_ref[...]
    for i in range(parts):
        loads[i].wait()
        total = total + dot(h_held[i], down_ref[i])
    result = total.astype(BF16)
    for i in range(experts):
        outs[i][...] = dot(picks[i], result).astype(BF16)


def down_last(offsets, counts, k, hs, before, experts, depth):
    parts = len(hs)
    size, units = hs[0].shape
    width = before[0].shape[1]
    return pl.pallas_call(
        functools.partial(down_last_kernel, parts, experts, k),
        out_shape=[jax.ShapeDtypeStruct((depth, width), BF16)] * experts,
        in_specs=[smem()] * 2 + whole(2) + apart(parts),
        out_specs=whole(experts),
        scratch_shapes=[pltpu.VMEM((parts, size, units), BF16), pltpu.SemaphoreType.DMA((parts,))],
        compiler_params=params(),
        cost_estimate=COST,
    )(offsets, counts, *before, *hs)


def weight_kernel(experts, place_ref, own_ref, logits_ref, code_ref, out_ref, score_ref):
    me = place_ref[0]
    kernel = jnp.exp(logits_ref[...])
    row_scale = jnp.ones((kernel.shape[0], 1, kernel.shape[2]), F32)
    for sweep in range(3):
        column = jnp.sum(jnp.sum(kernel * row_scale, axis=0, keepdims=True), axis=2, keepdims=True)
        column_scale = 1.0 / column
        row_scale = 1.0 / jnp.sum(kernel * column_scale, axis=1, keepdims=True)
    own = jnp.exp(own_ref[...])
    column_scale = column_scale[0]
    own_scale = 1.0 / jnp.sum(own * column_scale, axis=0, keepdims=True)
    score_ref[...] = own_scale * own * column_scale
    picked = []
    for shift in range(experts):
        score = score_ref[pl.ds(lax.rem(me + shift, experts), 1), :]
        picked.append(jnp.where(code_ref[pl.ds(shift, 1), :] >= 0, score, 0.0))
    total = picked[0]
    for one in picked[1:]:
        total = total + one
    total = jnp.maximum(total, 1.0 / experts)
    for shift in range(experts):
        out_ref[pl.ds(shift, 1), :] = picked[shift] / total


def slot_weights(place, own, logits, code):
    experts, rows = own.shape
    return pl.pallas_call(
        functools.partial(weight_kernel, experts),
        out_shape=jax.ShapeDtypeStruct((experts, rows), F32),
        in_specs=[smem()] + whole(3),
        out_specs=whole(1)[0],
        scratch_shapes=[pltpu.VMEM((experts, rows), F32)],
        compiler_params=params(),
        cost_estimate=COST,
    )(place, own, logits, code)


def combine_kernel(experts, k, code_ref, weight_ref, *refs):
    count = experts + (k > 0)
    blocks, out_ref = refs[:count], refs[count]
    held, sems = refs[count + 1], refs[count + 2]
    depth = blocks[0].shape[0]
    rows = code_ref.shape[1]
    targets = [held.at[pl.ds(i * depth, depth)] for i in range(experts)]
    if k > 0:
        targets.append(refs[count + 3])
    loads = start_all(blocks, targets, sems)
    slot_ids = lax.broadcasted_iota(I32, (depth, rows), 0) + k * depth
    parts = [
        jnp.where(slot_ids == code_ref[pl.ds(i, 1), :], weight_ref[pl.ds(i, 1), :], 0.0).astype(BF16)
        for i in range(experts)
    ]
    spread = jnp.concatenate(parts, axis=0)
    for load in loads:
        load.wait()
    total = lax.dot_general(spread, held[...], (((0,), (0,)), ((), ())), preferred_element_type=F32)
    if k > 0:
        total = total + refs[count + 3][...]
    out_ref[...] = total.astype(out_ref.dtype)


def combine(code, weights, k, blocks, so_far):
    experts = len(blocks)
    depth, width = blocks[0].shape
    rows = code.shape[1]
    last = k == BATCHES - 1
    more = [] if so_far is None else [so_far]
    return pl.pallas_call(
        functools.partial(combine_kernel, experts, k),
        out_shape=jax.ShapeDtypeStruct((rows, width), BF16 if last else F32),
        in_specs=whole(2) + apart(experts + len(more)),
        out_specs=whole(1)[0],
        scratch_shapes=[
            pltpu.VMEM((experts * depth, width), BF16),
            pltpu.SemaphoreType.DMA((experts + len(more),)),
        ]
        + [pltpu.VMEM((rows, width), F32)] * len(more),
        compiler_params=params(),
        cost_estimate=COST,
    )(code, weights, *blocks, *more)


def after(value, *first):
    return lax.optimization_barrier((value, first))[0]


def shards(tokens, router_weight, gate_weight, up_weight, down_weight, picks):
    experts = lax.axis_size("expert")
    width_parts = lax.axis_size("dp")
    me = lax.axis_index("expert")
    part = lax.axis_index("dp")
    rows = tokens.shape[0]
    capacity = picks.shape[1]
    depth = 2 * capacity // experts // BATCHES
    size = capacity // BATCHES
    place = me.astype(I32).reshape(1)

    def along_expert(x, shift):
        return lax.ppermute(x, "expert", [(i, (i + shift) % experts) for i in range(experts)])

    def swap(x, bit):
        return lax.ppermute(x, "dp", [(i, i ^ bit) for i in range(width_parts)])

    bits = []
    bit = width_parts // 2
    while bit:
        bits.append(bit)
        bit //= 2
    near = [0]
    for bit in bits[1:]:
        near = near + [m ^ bit for m in near]
    masks = near + [m ^ bits[0] for m in near]
    places = range(len(masks))
    near_places, far_places = places[: len(near)], places[len(near) :]
    order = jnp.stack([part ^ m for m in masks]).astype(I32)

    def swap_expert(x, bit):
        return lax.ppermute(x, "expert", [(i, i ^ bit) for i in range(experts)])

    expert_bits = [1 << i for i in range(experts.bit_length() - 1)]

    def spread(x):
        held = [x]
        for bit in bits[1:]:
            held = held + [swap(h, bit) for h in held]
        return held

    def both_parts(x):
        far = swap(x, bits[0])
        return spread(x), spread(far)

    code, logits, first = first_batch(place, picks, router_weight.T, tokens, depth)
    own_picks = lax.dynamic_slice_in_dim(picks, me, 1, axis=0)
    sources = lax.rem(me - jnp.arange(experts, dtype=I32) + experts, experts)
    start = jnp.sum((own_picks < (sources * rows)[:, None]).astype(I32), axis=1)
    stop = jnp.sum((own_picks < ((sources + 1) * rows)[:, None]).astype(I32), axis=1)
    ids = jnp.arange(BATCHES, dtype=I32)[:, None]
    offsets = (start[None, :] + (BATCHES - 1) - ids) // BATCHES
    counts = (stop[None, :] + (BATCHES - 1) - ids) // BATCHES - offsets

    present = [jnp.sum(counts[k]) > 0 for k in range(BATCHES)]

    def beside_first(logits):
        later = [tuple(later_batch(code, tokens, k, depth)) for k in range(1, BATCHES)]
        for bit in bits:
            logits = logits + swap(logits, bit)
        gathered = logits[None]
        for bit in expert_bits[:-1]:
            gathered = jnp.concatenate([gathered, swap_expert(gathered, bit)])
        return later, logits, gathered

    def nothing_first(logits):
        return jax.tree.map(lambda x: jnp.zeros(x.shape, x.dtype), jax.eval_shape(beside_first, logits))

    arrived = [[first[0]] + [along_expert(first[shift], shift) for shift in range(1, experts)]]
    later, logits, gathered = lax.cond(present[0], beside_first, nothing_first, logits)

    def far_half(far, sums):
        far = spread(far)
        hidden = gate_up_far(far, sums)
        far = swap(hidden, bits[0])
        partial = down_first(order, near_places, far_places, down_weight, spread(hidden))
        far, partial = lax.optimization_barrier((far, partial))
        return spread(far), partial

    def settle(k, far, partial):
        return tuple(
            down_last(offsets, counts, k, far, partial, experts, depth)
        )

    def fenced(k, run, *operands):
        def skip(*operands):
            return jax.tree.map(lambda x: jnp.zeros(x.shape, x.dtype), jax.eval_shape(run, *operands))

        return lax.cond(present[k], run, skip, *operands)

    def send_back(results):
        return [results[0]] + [along_expert(results[shift], -shift) for shift in range(1, experts)]

    waiting = []
    far = partial = None
    moved = gathered
    for k in range(BATCHES):
        blocks = after(arrived[k], moved)
        if k < BATCHES - 1:
            moving = after(later[k], blocks)
            arrived.append([moving[0]] + [along_expert(moving[shift], shift) for shift in range(1, experts)])
        block = compact(offsets, counts, k, blocks, size)
        across = swap(block, bits[0])
        near = spread(block)
        if k > 0:
            far, partial = after((far, partial), block)
            results = settle(k - 1, far, partial)
            if k > 1:
                results, waiting[k - 2] = lax.optimization_barrier((results, waiting[k - 2]))
            waiting.append(send_back(results))
            near = after(near, results)
        sums = gate_up_near(order, near_places, far_places, gate_weight, up_weight, near)
        across, sums = lax.optimization_barrier((across, sums))
        far, partial = fenced(k, far_half, across, sums)
        moved = partial
    results = settle(BATCHES - 1, far, partial)
    results, waiting[-1] = lax.optimization_barrier((results, waiting[-1]))
    waiting.append(send_back(results))
    gathered = after(gathered, results)
    gathered = jnp.concatenate([gathered, swap_expert(gathered, expert_bits[-1])])
    weights = slot_weights(place, logits, gathered, code)
    total = None
    for k in range(BATCHES):
        total = combine(code, weights, k, waiting[k], total)
    return total


def solution(mesh):
    return jax.shard_map(
        shards,
        mesh=mesh,
        in_specs=(
            P(("groups", "expert"), "dp"),
            P("dp", None),
            P("expert", None, "dp"),
            P("expert", None, "dp"),
            P("expert", None, "dp"),
            P("groups", None),
        ),
        out_specs=P(("groups", "expert"), "dp"),
        check_vma=False,
    )
```

```python
import functools

import jax
import jax.numpy as jnp
from jax import lax
from jax.experimental import pallas as pl
from jax.experimental.pallas import tpu as pltpu
from jax.sharding import PartitionSpec as P

BATCHES = 2
F32 = jnp.float32
BF16 = jnp.bfloat16
I32 = jnp.int32
VMEM_LIMIT = 16 * 1024 * 1024
COST = pl.CostEstimate(flops=1024, bytes_accessed=1024, transcendentals=0)


def whole(count):
    return [pl.BlockSpec(memory_space=pltpu.VMEM)] * count


def apart(count):
    return [pl.BlockSpec(memory_space=pl.ANY)] * count


def smem():
    return pl.BlockSpec(memory_space=pltpu.SMEM)


def params(limit=VMEM_LIMIT):
    return pltpu.CompilerParams(vmem_limit_bytes=limit)


def dot(a, b):
    return jnp.dot(a, b, preferred_element_type=F32)


def start_all(sources, targets, sems):
    copies = [pltpu.make_async_copy(a, b, sems.at[i]) for i, (a, b) in enumerate(zip(sources, targets))]
    for copy in copies:
        copy.start()
    return copies


def code_kernel(experts, depth, place_ref, picks_in, tokens_ref, code_ref, *refs):
    sends = refs[:experts]
    picks_ref, held, staged, in_sems, out_sems = refs[experts:]
    picks_load, load = start_all([picks_in, tokens_ref], [picks_ref, held], in_sems)
    me = place_ref[0]
    rows, width = held.shape
    capacity = picks_ref.shape[1]
    strips = rows // 128
    lanes = lax.broadcasted_iota(I32, (128, capacity), 0)
    strip_ids = lax.broadcasted_iota(I32, (8, capacity), 0)
    total = 8 * experts
    row_ids = lax.broadcasted_iota(I32, (total, total), 0)
    lane_ids = lax.broadcasted_iota(I32, (total, total), 1)
    same = lax.shift_right_logical(row_ids, 3) == lax.shift_right_logical(lane_ids, 3)
    before = (same & (lane_ids < row_ids)).astype(F32).astype(BF16)
    upper = (lax.broadcasted_iota(I32, (128, 128), 0) < lax.broadcasted_iota(I32, (128, 128), 1)).astype(BF16)
    ones = jnp.ones((128, 128), BF16)
    picks_load.wait()
    masks, starts = [], []
    for shift in range(experts):
        local = picks_ref[pl.ds(lax.rem(me + shift, experts), 1), :] - me * rows
        starts.append(jnp.broadcast_to(jnp.sum((local < 0).astype(F32), axis=1, keepdims=True), (8, 128)))
        strip = lax.shift_right_arithmetic(local, 7)
        place = jnp.bitwise_and(local, 127)
        high = ((strip == strip_ids) & (strip_ids < strips)).astype(F32).astype(BF16)
        low = (place == lanes).astype(F32).astype(BF16)
        masks.append(lax.dot_general(high, low, (((1,), (1,)), ((), ())), preferred_element_type=F32))
    mask = jnp.concatenate(masks, axis=0)
    start = jnp.concatenate(starts, axis=0).astype(I32)
    mask16 = mask.astype(BF16)
    totals = dot(mask16, ones)
    rank = (dot(mask16, upper) + dot(before, totals.astype(BF16))).astype(I32)
    slot = lax.rem(rank + start, BATCHES) * depth + lax.div(rank, BATCHES)
    code = jnp.where(mask > 0.5, slot, -1)
    code_rows = []
    for shift in range(experts):
        row = jnp.concatenate([code[8 * shift + i : 8 * shift + i + 1] for i in range(strips)], axis=1)
        code_ref[pl.ds(shift, 1), :] = row
        code_rows.append(row)
    load.wait()
    pack(0, depth, code_rows, held, staged, sends, out_sems)


def pack(k, depth, code_rows, held, staged, sends, sems):
    slot_ids = lax.broadcasted_iota(I32, (depth, held.shape[0]), 0) + k * depth
    copies = []
    for shift in list(range(1, len(sends))) + [0]:
        selector = (slot_ids == code_rows[shift]).astype(F32).astype(BF16)
        staged[shift] = dot(selector, held[...]).astype(BF16)
        copy = pltpu.make_async_copy(staged.at[shift], sends[shift], sems.at[shift])
        copy.start()
        copies.append(copy)
    for copy in copies:
        copy.wait()


def first_batch(place, picks, tokens, depth):
    rows, width = tokens.shape
    experts = picks.shape[0]
    out = pl.pallas_call(
        functools.partial(code_kernel, experts, depth),
        out_shape=[jax.ShapeDtypeStruct((experts, rows), I32)]
        + [jax.ShapeDtypeStruct((depth, width), BF16)] * experts,
        in_specs=[smem()] + apart(2),
        out_specs=whole(1) + apart(experts),
        scratch_shapes=[
            pltpu.VMEM(picks.shape, I32),
            pltpu.VMEM((rows, width), BF16),
            pltpu.VMEM((experts, depth, width), BF16),
            pltpu.SemaphoreType.DMA((2,)),
            pltpu.SemaphoreType.DMA((experts,)),
        ],
        compiler_params=params(60 * 1024 * 1024),
        cost_estimate=COST,
    )(place, picks, tokens)
    return out[0], out[1:]


def logits_kernel(router_ref, tokens_ref, out_ref):
    out_ref[...] = lax.dot_general(
        router_ref[...], tokens_ref[...], (((1,), (1,)), ((), ())), preferred_element_type=F32
    )


def partial_logits(router, tokens):
    return pl.pallas_call(
        logits_kernel,
        out_shape=jax.ShapeDtypeStruct((router.shape[0], tokens.shape[0]), F32),
        in_specs=whole(2),
        out_specs=whole(1)[0],
        compiler_params=params(),
        cost_estimate=COST,
    )(router, tokens)


def pack_kernel(experts, depth, k, code_ref, tokens_ref, *refs):
    sends = refs[:experts]
    held, staged, in_sems, out_sems = refs[experts:]
    start_all([tokens_ref], [held], in_sems)[0].wait()
    code_rows = [code_ref[pl.ds(shift, 1), :] for shift in range(experts)]
    pack(k, depth, code_rows, held, staged, sends, out_sems)


def later_batch(code, tokens, k, depth):
    rows, width = tokens.shape
    experts = code.shape[0]
    return pl.pallas_call(
        functools.partial(pack_kernel, experts, depth, k),
        out_shape=[jax.ShapeDtypeStruct((depth, width), BF16)] * experts,
        in_specs=whole(1) + apart(1),
        out_specs=apart(experts),
        scratch_shapes=[
            pltpu.VMEM((rows, width), BF16),
            pltpu.VMEM((experts, depth, width), BF16),
            pltpu.SemaphoreType.DMA((1,)),
            pltpu.SemaphoreType.DMA((experts,)),
        ],
        compiler_params=params(),
        cost_estimate=COST,
    )(code, tokens)


def compact_kernel(experts, k, offset_ref, count_ref, *refs):
    blocks, out_ref = refs[:experts], refs[experts]
    held, sems = refs[experts + 1 :]
    depth = blocks[0].shape[0]
    size = out_ref.shape[0]
    loads = start_all(blocks, [held.at[pl.ds(i * depth, depth)] for i in range(experts)], sems)
    row = lax.broadcasted_iota(I32, (size, depth), 0)
    lane = lax.broadcasted_iota(I32, (size, depth), 1)
    parts = [
        ((row - offset_ref[k, i] == lane) & (lane < count_ref[k, i])).astype(F32).astype(BF16)
        for i in range(experts)
    ]
    selector = jnp.concatenate(parts, axis=1)
    for load in loads:
        load.wait()
    out_ref[...] = dot(selector, held[...]).astype(BF16)


def compact(offsets, counts, k, blocks, size):
    experts = len(blocks)
    depth, width = blocks[0].shape
    return pl.pallas_call(
        functools.partial(compact_kernel, experts, k),
        out_shape=jax.ShapeDtypeStruct((size, width), BF16),
        in_specs=[smem(), smem()] + apart(experts),
        out_specs=whole(1)[0],
        scratch_shapes=[pltpu.VMEM((experts * depth, width), BF16), pltpu.SemaphoreType.DMA((experts,))],
        compiler_params=params(),
        cost_estimate=COST,
    )(offsets, counts, *blocks)


def gate_up_near_kernel(parts, near, far, order_ref, gate_ref, up_ref, *refs):
    xs, refs = refs[:parts], refs[parts:]
    gate_out, up_out, gate_far, up_far, gate_held, up_held, x_held, sems = refs
    width = xs[0].shape[1]

    def fetch(i, place, gate_to, up_to, base):
        first = pl.multiple_of(order_ref[place] * width, width)
        return start_all(
            [gate_ref.at[0, pl.ds(first, width), :], up_ref.at[0, pl.ds(first, width), :]],
            [gate_to.at[i], up_to.at[i]],
            sems.at[pl.ds(base, 2)],
        )

    x_loads = start_all(xs, [x_held.at[i] for i in range(parts)], sems.at[pl.ds(0, parts)])
    loads = [fetch(i, near[i], gate_held, up_held, parts + 2 * i) for i in range(parts)]
    late = [fetch(i, far[i], gate_far, up_far, 3 * parts + 2 * i) for i in range(len(far))]
    gate = up = None
    for i in range(parts):
        for copy in [x_loads[i]] + loads[i]:
            copy.wait()
        x = x_held[i]
        gate_term = dot(x, gate_held[i])
        up_term = dot(x, up_held[i])
        gate = gate_term if gate is None else gate + gate_term
        up = up_term if up is None else up + up_term
    gate_out[...] = gate
    up_out[...] = up
    for copies in late:
        for copy in copies:
            copy.wait()


def gate_up_near(order, near, far, gate_weight, up_weight, xs):
    parts = len(xs)
    size, width = xs[0].shape
    units = gate_weight.shape[2]
    held = jax.ShapeDtypeStruct((len(far), width, units), BF16)
    return pl.pallas_call(
        functools.partial(gate_up_near_kernel, parts, near, far),
        out_shape=[jax.ShapeDtypeStruct((size, units), F32)] * 2 + [held] * 2,
        in_specs=[smem()] + apart(2 + parts),
        out_specs=whole(4),
        scratch_shapes=[
            pltpu.VMEM((parts, width, units), BF16),
            pltpu.VMEM((parts, width, units), BF16),
            pltpu.VMEM((parts, size, width), BF16),
            pltpu.SemaphoreType.DMA((3 * parts + 2 * len(far),)),
        ],
        compiler_params=params(),
        cost_estimate=COST,
    )(order, gate_weight, up_weight, *xs)


def gate_up_far_kernel(parts, gate_before, up_before, gate_ref, up_ref, *refs):
    xs, out_ref = refs[:parts], refs[parts]
    gate, up = gate_before[...], up_before[...]
    for i in range(parts):
        x = xs[i][...]
        gate = gate + dot(x, gate_ref[i])
        up = up + dot(x, up_ref[i])
    out_ref[...] = (gate * jax.nn.sigmoid(gate) * up).astype(BF16)


def gate_up_far(xs, before):
    size, units = before[0].shape
    return pl.pallas_call(
        functools.partial(gate_up_far_kernel, len(xs)),
        out_shape=jax.ShapeDtypeStruct((size, units), BF16),
        in_specs=whole(4 + len(xs)),
        out_specs=whole(1)[0],
        compiler_params=params(),
        cost_estimate=COST,
    )(*before, *xs)


def down_first_kernel(parts, near, far, order_ref, down_ref, *refs):
    hs, (out_ref, far_ref, down_held, h_held, sems) = refs[:parts], refs[parts:]
    units = hs[0].shape[1]

    def fetch(i, place, target, sem):
        first = pl.multiple_of(order_ref[place] * units, units)
        copy = pltpu.make_async_copy(down_ref.at[0, pl.ds(first, units), :], target.at[i], sems.at[sem])
        copy.start()
        return copy

    h_loads = start_all(hs, [h_held.at[i] for i in range(parts)], sems.at[pl.ds(0, parts)])
    loads = [fetch(i, near[i], down_held, parts + i) for i in range(parts)]
    late = [fetch(i, far[i], far_ref, 2 * parts + i) for i in range(len(far))]
    total = None
    for i in range(parts):
        h_loads[i].wait()
        loads[i].wait()
        term = dot(h_held[i], down_held[i])
        total = term if total is None else total + term
    out_ref[...] = total
    for copy in late:
        copy.wait()


def down_first(order, near, far, down_weight, hs):
    parts = len(hs)
    size, units = hs[0].shape
    width = down_weight.shape[2]
    return pl.pallas_call(
        functools.partial(down_first_kernel, parts, near, far),
        out_shape=[
            jax.ShapeDtypeStruct((size, width), F32),
            jax.ShapeDtypeStruct((len(far), units, width), BF16),
        ],
        in_specs=[smem()] + apart(1 + parts),
        out_specs=whole(2),
        scratch_shapes=[
            pltpu.VMEM((parts, units, width), BF16),
            pltpu.VMEM((parts, size, units), BF16),
            pltpu.SemaphoreType.DMA((2 * parts + len(far),)),
        ],
        compiler_params=params(),
        cost_estimate=COST,
    )(order, down_weight, *hs)


def down_last_kernel(parts, experts, k, offset_ref, count_ref, before_ref, down_ref, *refs):
    hs, outs = refs[:parts], refs[parts : parts + experts]
    h_held, sems = refs[parts + experts :]
    loads = start_all(hs, [h_held.at[i] for i in range(parts)], sems)
    size = hs[0].shape[0]
    depth = outs[0].shape[0]
    row = lax.broadcasted_iota(I32, (depth, size), 0)
    lane = lax.broadcasted_iota(I32, (depth, size), 1)
    picks = [
        ((lane - offset_ref[k, i] == row) & (row < count_ref[k, i])).astype(F32).astype(BF16)
        for i in range(experts)
    ]
    total = before_ref[...]
    for i in range(parts):
        loads[i].wait()
        total = total + dot(h_held[i], down_ref[i])
    result = total.astype(BF16)
    for i in range(experts):
        outs[i][...] = dot(picks[i], result).astype(BF16)


def down_last(offsets, counts, k, hs, before, experts, depth):
    parts = len(hs)
    size, units = hs[0].shape
    width = before[0].shape[1]
    return pl.pallas_call(
        functools.partial(down_last_kernel, parts, experts, k),
        out_shape=[jax.ShapeDtypeStruct((depth, width), BF16)] * experts,
        in_specs=[smem()] * 2 + whole(2) + apart(parts),
        out_specs=whole(experts),
        scratch_shapes=[pltpu.VMEM((parts, size, units), BF16), pltpu.SemaphoreType.DMA((parts,))],
        compiler_params=params(),
        cost_estimate=COST,
    )(offsets, counts, *before, *hs)


def weight_kernel(experts, place_ref, own_ref, logits_ref, code_ref, out_ref, score_ref):
    me = place_ref[0]
    kernel = jnp.exp(logits_ref[...])
    row_scale = jnp.ones((kernel.shape[0], 1, kernel.shape[2]), F32)
    for sweep in range(3):
        column = jnp.sum(jnp.sum(kernel * row_scale, axis=0, keepdims=True), axis=2, keepdims=True)
        column_scale = 1.0 / column
        row_scale = 1.0 / jnp.sum(kernel * column_scale, axis=1, keepdims=True)
    own = jnp.exp(own_ref[...])
    column_scale = column_scale[0]
    own_scale = 1.0 / jnp.sum(own * column_scale, axis=0, keepdims=True)
    score_ref[...] = own_scale * own * column_scale
    picked = []
    for shift in range(experts):
        score = score_ref[pl.ds(lax.rem(me + shift, experts), 1), :]
        picked.append(jnp.where(code_ref[pl.ds(shift, 1), :] >= 0, score, 0.0))
    total = picked[0]
    for one in picked[1:]:
        total = total + one
    total = jnp.maximum(total, 1.0 / experts)
    for shift in range(experts):
        out_ref[pl.ds(shift, 1), :] = picked[shift] / total


def slot_weights(place, own, logits, code):
    experts, rows = own.shape
    return pl.pallas_call(
        functools.partial(weight_kernel, experts),
        out_shape=jax.ShapeDtypeStruct((experts, rows), F32),
        in_specs=[smem()] + whole(3),
        out_specs=whole(1)[0],
        scratch_shapes=[pltpu.VMEM((experts, rows), F32)],
        compiler_params=params(),
        cost_estimate=COST,
    )(place, own, logits, code)


def combine_kernel(experts, k, code_ref, weight_ref, *refs):
    before, refs = refs[: k > 0], refs[k > 0 :]
    blocks, (out_ref, held, sems) = refs[:experts], refs[experts:]
    depth = blocks[0].shape[0]
    rows = code_ref.shape[1]
    targets = [held.at[pl.ds(i * depth, depth)] for i in range(experts)]
    loads = start_all(blocks, targets, sems)
    slot_ids = lax.broadcasted_iota(I32, (depth, rows), 0) + k * depth
    parts = [
        jnp.where(slot_ids == code_ref[pl.ds(i, 1), :], weight_ref[pl.ds(i, 1), :], 0.0).astype(BF16)
        for i in range(experts)
    ]
    spread = jnp.concatenate(parts, axis=0)
    for load in loads:
        load.wait()
    total = lax.dot_general(spread, held[...], (((0,), (0,)), ((), ())), preferred_element_type=F32)
    if k > 0:
        total = total + before[0][...]
    out_ref[...] = total.astype(out_ref.dtype)


def combine(code, weights, k, blocks, so_far):
    experts = len(blocks)
    depth, width = blocks[0].shape
    rows = code.shape[1]
    last = k == BATCHES - 1
    more = [] if so_far is None else [so_far]
    return pl.pallas_call(
        functools.partial(combine_kernel, experts, k),
        out_shape=jax.ShapeDtypeStruct((rows, width), BF16 if last else F32),
        in_specs=whole(2 + len(more)) + apart(experts),
        out_specs=whole(1)[0],
        scratch_shapes=[pltpu.VMEM((experts * depth, width), BF16), pltpu.SemaphoreType.DMA((experts,))],
        compiler_params=params(),
        cost_estimate=COST,
    )(code, weights, *more, *blocks)


def after(value, *first):
    return lax.optimization_barrier((value, first))[0]


def shards(tokens, router_weight, gate_weight, up_weight, down_weight, picks):
    experts = lax.axis_size("expert")
    width_parts = lax.axis_size("dp")
    me = lax.axis_index("expert")
    part = lax.axis_index("dp")
    rows = tokens.shape[0]
    capacity = picks.shape[1]
    depth = 2 * capacity // experts // BATCHES
    size = capacity // BATCHES
    place = me.astype(I32).reshape(1)

    def along_expert(x, shift):
        return lax.ppermute(x, "expert", [(i, (i + shift) % experts) for i in range(experts)])

    def swap(x, bit):
        return lax.ppermute(x, "dp", [(i, i ^ bit) for i in range(width_parts)])

    bits = []
    bit = width_parts // 2
    while bit:
        bits.append(bit)
        bit //= 2
    near = [0]
    for bit in bits[1:]:
        near = near + [m ^ bit for m in near]
    masks = near + [m ^ bits[0] for m in near]
    places = range(len(masks))
    near_places, far_places = places[: len(near)], places[len(near) :]
    order = jnp.stack([part ^ m for m in masks]).astype(I32)

    def swap_expert(x, bit):
        return lax.ppermute(x, "expert", [(i, i ^ bit) for i in range(experts)])

    expert_bits = [1 << i for i in range(experts.bit_length() - 1)]

    def spread(x):
        held = [x]
        for bit in bits[1:]:
            held = held + [swap(h, bit) for h in held]
        return held

    def both_parts(x):
        far = swap(x, bits[0])
        return spread(x), spread(far)

    code, first = first_batch(place, picks, tokens, depth)
    own_picks = lax.dynamic_slice_in_dim(picks, me, 1, axis=0)
    sources = lax.rem(me - jnp.arange(experts, dtype=I32) + experts, experts)
    start = jnp.sum((own_picks < (sources * rows)[:, None]).astype(I32), axis=1)
    stop = jnp.sum((own_picks < ((sources + 1) * rows)[:, None]).astype(I32), axis=1)
    ids = jnp.arange(BATCHES, dtype=I32)[:, None]
    offsets = (start[None, :] + (BATCHES - 1) - ids) // BATCHES
    counts = (stop[None, :] + (BATCHES - 1) - ids) // BATCHES - offsets

    present = [jnp.sum(counts[k]) > 0 for k in range(BATCHES)]

    def beside_first(router):
        logits = partial_logits(router, tokens)
        later = [tuple(later_batch(code, tokens, k, depth)) for k in range(1, BATCHES)]
        for bit in bits:
            logits = logits + swap(logits, bit)
        gathered = logits[None]
        for bit in expert_bits[:-1]:
            gathered = jnp.concatenate([gathered, swap_expert(gathered, bit)])
        return later, logits, gathered

    def nothing_first(router):
        return jax.tree.map(lambda x: jnp.zeros(x.shape, x.dtype), jax.eval_shape(beside_first, router))

    arrived = [[first[0]] + [along_expert(first[shift], shift) for shift in range(1, experts)]]
    later, logits, gathered = lax.cond(present[0], beside_first, nothing_first, router_weight.T)

    def far_half(far, sums):
        far = spread(far)
        hidden = gate_up_far(far, sums)
        far = swap(hidden, bits[0])
        partial = down_first(order, near_places, far_places, down_weight, spread(hidden))
        far, partial = lax.optimization_barrier((far, partial))
        return spread(far), partial

    def settle(k, far, partial):
        return tuple(
            down_last(offsets, counts, k, far, partial, experts, depth)
        )

    def fenced(k, run, *operands):
        def skip(*operands):
            return jax.tree.map(lambda x: jnp.zeros(x.shape, x.dtype), jax.eval_shape(run, *operands))

        return lax.cond(present[k], run, skip, *operands)

    def send_back(results):
        return [results[0]] + [along_expert(results[shift], -shift) for shift in range(1, experts)]

    waiting = []
    far = partial = None
    moved = gathered
    for k in range(BATCHES):
        blocks = after(arrived[k], moved)
        if k < BATCHES - 1:
            moving = after(later[k], blocks)
            arrived.append([moving[0]] + [along_expert(moving[shift], shift) for shift in range(1, experts)])
        block = compact(offsets, counts, k, blocks, size)
        across = swap(block, bits[0])
        near = spread(block)
        if k == 1:
            gathered = after(gathered, blocks)
            gathered = jnp.concatenate([gathered, swap_expert(gathered, expert_bits[-1])])
        if k > 0:
            far, partial = after((far, partial), block)
            results = settle(k - 1, far, partial)
            if k == 1:
                results, gathered = lax.optimization_barrier((results, gathered))
            if k > 1:
                results, waiting[k - 2] = lax.optimization_barrier((results, waiting[k - 2]))
            waiting.append(send_back(results))
            near = after(near, results)
        sums = gate_up_near(order, near_places, far_places, gate_weight, up_weight, near)
        across, sums = lax.optimization_barrier((across, sums))
        far, partial = fenced(k, far_half, across, sums)
        moved = partial
    results = settle(BATCHES - 1, far, partial)
    results, waiting[-1] = lax.optimization_barrier((results, waiting[-1]))
    waiting.append(send_back(results))
    weights = slot_weights(place, logits, gathered, code)
    total = None
    for k in range(BATCHES):
        total = combine(code, weights, k, waiting[k], total)
    return total


def solution(mesh):
    return jax.shard_map(
        shards,
        mesh=mesh,
        in_specs=(
            P(("groups", "expert"), "dp"),
            P("dp", None),
            P("expert", None, "dp"),
            P("expert", None, "dp"),
            P("expert", None, "dp"),
            P("groups", None),
        ),
        out_specs=P(("groups", "expert"), "dp"),
        check_vma=False,
    )
```

```python
import functools

import jax
import jax.numpy as jnp
from jax import lax
from jax.experimental import pallas as pl
from jax.experimental.pallas import tpu as pltpu
from jax.sharding import PartitionSpec as P

BATCHES = 2
F32 = jnp.float32
BF16 = jnp.bfloat16
I32 = jnp.int32
VMEM_LIMIT = 16 * 1024 * 1024
COST = pl.CostEstimate(flops=1024, bytes_accessed=1024, transcendentals=0)


def whole(count):
    return [pl.BlockSpec(memory_space=pltpu.VMEM)] * count


def apart(count):
    return [pl.BlockSpec(memory_space=pl.ANY)] * count


def smem():
    return pl.BlockSpec(memory_space=pltpu.SMEM)


def params(limit=VMEM_LIMIT):
    return pltpu.CompilerParams(vmem_limit_bytes=limit)


def dot(a, b):
    return jnp.dot(a, b, preferred_element_type=F32)


def start_all(sources, targets, sems):
    copies = [pltpu.make_async_copy(a, b, sems.at[i]) for i, (a, b) in enumerate(zip(sources, targets))]
    for copy in copies:
        copy.start()
    return copies


def code_kernel(experts, depth, place_ref, picks_in, tokens_ref, code_ref, *refs):
    sends = refs[:experts]
    picks_ref, held, staged, in_sems, out_sems = refs[experts:]
    picks_load, load = start_all([picks_in, tokens_ref], [picks_ref, held], in_sems)
    me = place_ref[0]
    rows, width = held.shape
    capacity = picks_ref.shape[1]
    strips = rows // 128
    lanes = lax.broadcasted_iota(I32, (128, capacity), 0)
    strip_ids = lax.broadcasted_iota(I32, (8, capacity), 0)
    total = 8 * experts
    row_ids = lax.broadcasted_iota(I32, (total, total), 0)
    lane_ids = lax.broadcasted_iota(I32, (total, total), 1)
    same = lax.shift_right_logical(row_ids, 3) == lax.shift_right_logical(lane_ids, 3)
    before = (same & (lane_ids < row_ids)).astype(F32).astype(BF16)
    upper = (lax.broadcasted_iota(I32, (128, 128), 0) < lax.broadcasted_iota(I32, (128, 128), 1)).astype(BF16)
    ones = jnp.ones((128, 128), BF16)
    picks_load.wait()
    masks, starts = [], []
    for shift in range(experts):
        local = picks_ref[pl.ds(lax.rem(me + shift, experts), 1), :] - me * rows
        starts.append(jnp.broadcast_to(jnp.sum((local < 0).astype(F32), axis=1, keepdims=True), (8, 128)))
        strip = lax.shift_right_arithmetic(local, 7)
        place = jnp.bitwise_and(local, 127)
        high = ((strip == strip_ids) & (strip_ids < strips)).astype(F32).astype(BF16)
        low = (place == lanes).astype(F32).astype(BF16)
        masks.append(lax.dot_general(high, low, (((1,), (1,)), ((), ())), preferred_element_type=F32))
    mask = jnp.concatenate(masks, axis=0)
    start = jnp.concatenate(starts, axis=0).astype(I32)
    mask16 = mask.astype(BF16)
    totals = dot(mask16, ones)
    rank = (dot(mask16, upper) + dot(before, totals.astype(BF16))).astype(I32)
    slot = lax.rem(rank + start, BATCHES) * depth + lax.div(rank, BATCHES)
    code = jnp.where(mask > 0.5, slot, -1)
    code_rows = []
    for shift in range(experts):
        row = jnp.concatenate([code[8 * shift + i : 8 * shift + i + 1] for i in range(strips)], axis=1)
        code_ref[pl.ds(shift, 1), :] = row
        code_rows.append(row)
    load.wait()
    pack(0, depth, code_rows, held, staged, sends, out_sems)


def pack(k, depth, code_rows, held, staged, sends, sems):
    slot_ids = lax.broadcasted_iota(I32, (depth, held.shape[0]), 0) + k * depth
    copies = []
    for shift in list(range(1, len(sends))) + [0]:
        selector = (slot_ids == code_rows[shift]).astype(F32).astype(BF16)
        staged[shift] = dot(selector, held[...]).astype(BF16)
        copy = pltpu.make_async_copy(staged.at[shift], sends[shift], sems.at[shift])
        copy.start()
        copies.append(copy)
    for copy in copies:
        copy.wait()


def first_batch(place, picks, tokens, depth):
    rows, width = tokens.shape
    experts = picks.shape[0]
    out = pl.pallas_call(
        functools.partial(code_kernel, experts, depth),
        out_shape=[jax.ShapeDtypeStruct((experts, rows), I32)]
        + [jax.ShapeDtypeStruct((depth, width), BF16)] * experts,
        in_specs=[smem()] + apart(2),
        out_specs=whole(1) + apart(experts),
        scratch_shapes=[
            pltpu.VMEM(picks.shape, I32),
            pltpu.VMEM((rows, width), BF16),
            pltpu.VMEM((experts, depth, width), BF16),
            pltpu.SemaphoreType.DMA((2,)),
            pltpu.SemaphoreType.DMA((experts,)),
        ],
        compiler_params=params(60 * 1024 * 1024),
        cost_estimate=COST,
    )(place, picks, tokens)
    return out[0], out[1:]


def logits_kernel(router_ref, tokens_ref, out_ref):
    out_ref[...] = lax.dot_general(
        router_ref[...], tokens_ref[...], (((1,), (1,)), ((), ())), preferred_element_type=F32
    )


def partial_logits(router, tokens):
    return pl.pallas_call(
        logits_kernel,
        out_shape=jax.ShapeDtypeStruct((router.shape[0], tokens.shape[0]), F32),
        in_specs=whole(2),
        out_specs=whole(1)[0],
        compiler_params=params(),
        cost_estimate=COST,
    )(router, tokens)


def pack_kernel(experts, depth, k, code_ref, tokens_ref, *refs):
    sends = refs[:experts]
    held, staged, in_sems, out_sems = refs[experts:]
    start_all([tokens_ref], [held], in_sems)[0].wait()
    code_rows = [code_ref[pl.ds(shift, 1), :] for shift in range(experts)]
    pack(k, depth, code_rows, held, staged, sends, out_sems)


def later_batch(code, tokens, k, depth):
    rows, width = tokens.shape
    experts = code.shape[0]
    return pl.pallas_call(
        functools.partial(pack_kernel, experts, depth, k),
        out_shape=[jax.ShapeDtypeStruct((depth, width), BF16)] * experts,
        in_specs=whole(1) + apart(1),
        out_specs=apart(experts),
        scratch_shapes=[
            pltpu.VMEM((rows, width), BF16),
            pltpu.VMEM((experts, depth, width), BF16),
            pltpu.SemaphoreType.DMA((1,)),
            pltpu.SemaphoreType.DMA((experts,)),
        ],
        compiler_params=params(),
        cost_estimate=COST,
    )(code, tokens)


def compact_kernel(experts, k, offset_ref, count_ref, *refs):
    blocks, out_ref = refs[:experts], refs[experts]
    held, sems = refs[experts + 1 :]
    depth = blocks[0].shape[0]
    size = out_ref.shape[0]
    loads = start_all(blocks, [held.at[pl.ds(i * depth, depth)] for i in range(experts)], sems)
    row = lax.broadcasted_iota(I32, (size, depth), 0)
    lane = lax.broadcasted_iota(I32, (size, depth), 1)
    parts = [
        ((row - offset_ref[k, i] == lane) & (lane < count_ref[k, i])).astype(F32).astype(BF16)
        for i in range(experts)
    ]
    selector = jnp.concatenate(parts, axis=1)
    for load in loads:
        load.wait()
    out_ref[...] = dot(selector, held[...]).astype(BF16)


def compact(offsets, counts, k, blocks, size):
    experts = len(blocks)
    depth, width = blocks[0].shape
    return pl.pallas_call(
        functools.partial(compact_kernel, experts, k),
        out_shape=jax.ShapeDtypeStruct((size, width), BF16),
        in_specs=[smem(), smem()] + apart(experts),
        out_specs=whole(1)[0],
        scratch_shapes=[pltpu.VMEM((experts * depth, width), BF16), pltpu.SemaphoreType.DMA((experts,))],
        compiler_params=params(),
        cost_estimate=COST,
    )(offsets, counts, *blocks)


def gate_up_near_kernel(parts, near, far, order_ref, gate_ref, up_ref, *refs):
    xs, refs = refs[:parts], refs[parts:]
    gate_out, up_out, gate_far, up_far, gate_held, up_held, x_held, sems = refs
    width = xs[0].shape[1]

    def fetch(i, place, gate_to, up_to, base):
        first = pl.multiple_of(order_ref[place] * width, width)
        return start_all(
            [gate_ref.at[0, pl.ds(first, width), :], up_ref.at[0, pl.ds(first, width), :]],
            [gate_to.at[i], up_to.at[i]],
            sems.at[pl.ds(base, 2)],
        )

    x_loads = start_all(xs, [x_held.at[i] for i in range(parts)], sems.at[pl.ds(0, parts)])
    loads = [fetch(i, near[i], gate_held, up_held, parts + 2 * i) for i in range(parts)]
    late = [fetch(i, far[i], gate_far, up_far, 3 * parts + 2 * i) for i in range(len(far))]
    gate = up = None
    for i in range(parts):
        for copy in [x_loads[i]] + loads[i]:
            copy.wait()
        x = x_held[i]
        gate_term = dot(x, gate_held[i])
        up_term = dot(x, up_held[i])
        gate = gate_term if gate is None else gate + gate_term
        up = up_term if up is None else up + up_term
    gate_out[...] = gate
    up_out[...] = up
    for copies in late:
        for copy in copies:
            copy.wait()


def gate_up_near(order, near, far, gate_weight, up_weight, xs):
    parts = len(xs)
    size, width = xs[0].shape
    units = gate_weight.shape[2]
    held = jax.ShapeDtypeStruct((len(far), width, units), BF16)
    return pl.pallas_call(
        functools.partial(gate_up_near_kernel, parts, near, far),
        out_shape=[jax.ShapeDtypeStruct((size, units), F32)] * 2 + [held] * 2,
        in_specs=[smem()] + apart(2 + parts),
        out_specs=whole(4),
        scratch_shapes=[
            pltpu.VMEM((parts, width, units), BF16),
            pltpu.VMEM((parts, width, units), BF16),
            pltpu.VMEM((parts, size, width), BF16),
            pltpu.SemaphoreType.DMA((3 * parts + 2 * len(far),)),
        ],
        compiler_params=params(),
        cost_estimate=COST,
    )(order, gate_weight, up_weight, *xs)


def gate_up_far_kernel(parts, gate_before, up_before, gate_ref, up_ref, *refs):
    xs, out_ref = refs[:parts], refs[parts]
    gate, up = gate_before[...], up_before[...]
    for i in range(parts):
        x = xs[i][...]
        gate = gate + dot(x, gate_ref[i])
        up = up + dot(x, up_ref[i])
    out_ref[...] = (gate * jax.nn.sigmoid(gate) * up).astype(BF16)


def gate_up_far(xs, before):
    size, units = before[0].shape
    return pl.pallas_call(
        functools.partial(gate_up_far_kernel, len(xs)),
        out_shape=jax.ShapeDtypeStruct((size, units), BF16),
        in_specs=whole(4 + len(xs)),
        out_specs=whole(1)[0],
        compiler_params=params(),
        cost_estimate=COST,
    )(*before, *xs)


def down_first_kernel(parts, near, far, order_ref, down_ref, *refs):
    hs, (out_ref, far_ref, down_held, h_held, sems) = refs[:parts], refs[parts:]
    units = hs[0].shape[1]

    def fetch(i, place, target, sem):
        first = pl.multiple_of(order_ref[place] * units, units)
        copy = pltpu.make_async_copy(down_ref.at[0, pl.ds(first, units), :], target.at[i], sems.at[sem])
        copy.start()
        return copy

    h_loads = start_all(hs, [h_held.at[i] for i in range(parts)], sems.at[pl.ds(0, parts)])
    loads = [fetch(i, near[i], down_held, parts + i) for i in range(parts)]
    late = [fetch(i, far[i], far_ref, 2 * parts + i) for i in range(len(far))]
    total = None
    for i in range(parts):
        h_loads[i].wait()
        loads[i].wait()
        term = dot(h_held[i], down_held[i])
        total = term if total is None else total + term
    out_ref[...] = total
    for copy in late:
        copy.wait()


def down_first(order, near, far, down_weight, hs):
    parts = len(hs)
    size, units = hs[0].shape
    width = down_weight.shape[2]
    return pl.pallas_call(
        functools.partial(down_first_kernel, parts, near, far),
        out_shape=[
            jax.ShapeDtypeStruct((size, width), F32),
            jax.ShapeDtypeStruct((len(far), units, width), BF16),
        ],
        in_specs=[smem()] + apart(1 + parts),
        out_specs=whole(2),
        scratch_shapes=[
            pltpu.VMEM((parts, units, width), BF16),
            pltpu.VMEM((parts, size, units), BF16),
            pltpu.SemaphoreType.DMA((2 * parts + len(far),)),
        ],
        compiler_params=params(),
        cost_estimate=COST,
    )(order, down_weight, *hs)


def down_last_kernel(parts, experts, k, direct, offset_ref, count_ref, before_ref, down_ref, *refs):
    hs, outs = refs[:parts], refs[parts : parts + experts]
    h_held, sems, *staged = refs[parts + experts :]
    loads = start_all(hs, [h_held.at[i] for i in range(parts)], sems)
    size = hs[0].shape[0]
    depth = outs[0].shape[0]
    row = lax.broadcasted_iota(I32, (depth, size), 0)
    lane = lax.broadcasted_iota(I32, (depth, size), 1)
    picks = [
        ((lane - offset_ref[k, i] == row) & (row < count_ref[k, i])).astype(F32).astype(BF16)
        for i in range(experts)
    ]
    total = before_ref[...]
    for i in range(parts):
        loads[i].wait()
        total = total + dot(h_held[i], down_ref[i])
    result = total.astype(BF16)
    if direct:
        for i in range(experts):
            outs[i][...] = dot(picks[i], result).astype(BF16)
        return
    staged_ref, out_sems = staged
    copies = []
    for i in list(range(1, experts)) + [0]:
        staged_ref[i] = dot(picks[i], result).astype(BF16)
        copy = pltpu.make_async_copy(staged_ref.at[i], outs[i], out_sems.at[i])
        copy.start()
        copies.append(copy)
    for copy in copies:
        copy.wait()


def down_last(offsets, counts, k, hs, before, experts, depth, direct):
    parts = len(hs)
    size, units = hs[0].shape
    width = before[0].shape[1]
    return pl.pallas_call(
        functools.partial(down_last_kernel, parts, experts, k, direct),
        out_shape=[jax.ShapeDtypeStruct((depth, width), BF16)] * experts,
        in_specs=[smem()] * 2 + whole(2) + apart(parts),
        out_specs=whole(experts) if direct else apart(experts),
        scratch_shapes=[pltpu.VMEM((parts, size, units), BF16), pltpu.SemaphoreType.DMA((parts,))]
        + ([] if direct else [pltpu.VMEM((experts, depth, width), BF16), pltpu.SemaphoreType.DMA((experts,))]),
        compiler_params=params(),
        cost_estimate=COST,
    )(offsets, counts, *before, *hs)


def weight_kernel(experts, place_ref, own_ref, logits_ref, code_ref, out_ref, score_ref):
    me = place_ref[0]
    kernel = jnp.exp(logits_ref[...])
    row_scale = jnp.ones((kernel.shape[0], 1, kernel.shape[2]), F32)
    for sweep in range(3):
        column = jnp.sum(jnp.sum(kernel * row_scale, axis=0, keepdims=True), axis=2, keepdims=True)
        column_scale = 1.0 / column
        row_scale = 1.0 / jnp.sum(kernel * column_scale, axis=1, keepdims=True)
    own = jnp.exp(own_ref[...])
    column_scale = column_scale[0]
    own_scale = 1.0 / jnp.sum(own * column_scale, axis=0, keepdims=True)
    score_ref[...] = own_scale * own * column_scale
    picked = []
    for shift in range(experts):
        score = score_ref[pl.ds(lax.rem(me + shift, experts), 1), :]
        picked.append(jnp.where(code_ref[pl.ds(shift, 1), :] >= 0, score, 0.0))
    total = picked[0]
    for one in picked[1:]:
        total = total + one
    total = jnp.maximum(total, 1.0 / experts)
    for shift in range(experts):
        out_ref[pl.ds(shift, 1), :] = picked[shift] / total


def slot_weights(place, own, logits, code):
    experts, rows = own.shape
    return pl.pallas_call(
        functools.partial(weight_kernel, experts),
        out_shape=jax.ShapeDtypeStruct((experts, rows), F32),
        in_specs=[smem()] + whole(3),
        out_specs=whole(1)[0],
        scratch_shapes=[pltpu.VMEM((experts, rows), F32)],
        compiler_params=params(),
        cost_estimate=COST,
    )(place, own, logits, code)


def combine_kernel(experts, k, code_ref, weight_ref, *refs):
    before, refs = refs[: k > 0], refs[k > 0 :]
    blocks, (out_ref, held, sems) = refs[:experts], refs[experts:]
    depth = blocks[0].shape[0]
    rows = code_ref.shape[1]
    targets = [held.at[pl.ds(i * depth, depth)] for i in range(experts)]
    loads = start_all(blocks, targets, sems)
    slot_ids = lax.broadcasted_iota(I32, (depth, rows), 0) + k * depth
    parts = [
        jnp.where(slot_ids == code_ref[pl.ds(i, 1), :], weight_ref[pl.ds(i, 1), :], 0.0).astype(BF16)
        for i in range(experts)
    ]
    spread = jnp.concatenate(parts, axis=0)
    for load in loads:
        load.wait()
    total = lax.dot_general(spread, held[...], (((0,), (0,)), ((), ())), preferred_element_type=F32)
    if k > 0:
        total = total + before[0][...]
    out_ref[...] = total.astype(out_ref.dtype)


def combine(code, weights, k, blocks, so_far):
    experts = len(blocks)
    depth, width = blocks[0].shape
    rows = code.shape[1]
    last = k == BATCHES - 1
    more = [] if so_far is None else [so_far]
    return pl.pallas_call(
        functools.partial(combine_kernel, experts, k),
        out_shape=jax.ShapeDtypeStruct((rows, width), BF16 if last else F32),
        in_specs=whole(2 + len(more)) + apart(experts),
        out_specs=whole(1)[0],
        scratch_shapes=[pltpu.VMEM((experts * depth, width), BF16), pltpu.SemaphoreType.DMA((experts,))],
        compiler_params=params(),
        cost_estimate=COST,
    )(code, weights, *more, *blocks)


def after(value, *first):
    return lax.optimization_barrier((value, first))[0]


def shards(tokens, router_weight, gate_weight, up_weight, down_weight, picks):
    experts = lax.axis_size("expert")
    width_parts = lax.axis_size("dp")
    me = lax.axis_index("expert")
    part = lax.axis_index("dp")
    rows = tokens.shape[0]
    capacity = picks.shape[1]
    depth = 2 * capacity // experts // BATCHES
    size = capacity // BATCHES
    place = me.astype(I32).reshape(1)

    def along_expert(x, shift):
        return lax.ppermute(x, "expert", [(i, (i + shift) % experts) for i in range(experts)])

    def swap(x, bit):
        return lax.ppermute(x, "dp", [(i, i ^ bit) for i in range(width_parts)])

    bits = []
    bit = width_parts // 2
    while bit:
        bits.append(bit)
        bit //= 2
    near = [0]
    for bit in bits[1:]:
        near = near + [m ^ bit for m in near]
    masks = near + [m ^ bits[0] for m in near]
    places = range(len(masks))
    near_places, far_places = places[: len(near)], places[len(near) :]
    order = jnp.stack([part ^ m for m in masks]).astype(I32)

    def swap_expert(x, bit):
        return lax.ppermute(x, "expert", [(i, i ^ bit) for i in range(experts)])

    expert_bits = [1 << i for i in range(experts.bit_length() - 1)]

    def spread(x):
        held = [x]
        for bit in bits[1:]:
            held = held + [swap(h, bit) for h in held]
        return held

    def both_parts(x):
        far = swap(x, bits[0])
        return spread(x), spread(far)

    code, first = first_batch(place, picks, tokens, depth)
    own_picks = lax.dynamic_slice_in_dim(picks, me, 1, axis=0)
    sources = lax.rem(me - jnp.arange(experts, dtype=I32) + experts, experts)
    start = jnp.sum((own_picks < (sources * rows)[:, None]).astype(I32), axis=1)
    stop = jnp.sum((own_picks < ((sources + 1) * rows)[:, None]).astype(I32), axis=1)
    ids = jnp.arange(BATCHES, dtype=I32)[:, None]
    offsets = (start[None, :] + (BATCHES - 1) - ids) // BATCHES
    counts = (stop[None, :] + (BATCHES - 1) - ids) // BATCHES - offsets

    present = [jnp.sum(counts[k]) > 0 for k in range(BATCHES)]

    def beside_first(router):
        logits = partial_logits(router, tokens)
        later = [tuple(later_batch(code, tokens, k, depth)) for k in range(1, BATCHES)]
        for bit in bits:
            logits = logits + swap(logits, bit)
        gathered = logits[None]
        for bit in expert_bits[:-1]:
            gathered = jnp.concatenate([gathered, swap_expert(gathered, bit)])
        return later, logits, gathered

    def nothing_first(router):
        return jax.tree.map(lambda x: jnp.zeros(x.shape, x.dtype), jax.eval_shape(beside_first, router))

    arrived = [[first[0]] + [along_expert(first[shift], shift) for shift in range(1, experts)]]
    later, logits, gathered = lax.cond(present[0], beside_first, nothing_first, router_weight.T)

    def far_half(far, sums):
        far = spread(far)
        hidden = gate_up_far(far, sums)
        far = swap(hidden, bits[0])
        partial = down_first(order, near_places, far_places, down_weight, spread(hidden))
        far, partial = lax.optimization_barrier((far, partial))
        return spread(far), partial

    def settle(k, far, partial):
        return tuple(
            down_last(offsets, counts, k, far, partial, experts, depth, k == BATCHES - 1)
        )

    def fenced(k, run, *operands):
        def skip(*operands):
            return jax.tree.map(lambda x: jnp.zeros(x.shape, x.dtype), jax.eval_shape(run, *operands))

        return lax.cond(present[k], run, skip, *operands)

    def send_back(results):
        return [results[0]] + [along_expert(results[shift], -shift) for shift in range(1, experts)]

    waiting = []
    far = partial = None
    moved = gathered
    for k in range(BATCHES):
        blocks = after(arrived[k], moved)
        if k < BATCHES - 1:
            moving = after(later[k], blocks)
            arrived.append([moving[0]] + [along_expert(moving[shift], shift) for shift in range(1, experts)])
        if k == 0:
            block = fenced(k, lambda *blocks: compact(offsets, counts, 0, blocks, size), *blocks)
        else:
            block = compact(offsets, counts, k, blocks, size)
        across = swap(block, bits[0])
        near = spread(block)
        if k > 0:
            far, partial = after((far, partial), block)
            results = settle(k - 1, far, partial)
            if k > 1:
                results, waiting[k - 2] = lax.optimization_barrier((results, waiting[k - 2]))
            waiting.append(send_back(results))
            near = after(near, results)
        sums = gate_up_near(order, near_places, far_places, gate_weight, up_weight, near)
        across, sums = lax.optimization_barrier((across, sums))
        if k == BATCHES - 1:
            gathered = after(gathered, sums)
            gathered = jnp.concatenate([gathered, swap_expert(gathered, expert_bits[-1])])
        far, partial = fenced(k, far_half, across, sums)
        moved = partial
    results = settle(BATCHES - 1, far, partial)
    results, gathered, waiting[-1] = lax.optimization_barrier((results, gathered, waiting[-1]))
    waiting.append(send_back(results))
    weights = slot_weights(place, logits, gathered, code)
    total = None
    for k in range(BATCHES):
        total = combine(code, weights, k, waiting[k], total)
    return total


def solution(mesh):
    return jax.shard_map(
        shards,
        mesh=mesh,
        in_specs=(
            P(("groups", "expert"), "dp"),
            P("dp", None),
            P("expert", None, "dp"),
            P("expert", None, "dp"),
            P("expert", None, "dp"),
            P("groups", None),
        ),
        out_specs=P(("groups", "expert"), "dp"),
        check_vma=False,
    )
```

```python
import functools

import jax
import jax.numpy as jnp
from jax import lax
from jax.experimental import pallas as pl
from jax.experimental.pallas import tpu as pltpu
from jax.sharding import PartitionSpec as P

BATCHES = 2
F32 = jnp.float32
BF16 = jnp.bfloat16
I32 = jnp.int32
VMEM_LIMIT = 16 * 1024 * 1024
COST = pl.CostEstimate(flops=1024, bytes_accessed=1024, transcendentals=0)


def whole(count):
    return [pl.BlockSpec(memory_space=pltpu.VMEM)] * count


def apart(count):
    return [pl.BlockSpec(memory_space=pl.ANY)] * count


def smem():
    return pl.BlockSpec(memory_space=pltpu.SMEM)


def params(limit=VMEM_LIMIT):
    return pltpu.CompilerParams(vmem_limit_bytes=limit)


def partner(place, experts):
    return -place % experts


def dot(a, b):
    return jnp.dot(a, b, preferred_element_type=F32)


def start_all(sources, targets, sems):
    copies = [pltpu.make_async_copy(a, b, sems.at[i]) for i, (a, b) in enumerate(zip(sources, targets))]
    for copy in copies:
        copy.start()
    return copies


def code_kernel(experts, depth, place_ref, picks_in, tokens_ref, code_ref, *refs):
    sends = refs[:experts]
    picks_ref, held, staged, in_sems, out_sems = refs[experts:]
    picks_load, load = start_all([picks_in, tokens_ref], [picks_ref, held], in_sems)
    me = place_ref[0]
    rows, width = held.shape
    capacity = picks_ref.shape[1]
    strips = rows // 128
    lanes = lax.broadcasted_iota(I32, (128, capacity), 0)
    strip_ids = lax.broadcasted_iota(I32, (8, capacity), 0)
    total = 8 * experts
    row_ids = lax.broadcasted_iota(I32, (total, total), 0)
    lane_ids = lax.broadcasted_iota(I32, (total, total), 1)
    same = lax.shift_right_logical(row_ids, 3) == lax.shift_right_logical(lane_ids, 3)
    before = (same & (lane_ids < row_ids)).astype(F32).astype(BF16)
    upper = (lax.broadcasted_iota(I32, (128, 128), 0) < lax.broadcasted_iota(I32, (128, 128), 1)).astype(BF16)
    ones = jnp.ones((128, 128), BF16)
    picks_load.wait()
    masks, starts = [], []
    for shift in range(experts):
        local = picks_ref[pl.ds(jnp.bitwise_xor(me, partner(shift, experts)), 1), :] - me * rows
        starts.append(jnp.broadcast_to(jnp.sum((local < 0).astype(F32), axis=1, keepdims=True), (8, 128)))
        strip = lax.shift_right_arithmetic(local, 7)
        place = jnp.bitwise_and(local, 127)
        high = ((strip == strip_ids) & (strip_ids < strips)).astype(F32).astype(BF16)
        low = (place == lanes).astype(F32).astype(BF16)
        masks.append(lax.dot_general(high, low, (((1,), (1,)), ((), ())), preferred_element_type=F32))
    mask = jnp.concatenate(masks, axis=0)
    start = jnp.concatenate(starts, axis=0).astype(I32)
    mask16 = mask.astype(BF16)
    totals = dot(mask16, ones)
    rank = (dot(mask16, upper) + dot(before, totals.astype(BF16))).astype(I32)
    slot = lax.rem(rank + start, BATCHES) * depth + lax.div(rank, BATCHES)
    code = jnp.where(mask > 0.5, slot, -1)
    code_rows = []
    for shift in range(experts):
        row = jnp.concatenate([code[8 * shift + i : 8 * shift + i + 1] for i in range(strips)], axis=1)
        code_ref[pl.ds(shift, 1), :] = row
        code_rows.append(row)
    load.wait()
    pack(0, depth, code_rows, held, staged, sends, out_sems)


def pack(k, depth, code_rows, held, staged, sends, sems):
    slot_ids = lax.broadcasted_iota(I32, (depth, held.shape[0]), 0) + k * depth
    copies = []
    for shift in list(range(1, len(sends))) + [0]:
        selector = (slot_ids == code_rows[shift]).astype(F32).astype(BF16)
        staged[shift] = dot(selector, held[...]).astype(BF16)
        copy = pltpu.make_async_copy(staged.at[shift], sends[shift], sems.at[shift])
        copy.start()
        copies.append(copy)
    for copy in copies:
        copy.wait()


def first_batch(place, picks, tokens, depth):
    rows, width = tokens.shape
    experts = picks.shape[0]
    out = pl.pallas_call(
        functools.partial(code_kernel, experts, depth),
        out_shape=[jax.ShapeDtypeStruct((experts, rows), I32)]
        + [jax.ShapeDtypeStruct((depth, width), BF16)] * experts,
        in_specs=[smem()] + apart(2),
        out_specs=whole(1) + apart(experts),
        scratch_shapes=[
            pltpu.VMEM(picks.shape, I32),
            pltpu.VMEM((rows, width), BF16),
            pltpu.VMEM((experts, depth, width), BF16),
            pltpu.SemaphoreType.DMA((2,)),
            pltpu.SemaphoreType.DMA((experts,)),
        ],
        compiler_params=params(60 * 1024 * 1024),
        cost_estimate=COST,
    )(place, picks, tokens)
    return out[0], out[1:]


def logits_kernel(router_ref, tokens_ref, out_ref):
    out_ref[...] = lax.dot_general(
        router_ref[...], tokens_ref[...], (((1,), (1,)), ((), ())), preferred_element_type=F32
    )


def partial_logits(router, tokens):
    return pl.pallas_call(
        logits_kernel,
        out_shape=jax.ShapeDtypeStruct((router.shape[0], tokens.shape[0]), F32),
        in_specs=whole(2),
        out_specs=whole(1)[0],
        compiler_params=params(),
        cost_estimate=COST,
    )(router, tokens)


def pack_kernel(experts, depth, k, code_ref, tokens_ref, *refs):
    sends = refs[:experts]
    held, staged, in_sems, out_sems = refs[experts:]
    start_all([tokens_ref], [held], in_sems)[0].wait()
    code_rows = [code_ref[pl.ds(shift, 1), :] for shift in range(experts)]
    pack(k, depth, code_rows, held, staged, sends, out_sems)


def later_batch(code, tokens, k, depth):
    rows, width = tokens.shape
    experts = code.shape[0]
    return pl.pallas_call(
        functools.partial(pack_kernel, experts, depth, k),
        out_shape=[jax.ShapeDtypeStruct((depth, width), BF16)] * experts,
        in_specs=whole(1) + apart(1),
        out_specs=apart(experts),
        scratch_shapes=[
            pltpu.VMEM((rows, width), BF16),
            pltpu.VMEM((experts, depth, width), BF16),
            pltpu.SemaphoreType.DMA((1,)),
            pltpu.SemaphoreType.DMA((experts,)),
        ],
        compiler_params=params(),
        cost_estimate=COST,
    )(code, tokens)


def compact_kernel(experts, k, offset_ref, count_ref, *refs):
    blocks, out_ref = refs[:experts], refs[experts]
    held, sems = refs[experts + 1 :]
    depth = blocks[0].shape[0]
    size = out_ref.shape[0]
    loads = start_all(blocks, [held.at[pl.ds(i * depth, depth)] for i in range(experts)], sems)
    row = lax.broadcasted_iota(I32, (size, depth), 0)
    lane = lax.broadcasted_iota(I32, (size, depth), 1)
    parts = [
        ((row - offset_ref[k, i] == lane) & (lane < count_ref[k, i])).astype(F32).astype(BF16)
        for i in range(experts)
    ]
    selector = jnp.concatenate(parts, axis=1)
    for load in loads:
        load.wait()
    out_ref[...] = dot(selector, held[...]).astype(BF16)


def compact(offsets, counts, k, blocks, size):
    experts = len(blocks)
    depth, width = blocks[0].shape
    return pl.pallas_call(
        functools.partial(compact_kernel, experts, k),
        out_shape=jax.ShapeDtypeStruct((size, width), BF16),
        in_specs=[smem(), smem()] + apart(experts),
        out_specs=whole(1)[0],
        scratch_shapes=[pltpu.VMEM((experts * depth, width), BF16), pltpu.SemaphoreType.DMA((experts,))],
        compiler_params=params(),
        cost_estimate=COST,
    )(offsets, counts, *blocks)


def gate_up_near_kernel(parts, near, far, order_ref, gate_ref, up_ref, *refs):
    xs, refs = refs[:parts], refs[parts:]
    gate_out, up_out, gate_far, up_far, gate_held, up_held, x_held, sems = refs
    width = xs[0].shape[1]

    def fetch(i, place, gate_to, up_to, base):
        first = pl.multiple_of(order_ref[place] * width, width)
        return start_all(
            [gate_ref.at[0, pl.ds(first, width), :], up_ref.at[0, pl.ds(first, width), :]],
            [gate_to.at[i], up_to.at[i]],
            sems.at[pl.ds(base, 2)],
        )

    x_loads = start_all(xs, [x_held.at[i] for i in range(parts)], sems.at[pl.ds(0, parts)])
    loads = [fetch(i, near[i], gate_held, up_held, parts + 2 * i) for i in range(parts)]
    late = [fetch(i, far[i], gate_far, up_far, 3 * parts + 2 * i) for i in range(len(far))]
    gate = up = None
    for i in range(parts):
        for copy in [x_loads[i]] + loads[i]:
            copy.wait()
        x = x_held[i]
        gate_term = dot(x, gate_held[i])
        up_term = dot(x, up_held[i])
        gate = gate_term if gate is None else gate + gate_term
        up = up_term if up is None else up + up_term
    gate_out[...] = gate
    up_out[...] = up
    for copies in late:
        for copy in copies:
            copy.wait()


def gate_up_near(order, near, far, gate_weight, up_weight, xs):
    parts = len(xs)
    size, width = xs[0].shape
    units = gate_weight.shape[2]
    held = jax.ShapeDtypeStruct((len(far), width, units), BF16)
    return pl.pallas_call(
        functools.partial(gate_up_near_kernel, parts, near, far),
        out_shape=[jax.ShapeDtypeStruct((size, units), F32)] * 2 + [held] * 2,
        in_specs=[smem()] + apart(2 + parts),
        out_specs=whole(4),
        scratch_shapes=[
            pltpu.VMEM((parts, width, units), BF16),
            pltpu.VMEM((parts, width, units), BF16),
            pltpu.VMEM((parts, size, width), BF16),
            pltpu.SemaphoreType.DMA((3 * parts + 2 * len(far),)),
        ],
        compiler_params=params(),
        cost_estimate=COST,
    )(order, gate_weight, up_weight, *xs)


def gate_up_far_kernel(parts, gate_before, up_before, gate_ref, up_ref, *refs):
    xs, out_ref = refs[:parts], refs[parts]
    gate, up = gate_before[...], up_before[...]
    for i in range(parts):
        x = xs[i][...]
        gate = gate + dot(x, gate_ref[i])
        up = up + dot(x, up_ref[i])
    out_ref[...] = (gate * jax.nn.sigmoid(gate) * up).astype(BF16)


def gate_up_far(xs, before):
    size, units = before[0].shape
    return pl.pallas_call(
        functools.partial(gate_up_far_kernel, len(xs)),
        out_shape=jax.ShapeDtypeStruct((size, units), BF16),
        in_specs=whole(4 + len(xs)),
        out_specs=whole(1)[0],
        compiler_params=params(),
        cost_estimate=COST,
    )(*before, *xs)


def down_first_kernel(parts, near, far, order_ref, down_ref, *refs):
    hs, (out_ref, far_ref, down_held, h_held, sems) = refs[:parts], refs[parts:]
    units = hs[0].shape[1]

    def fetch(i, place, target, sem):
        first = pl.multiple_of(order_ref[place] * units, units)
        copy = pltpu.make_async_copy(down_ref.at[0, pl.ds(first, units), :], target.at[i], sems.at[sem])
        copy.start()
        return copy

    h_loads = start_all(hs, [h_held.at[i] for i in range(parts)], sems.at[pl.ds(0, parts)])
    loads = [fetch(i, near[i], down_held, parts + i) for i in range(parts)]
    late = [fetch(i, far[i], far_ref, 2 * parts + i) for i in range(len(far))]
    total = None
    for i in range(parts):
        h_loads[i].wait()
        loads[i].wait()
        term = dot(h_held[i], down_held[i])
        total = term if total is None else total + term
    out_ref[...] = total
    for copy in late:
        copy.wait()


def down_first(order, near, far, down_weight, hs):
    parts = len(hs)
    size, units = hs[0].shape
    width = down_weight.shape[2]
    return pl.pallas_call(
        functools.partial(down_first_kernel, parts, near, far),
        out_shape=[
            jax.ShapeDtypeStruct((size, width), F32),
            jax.ShapeDtypeStruct((len(far), units, width), BF16),
        ],
        in_specs=[smem()] + apart(1 + parts),
        out_specs=whole(2),
        scratch_shapes=[
            pltpu.VMEM((parts, units, width), BF16),
            pltpu.VMEM((parts, size, units), BF16),
            pltpu.SemaphoreType.DMA((2 * parts + len(far),)),
        ],
        compiler_params=params(),
        cost_estimate=COST,
    )(order, down_weight, *hs)


def down_last_kernel(parts, experts, k, direct, offset_ref, count_ref, before_ref, down_ref, *refs):
    hs, outs = refs[:parts], refs[parts : parts + experts]
    h_held, sems, *staged = refs[parts + experts :]
    loads = start_all(hs, [h_held.at[i] for i in range(parts)], sems)
    size = hs[0].shape[0]
    depth = outs[0].shape[0]
    row = lax.broadcasted_iota(I32, (depth, size), 0)
    lane = lax.broadcasted_iota(I32, (depth, size), 1)
    picks = [
        ((lane - offset_ref[k, i] == row) & (row < count_ref[k, i])).astype(F32).astype(BF16)
        for i in range(experts)
    ]
    total = before_ref[...]
    for i in range(parts):
        loads[i].wait()
        total = total + dot(h_held[i], down_ref[i])
    result = total.astype(BF16)
    if direct:
        for i in range(experts):
            outs[i][...] = dot(picks[i], result).astype(BF16)
        return
    staged_ref, out_sems = staged
    copies = []
    for i in list(range(1, experts)) + [0]:
        staged_ref[i] = dot(picks[i], result).astype(BF16)
        copy = pltpu.make_async_copy(staged_ref.at[i], outs[i], out_sems.at[i])
        copy.start()
        copies.append(copy)
    for copy in copies:
        copy.wait()


def down_last(offsets, counts, k, hs, before, experts, depth, direct):
    parts = len(hs)
    size, units = hs[0].shape
    width = before[0].shape[1]
    return pl.pallas_call(
        functools.partial(down_last_kernel, parts, experts, k, direct),
        out_shape=[jax.ShapeDtypeStruct((depth, width), BF16)] * experts,
        in_specs=[smem()] * 2 + whole(2) + apart(parts),
        out_specs=whole(experts) if direct else apart(experts),
        scratch_shapes=[pltpu.VMEM((parts, size, units), BF16), pltpu.SemaphoreType.DMA((parts,))]
        + ([] if direct else [pltpu.VMEM((experts, depth, width), BF16), pltpu.SemaphoreType.DMA((experts,))]),
        compiler_params=params(),
        cost_estimate=COST,
    )(offsets, counts, *before, *hs)


def weight_kernel(experts, place_ref, own_ref, logits_ref, code_ref, out_ref, score_ref):
    me = place_ref[0]
    kernel = jnp.exp(logits_ref[...])
    row_scale = jnp.ones((kernel.shape[0], 1, kernel.shape[2]), F32)
    for sweep in range(3):
        column = jnp.sum(jnp.sum(kernel * row_scale, axis=0, keepdims=True), axis=2, keepdims=True)
        column_scale = 1.0 / column
        row_scale = 1.0 / jnp.sum(kernel * column_scale, axis=1, keepdims=True)
    own = jnp.exp(own_ref[...])
    column_scale = column_scale[0]
    own_scale = 1.0 / jnp.sum(own * column_scale, axis=0, keepdims=True)
    score_ref[...] = own_scale * own * column_scale
    picked = []
    for shift in range(experts):
        score = score_ref[pl.ds(jnp.bitwise_xor(me, partner(shift, experts)), 1), :]
        picked.append(jnp.where(code_ref[pl.ds(shift, 1), :] >= 0, score, 0.0))
    total = picked[0]
    for one in picked[1:]:
        total = total + one
    total = jnp.maximum(total, 1.0 / experts)
    for shift in range(experts):
        out_ref[pl.ds(shift, 1), :] = picked[shift] / total


def slot_weights(place, own, logits, code):
    experts, rows = own.shape
    return pl.pallas_call(
        functools.partial(weight_kernel, experts),
        out_shape=jax.ShapeDtypeStruct((experts, rows), F32),
        in_specs=[smem()] + whole(3),
        out_specs=whole(1)[0],
        scratch_shapes=[pltpu.VMEM((experts, rows), F32)],
        compiler_params=params(),
        cost_estimate=COST,
    )(place, own, logits, code)


def combine_kernel(experts, k, code_ref, weight_ref, *refs):
    before, refs = refs[: k > 0], refs[k > 0 :]
    blocks, (out_ref, held, sems) = refs[:experts], refs[experts:]
    depth = blocks[0].shape[0]
    rows = code_ref.shape[1]
    targets = [held.at[pl.ds(i * depth, depth)] for i in range(experts)]
    loads = start_all(blocks, targets, sems)
    slot_ids = lax.broadcasted_iota(I32, (depth, rows), 0) + k * depth
    parts = [
        jnp.where(slot_ids == code_ref[pl.ds(i, 1), :], weight_ref[pl.ds(i, 1), :], 0.0).astype(BF16)
        for i in range(experts)
    ]
    spread = jnp.concatenate(parts, axis=0)
    for load in loads:
        load.wait()
    total = lax.dot_general(spread, held[...], (((0,), (0,)), ((), ())), preferred_element_type=F32)
    if k > 0:
        total = total + before[0][...]
    out_ref[...] = total.astype(out_ref.dtype)


def combine(code, weights, k, blocks, so_far):
    experts = len(blocks)
    depth, width = blocks[0].shape
    rows = code.shape[1]
    last = k == BATCHES - 1
    more = [] if so_far is None else [so_far]
    return pl.pallas_call(
        functools.partial(combine_kernel, experts, k),
        out_shape=jax.ShapeDtypeStruct((rows, width), BF16 if last else F32),
        in_specs=whole(2 + len(more)) + apart(experts),
        out_specs=whole(1)[0],
        scratch_shapes=[pltpu.VMEM((experts * depth, width), BF16), pltpu.SemaphoreType.DMA((experts,))],
        compiler_params=params(),
        cost_estimate=COST,
    )(code, weights, *more, *blocks)


def after(value, *first):
    return lax.optimization_barrier((value, first))[0]


def shards(tokens, router_weight, gate_weight, up_weight, down_weight, picks):
    experts = lax.axis_size("expert")
    width_parts = lax.axis_size("dp")
    me = lax.axis_index("expert")
    part = lax.axis_index("dp")
    rows = tokens.shape[0]
    capacity = picks.shape[1]
    depth = 2 * capacity // experts // BATCHES
    size = capacity // BATCHES
    place = me.astype(I32).reshape(1)

    def along_expert(x, shift):
        return lax.ppermute(x, "expert", [(i, i ^ shift) for i in range(experts)])

    def swap(x, bit):
        return lax.ppermute(x, "dp", [(i, i ^ bit) for i in range(width_parts)])

    bits = []
    bit = width_parts // 2
    while bit:
        bits.append(bit)
        bit //= 2
    near = [0]
    for bit in bits[1:]:
        near = near + [m ^ bit for m in near]
    masks = near + [m ^ bits[0] for m in near]
    places = range(len(masks))
    near_places, far_places = places[: len(near)], places[len(near) :]
    order = jnp.stack([part ^ m for m in masks]).astype(I32)

    def exchange(blocks):
        return [blocks[0]] + [along_expert(blocks[i], partner(i, experts)) for i in range(1, experts)]

    expert_bits = [1 << i for i in range(experts.bit_length() - 1)]

    def spread(x):
        held = [x]
        for bit in bits[1:]:
            held = held + [swap(h, bit) for h in held]
        return held

    def both_parts(x):
        far = swap(x, bits[0])
        return spread(x), spread(far)

    code, first = first_batch(place, picks, tokens, depth)
    own_picks = lax.dynamic_slice_in_dim(picks, me, 1, axis=0)
    sources = jnp.bitwise_xor(me, jnp.array([partner(i, experts) for i in range(experts)], I32))
    start = jnp.sum((own_picks < (sources * rows)[:, None]).astype(I32), axis=1)
    stop = jnp.sum((own_picks < ((sources + 1) * rows)[:, None]).astype(I32), axis=1)
    ids = jnp.arange(BATCHES, dtype=I32)[:, None]
    offsets = (start[None, :] + (BATCHES - 1) - ids) // BATCHES
    counts = (stop[None, :] + (BATCHES - 1) - ids) // BATCHES - offsets

    present = [jnp.sum(counts[k]) > 0 for k in range(BATCHES)]

    def beside_first(router):
        logits = partial_logits(router, tokens)
        later = [tuple(later_batch(code, tokens, k, depth)) for k in range(1, BATCHES)]
        for bit in bits:
            logits = logits + swap(logits, bit)
        gathered = logits[None]
        for bit in expert_bits[:-1]:
            gathered = jnp.concatenate([gathered, along_expert(gathered, bit)])
        return later, logits, gathered

    def nothing_first(router):
        return jax.tree.map(lambda x: jnp.zeros(x.shape, x.dtype), jax.eval_shape(beside_first, router))

    arrived = [exchange(first)]
    later, logits, gathered = lax.cond(present[0], beside_first, nothing_first, router_weight.T)

    def far_half(far, sums):
        far = spread(far)
        hidden = gate_up_far(far, sums)
        far = swap(hidden, bits[0])
        partial = down_first(order, near_places, far_places, down_weight, spread(hidden))
        far, partial = lax.optimization_barrier((far, partial))
        return spread(far), partial

    def settle(k, far, partial):
        return tuple(
            down_last(offsets, counts, k, far, partial, experts, depth, k == BATCHES - 1)
        )

    def fenced(k, run, *operands):
        def skip(*operands):
            return jax.tree.map(lambda x: jnp.zeros(x.shape, x.dtype), jax.eval_shape(run, *operands))

        return lax.cond(present[k], run, skip, *operands)

    waiting = []
    far = partial = None
    moved = gathered
    for k in range(BATCHES):
        blocks = after(arrived[k], moved)
        if k < BATCHES - 1:
            moving = after(later[k], blocks)
            arrived.append(exchange(moving))
        if k == 0:
            block = fenced(k, lambda *blocks: compact(offsets, counts, 0, blocks, size), *blocks)
        else:
            block = compact(offsets, counts, k, blocks, size)
        across = swap(block, bits[0])
        near = spread(block)
        if k > 0:
            far, partial = after((far, partial), block)
            results = settle(k - 1, far, partial)
            if k > 1:
                results, waiting[k - 2] = lax.optimization_barrier((results, waiting[k - 2]))
            waiting.append(exchange(results))
            near = after(near, results)
        sums = gate_up_near(order, near_places, far_places, gate_weight, up_weight, near)
        across, sums = lax.optimization_barrier((across, sums))
        if k == BATCHES - 1:
            gathered = after(gathered, sums)
            gathered = jnp.concatenate([gathered, along_expert(gathered, expert_bits[-1])])
        far, partial = fenced(k, far_half, across, sums)
        moved = partial
    results = settle(BATCHES - 1, far, partial)
    results, gathered, waiting[-1] = lax.optimization_barrier((results, gathered, waiting[-1]))
    waiting.append(exchange(results))
    weights = slot_weights(place, logits, gathered, code)
    total = None
    for k in range(BATCHES):
        total = combine(code, weights, k, waiting[k], total)
    return total


def solution(mesh):
    return jax.shard_map(
        shards,
        mesh=mesh,
        in_specs=(
            P(("groups", "expert"), "dp"),
            P("dp", None),
            P("expert", None, "dp"),
            P("expert", None, "dp"),
            P("expert", None, "dp"),
            P("groups", None),
        ),
        out_specs=P(("groups", "expert"), "dp"),
        check_vma=False,
    )
```

```python
import functools

import jax
import jax.numpy as jnp
from jax import lax
from jax.experimental import pallas as pl
from jax.experimental.pallas import tpu as pltpu
from jax.sharding import PartitionSpec as P

BATCHES = 2
F32 = jnp.float32
BF16 = jnp.bfloat16
I32 = jnp.int32
VMEM_LIMIT = 16 * 1024 * 1024
COST = pl.CostEstimate(flops=1024, bytes_accessed=1024, transcendentals=0)


def whole(count):
    return [pl.BlockSpec(memory_space=pltpu.VMEM)] * count


def apart(count):
    return [pl.BlockSpec(memory_space=pl.ANY)] * count


def smem():
    return pl.BlockSpec(memory_space=pltpu.SMEM)


def params(limit=VMEM_LIMIT):
    return pltpu.CompilerParams(vmem_limit_bytes=limit)


def partner(place, experts):
    return -place % experts


def dot(a, b):
    return jnp.dot(a, b, preferred_element_type=F32)


def start_all(sources, targets, sems):
    copies = [pltpu.make_async_copy(a, b, sems.at[i]) for i, (a, b) in enumerate(zip(sources, targets))]
    for copy in copies:
        copy.start()
    return copies


def code_kernel(experts, depth, place_ref, picks_in, tokens_ref, code_ref, *refs):
    sends = refs[:experts]
    picks_ref, held, staged, in_sems, out_sems = refs[experts:]
    picks_load, load = start_all([picks_in, tokens_ref], [picks_ref, held], in_sems)
    me = place_ref[0]
    rows, width = held.shape
    capacity = picks_ref.shape[1]
    strips = rows // 128
    lanes = lax.broadcasted_iota(I32, (128, capacity), 0)
    strip_ids = lax.broadcasted_iota(I32, (8, capacity), 0)
    total = 8 * experts
    row_ids = lax.broadcasted_iota(I32, (total, total), 0)
    lane_ids = lax.broadcasted_iota(I32, (total, total), 1)
    same = lax.shift_right_logical(row_ids, 3) == lax.shift_right_logical(lane_ids, 3)
    before = (same & (lane_ids < row_ids)).astype(F32).astype(BF16)
    upper = (lax.broadcasted_iota(I32, (128, 128), 0) < lax.broadcasted_iota(I32, (128, 128), 1)).astype(BF16)
    ones = jnp.ones((128, 128), BF16)
    picks_load.wait()
    masks, starts = [], []
    for shift in range(experts):
        local = picks_ref[pl.ds(jnp.bitwise_xor(me, partner(shift, experts)), 1), :] - me * rows
        starts.append(jnp.broadcast_to(jnp.sum((local < 0).astype(F32), axis=1, keepdims=True), (8, 128)))
        strip = lax.shift_right_arithmetic(local, 7)
        place = jnp.bitwise_and(local, 127)
        high = ((strip == strip_ids) & (strip_ids < strips)).astype(F32).astype(BF16)
        low = (place == lanes).astype(F32).astype(BF16)
        masks.append(lax.dot_general(high, low, (((1,), (1,)), ((), ())), preferred_element_type=F32))
    mask = jnp.concatenate(masks, axis=0)
    start = jnp.concatenate(starts, axis=0).astype(I32)
    mask16 = mask.astype(BF16)
    totals = dot(mask16, ones)
    rank = (dot(mask16, upper) + dot(before, totals.astype(BF16))).astype(I32)
    slot = lax.rem(rank + start, BATCHES) * depth + lax.div(rank, BATCHES)
    code = jnp.where(mask > 0.5, slot, -1)
    code_rows = []
    for shift in range(experts):
        row = jnp.concatenate([code[8 * shift + i : 8 * shift + i + 1] for i in range(strips)], axis=1)
        code_ref[pl.ds(shift, 1), :] = row
        code_rows.append(row)
    load.wait()
    pack(0, depth, code_rows, held, staged, sends, out_sems)


def pack(k, depth, code_rows, held, staged, sends, sems):
    slot_ids = lax.broadcasted_iota(I32, (depth, held.shape[0]), 0) + k * depth
    copies = []
    for shift in list(range(1, len(sends))) + [0]:
        selector = (slot_ids == code_rows[shift]).astype(F32).astype(BF16)
        staged[shift] = dot(selector, held[...]).astype(BF16)
        copy = pltpu.make_async_copy(staged.at[shift], sends[shift], sems.at[shift])
        copy.start()
        copies.append(copy)
    for copy in copies:
        copy.wait()


def first_batch(place, picks, tokens, depth):
    rows, width = tokens.shape
    experts = picks.shape[0]
    out = pl.pallas_call(
        functools.partial(code_kernel, experts, depth),
        out_shape=[jax.ShapeDtypeStruct((experts, rows), I32)]
        + [jax.ShapeDtypeStruct((depth, width), BF16)] * experts,
        in_specs=[smem()] + apart(2),
        out_specs=whole(1) + apart(experts),
        scratch_shapes=[
            pltpu.VMEM(picks.shape, I32),
            pltpu.VMEM((rows, width), BF16),
            pltpu.VMEM((experts, depth, width), BF16),
            pltpu.SemaphoreType.DMA((2,)),
            pltpu.SemaphoreType.DMA((experts,)),
        ],
        compiler_params=params(60 * 1024 * 1024),
        cost_estimate=COST,
    )(place, picks, tokens)
    return out[0], out[1:]


def logits_kernel(router_ref, tokens_ref, out_ref):
    out_ref[...] = lax.dot_general(
        router_ref[...], tokens_ref[...], (((1,), (1,)), ((), ())), preferred_element_type=F32
    )


def partial_logits(router, tokens):
    return pl.pallas_call(
        logits_kernel,
        out_shape=jax.ShapeDtypeStruct((router.shape[0], tokens.shape[0]), F32),
        in_specs=whole(2),
        out_specs=whole(1)[0],
        compiler_params=params(),
        cost_estimate=COST,
    )(router, tokens)


def pack_kernel(experts, depth, k, code_ref, tokens_ref, *refs):
    sends = refs[:experts]
    held, staged, in_sems, out_sems = refs[experts:]
    start_all([tokens_ref], [held], in_sems)[0].wait()
    code_rows = [code_ref[pl.ds(shift, 1), :] for shift in range(experts)]
    pack(k, depth, code_rows, held, staged, sends, out_sems)


def later_batch(code, tokens, k, depth):
    rows, width = tokens.shape
    experts = code.shape[0]
    return pl.pallas_call(
        functools.partial(pack_kernel, experts, depth, k),
        out_shape=[jax.ShapeDtypeStruct((depth, width), BF16)] * experts,
        in_specs=whole(1) + apart(1),
        out_specs=apart(experts),
        scratch_shapes=[
            pltpu.VMEM((rows, width), BF16),
            pltpu.VMEM((experts, depth, width), BF16),
            pltpu.SemaphoreType.DMA((1,)),
            pltpu.SemaphoreType.DMA((experts,)),
        ],
        compiler_params=params(),
        cost_estimate=COST,
    )(code, tokens)


def compact_kernel(experts, k, offset_ref, count_ref, *refs):
    blocks, out_ref = refs[:experts], refs[experts]
    held, sems = refs[experts + 1 :]
    depth = blocks[0].shape[0]
    size = out_ref.shape[0]
    loads = start_all(blocks, [held.at[pl.ds(i * depth, depth)] for i in range(experts)], sems)
    row = lax.broadcasted_iota(I32, (size, depth), 0)
    lane = lax.broadcasted_iota(I32, (size, depth), 1)
    parts = [
        ((row - offset_ref[k, i] == lane) & (lane < count_ref[k, i])).astype(F32).astype(BF16)
        for i in range(experts)
    ]
    selector = jnp.concatenate(parts, axis=1)
    for load in loads:
        load.wait()
    out_ref[...] = dot(selector, held[...]).astype(BF16)


def compact(offsets, counts, k, blocks, size):
    experts = len(blocks)
    depth, width = blocks[0].shape
    return pl.pallas_call(
        functools.partial(compact_kernel, experts, k),
        out_shape=jax.ShapeDtypeStruct((size, width), BF16),
        in_specs=[smem(), smem()] + apart(experts),
        out_specs=whole(1)[0],
        scratch_shapes=[pltpu.VMEM((experts * depth, width), BF16), pltpu.SemaphoreType.DMA((experts,))],
        compiler_params=params(),
        cost_estimate=COST,
    )(offsets, counts, *blocks)


def gate_up_near_kernel(parts, near, far, order_ref, gate_ref, up_ref, *refs):
    xs, refs = refs[:parts], refs[parts:]
    gate_out, up_out, gate_far, up_far, gate_held, up_held, x_held, sems = refs
    width = xs[0].shape[1]

    def fetch(i, place, gate_to, up_to, base):
        first = pl.multiple_of(order_ref[place] * width, width)
        return start_all(
            [gate_ref.at[0, pl.ds(first, width), :], up_ref.at[0, pl.ds(first, width), :]],
            [gate_to.at[i], up_to.at[i]],
            sems.at[pl.ds(base, 2)],
        )

    x_loads = start_all(xs, [x_held.at[i] for i in range(parts)], sems.at[pl.ds(0, parts)])
    loads = [fetch(i, near[i], gate_held, up_held, parts + 2 * i) for i in range(parts)]
    late = [fetch(i, far[i], gate_far, up_far, 3 * parts + 2 * i) for i in range(len(far))]
    gate = up = None
    for i in range(parts):
        for copy in [x_loads[i]] + loads[i]:
            copy.wait()
        x = x_held[i]
        gate_term = dot(x, gate_held[i])
        up_term = dot(x, up_held[i])
        gate = gate_term if gate is None else gate + gate_term
        up = up_term if up is None else up + up_term
    gate_out[...] = gate
    up_out[...] = up
    for copies in late:
        for copy in copies:
            copy.wait()


def gate_up_near(order, near, far, gate_weight, up_weight, xs):
    parts = len(xs)
    size, width = xs[0].shape
    units = gate_weight.shape[2]
    held = jax.ShapeDtypeStruct((len(far), width, units), BF16)
    return pl.pallas_call(
        functools.partial(gate_up_near_kernel, parts, near, far),
        out_shape=[jax.ShapeDtypeStruct((size, units), F32)] * 2 + [held] * 2,
        in_specs=[smem()] + apart(2 + parts),
        out_specs=whole(4),
        scratch_shapes=[
            pltpu.VMEM((parts, width, units), BF16),
            pltpu.VMEM((parts, width, units), BF16),
            pltpu.VMEM((parts, size, width), BF16),
            pltpu.SemaphoreType.DMA((3 * parts + 2 * len(far),)),
        ],
        compiler_params=params(),
        cost_estimate=COST,
    )(order, gate_weight, up_weight, *xs)


def gate_up_far_kernel(parts, gate_before, up_before, gate_ref, up_ref, *refs):
    xs, out_ref = refs[:parts], refs[parts]
    gate, up = gate_before[...], up_before[...]
    for i in range(parts):
        x = xs[i][...]
        gate = gate + dot(x, gate_ref[i])
        up = up + dot(x, up_ref[i])
    out_ref[...] = (gate * jax.nn.sigmoid(gate) * up).astype(BF16)


def gate_up_far(xs, before):
    size, units = before[0].shape
    return pl.pallas_call(
        functools.partial(gate_up_far_kernel, len(xs)),
        out_shape=jax.ShapeDtypeStruct((size, units), BF16),
        in_specs=whole(4 + len(xs)),
        out_specs=whole(1)[0],
        compiler_params=params(),
        cost_estimate=COST,
    )(*before, *xs)


def down_first_kernel(parts, near, far, order_ref, down_ref, *refs):
    hs, (out_ref, far_ref, down_held, h_held, sems) = refs[:parts], refs[parts:]
    units = hs[0].shape[1]

    def fetch(i, place, target, sem):
        first = pl.multiple_of(order_ref[place] * units, units)
        copy = pltpu.make_async_copy(down_ref.at[0, pl.ds(first, units), :], target.at[i], sems.at[sem])
        copy.start()
        return copy

    h_loads = start_all(hs, [h_held.at[i] for i in range(parts)], sems.at[pl.ds(0, parts)])
    loads = [fetch(i, near[i], down_held, parts + i) for i in range(parts)]
    late = [fetch(i, far[i], far_ref, 2 * parts + i) for i in range(len(far))]
    total = None
    for i in range(parts):
        h_loads[i].wait()
        loads[i].wait()
        term = dot(h_held[i], down_held[i])
        total = term if total is None else total + term
    out_ref[...] = total
    for copy in late:
        copy.wait()


def down_first(order, near, far, down_weight, hs):
    parts = len(hs)
    size, units = hs[0].shape
    width = down_weight.shape[2]
    return pl.pallas_call(
        functools.partial(down_first_kernel, parts, near, far),
        out_shape=[
            jax.ShapeDtypeStruct((size, width), F32),
            jax.ShapeDtypeStruct((len(far), units, width), BF16),
        ],
        in_specs=[smem()] + apart(1 + parts),
        out_specs=whole(2),
        scratch_shapes=[
            pltpu.VMEM((parts, units, width), BF16),
            pltpu.VMEM((parts, size, units), BF16),
            pltpu.SemaphoreType.DMA((2 * parts + len(far),)),
        ],
        compiler_params=params(),
        cost_estimate=COST,
    )(order, down_weight, *hs)


def down_last_kernel(parts, experts, k, direct, offset_ref, count_ref, before_ref, down_ref, *refs):
    hs, outs = refs[:parts], refs[parts : parts + experts]
    h_held, sems, *staged = refs[parts + experts :]
    loads = start_all(hs, [h_held.at[i] for i in range(parts)], sems)
    size = hs[0].shape[0]
    depth = outs[0].shape[0]
    row = lax.broadcasted_iota(I32, (depth, size), 0)
    lane = lax.broadcasted_iota(I32, (depth, size), 1)
    picks = [
        ((lane - offset_ref[k, i] == row) & (row < count_ref[k, i])).astype(F32).astype(BF16)
        for i in range(experts)
    ]
    total = before_ref[...]
    for i in range(parts):
        loads[i].wait()
        total = total + dot(h_held[i], down_ref[i])
    result = total.astype(BF16)
    if direct:
        for i in range(experts):
            outs[i][...] = dot(picks[i], result).astype(BF16)
        return
    staged_ref, out_sems = staged
    copies = []
    for i in list(range(1, experts)) + [0]:
        staged_ref[i] = dot(picks[i], result).astype(BF16)
        copy = pltpu.make_async_copy(staged_ref.at[i], outs[i], out_sems.at[i])
        copy.start()
        copies.append(copy)
    for copy in copies:
        copy.wait()


def down_last(offsets, counts, k, hs, before, experts, depth, direct):
    parts = len(hs)
    size, units = hs[0].shape
    width = before[0].shape[1]
    return pl.pallas_call(
        functools.partial(down_last_kernel, parts, experts, k, direct),
        out_shape=[jax.ShapeDtypeStruct((depth, width), BF16)] * experts,
        in_specs=[smem()] * 2 + whole(2) + apart(parts),
        out_specs=whole(experts) if direct else apart(experts),
        scratch_shapes=[pltpu.VMEM((parts, size, units), BF16), pltpu.SemaphoreType.DMA((parts,))]
        + ([] if direct else [pltpu.VMEM((experts, depth, width), BF16), pltpu.SemaphoreType.DMA((experts,))]),
        compiler_params=params(),
        cost_estimate=COST,
    )(offsets, counts, *before, *hs)


def weight_kernel(experts, place_ref, own_ref, logits_ref, code_ref, out_ref, score_ref):
    me = place_ref[0]
    kernel = jnp.exp(logits_ref[...])
    row_scale = jnp.ones((kernel.shape[0], 1, kernel.shape[2]), F32)
    for sweep in range(3):
        column = jnp.sum(jnp.sum(kernel * row_scale, axis=0, keepdims=True), axis=2, keepdims=True)
        column_scale = 1.0 / column
        row_scale = 1.0 / jnp.sum(kernel * column_scale, axis=1, keepdims=True)
    own = jnp.exp(own_ref[...])
    column_scale = column_scale[0]
    own_scale = 1.0 / jnp.sum(own * column_scale, axis=0, keepdims=True)
    score_ref[...] = own_scale * own * column_scale
    picked = []
    for shift in range(experts):
        score = score_ref[pl.ds(jnp.bitwise_xor(me, partner(shift, experts)), 1), :]
        picked.append(jnp.where(code_ref[pl.ds(shift, 1), :] >= 0, score, 0.0))
    total = picked[0]
    for one in picked[1:]:
        total = total + one
    total = jnp.maximum(total, 1.0 / experts)
    for shift in range(experts):
        out_ref[pl.ds(shift, 1), :] = picked[shift] / total


def slot_weights(place, own, logits, code):
    experts, rows = own.shape
    return pl.pallas_call(
        functools.partial(weight_kernel, experts),
        out_shape=jax.ShapeDtypeStruct((experts, rows), F32),
        in_specs=[smem()] + whole(3),
        out_specs=whole(1)[0],
        scratch_shapes=[pltpu.VMEM((experts, rows), F32)],
        compiler_params=params(),
        cost_estimate=COST,
    )(place, own, logits, code)


def combine_kernel(experts, k, code_ref, weight_ref, *refs):
    before, refs = refs[: k > 0], refs[k > 0 :]
    blocks, (out_ref, held, sems) = refs[:experts], refs[experts:]
    depth = blocks[0].shape[0]
    rows = code_ref.shape[1]
    targets = [held.at[pl.ds(i * depth, depth)] for i in range(experts)]
    loads = start_all(blocks, targets, sems)
    slot_ids = lax.broadcasted_iota(I32, (depth, rows), 0) + k * depth
    parts = [
        jnp.where(slot_ids == code_ref[pl.ds(i, 1), :], weight_ref[pl.ds(i, 1), :], 0.0).astype(BF16)
        for i in range(experts)
    ]
    spread = jnp.concatenate(parts, axis=0)
    for load in loads:
        load.wait()
    total = lax.dot_general(spread, held[...], (((0,), (0,)), ((), ())), preferred_element_type=F32)
    if k > 0:
        total = total + before[0][...]
    out_ref[...] = total.astype(out_ref.dtype)


def combine(code, weights, k, blocks, so_far):
    experts = len(blocks)
    depth, width = blocks[0].shape
    rows = code.shape[1]
    last = k == BATCHES - 1
    more = [] if so_far is None else [so_far]
    return pl.pallas_call(
        functools.partial(combine_kernel, experts, k),
        out_shape=jax.ShapeDtypeStruct((rows, width), BF16 if last else F32),
        in_specs=whole(2 + len(more)) + apart(experts),
        out_specs=whole(1)[0],
        scratch_shapes=[pltpu.VMEM((experts * depth, width), BF16), pltpu.SemaphoreType.DMA((experts,))],
        compiler_params=params(),
        cost_estimate=COST,
    )(code, weights, *more, *blocks)


def after(value, *first):
    return lax.optimization_barrier((value, first))[0]


def shards(tokens, router_weight, gate_weight, up_weight, down_weight, picks):
    experts = lax.axis_size("expert")
    width_parts = lax.axis_size("dp")
    me = lax.axis_index("expert")
    part = lax.axis_index("dp")
    rows = tokens.shape[0]
    capacity = picks.shape[1]
    depth = 2 * capacity // experts // BATCHES
    size = capacity // BATCHES
    place = me.astype(I32).reshape(1)

    def along_expert(x, shift):
        return lax.ppermute(x, "expert", [(i, i ^ shift) for i in range(experts)])

    def swap(x, bit):
        return lax.ppermute(x, "dp", [(i, i ^ bit) for i in range(width_parts)])

    bits = []
    bit = width_parts // 2
    while bit:
        bits.append(bit)
        bit //= 2
    near = [0]
    for bit in bits[1:]:
        near = near + [m ^ bit for m in near]
    masks = near + [m ^ bits[0] for m in near]
    places = range(len(masks))
    near_places, far_places = places[: len(near)], places[len(near) :]
    order = jnp.stack([part ^ m for m in masks]).astype(I32)

    def exchange(blocks):
        return [blocks[0]] + [along_expert(blocks[i], partner(i, experts)) for i in range(1, experts)]

    expert_bits = [1 << i for i in range(experts.bit_length() - 1)]

    def spread(x):
        held = [x]
        for bit in bits[1:]:
            held = held + [swap(h, bit) for h in held]
        return held

    def both_parts(x):
        far = swap(x, bits[0])
        return spread(x), spread(far)

    code, first = first_batch(place, picks, tokens, depth)
    own_picks = lax.dynamic_slice_in_dim(picks, me, 1, axis=0)
    sources = jnp.bitwise_xor(me, jnp.array([partner(i, experts) for i in range(experts)], I32))
    start = jnp.sum((own_picks < (sources * rows)[:, None]).astype(I32), axis=1)
    stop = jnp.sum((own_picks < ((sources + 1) * rows)[:, None]).astype(I32), axis=1)
    ids = jnp.arange(BATCHES, dtype=I32)[:, None]
    offsets = (start[None, :] + (BATCHES - 1) - ids) // BATCHES
    counts = (stop[None, :] + (BATCHES - 1) - ids) // BATCHES - offsets

    present = [jnp.sum(counts[k]) > 0 for k in range(BATCHES)]

    def beside_first(router):
        gathered = partial_logits(router, tokens)[None]
        for bit in expert_bits:
            gathered = jnp.concatenate([gathered, along_expert(gathered, bit)])
        later = [tuple(later_batch(code, tokens, k, depth)) for k in range(1, BATCHES)]
        for bit in bits:
            gathered = gathered + swap(gathered, bit)
        return later, gathered

    def nothing_first(router):
        return jax.tree.map(lambda x: jnp.zeros(x.shape, x.dtype), jax.eval_shape(beside_first, router))

    arrived = [exchange(first)]
    later, gathered = lax.cond(present[0], beside_first, nothing_first, router_weight.T)

    def far_half(far, sums):
        far = spread(far)
        hidden = gate_up_far(far, sums)
        far = swap(hidden, bits[0])
        partial = down_first(order, near_places, far_places, down_weight, spread(hidden))
        far, partial = lax.optimization_barrier((far, partial))
        return spread(far), partial

    def settle(k, far, partial):
        return tuple(
            down_last(offsets, counts, k, far, partial, experts, depth, k == BATCHES - 1)
        )

    def fenced(k, run, *operands):
        def skip(*operands):
            return jax.tree.map(lambda x: jnp.zeros(x.shape, x.dtype), jax.eval_shape(run, *operands))

        return lax.cond(present[k], run, skip, *operands)

    waiting = []
    far = partial = None
    moved = gathered
    for k in range(BATCHES):
        blocks = after(arrived[k], moved)
        if k < BATCHES - 1:
            moving = after(later[k], blocks)
            arrived.append(exchange(moving))
        if k == 0:
            block = fenced(k, lambda *blocks: compact(offsets, counts, 0, blocks, size), *blocks)
        else:
            block = compact(offsets, counts, k, blocks, size)
        across = swap(block, bits[0])
        near = spread(block)
        if k > 0:
            far, partial = after((far, partial), block)
            results = settle(k - 1, far, partial)
            if k > 1:
                results, waiting[k - 2] = lax.optimization_barrier((results, waiting[k - 2]))
            waiting.append(exchange(results))
            near = after(near, results)
        sums = gate_up_near(order, near_places, far_places, gate_weight, up_weight, near)
        across, sums = lax.optimization_barrier((across, sums))
        far, partial = fenced(k, far_half, across, sums)
        moved = partial
    results = settle(BATCHES - 1, far, partial)
    results, gathered, waiting[-1] = lax.optimization_barrier((results, gathered, waiting[-1]))
    waiting.append(exchange(results))
    weights = slot_weights(place, gathered[0], gathered, code)
    total = None
    for k in range(BATCHES):
        total = combine(code, weights, k, waiting[k], total)
    return total


def solution(mesh):
    return jax.shard_map(
        shards,
        mesh=mesh,
        in_specs=(
            P(("groups", "expert"), "dp"),
            P("dp", None),
            P("expert", None, "dp"),
            P("expert", None, "dp"),
            P("expert", None, "dp"),
            P("groups", None),
        ),
        out_specs=P(("groups", "expert"), "dp"),
        check_vma=False,
    )
```

```python
import functools

import jax
import jax.numpy as jnp
from jax import lax
from jax.experimental import pallas as pl
from jax.experimental.pallas import tpu as pltpu
from jax.sharding import PartitionSpec as P

BATCHES = 2
F32 = jnp.float32
BF16 = jnp.bfloat16
I32 = jnp.int32
VMEM_LIMIT = 16 * 1024 * 1024
COST = pl.CostEstimate(flops=1024, bytes_accessed=1024, transcendentals=0)


def whole(count):
    return [pl.BlockSpec(memory_space=pltpu.VMEM)] * count


def apart(count):
    return [pl.BlockSpec(memory_space=pl.ANY)] * count


def smem():
    return pl.BlockSpec(memory_space=pltpu.SMEM)


def params(limit=VMEM_LIMIT):
    return pltpu.CompilerParams(vmem_limit_bytes=limit)


def partner(place, experts):
    return -place % experts


def dot(a, b):
    return jnp.dot(a, b, preferred_element_type=F32)


def start_all(sources, targets, sems):
    copies = [pltpu.make_async_copy(a, b, sems.at[i]) for i, (a, b) in enumerate(zip(sources, targets))]
    for copy in copies:
        copy.start()
    return copies


def code_kernel(experts, depth, place_ref, picks_in, tokens_ref, code_ref, *refs):
    sends = refs[:experts]
    picks_ref, held, staged, in_sems, out_sems = refs[experts:]
    picks_load, load = start_all([picks_in, tokens_ref], [picks_ref, held], in_sems)
    me = place_ref[0]
    rows, width = held.shape
    capacity = picks_ref.shape[1]
    strips = rows // 128
    lanes = lax.broadcasted_iota(I32, (128, capacity), 0)
    strip_ids = lax.broadcasted_iota(I32, (8, capacity), 0)
    total = 8 * experts
    row_ids = lax.broadcasted_iota(I32, (total, total), 0)
    lane_ids = lax.broadcasted_iota(I32, (total, total), 1)
    same = lax.shift_right_logical(row_ids, 3) == lax.shift_right_logical(lane_ids, 3)
    before = (same & (lane_ids < row_ids)).astype(F32).astype(BF16)
    upper = (lax.broadcasted_iota(I32, (128, 128), 0) < lax.broadcasted_iota(I32, (128, 128), 1)).astype(BF16)
    ones = jnp.ones((128, 128), BF16)
    picks_load.wait()
    masks, starts = [], []
    for shift in range(experts):
        local = picks_ref[pl.ds(jnp.bitwise_xor(me, partner(shift, experts)), 1), :] - me * rows
        starts.append(jnp.broadcast_to(jnp.sum((local < 0).astype(F32), axis=1, keepdims=True), (8, 128)))
        strip = lax.shift_right_arithmetic(local, 7)
        place = jnp.bitwise_and(local, 127)
        high = ((strip == strip_ids) & (strip_ids < strips)).astype(F32).astype(BF16)
        low = (place == lanes).astype(F32).astype(BF16)
        masks.append(lax.dot_general(high, low, (((1,), (1,)), ((), ())), preferred_element_type=F32))
    mask = jnp.concatenate(masks, axis=0)
    start = jnp.concatenate(starts, axis=0).astype(I32)
    mask16 = mask.astype(BF16)
    totals = dot(mask16, ones)
    rank = (dot(mask16, upper) + dot(before, totals.astype(BF16))).astype(I32)
    slot = lax.rem(rank + start, BATCHES) * depth + lax.div(rank, BATCHES)
    code = jnp.where(mask > 0.5, slot, -1)
    code_rows = []
    for shift in range(experts):
        row = jnp.concatenate([code[8 * shift + i : 8 * shift + i + 1] for i in range(strips)], axis=1)
        code_ref[pl.ds(shift, 1), :] = row
        code_rows.append(row)
    load.wait()
    pack(0, depth, code_rows, held, staged, sends, out_sems)


def pack(k, depth, code_rows, held, staged, sends, sems):
    slot_ids = lax.broadcasted_iota(I32, (depth, held.shape[0]), 0) + k * depth
    copies = []
    for shift in list(range(1, len(sends))) + [0]:
        selector = (slot_ids == code_rows[shift]).astype(F32).astype(BF16)
        staged[shift] = dot(selector, held[...]).astype(BF16)
        copy = pltpu.make_async_copy(staged.at[shift], sends[shift], sems.at[shift])
        copy.start()
        copies.append(copy)
    for copy in copies:
        copy.wait()


def first_batch(place, picks, tokens, depth):
    rows, width = tokens.shape
    experts = picks.shape[0]
    out = pl.pallas_call(
        functools.partial(code_kernel, experts, depth),
        out_shape=[jax.ShapeDtypeStruct((experts, rows), I32)]
        + [jax.ShapeDtypeStruct((depth, width), BF16)] * experts,
        in_specs=[smem()] + apart(2),
        out_specs=whole(1) + apart(experts),
        scratch_shapes=[
            pltpu.VMEM(picks.shape, I32),
            pltpu.VMEM((rows, width), BF16),
            pltpu.VMEM((experts, depth, width), BF16),
            pltpu.SemaphoreType.DMA((2,)),
            pltpu.SemaphoreType.DMA((experts,)),
        ],
        compiler_params=params(60 * 1024 * 1024),
        cost_estimate=COST,
    )(place, picks, tokens)
    return out[0], out[1:]


def logits_kernel(router_ref, tokens_ref, out_ref):
    out_ref[...] = lax.dot_general(
        router_ref[...], tokens_ref[...], (((1,), (1,)), ((), ())), preferred_element_type=F32
    )


def partial_logits(router, tokens):
    return pl.pallas_call(
        logits_kernel,
        out_shape=jax.ShapeDtypeStruct((router.shape[0], tokens.shape[0]), F32),
        in_specs=whole(2),
        out_specs=whole(1)[0],
        compiler_params=params(),
        cost_estimate=COST,
    )(router, tokens)


def pack_kernel(experts, depth, k, code_ref, tokens_ref, *refs):
    sends = refs[:experts]
    held, staged, in_sems, out_sems = refs[experts:]
    start_all([tokens_ref], [held], in_sems)[0].wait()
    code_rows = [code_ref[pl.ds(shift, 1), :] for shift in range(experts)]
    pack(k, depth, code_rows, held, staged, sends, out_sems)


def later_batch(code, tokens, k, depth):
    rows, width = tokens.shape
    experts = code.shape[0]
    return pl.pallas_call(
        functools.partial(pack_kernel, experts, depth, k),
        out_shape=[jax.ShapeDtypeStruct((depth, width), BF16)] * experts,
        in_specs=whole(1) + apart(1),
        out_specs=apart(experts),
        scratch_shapes=[
            pltpu.VMEM((rows, width), BF16),
            pltpu.VMEM((experts, depth, width), BF16),
            pltpu.SemaphoreType.DMA((1,)),
            pltpu.SemaphoreType.DMA((experts,)),
        ],
        compiler_params=params(),
        cost_estimate=COST,
    )(code, tokens)


def compact_kernel(experts, k, offset_ref, count_ref, *refs):
    blocks, out_ref = refs[:experts], refs[experts]
    held, sems = refs[experts + 1 :]
    depth = blocks[0].shape[0]
    size = out_ref.shape[0]
    loads = start_all(blocks, [held.at[pl.ds(i * depth, depth)] for i in range(experts)], sems)
    row = lax.broadcasted_iota(I32, (size, depth), 0)
    lane = lax.broadcasted_iota(I32, (size, depth), 1)
    parts = [
        ((row - offset_ref[k, i] == lane) & (lane < count_ref[k, i])).astype(F32).astype(BF16)
        for i in range(experts)
    ]
    selector = jnp.concatenate(parts, axis=1)
    for load in loads:
        load.wait()
    out_ref[...] = dot(selector, held[...]).astype(BF16)


def compact(offsets, counts, k, blocks, size):
    experts = len(blocks)
    depth, width = blocks[0].shape
    return pl.pallas_call(
        functools.partial(compact_kernel, experts, k),
        out_shape=jax.ShapeDtypeStruct((size, width), BF16),
        in_specs=[smem(), smem()] + apart(experts),
        out_specs=whole(1)[0],
        scratch_shapes=[pltpu.VMEM((experts * depth, width), BF16), pltpu.SemaphoreType.DMA((experts,))],
        compiler_params=params(),
        cost_estimate=COST,
    )(offsets, counts, *blocks)


def gate_up_near_kernel(parts, near, far, order_ref, gate_ref, up_ref, *refs):
    xs, refs = refs[:parts], refs[parts:]
    gate_out, up_out, gate_far, up_far, gate_held, up_held, x_held, sems = refs
    width = xs[0].shape[1]

    def fetch(i, place, gate_to, up_to, base):
        first = pl.multiple_of(order_ref[place] * width, width)
        return start_all(
            [gate_ref.at[0, pl.ds(first, width), :], up_ref.at[0, pl.ds(first, width), :]],
            [gate_to.at[i], up_to.at[i]],
            sems.at[pl.ds(base, 2)],
        )

    x_loads = start_all(xs, [x_held.at[i] for i in range(parts)], sems.at[pl.ds(0, parts)])
    loads = [fetch(i, near[i], gate_held, up_held, parts + 2 * i) for i in range(parts)]
    late = [fetch(i, far[i], gate_far, up_far, 3 * parts + 2 * i) for i in range(len(far))]
    gate = up = None
    for i in range(parts):
        for copy in [x_loads[i]] + loads[i]:
            copy.wait()
        x = x_held[i]
        gate_term = dot(x, gate_held[i])
        up_term = dot(x, up_held[i])
        gate = gate_term if gate is None else gate + gate_term
        up = up_term if up is None else up + up_term
    gate_out[...] = gate
    up_out[...] = up
    for copies in late:
        for copy in copies:
            copy.wait()


def gate_up_near(order, near, far, gate_weight, up_weight, xs):
    parts = len(xs)
    size, width = xs[0].shape
    units = gate_weight.shape[2]
    held = jax.ShapeDtypeStruct((len(far), width, units), BF16)
    return pl.pallas_call(
        functools.partial(gate_up_near_kernel, parts, near, far),
        out_shape=[jax.ShapeDtypeStruct((size, units), F32)] * 2 + [held] * 2,
        in_specs=[smem()] + apart(2 + parts),
        out_specs=whole(4),
        scratch_shapes=[
            pltpu.VMEM((parts, width, units), BF16),
            pltpu.VMEM((parts, width, units), BF16),
            pltpu.VMEM((parts, size, width), BF16),
            pltpu.SemaphoreType.DMA((3 * parts + 2 * len(far),)),
        ],
        compiler_params=params(),
        cost_estimate=COST,
    )(order, gate_weight, up_weight, *xs)


def gate_up_far_kernel(parts, gate_before, up_before, gate_ref, up_ref, *refs):
    xs, out_ref = refs[:parts], refs[parts]
    gate, up = gate_before[...], up_before[...]
    for i in range(parts):
        x = xs[i][...]
        gate = gate + dot(x, gate_ref[i])
        up = up + dot(x, up_ref[i])
    out_ref[...] = (gate * jax.nn.sigmoid(gate) * up).astype(BF16)


def gate_up_far(xs, before):
    size, units = before[0].shape
    return pl.pallas_call(
        functools.partial(gate_up_far_kernel, len(xs)),
        out_shape=jax.ShapeDtypeStruct((size, units), BF16),
        in_specs=whole(4 + len(xs)),
        out_specs=whole(1)[0],
        compiler_params=params(),
        cost_estimate=COST,
    )(*before, *xs)


def down_first_kernel(parts, near, far, order_ref, down_ref, *refs):
    hs, (out_ref, far_ref, down_held, h_held, sems) = refs[:parts], refs[parts:]
    units = hs[0].shape[1]

    def fetch(i, place, target, sem):
        first = pl.multiple_of(order_ref[place] * units, units)
        copy = pltpu.make_async_copy(down_ref.at[0, pl.ds(first, units), :], target.at[i], sems.at[sem])
        copy.start()
        return copy

    h_loads = start_all(hs, [h_held.at[i] for i in range(parts)], sems.at[pl.ds(0, parts)])
    loads = [fetch(i, near[i], down_held, parts + i) for i in range(parts)]
    late = [fetch(i, far[i], far_ref, 2 * parts + i) for i in range(len(far))]
    total = None
    for i in range(parts):
        h_loads[i].wait()
        loads[i].wait()
        term = dot(h_held[i], down_held[i])
        total = term if total is None else total + term
    out_ref[...] = total
    for copy in late:
        copy.wait()


def down_first(order, near, far, down_weight, hs):
    parts = len(hs)
    size, units = hs[0].shape
    width = down_weight.shape[2]
    return pl.pallas_call(
        functools.partial(down_first_kernel, parts, near, far),
        out_shape=[
            jax.ShapeDtypeStruct((size, width), F32),
            jax.ShapeDtypeStruct((len(far), units, width), BF16),
        ],
        in_specs=[smem()] + apart(1 + parts),
        out_specs=whole(2),
        scratch_shapes=[
            pltpu.VMEM((parts, units, width), BF16),
            pltpu.VMEM((parts, size, units), BF16),
            pltpu.SemaphoreType.DMA((2 * parts + len(far),)),
        ],
        compiler_params=params(),
        cost_estimate=COST,
    )(order, down_weight, *hs)


def down_last_kernel(parts, experts, k, direct, offset_ref, count_ref, before_ref, down_ref, *refs):
    hs, outs = refs[:parts], refs[parts : parts + experts]
    h_held, sems, *staged = refs[parts + experts :]
    loads = start_all(hs, [h_held.at[i] for i in range(parts)], sems)
    size = hs[0].shape[0]
    depth = outs[0].shape[0]
    row = lax.broadcasted_iota(I32, (depth, size), 0)
    lane = lax.broadcasted_iota(I32, (depth, size), 1)
    picks = [
        ((lane - offset_ref[k, i] == row) & (row < count_ref[k, i])).astype(F32).astype(BF16)
        for i in range(experts)
    ]
    total = before_ref[...]
    for i in range(parts):
        loads[i].wait()
        total = total + dot(h_held[i], down_ref[i])
    result = total.astype(BF16)
    if direct:
        for i in range(experts):
            outs[i][...] = dot(picks[i], result).astype(BF16)
        return
    staged_ref, out_sems = staged
    copies = []
    for i in list(range(1, experts)) + [0]:
        staged_ref[i] = dot(picks[i], result).astype(BF16)
        copy = pltpu.make_async_copy(staged_ref.at[i], outs[i], out_sems.at[i])
        copy.start()
        copies.append(copy)
    for copy in copies:
        copy.wait()


def down_last(offsets, counts, k, hs, before, experts, depth, direct):
    parts = len(hs)
    size, units = hs[0].shape
    width = before[0].shape[1]
    return pl.pallas_call(
        functools.partial(down_last_kernel, parts, experts, k, direct),
        out_shape=[jax.ShapeDtypeStruct((depth, width), BF16)] * experts,
        in_specs=[smem()] * 2 + whole(2) + apart(parts),
        out_specs=whole(experts) if direct else apart(experts),
        scratch_shapes=[pltpu.VMEM((parts, size, units), BF16), pltpu.SemaphoreType.DMA((parts,))]
        + ([] if direct else [pltpu.VMEM((experts, depth, width), BF16), pltpu.SemaphoreType.DMA((experts,))]),
        compiler_params=params(),
        cost_estimate=COST,
    )(offsets, counts, *before, *hs)


def weight_kernel(experts, place_ref, own_ref, logits_ref, code_ref, out_ref, score_ref):
    me = place_ref[0]
    kernel = jnp.exp(logits_ref[...])
    row_scale = jnp.ones((kernel.shape[0], 1, kernel.shape[2]), F32)
    for sweep in range(3):
        column = jnp.sum(jnp.sum(kernel * row_scale, axis=0, keepdims=True), axis=2, keepdims=True)
        column_scale = 1.0 / column
        row_scale = 1.0 / jnp.sum(kernel * column_scale, axis=1, keepdims=True)
    own = jnp.exp(own_ref[...])
    column_scale = column_scale[0]
    own_scale = 1.0 / jnp.sum(own * column_scale, axis=0, keepdims=True)
    score_ref[...] = own_scale * own * column_scale
    picked = []
    for shift in range(experts):
        score = score_ref[pl.ds(jnp.bitwise_xor(me, partner(shift, experts)), 1), :]
        picked.append(jnp.where(code_ref[pl.ds(shift, 1), :] >= 0, score, 0.0))
    total = picked[0]
    for one in picked[1:]:
        total = total + one
    total = jnp.maximum(total, 1.0 / experts)
    for shift in range(experts):
        out_ref[pl.ds(shift, 1), :] = picked[shift] / total


def slot_weights(place, own, logits, code):
    experts, rows = own.shape
    return pl.pallas_call(
        functools.partial(weight_kernel, experts),
        out_shape=jax.ShapeDtypeStruct((experts, rows), F32),
        in_specs=[smem()] + whole(3),
        out_specs=whole(1)[0],
        scratch_shapes=[pltpu.VMEM((experts, rows), F32)],
        compiler_params=params(),
        cost_estimate=COST,
    )(place, own, logits, code)


def combine_kernel(experts, k, code_ref, weight_ref, *refs):
    before, refs = refs[: k > 0], refs[k > 0 :]
    blocks, (out_ref, held, sems) = refs[:experts], refs[experts:]
    depth = blocks[0].shape[0]
    rows = code_ref.shape[1]
    targets = [held.at[pl.ds(i * depth, depth)] for i in range(experts)]
    loads = start_all(blocks, targets, sems)
    slot_ids = lax.broadcasted_iota(I32, (depth, rows), 0) + k * depth
    parts = [
        jnp.where(slot_ids == code_ref[pl.ds(i, 1), :], weight_ref[pl.ds(i, 1), :], 0.0).astype(BF16)
        for i in range(experts)
    ]
    spread = jnp.concatenate(parts, axis=0)
    for load in loads:
        load.wait()
    total = lax.dot_general(spread, held[...], (((0,), (0,)), ((), ())), preferred_element_type=F32)
    if k > 0:
        total = total + before[0][...]
    out_ref[...] = total.astype(out_ref.dtype)


def combine(code, weights, k, blocks, so_far):
    experts = len(blocks)
    depth, width = blocks[0].shape
    rows = code.shape[1]
    last = k == BATCHES - 1
    more = [] if so_far is None else [so_far]
    return pl.pallas_call(
        functools.partial(combine_kernel, experts, k),
        out_shape=jax.ShapeDtypeStruct((rows, width), BF16 if last else F32),
        in_specs=whole(2 + len(more)) + apart(experts),
        out_specs=whole(1)[0],
        scratch_shapes=[pltpu.VMEM((experts * depth, width), BF16), pltpu.SemaphoreType.DMA((experts,))],
        compiler_params=params(),
        cost_estimate=COST,
    )(code, weights, *more, *blocks)


def after(value, *first):
    return lax.optimization_barrier((value, first))[0]


def shards(tokens, router_weight, gate_weight, up_weight, down_weight, picks):
    experts = lax.axis_size("expert")
    width_parts = lax.axis_size("dp")
    me = lax.axis_index("expert")
    part = lax.axis_index("dp")
    rows = tokens.shape[0]
    capacity = picks.shape[1]
    depth = 2 * capacity // experts // BATCHES
    size = capacity // BATCHES
    place = me.astype(I32).reshape(1)

    def along_expert(x, shift):
        return lax.ppermute(x, "expert", [(i, i ^ shift) for i in range(experts)])

    def swap(x, bit):
        return lax.ppermute(x, "dp", [(i, i ^ bit) for i in range(width_parts)])

    bits = []
    bit = width_parts // 2
    while bit:
        bits.append(bit)
        bit //= 2
    near = [0]
    for bit in bits[1:]:
        near = near + [m ^ bit for m in near]
    masks = near + [m ^ bits[0] for m in near]
    places = range(len(masks))
    near_places, far_places = places[: len(near)], places[len(near) :]
    order = jnp.stack([part ^ m for m in masks]).astype(I32)

    def exchange(blocks):
        return [blocks[0]] + [along_expert(blocks[i], partner(i, experts)) for i in range(1, experts)]

    expert_bits = [1 << i for i in range(experts.bit_length() - 1)]

    def spread(x):
        held = [x]
        for bit in bits[1:]:
            held = held + [swap(h, bit) for h in held]
        return held

    def both_parts(x):
        far = swap(x, bits[0])
        return spread(x), spread(far)

    code, first = first_batch(place, picks, tokens, depth)
    own_picks = lax.dynamic_slice_in_dim(picks, me, 1, axis=0)
    sources = jnp.bitwise_xor(me, jnp.array([partner(i, experts) for i in range(experts)], I32))
    start = jnp.sum((own_picks < (sources * rows)[:, None]).astype(I32), axis=1)
    stop = jnp.sum((own_picks < ((sources + 1) * rows)[:, None]).astype(I32), axis=1)
    ids = jnp.arange(BATCHES, dtype=I32)[:, None]
    offsets = (start[None, :] + (BATCHES - 1) - ids) // BATCHES
    counts = (stop[None, :] + (BATCHES - 1) - ids) // BATCHES - offsets

    present = [jnp.sum(counts[k]) > 0 for k in range(BATCHES)]

    def beside_first(router):
        logits = partial_logits(router, tokens)
        later = [tuple(later_batch(code, tokens, k, depth)) for k in range(1, BATCHES)]
        for bit in bits:
            logits = logits + swap(logits, bit)
        gathered = logits[None]
        for bit in expert_bits[:-1]:
            gathered = jnp.concatenate([gathered, along_expert(gathered, bit)])
        return later, logits, gathered

    def nothing_first(router):
        return jax.tree.map(lambda x: jnp.zeros(x.shape, x.dtype), jax.eval_shape(beside_first, router))

    arrived = [exchange(first)]
    later, logits, gathered = lax.cond(present[0], beside_first, nothing_first, router_weight.T)

    def far_half(far, sums):
        far = spread(far)
        hidden = gate_up_far(far, sums)
        far = swap(hidden, bits[0])
        partial = down_first(order, near_places, far_places, down_weight, spread(hidden))
        far, partial = lax.optimization_barrier((far, partial))
        return spread(far), partial

    def settle(k, far, partial):
        return tuple(
            down_last(offsets, counts, k, far, partial, experts, depth, k == BATCHES - 1)
        )

    def fenced(k, run, *operands):
        def skip(*operands):
            return jax.tree.map(lambda x: jnp.zeros(x.shape, x.dtype), jax.eval_shape(run, *operands))

        return lax.cond(present[k], run, skip, *operands)

    waiting = []
    far = partial = None
    moved = gathered
    for k in range(BATCHES):
        blocks = after(arrived[k], moved)
        if k == 0:
            block = fenced(k, lambda *blocks: compact(offsets, counts, 0, blocks, size), *blocks)
        else:
            block = compact(offsets, counts, k, blocks, size)
        across = swap(block, bits[0])
        near = spread(block)
        if k == 0:
            gathered = after(gathered, block)
            gathered = jnp.concatenate([gathered, along_expert(gathered, expert_bits[-1])])
        if k < BATCHES - 1:
            arrived.append(exchange(after(later[k], blocks, gathered)))
        if k > 0:
            far, partial = after((far, partial), block)
            results = settle(k - 1, far, partial)
            if k > 1:
                results, waiting[k - 2] = lax.optimization_barrier((results, waiting[k - 2]))
            waiting.append(exchange(results))
            near = after(near, results)
        sums = gate_up_near(order, near_places, far_places, gate_weight, up_weight, near)
        across, sums = lax.optimization_barrier((across, sums))
        far, partial = fenced(k, far_half, across, sums)
        moved = partial
    results = settle(BATCHES - 1, far, partial)
    results, gathered, waiting[-1] = lax.optimization_barrier((results, gathered, waiting[-1]))
    waiting.append(exchange(results))
    weights = slot_weights(place, logits, gathered, code)
    total = None
    for k in range(BATCHES):
        total = combine(code, weights, k, waiting[k], total)
    return total


def solution(mesh):
    return jax.shard_map(
        shards,
        mesh=mesh,
        in_specs=(
            P(("groups", "expert"), "dp"),
            P("dp", None),
            P("expert", None, "dp"),
            P("expert", None, "dp"),
            P("expert", None, "dp"),
            P("groups", None),
        ),
        out_specs=P(("groups", "expert"), "dp"),
        check_vma=False,
    )
```

```python
import functools

import jax
import jax.numpy as jnp
from jax import lax
from jax.experimental import pallas as pl
from jax.experimental.pallas import tpu as pltpu
from jax.sharding import PartitionSpec as P

BATCHES = 2
F32 = jnp.float32
BF16 = jnp.bfloat16
I32 = jnp.int32
VMEM_LIMIT = 16 * 1024 * 1024
COST = pl.CostEstimate(flops=1024, bytes_accessed=1024, transcendentals=0)


def whole(count):
    return [pl.BlockSpec(memory_space=pltpu.VMEM)] * count


def apart(count):
    return [pl.BlockSpec(memory_space=pl.ANY)] * count


def smem():
    return pl.BlockSpec(memory_space=pltpu.SMEM)


def params(limit=VMEM_LIMIT):
    return pltpu.CompilerParams(vmem_limit_bytes=limit)


def partner(place, experts):
    return -place % experts


def dot(a, b):
    return jnp.dot(a, b, preferred_element_type=F32)


def start_all(sources, targets, sems):
    copies = [pltpu.make_async_copy(a, b, sems.at[i]) for i, (a, b) in enumerate(zip(sources, targets))]
    for copy in copies:
        copy.start()
    return copies


def code_kernel(experts, depth, place_ref, picks_in, tokens_ref, code_ref, *refs):
    sends = refs[:experts]
    picks_ref, held, staged, in_sems, out_sems = refs[experts:]
    picks_load, load = start_all([picks_in, tokens_ref], [picks_ref, held], in_sems)
    me = place_ref[0]
    rows, width = held.shape
    capacity = picks_ref.shape[1]
    strips = rows // 128
    lanes = lax.broadcasted_iota(I32, (128, capacity), 0)
    strip_ids = lax.broadcasted_iota(I32, (8, capacity), 0)
    total = 8 * experts
    row_ids = lax.broadcasted_iota(I32, (total, total), 0)
    lane_ids = lax.broadcasted_iota(I32, (total, total), 1)
    same = lax.shift_right_logical(row_ids, 3) == lax.shift_right_logical(lane_ids, 3)
    before = (same & (lane_ids < row_ids)).astype(F32).astype(BF16)
    upper = (lax.broadcasted_iota(I32, (128, 128), 0) < lax.broadcasted_iota(I32, (128, 128), 1)).astype(BF16)
    ones = jnp.ones((128, 128), BF16)
    picks_load.wait()
    masks, starts = [], []
    for shift in range(experts):
        local = picks_ref[pl.ds(jnp.bitwise_xor(me, partner(shift, experts)), 1), :] - me * rows
        starts.append(jnp.broadcast_to(jnp.sum((local < 0).astype(F32), axis=1, keepdims=True), (8, 128)))
        strip = lax.shift_right_arithmetic(local, 7)
        place = jnp.bitwise_and(local, 127)
        high = ((strip == strip_ids) & (strip_ids < strips)).astype(F32).astype(BF16)
        low = (place == lanes).astype(F32).astype(BF16)
        masks.append(lax.dot_general(high, low, (((1,), (1,)), ((), ())), preferred_element_type=F32))
    mask = jnp.concatenate(masks, axis=0)
    start = jnp.concatenate(starts, axis=0).astype(I32)
    mask16 = mask.astype(BF16)
    totals = dot(mask16, ones)
    rank = (dot(mask16, upper) + dot(before, totals.astype(BF16))).astype(I32)
    slot = lax.rem(rank + start, BATCHES) * depth + lax.div(rank, BATCHES)
    code = jnp.where(mask > 0.5, slot, -1)
    code_rows = []
    for shift in range(experts):
        row = jnp.concatenate([code[8 * shift + i : 8 * shift + i + 1] for i in range(strips)], axis=1)
        code_ref[pl.ds(shift, 1), :] = row
        code_rows.append(row)
    load.wait()
    pack(0, depth, code_rows, held, staged, sends, out_sems)


def pack(k, depth, code_rows, held, staged, sends, sems):
    slot_ids = lax.broadcasted_iota(I32, (depth, held.shape[0]), 0) + k * depth
    copies = []
    for shift in list(range(1, len(sends))) + [0]:
        selector = (slot_ids == code_rows[shift]).astype(F32).astype(BF16)
        staged[shift] = dot(selector, held[...]).astype(BF16)
        copy = pltpu.make_async_copy(staged.at[shift], sends[shift], sems.at[shift])
        copy.start()
        copies.append(copy)
    for copy in copies:
        copy.wait()


def first_batch(place, picks, tokens, depth):
    rows, width = tokens.shape
    experts = picks.shape[0]
    out = pl.pallas_call(
        functools.partial(code_kernel, experts, depth),
        out_shape=[jax.ShapeDtypeStruct((experts, rows), I32)]
        + [jax.ShapeDtypeStruct((depth, width), BF16)] * experts,
        in_specs=[smem()] + apart(2),
        out_specs=whole(1) + apart(experts),
        scratch_shapes=[
            pltpu.VMEM(picks.shape, I32),
            pltpu.VMEM((rows, width), BF16),
            pltpu.VMEM((experts, depth, width), BF16),
            pltpu.SemaphoreType.DMA((2,)),
            pltpu.SemaphoreType.DMA((experts,)),
        ],
        compiler_params=params(60 * 1024 * 1024),
        cost_estimate=COST,
    )(place, picks, tokens)
    return out[0], out[1:]


def logits_kernel(router_ref, tokens_ref, out_ref):
    out_ref[...] = lax.dot_general(
        router_ref[...], tokens_ref[...], (((1,), (1,)), ((), ())), preferred_element_type=F32
    )


def partial_logits(router, tokens):
    return pl.pallas_call(
        logits_kernel,
        out_shape=jax.ShapeDtypeStruct((router.shape[0], tokens.shape[0]), F32),
        in_specs=whole(2),
        out_specs=whole(1)[0],
        compiler_params=params(),
        cost_estimate=COST,
    )(router, tokens)


def pack_kernel(experts, depth, k, code_ref, tokens_ref, *refs):
    sends = refs[:experts]
    held, staged, in_sems, out_sems = refs[experts:]
    start_all([tokens_ref], [held], in_sems)[0].wait()
    code_rows = [code_ref[pl.ds(shift, 1), :] for shift in range(experts)]
    pack(k, depth, code_rows, held, staged, sends, out_sems)


def later_batch(code, tokens, k, depth):
    rows, width = tokens.shape
    experts = code.shape[0]
    return pl.pallas_call(
        functools.partial(pack_kernel, experts, depth, k),
        out_shape=[jax.ShapeDtypeStruct((depth, width), BF16)] * experts,
        in_specs=whole(1) + apart(1),
        out_specs=apart(experts),
        scratch_shapes=[
            pltpu.VMEM((rows, width), BF16),
            pltpu.VMEM((experts, depth, width), BF16),
            pltpu.SemaphoreType.DMA((1,)),
            pltpu.SemaphoreType.DMA((experts,)),
        ],
        compiler_params=params(),
        cost_estimate=COST,
    )(code, tokens)


def compact_kernel(experts, k, offset_ref, count_ref, *refs):
    blocks, out_ref = refs[:experts], refs[experts]
    held, sems = refs[experts + 1 :]
    depth = blocks[0].shape[0]
    size = out_ref.shape[0]
    loads = start_all(blocks, [held.at[pl.ds(i * depth, depth)] for i in range(experts)], sems)
    row = lax.broadcasted_iota(I32, (size, depth), 0)
    lane = lax.broadcasted_iota(I32, (size, depth), 1)
    parts = [
        ((row - offset_ref[k, i] == lane) & (lane < count_ref[k, i])).astype(F32).astype(BF16)
        for i in range(experts)
    ]
    selector = jnp.concatenate(parts, axis=1)
    for load in loads:
        load.wait()
    out_ref[...] = dot(selector, held[...]).astype(BF16)


def compact(offsets, counts, k, blocks, size):
    experts = len(blocks)
    depth, width = blocks[0].shape
    return pl.pallas_call(
        functools.partial(compact_kernel, experts, k),
        out_shape=jax.ShapeDtypeStruct((size, width), BF16),
        in_specs=[smem(), smem()] + apart(experts),
        out_specs=whole(1)[0],
        scratch_shapes=[pltpu.VMEM((experts * depth, width), BF16), pltpu.SemaphoreType.DMA((experts,))],
        compiler_params=params(),
        cost_estimate=COST,
    )(offsets, counts, *blocks)


def gate_up_near_kernel(parts, near, far, order_ref, gate_ref, up_ref, *refs):
    xs, refs = refs[:parts], refs[parts:]
    gate_out, up_out, gate_far, up_far, gate_held, up_held, x_held, sems = refs
    width = xs[0].shape[1]

    def fetch(i, place, gate_to, up_to, base):
        first = pl.multiple_of(order_ref[place] * width, width)
        return start_all(
            [gate_ref.at[0, pl.ds(first, width), :], up_ref.at[0, pl.ds(first, width), :]],
            [gate_to.at[i], up_to.at[i]],
            sems.at[pl.ds(base, 2)],
        )

    x_loads = start_all(xs, [x_held.at[i] for i in range(parts)], sems.at[pl.ds(0, parts)])
    loads = [fetch(i, near[i], gate_held, up_held, parts + 2 * i) for i in range(parts)]
    late = [fetch(i, far[i], gate_far, up_far, 3 * parts + 2 * i) for i in range(len(far))]
    gate = up = None
    for i in range(parts):
        for copy in [x_loads[i]] + loads[i]:
            copy.wait()
        x = x_held[i]
        gate_term = dot(x, gate_held[i])
        up_term = dot(x, up_held[i])
        gate = gate_term if gate is None else gate + gate_term
        up = up_term if up is None else up + up_term
    gate_out[...] = gate
    up_out[...] = up
    for copies in late:
        for copy in copies:
            copy.wait()


def gate_up_near(order, near, far, gate_weight, up_weight, xs):
    parts = len(xs)
    size, width = xs[0].shape
    units = gate_weight.shape[2]
    held = jax.ShapeDtypeStruct((len(far), width, units), BF16)
    return pl.pallas_call(
        functools.partial(gate_up_near_kernel, parts, near, far),
        out_shape=[jax.ShapeDtypeStruct((size, units), F32)] * 2 + [held] * 2,
        in_specs=[smem()] + apart(2 + parts),
        out_specs=whole(4),
        scratch_shapes=[
            pltpu.VMEM((parts, width, units), BF16),
            pltpu.VMEM((parts, width, units), BF16),
            pltpu.VMEM((parts, size, width), BF16),
            pltpu.SemaphoreType.DMA((3 * parts + 2 * len(far),)),
        ],
        compiler_params=params(),
        cost_estimate=COST,
    )(order, gate_weight, up_weight, *xs)


def gate_up_far_kernel(parts, gate_before, up_before, gate_ref, up_ref, *refs):
    xs, out_ref = refs[:parts], refs[parts]
    gate, up = gate_before[...], up_before[...]
    for i in range(parts):
        x = xs[i][...]
        gate = gate + dot(x, gate_ref[i])
        up = up + dot(x, up_ref[i])
    out_ref[...] = (gate * jax.nn.sigmoid(gate) * up).astype(BF16)


def gate_up_far(xs, before):
    size, units = before[0].shape
    return pl.pallas_call(
        functools.partial(gate_up_far_kernel, len(xs)),
        out_shape=jax.ShapeDtypeStruct((size, units), BF16),
        in_specs=whole(4 + len(xs)),
        out_specs=whole(1)[0],
        compiler_params=params(),
        cost_estimate=COST,
    )(*before, *xs)


def down_first_kernel(parts, near, far, order_ref, down_ref, *refs):
    hs, (out_ref, far_ref, down_held, h_held, sems) = refs[:parts], refs[parts:]
    units = hs[0].shape[1]

    def fetch(i, place, target, sem):
        first = pl.multiple_of(order_ref[place] * units, units)
        copy = pltpu.make_async_copy(down_ref.at[0, pl.ds(first, units), :], target.at[i], sems.at[sem])
        copy.start()
        return copy

    h_loads = start_all(hs, [h_held.at[i] for i in range(parts)], sems.at[pl.ds(0, parts)])
    loads = [fetch(i, near[i], down_held, parts + i) for i in range(parts)]
    late = [fetch(i, far[i], far_ref, 2 * parts + i) for i in range(len(far))]
    total = None
    for i in range(parts):
        h_loads[i].wait()
        loads[i].wait()
        term = dot(h_held[i], down_held[i])
        total = term if total is None else total + term
    out_ref[...] = total
    for copy in late:
        copy.wait()


def down_first(order, near, far, down_weight, hs):
    parts = len(hs)
    size, units = hs[0].shape
    width = down_weight.shape[2]
    return pl.pallas_call(
        functools.partial(down_first_kernel, parts, near, far),
        out_shape=[
            jax.ShapeDtypeStruct((size, width), F32),
            jax.ShapeDtypeStruct((len(far), units, width), BF16),
        ],
        in_specs=[smem()] + apart(1 + parts),
        out_specs=whole(2),
        scratch_shapes=[
            pltpu.VMEM((parts, units, width), BF16),
            pltpu.VMEM((parts, size, units), BF16),
            pltpu.SemaphoreType.DMA((2 * parts + len(far),)),
        ],
        compiler_params=params(),
        cost_estimate=COST,
    )(order, down_weight, *hs)


def down_last_kernel(parts, experts, k, direct, offset_ref, count_ref, before_ref, down_ref, *refs):
    hs, outs = refs[:parts], refs[parts : parts + experts]
    h_held, sems, *staged = refs[parts + experts :]
    loads = start_all(hs, [h_held.at[i] for i in range(parts)], sems)
    size = hs[0].shape[0]
    depth = outs[0].shape[0]
    row = lax.broadcasted_iota(I32, (depth, size), 0)
    lane = lax.broadcasted_iota(I32, (depth, size), 1)
    picks = [
        ((lane - offset_ref[k, i] == row) & (row < count_ref[k, i])).astype(F32).astype(BF16)
        for i in range(experts)
    ]
    total = before_ref[...]
    for i in range(parts):
        loads[i].wait()
        total = total + dot(h_held[i], down_ref[i])
    result = total.astype(BF16)
    if direct:
        for i in range(experts):
            outs[i][...] = dot(picks[i], result).astype(BF16)
        return
    staged_ref, out_sems = staged
    copies = []
    for i in list(range(1, experts)) + [0]:
        staged_ref[i] = dot(picks[i], result).astype(BF16)
        copy = pltpu.make_async_copy(staged_ref.at[i], outs[i], out_sems.at[i])
        copy.start()
        copies.append(copy)
    for copy in copies:
        copy.wait()


def down_last(offsets, counts, k, hs, before, experts, depth, direct):
    parts = len(hs)
    size, units = hs[0].shape
    width = before[0].shape[1]
    return pl.pallas_call(
        functools.partial(down_last_kernel, parts, experts, k, direct),
        out_shape=[jax.ShapeDtypeStruct((depth, width), BF16)] * experts,
        in_specs=[smem()] * 2 + whole(2) + apart(parts),
        out_specs=whole(experts) if direct else apart(experts),
        scratch_shapes=[pltpu.VMEM((parts, size, units), BF16), pltpu.SemaphoreType.DMA((parts,))]
        + ([] if direct else [pltpu.VMEM((experts, depth, width), BF16), pltpu.SemaphoreType.DMA((experts,))]),
        compiler_params=params(),
        cost_estimate=COST,
    )(offsets, counts, *before, *hs)


def weight_kernel(experts, place_ref, own_ref, logits_ref, code_ref, out_ref, score_ref):
    me = place_ref[0]
    kernel = jnp.exp(logits_ref[...])
    row_scale = jnp.ones((kernel.shape[0], 1, kernel.shape[2]), F32)
    for sweep in range(3):
        column = jnp.sum(jnp.sum(kernel * row_scale, axis=0, keepdims=True), axis=2, keepdims=True)
        column_scale = 1.0 / column
        row_scale = 1.0 / jnp.sum(kernel * column_scale, axis=1, keepdims=True)
    own = jnp.exp(own_ref[...])
    column_scale = column_scale[0]
    own_scale = 1.0 / jnp.sum(own * column_scale, axis=0, keepdims=True)
    score_ref[...] = own_scale * own * column_scale
    picked = []
    for shift in range(experts):
        score = score_ref[pl.ds(jnp.bitwise_xor(me, partner(shift, experts)), 1), :]
        picked.append(jnp.where(code_ref[pl.ds(shift, 1), :] >= 0, score, 0.0))
    total = picked[0]
    for one in picked[1:]:
        total = total + one
    total = jnp.maximum(total, 1.0 / experts)
    for shift in range(experts):
        out_ref[pl.ds(shift, 1), :] = picked[shift] / total


def slot_weights(place, own, logits, code):
    experts, rows = own.shape
    return pl.pallas_call(
        functools.partial(weight_kernel, experts),
        out_shape=jax.ShapeDtypeStruct((experts, rows), F32),
        in_specs=[smem()] + whole(3),
        out_specs=whole(1)[0],
        scratch_shapes=[pltpu.VMEM((experts, rows), F32)],
        compiler_params=params(),
        cost_estimate=COST,
    )(place, own, logits, code)


def combine_kernel(experts, k, code_ref, weight_ref, *refs):
    before, refs = refs[: k > 0], refs[k > 0 :]
    blocks, (out_ref, held, sems) = refs[:experts], refs[experts:]
    depth = blocks[0].shape[0]
    rows = code_ref.shape[1]
    targets = [held.at[pl.ds(i * depth, depth)] for i in range(experts)]
    loads = start_all(blocks, targets, sems)
    slot_ids = lax.broadcasted_iota(I32, (depth, rows), 0) + k * depth
    parts = [
        jnp.where(slot_ids == code_ref[pl.ds(i, 1), :], weight_ref[pl.ds(i, 1), :], 0.0).astype(BF16)
        for i in range(experts)
    ]
    spread = jnp.concatenate(parts, axis=0)
    for load in loads:
        load.wait()
    total = lax.dot_general(spread, held[...], (((0,), (0,)), ((), ())), preferred_element_type=F32)
    if k > 0:
        total = total + before[0][...]
    out_ref[...] = total.astype(out_ref.dtype)


def combine(code, weights, k, blocks, so_far):
    experts = len(blocks)
    depth, width = blocks[0].shape
    rows = code.shape[1]
    last = k == BATCHES - 1
    more = [] if so_far is None else [so_far]
    return pl.pallas_call(
        functools.partial(combine_kernel, experts, k),
        out_shape=jax.ShapeDtypeStruct((rows, width), BF16 if last else F32),
        in_specs=whole(2 + len(more)) + apart(experts),
        out_specs=whole(1)[0],
        scratch_shapes=[pltpu.VMEM((experts * depth, width), BF16), pltpu.SemaphoreType.DMA((experts,))],
        compiler_params=params(),
        cost_estimate=COST,
    )(code, weights, *more, *blocks)


def after(value, *first):
    return lax.optimization_barrier((value, first))[0]


def shards(tokens, router_weight, gate_weight, up_weight, down_weight, picks):
    experts = lax.axis_size("expert")
    width_parts = lax.axis_size("dp")
    me = lax.axis_index("expert")
    part = lax.axis_index("dp")
    rows = tokens.shape[0]
    capacity = picks.shape[1]
    depth = 2 * capacity // experts // BATCHES
    size = capacity // BATCHES
    place = me.astype(I32).reshape(1)

    def along_expert(x, shift):
        return lax.ppermute(x, "expert", [(i, i ^ shift) for i in range(experts)])

    def swap(x, bit):
        return lax.ppermute(x, "dp", [(i, i ^ bit) for i in range(width_parts)])

    bits = []
    bit = width_parts // 2
    while bit:
        bits.append(bit)
        bit //= 2
    near = [0]
    for bit in bits[1:]:
        near = near + [m ^ bit for m in near]
    masks = near + [m ^ bits[0] for m in near]
    places = range(len(masks))
    near_places, far_places = places[: len(near)], places[len(near) :]
    order = jnp.stack([part ^ m for m in masks]).astype(I32)

    def exchange(blocks):
        return [blocks[0]] + [along_expert(blocks[i], partner(i, experts)) for i in range(1, experts)]

    expert_bits = [1 << i for i in range(experts.bit_length() - 1)]

    def spread(x):
        held = [x]
        for bit in bits[1:]:
            held = held + [swap(h, bit) for h in held]
        return held

    def both_parts(x):
        far = swap(x, bits[0])
        return spread(x), spread(far)

    code, first = first_batch(place, picks, tokens, depth)
    own_picks = lax.dynamic_slice_in_dim(picks, me, 1, axis=0)
    sources = jnp.bitwise_xor(me, jnp.array([partner(i, experts) for i in range(experts)], I32))
    start = jnp.sum((own_picks < (sources * rows)[:, None]).astype(I32), axis=1)
    stop = jnp.sum((own_picks < ((sources + 1) * rows)[:, None]).astype(I32), axis=1)
    ids = jnp.arange(BATCHES, dtype=I32)[:, None]
    offsets = (start[None, :] + (BATCHES - 1) - ids) // BATCHES
    counts = (stop[None, :] + (BATCHES - 1) - ids) // BATCHES - offsets

    present = [jnp.sum(counts[k]) > 0 for k in range(BATCHES)]

    def beside_first(router):
        logits = partial_logits(router, tokens)
        later = [tuple(later_batch(code, tokens, k, depth)) for k in range(1, BATCHES)]
        for bit in bits:
            logits = logits + swap(logits, bit)
        gathered = logits[None]
        for bit in expert_bits:
            if bit == expert_bits[-1]:
                gathered, later = lax.optimization_barrier((gathered, later))
            gathered = jnp.concatenate([gathered, along_expert(gathered, bit)])
        return later, logits, gathered

    def nothing_first(router):
        return jax.tree.map(lambda x: jnp.zeros(x.shape, x.dtype), jax.eval_shape(beside_first, router))

    arrived = [exchange(first)]
    later, logits, gathered = lax.cond(present[0], beside_first, nothing_first, router_weight.T)

    def far_half(far, sums):
        far = spread(far)
        hidden = gate_up_far(far, sums)
        far = swap(hidden, bits[0])
        partial = down_first(order, near_places, far_places, down_weight, spread(hidden))
        far, partial = lax.optimization_barrier((far, partial))
        return spread(far), partial

    def settle(k, far, partial):
        return tuple(
            down_last(offsets, counts, k, far, partial, experts, depth, k == BATCHES - 1)
        )

    def fenced(k, run, *operands):
        def skip(*operands):
            return jax.tree.map(lambda x: jnp.zeros(x.shape, x.dtype), jax.eval_shape(run, *operands))

        return lax.cond(present[k], run, skip, *operands)

    waiting = []
    far = partial = None
    moved = gathered
    for k in range(BATCHES):
        blocks = after(arrived[k], moved)
        if k == 0:
            block = fenced(k, lambda *blocks: compact(offsets, counts, 0, blocks, size), *blocks)
        else:
            block = compact(offsets, counts, k, blocks, size)
        across = swap(block, bits[0])
        near = spread(block)
        if k < BATCHES - 1:
            arrived.append(exchange(after(later[k], blocks)))
        if k > 0:
            far, partial = after((far, partial), block)
            results = settle(k - 1, far, partial)
            if k > 1:
                results, waiting[k - 2] = lax.optimization_barrier((results, waiting[k - 2]))
            waiting.append(exchange(results))
            near = after(near, results)
        sums = gate_up_near(order, near_places, far_places, gate_weight, up_weight, near)
        across, sums = lax.optimization_barrier((across, sums))
        far, partial = fenced(k, far_half, across, sums)
        moved = partial
    results = settle(BATCHES - 1, far, partial)
    results, gathered, waiting[-1] = lax.optimization_barrier((results, gathered, waiting[-1]))
    waiting.append(exchange(results))
    weights = slot_weights(place, logits, gathered, code)
    total = None
    for k in range(BATCHES):
        total = combine(code, weights, k, waiting[k], total)
    return total


def solution(mesh):
    return jax.shard_map(
        shards,
        mesh=mesh,
        in_specs=(
            P(("groups", "expert"), "dp"),
            P("dp", None),
            P("expert", None, "dp"),
            P("expert", None, "dp"),
            P("expert", None, "dp"),
            P("groups", None),
        ),
        out_specs=P(("groups", "expert"), "dp"),
        check_vma=False,
    )
```

```python
import functools

import jax
import jax.numpy as jnp
from jax import lax
from jax.experimental import pallas as pl
from jax.experimental.pallas import tpu as pltpu
from jax.sharding import PartitionSpec as P

BATCHES = 2
F32 = jnp.float32
BF16 = jnp.bfloat16
I32 = jnp.int32
VMEM_LIMIT = 16 * 1024 * 1024
COST = pl.CostEstimate(flops=1024, bytes_accessed=1024, transcendentals=0)


def whole(count):
    return [pl.BlockSpec(memory_space=pltpu.VMEM)] * count


def apart(count):
    return [pl.BlockSpec(memory_space=pl.ANY)] * count


def smem():
    return pl.BlockSpec(memory_space=pltpu.SMEM)


def params(limit=VMEM_LIMIT):
    return pltpu.CompilerParams(vmem_limit_bytes=limit)


def partner(place, experts):
    return -place % experts


def dot(a, b):
    return jnp.dot(a, b, preferred_element_type=F32)


def start_all(sources, targets, sems):
    copies = [pltpu.make_async_copy(a, b, sems.at[i]) for i, (a, b) in enumerate(zip(sources, targets))]
    for copy in copies:
        copy.start()
    return copies


def code_kernel(experts, depth, place_ref, picks_in, tokens_ref, code_ref, *refs):
    sends = refs[:experts]
    picks_ref, held, staged, in_sems, out_sems = refs[experts:]
    picks_load, load = start_all([picks_in, tokens_ref], [picks_ref, held], in_sems)
    me = place_ref[0]
    rows, width = held.shape
    capacity = picks_ref.shape[1]
    strips = rows // 128
    lanes = lax.broadcasted_iota(I32, (128, capacity), 0)
    strip_ids = lax.broadcasted_iota(I32, (8, capacity), 0)
    total = 8 * experts
    row_ids = lax.broadcasted_iota(I32, (total, total), 0)
    lane_ids = lax.broadcasted_iota(I32, (total, total), 1)
    same = lax.shift_right_logical(row_ids, 3) == lax.shift_right_logical(lane_ids, 3)
    before = (same & (lane_ids < row_ids)).astype(F32).astype(BF16)
    upper = (lax.broadcasted_iota(I32, (128, 128), 0) < lax.broadcasted_iota(I32, (128, 128), 1)).astype(BF16)
    ones = jnp.ones((128, 128), BF16)
    picks_load.wait()
    masks, starts = [], []
    for shift in range(experts):
        local = picks_ref[pl.ds(jnp.bitwise_xor(me, partner(shift, experts)), 1), :] - me * rows
        starts.append(jnp.broadcast_to(jnp.sum((local < 0).astype(F32), axis=1, keepdims=True), (8, 128)))
        strip = lax.shift_right_arithmetic(local, 7)
        place = jnp.bitwise_and(local, 127)
        high = ((strip == strip_ids) & (strip_ids < strips)).astype(F32).astype(BF16)
        low = (place == lanes).astype(F32).astype(BF16)
        masks.append(lax.dot_general(high, low, (((1,), (1,)), ((), ())), preferred_element_type=F32))
    mask = jnp.concatenate(masks, axis=0)
    start = jnp.concatenate(starts, axis=0).astype(I32)
    mask16 = mask.astype(BF16)
    totals = dot(mask16, ones)
    rank = (dot(mask16, upper) + dot(before, totals.astype(BF16))).astype(I32)
    slot = lax.rem(rank + start, BATCHES) * depth + lax.div(rank, BATCHES)
    code = jnp.where(mask > 0.5, slot, -1)
    code_rows = []
    for shift in range(experts):
        row = jnp.concatenate([code[8 * shift + i : 8 * shift + i + 1] for i in range(strips)], axis=1)
        code_ref[pl.ds(shift, 1), :] = row
        code_rows.append(row)
    load.wait()
    pack(0, depth, code_rows, held, staged, sends, out_sems)


def pack(k, depth, code_rows, held, staged, sends, sems):
    slot_ids = lax.broadcasted_iota(I32, (depth, held.shape[0]), 0) + k * depth
    copies = []
    for shift in list(range(1, len(sends))) + [0]:
        selector = (slot_ids == code_rows[shift]).astype(F32).astype(BF16)
        staged[shift] = dot(selector, held[...]).astype(BF16)
        copy = pltpu.make_async_copy(staged.at[shift], sends[shift], sems.at[shift])
        copy.start()
        copies.append(copy)
    for copy in copies:
        copy.wait()


def first_batch(place, picks, tokens, depth):
    rows, width = tokens.shape
    experts = picks.shape[0]
    out = pl.pallas_call(
        functools.partial(code_kernel, experts, depth),
        out_shape=[jax.ShapeDtypeStruct((experts, rows), I32)]
        + [jax.ShapeDtypeStruct((depth, width), BF16)] * experts,
        in_specs=[smem()] + apart(2),
        out_specs=whole(1) + apart(experts),
        scratch_shapes=[
            pltpu.VMEM(picks.shape, I32),
            pltpu.VMEM((rows, width), BF16),
            pltpu.VMEM((experts, depth, width), BF16),
            pltpu.SemaphoreType.DMA((2,)),
            pltpu.SemaphoreType.DMA((experts,)),
        ],
        compiler_params=params(60 * 1024 * 1024),
        cost_estimate=COST,
    )(place, picks, tokens)
    return out[0], out[1:]


def logits_kernel(router_ref, tokens_ref, out_ref):
    out_ref[...] = lax.dot_general(
        router_ref[...], tokens_ref[...], (((1,), (1,)), ((), ())), preferred_element_type=F32
    )


def partial_logits(router, tokens):
    return pl.pallas_call(
        logits_kernel,
        out_shape=jax.ShapeDtypeStruct((router.shape[0], tokens.shape[0]), F32),
        in_specs=whole(2),
        out_specs=whole(1)[0],
        compiler_params=params(),
        cost_estimate=COST,
    )(router, tokens)


def pack_kernel(experts, depth, k, code_ref, tokens_ref, *refs):
    sends = refs[:experts]
    held, staged, in_sems, out_sems = refs[experts:]
    start_all([tokens_ref], [held], in_sems)[0].wait()
    code_rows = [code_ref[pl.ds(shift, 1), :] for shift in range(experts)]
    pack(k, depth, code_rows, held, staged, sends, out_sems)


def later_batch(code, tokens, k, depth):
    rows, width = tokens.shape
    experts = code.shape[0]
    return pl.pallas_call(
        functools.partial(pack_kernel, experts, depth, k),
        out_shape=[jax.ShapeDtypeStruct((depth, width), BF16)] * experts,
        in_specs=whole(1) + apart(1),
        out_specs=apart(experts),
        scratch_shapes=[
            pltpu.VMEM((rows, width), BF16),
            pltpu.VMEM((experts, depth, width), BF16),
            pltpu.SemaphoreType.DMA((1,)),
            pltpu.SemaphoreType.DMA((experts,)),
        ],
        compiler_params=params(),
        cost_estimate=COST,
    )(code, tokens)


def compact_kernel(experts, k, offset_ref, count_ref, *refs):
    blocks, out_ref = refs[:experts], refs[experts]
    held, sems = refs[experts + 1 :]
    depth = blocks[0].shape[0]
    size = out_ref.shape[0]
    loads = start_all(blocks, [held.at[pl.ds(i * depth, depth)] for i in range(experts)], sems)
    row = lax.broadcasted_iota(I32, (size, depth), 0)
    lane = lax.broadcasted_iota(I32, (size, depth), 1)
    parts = [
        ((row - offset_ref[k, i] == lane) & (lane < count_ref[k, i])).astype(F32).astype(BF16)
        for i in range(experts)
    ]
    selector = jnp.concatenate(parts, axis=1)
    for load in loads:
        load.wait()
    out_ref[...] = dot(selector, held[...]).astype(BF16)


def compact(offsets, counts, k, blocks, size):
    experts = len(blocks)
    depth, width = blocks[0].shape
    return pl.pallas_call(
        functools.partial(compact_kernel, experts, k),
        out_shape=jax.ShapeDtypeStruct((size, width), BF16),
        in_specs=[smem(), smem()] + apart(experts),
        out_specs=whole(1)[0],
        scratch_shapes=[pltpu.VMEM((experts * depth, width), BF16), pltpu.SemaphoreType.DMA((experts,))],
        compiler_params=params(),
        cost_estimate=COST,
    )(offsets, counts, *blocks)


def gate_up_near_kernel(parts, near, far, order_ref, gate_ref, up_ref, *refs):
    xs, refs = refs[:parts], refs[parts:]
    gate_out, up_out, gate_far, up_far, gate_held, up_held, x_held, sems = refs
    width = xs[0].shape[1]

    def fetch(i, place, gate_to, up_to, base):
        first = pl.multiple_of(order_ref[place] * width, width)
        return start_all(
            [gate_ref.at[0, pl.ds(first, width), :], up_ref.at[0, pl.ds(first, width), :]],
            [gate_to.at[i], up_to.at[i]],
            sems.at[pl.ds(base, 2)],
        )

    x_loads = start_all(xs, [x_held.at[i] for i in range(parts)], sems.at[pl.ds(0, parts)])
    loads = [fetch(i, near[i], gate_held, up_held, parts + 2 * i) for i in range(parts)]
    late = [fetch(i, far[i], gate_far, up_far, 3 * parts + 2 * i) for i in range(len(far))]
    gate = up = None
    for i in range(parts):
        for copy in [x_loads[i]] + loads[i]:
            copy.wait()
        x = x_held[i]
        gate_term = dot(x, gate_held[i])
        up_term = dot(x, up_held[i])
        gate = gate_term if gate is None else gate + gate_term
        up = up_term if up is None else up + up_term
    gate_out[...] = gate
    up_out[...] = up
    for copies in late:
        for copy in copies:
            copy.wait()


def gate_up_near(order, near, far, gate_weight, up_weight, xs):
    parts = len(xs)
    size, width = xs[0].shape
    units = gate_weight.shape[2]
    held = jax.ShapeDtypeStruct((len(far), width, units), BF16)
    return pl.pallas_call(
        functools.partial(gate_up_near_kernel, parts, near, far),
        out_shape=[jax.ShapeDtypeStruct((size, units), F32)] * 2 + [held] * 2,
        in_specs=[smem()] + apart(2 + parts),
        out_specs=whole(4),
        scratch_shapes=[
            pltpu.VMEM((parts, width, units), BF16),
            pltpu.VMEM((parts, width, units), BF16),
            pltpu.VMEM((parts, size, width), BF16),
            pltpu.SemaphoreType.DMA((3 * parts + 2 * len(far),)),
        ],
        compiler_params=params(),
        cost_estimate=COST,
    )(order, gate_weight, up_weight, *xs)


def gate_up_far_kernel(parts, first, last, gate_before, up_before, gate_ref, up_ref, *refs):
    xs, outs = refs[:parts], refs[parts:]
    gate, up = gate_before[...], up_before[...]
    for i in range(parts):
        x = xs[i][...]
        gate = gate + dot(x, gate_ref[first + i])
        up = up + dot(x, up_ref[first + i])
    if last:
        outs[0][...] = (gate * jax.nn.sigmoid(gate) * up).astype(BF16)
    else:
        outs[0][...] = gate
        outs[1][...] = up


def gate_up_far(xs, before, first, last):
    shape = before[0].shape
    sums = [jax.ShapeDtypeStruct(shape, F32)] * 2
    return pl.pallas_call(
        functools.partial(gate_up_far_kernel, len(xs), first, last),
        out_shape=[jax.ShapeDtypeStruct(shape, BF16)] if last else sums,
        in_specs=whole(4 + len(xs)),
        out_specs=whole(1 if last else 2),
        compiler_params=params(),
        cost_estimate=COST,
    )(*before, *xs)


def down_first_kernel(parts, near, far, order_ref, down_ref, *refs):
    hs, (out_ref, far_ref, down_held, h_held, sems) = refs[:parts], refs[parts:]
    units = hs[0].shape[1]

    def fetch(i, place, target, sem):
        first = pl.multiple_of(order_ref[place] * units, units)
        copy = pltpu.make_async_copy(down_ref.at[0, pl.ds(first, units), :], target.at[i], sems.at[sem])
        copy.start()
        return copy

    h_loads = start_all(hs, [h_held.at[i] for i in range(parts)], sems.at[pl.ds(0, parts)])
    loads = [fetch(i, near[i], down_held, parts + i) for i in range(parts)]
    late = [fetch(i, far[i], far_ref, 2 * parts + i) for i in range(len(far))]
    total = None
    for i in range(parts):
        h_loads[i].wait()
        loads[i].wait()
        term = dot(h_held[i], down_held[i])
        total = term if total is None else total + term
    out_ref[...] = total
    for copy in late:
        copy.wait()


def down_first(order, near, far, down_weight, hs):
    parts = len(hs)
    size, units = hs[0].shape
    width = down_weight.shape[2]
    return pl.pallas_call(
        functools.partial(down_first_kernel, parts, near, far),
        out_shape=[
            jax.ShapeDtypeStruct((size, width), F32),
            jax.ShapeDtypeStruct((len(far), units, width), BF16),
        ],
        in_specs=[smem()] + apart(1 + parts),
        out_specs=whole(2),
        scratch_shapes=[
            pltpu.VMEM((parts, units, width), BF16),
            pltpu.VMEM((parts, size, units), BF16),
            pltpu.SemaphoreType.DMA((2 * parts + len(far),)),
        ],
        compiler_params=params(),
        cost_estimate=COST,
    )(order, down_weight, *hs)


def down_last_kernel(parts, experts, k, direct, offset_ref, count_ref, before_ref, down_ref, *refs):
    hs, outs = refs[:parts], refs[parts : parts + experts]
    h_held, sems, *staged = refs[parts + experts :]
    loads = start_all(hs, [h_held.at[i] for i in range(parts)], sems)
    size = hs[0].shape[0]
    depth = outs[0].shape[0]
    row = lax.broadcasted_iota(I32, (depth, size), 0)
    lane = lax.broadcasted_iota(I32, (depth, size), 1)
    picks = [
        ((lane - offset_ref[k, i] == row) & (row < count_ref[k, i])).astype(F32).astype(BF16)
        for i in range(experts)
    ]
    total = before_ref[...]
    for i in range(parts):
        loads[i].wait()
        total = total + dot(h_held[i], down_ref[i])
    result = total.astype(BF16)
    if direct:
        for i in range(experts):
            outs[i][...] = dot(picks[i], result).astype(BF16)
        return
    staged_ref, out_sems = staged
    copies = []
    for i in list(range(1, experts)) + [0]:
        staged_ref[i] = dot(picks[i], result).astype(BF16)
        copy = pltpu.make_async_copy(staged_ref.at[i], outs[i], out_sems.at[i])
        copy.start()
        copies.append(copy)
    for copy in copies:
        copy.wait()


def down_last(offsets, counts, k, hs, before, experts, depth, direct):
    parts = len(hs)
    size, units = hs[0].shape
    width = before[0].shape[1]
    return pl.pallas_call(
        functools.partial(down_last_kernel, parts, experts, k, direct),
        out_shape=[jax.ShapeDtypeStruct((depth, width), BF16)] * experts,
        in_specs=[smem()] * 2 + whole(2) + apart(parts),
        out_specs=whole(experts) if direct else apart(experts),
        scratch_shapes=[pltpu.VMEM((parts, size, units), BF16), pltpu.SemaphoreType.DMA((parts,))]
        + ([] if direct else [pltpu.VMEM((experts, depth, width), BF16), pltpu.SemaphoreType.DMA((experts,))]),
        compiler_params=params(),
        cost_estimate=COST,
    )(offsets, counts, *before, *hs)


def weight_kernel(experts, place_ref, own_ref, logits_ref, code_ref, out_ref, score_ref):
    me = place_ref[0]
    kernel = jnp.exp(logits_ref[...])
    row_scale = jnp.ones((kernel.shape[0], 1, kernel.shape[2]), F32)
    for sweep in range(3):
        column = jnp.sum(jnp.sum(kernel * row_scale, axis=0, keepdims=True), axis=2, keepdims=True)
        column_scale = 1.0 / column
        row_scale = 1.0 / jnp.sum(kernel * column_scale, axis=1, keepdims=True)
    own = jnp.exp(own_ref[...])
    column_scale = column_scale[0]
    own_scale = 1.0 / jnp.sum(own * column_scale, axis=0, keepdims=True)
    score_ref[...] = own_scale * own * column_scale
    picked = []
    for shift in range(experts):
        score = score_ref[pl.ds(jnp.bitwise_xor(me, partner(shift, experts)), 1), :]
        picked.append(jnp.where(code_ref[pl.ds(shift, 1), :] >= 0, score, 0.0))
    total = picked[0]
    for one in picked[1:]:
        total = total + one
    total = jnp.maximum(total, 1.0 / experts)
    for shift in range(experts):
        out_ref[pl.ds(shift, 1), :] = picked[shift] / total


def slot_weights(place, own, logits, code):
    experts, rows = own.shape
    return pl.pallas_call(
        functools.partial(weight_kernel, experts),
        out_shape=jax.ShapeDtypeStruct((experts, rows), F32),
        in_specs=[smem()] + whole(3),
        out_specs=whole(1)[0],
        scratch_shapes=[pltpu.VMEM((experts, rows), F32)],
        compiler_params=params(),
        cost_estimate=COST,
    )(place, own, logits, code)


def combine_kernel(experts, k, code_ref, weight_ref, *refs):
    before, refs = refs[: k > 0], refs[k > 0 :]
    blocks, (out_ref, held, sems) = refs[:experts], refs[experts:]
    depth = blocks[0].shape[0]
    rows = code_ref.shape[1]
    targets = [held.at[pl.ds(i * depth, depth)] for i in range(experts)]
    loads = start_all(blocks, targets, sems)
    slot_ids = lax.broadcasted_iota(I32, (depth, rows), 0) + k * depth
    parts = [
        jnp.where(slot_ids == code_ref[pl.ds(i, 1), :], weight_ref[pl.ds(i, 1), :], 0.0).astype(BF16)
        for i in range(experts)
    ]
    spread = jnp.concatenate(parts, axis=0)
    for load in loads:
        load.wait()
    total = lax.dot_general(spread, held[...], (((0,), (0,)), ((), ())), preferred_element_type=F32)
    if k > 0:
        total = total + before[0][...]
    out_ref[...] = total.astype(out_ref.dtype)


def combine(code, weights, k, blocks, so_far):
    experts = len(blocks)
    depth, width = blocks[0].shape
    rows = code.shape[1]
    last = k == BATCHES - 1
    more = [] if so_far is None else [so_far]
    return pl.pallas_call(
        functools.partial(combine_kernel, experts, k),
        out_shape=jax.ShapeDtypeStruct((rows, width), BF16 if last else F32),
        in_specs=whole(2 + len(more)) + apart(experts),
        out_specs=whole(1)[0],
        scratch_shapes=[pltpu.VMEM((experts * depth, width), BF16), pltpu.SemaphoreType.DMA((experts,))],
        compiler_params=params(),
        cost_estimate=COST,
    )(code, weights, *more, *blocks)


def after(value, *first):
    return lax.optimization_barrier((value, first))[0]


def shards(tokens, router_weight, gate_weight, up_weight, down_weight, picks):
    experts = lax.axis_size("expert")
    width_parts = lax.axis_size("dp")
    me = lax.axis_index("expert")
    part = lax.axis_index("dp")
    rows = tokens.shape[0]
    capacity = picks.shape[1]
    depth = 2 * capacity // experts // BATCHES
    size = capacity // BATCHES
    place = me.astype(I32).reshape(1)

    def along_expert(x, shift):
        return lax.ppermute(x, "expert", [(i, i ^ shift) for i in range(experts)])

    def swap(x, bit):
        return lax.ppermute(x, "dp", [(i, i ^ bit) for i in range(width_parts)])

    bits = []
    bit = width_parts // 2
    while bit:
        bits.append(bit)
        bit //= 2
    near = [0]
    for bit in bits[1:]:
        near = near + [m ^ bit for m in near]
    masks = near + [m ^ bits[0] for m in near]
    places = range(len(masks))
    near_places, far_places = places[: len(near)], places[len(near) :]
    order = jnp.stack([part ^ m for m in masks]).astype(I32)

    def exchange(blocks):
        return [blocks[0]] + [along_expert(blocks[i], partner(i, experts)) for i in range(1, experts)]

    expert_bits = [1 << i for i in range(experts.bit_length() - 1)]

    def spread(x):
        held = [x]
        for bit in bits[1:]:
            held = held + [swap(h, bit) for h in held]
        return held

    def both_parts(x):
        far = swap(x, bits[0])
        return spread(x), spread(far)

    code, first = first_batch(place, picks, tokens, depth)
    own_picks = lax.dynamic_slice_in_dim(picks, me, 1, axis=0)
    sources = jnp.bitwise_xor(me, jnp.array([partner(i, experts) for i in range(experts)], I32))
    start = jnp.sum((own_picks < (sources * rows)[:, None]).astype(I32), axis=1)
    stop = jnp.sum((own_picks < ((sources + 1) * rows)[:, None]).astype(I32), axis=1)
    ids = jnp.arange(BATCHES, dtype=I32)[:, None]
    offsets = (start[None, :] + (BATCHES - 1) - ids) // BATCHES
    counts = (stop[None, :] + (BATCHES - 1) - ids) // BATCHES - offsets

    present = [jnp.sum(counts[k]) > 0 for k in range(BATCHES)]

    def beside_first(router):
        logits = partial_logits(router, tokens)
        later = [tuple(later_batch(code, tokens, k, depth)) for k in range(1, BATCHES)]
        for bit in bits:
            logits = logits + swap(logits, bit)
        gathered = logits[None]
        for bit in expert_bits[:-1]:
            gathered = jnp.concatenate([gathered, along_expert(gathered, bit)])
        return later, logits, gathered

    def nothing_first(router):
        return jax.tree.map(lambda x: jnp.zeros(x.shape, x.dtype), jax.eval_shape(beside_first, router))

    arrived = [exchange(first)]
    later, logits, gathered = lax.cond(present[0], beside_first, nothing_first, router_weight.T)

    def far_half(far, sums):
        far = spread(far)
        gate, up, *weights = sums
        sums = gate_up_far(far[:1], (gate, up, *weights), 0, False)
        far, sums = lax.optimization_barrier((far[1:], sums))
        hidden = gate_up_far(far, (*sums, *weights), 1, True)[0]
        far = swap(hidden, bits[0])
        partial = down_first(order, near_places, far_places, down_weight, spread(hidden))
        far, partial = lax.optimization_barrier((far, partial))
        return spread(far), partial

    def settle(k, far, partial):
        return tuple(
            down_last(offsets, counts, k, far, partial, experts, depth, k == BATCHES - 1)
        )

    def fenced(k, run, *operands):
        def skip(*operands):
            return jax.tree.map(lambda x: jnp.zeros(x.shape, x.dtype), jax.eval_shape(run, *operands))

        return lax.cond(present[k], run, skip, *operands)

    waiting = []
    far = partial = None
    moved = gathered
    for k in range(BATCHES):
        blocks = after(arrived[k], moved)
        if k < BATCHES - 1:
            moving = after(later[k], blocks)
            arrived.append(exchange(moving))
        if k == 0:
            block = fenced(k, lambda *blocks: compact(offsets, counts, 0, blocks, size), *blocks)
        else:
            block = compact(offsets, counts, k, blocks, size)
        across = swap(block, bits[0])
        near = spread(block)
        if k > 0:
            far, partial = after((far, partial), block)
            results = settle(k - 1, far, partial)
            if k > 1:
                results, waiting[k - 2] = lax.optimization_barrier((results, waiting[k - 2]))
            waiting.append(exchange(results))
            near = after(near, results)
        sums = gate_up_near(order, near_places, far_places, gate_weight, up_weight, near)
        across, sums = lax.optimization_barrier((across, sums))
        if k == BATCHES - 1:
            gathered = after(gathered, sums)
            gathered = jnp.concatenate([gathered, along_expert(gathered, expert_bits[-1])])
        far, partial = fenced(k, far_half, across, sums)
        moved = partial
    results = settle(BATCHES - 1, far, partial)
    results, waiting[-1] = lax.optimization_barrier((list(results), waiting[-1]))
    results[-1], gathered = lax.optimization_barrier((results[-1], gathered))
    waiting.append(exchange(results))
    weights = slot_weights(place, logits, gathered, code)
    total = None
    for k in range(BATCHES):
        total = combine(code, weights, k, waiting[k], total)
    return total


def solution(mesh):
    return jax.shard_map(
        shards,
        mesh=mesh,
        in_specs=(
            P(("groups", "expert"), "dp"),
            P("dp", None),
            P("expert", None, "dp"),
            P("expert", None, "dp"),
            P("expert", None, "dp"),
            P("groups", None),
        ),
        out_specs=P(("groups", "expert"), "dp"),
        check_vma=False,
    )
```

```python
import functools

import jax
import jax.numpy as jnp
from jax import lax
from jax.experimental import pallas as pl
from jax.experimental.pallas import tpu as pltpu
from jax.sharding import PartitionSpec as P

BATCHES = 2
F32 = jnp.float32
BF16 = jnp.bfloat16
I32 = jnp.int32
VMEM_LIMIT = 16 * 1024 * 1024
COST = pl.CostEstimate(flops=1024, bytes_accessed=1024, transcendentals=0)


def whole(count):
    return [pl.BlockSpec(memory_space=pltpu.VMEM)] * count


def apart(count):
    return [pl.BlockSpec(memory_space=pl.ANY)] * count


def smem():
    return pl.BlockSpec(memory_space=pltpu.SMEM)


def params(limit=VMEM_LIMIT):
    return pltpu.CompilerParams(vmem_limit_bytes=limit)


def partner(place, experts):
    return -place % experts


def dot(a, b):
    return jnp.dot(a, b, preferred_element_type=F32)


def start_all(sources, targets, sems):
    copies = [pltpu.make_async_copy(a, b, sems.at[i]) for i, (a, b) in enumerate(zip(sources, targets))]
    for copy in copies:
        copy.start()
    return copies


def code_kernel(experts, depth, place_ref, picks_in, tokens_ref, code_ref, *refs):
    sends = refs[:experts]
    picks_ref, held, staged, in_sems, out_sems = refs[experts:]
    picks_load, load = start_all([picks_in, tokens_ref], [picks_ref, held], in_sems)
    me = place_ref[0]
    rows, width = held.shape
    capacity = picks_ref.shape[1]
    strips = rows // 128
    lanes = lax.broadcasted_iota(I32, (128, capacity), 0)
    strip_ids = lax.broadcasted_iota(I32, (8, capacity), 0)
    total = 8 * experts
    row_ids = lax.broadcasted_iota(I32, (total, total), 0)
    lane_ids = lax.broadcasted_iota(I32, (total, total), 1)
    same = lax.shift_right_logical(row_ids, 3) == lax.shift_right_logical(lane_ids, 3)
    before = (same & (lane_ids < row_ids)).astype(F32).astype(BF16)
    upper = (lax.broadcasted_iota(I32, (128, 128), 0) < lax.broadcasted_iota(I32, (128, 128), 1)).astype(BF16)
    ones = jnp.ones((128, 128), BF16)
    picks_load.wait()
    masks, starts = [], []
    for shift in range(experts):
        local = picks_ref[pl.ds(jnp.bitwise_xor(me, partner(shift, experts)), 1), :] - me * rows
        starts.append(jnp.broadcast_to(jnp.sum((local < 0).astype(F32), axis=1, keepdims=True), (8, 128)))
        strip = lax.shift_right_arithmetic(local, 7)
        place = jnp.bitwise_and(local, 127)
        high = ((strip == strip_ids) & (strip_ids < strips)).astype(F32).astype(BF16)
        low = (place == lanes).astype(F32).astype(BF16)
        masks.append(lax.dot_general(high, low, (((1,), (1,)), ((), ())), preferred_element_type=F32))
    mask = jnp.concatenate(masks, axis=0)
    start = jnp.concatenate(starts, axis=0).astype(I32)
    mask16 = mask.astype(BF16)
    totals = dot(mask16, ones)
    rank = (dot(mask16, upper) + dot(before, totals.astype(BF16))).astype(I32)
    slot = lax.rem(rank + start, BATCHES) * depth + lax.div(rank, BATCHES)
    code = jnp.where(mask > 0.5, slot, -1)
    code_rows = []
    for shift in range(experts):
        row = jnp.concatenate([code[8 * shift + i : 8 * shift + i + 1] for i in range(strips)], axis=1)
        code_ref[pl.ds(shift, 1), :] = row
        code_rows.append(row)
    load.wait()
    pack(0, depth, code_rows, held, staged, sends, out_sems)


def pack(k, depth, code_rows, held, staged, sends, sems):
    slot_ids = lax.broadcasted_iota(I32, (depth, held.shape[0]), 0) + k * depth
    copies = []
    for shift in list(range(1, len(sends))) + [0]:
        selector = (slot_ids == code_rows[shift]).astype(F32).astype(BF16)
        staged[shift] = dot(selector, held[...]).astype(BF16)
        copy = pltpu.make_async_copy(staged.at[shift], sends[shift], sems.at[shift])
        copy.start()
        copies.append(copy)
    for copy in copies:
        copy.wait()


def first_batch(place, picks, tokens, depth):
    rows, width = tokens.shape
    experts = picks.shape[0]
    out = pl.pallas_call(
        functools.partial(code_kernel, experts, depth),
        out_shape=[jax.ShapeDtypeStruct((experts, rows), I32)]
        + [jax.ShapeDtypeStruct((depth, width), BF16)] * experts,
        in_specs=[smem()] + apart(2),
        out_specs=whole(1) + apart(experts),
        scratch_shapes=[
            pltpu.VMEM(picks.shape, I32),
            pltpu.VMEM((rows, width), BF16),
            pltpu.VMEM((experts, depth, width), BF16),
            pltpu.SemaphoreType.DMA((2,)),
            pltpu.SemaphoreType.DMA((experts,)),
        ],
        compiler_params=params(60 * 1024 * 1024),
        cost_estimate=COST,
    )(place, picks, tokens)
    return out[0], out[1:]


def logits_kernel(router_ref, tokens_ref, out_ref):
    out_ref[...] = lax.dot_general(
        router_ref[...], tokens_ref[...], (((1,), (1,)), ((), ())), preferred_element_type=F32
    )


def partial_logits(router, tokens):
    return pl.pallas_call(
        logits_kernel,
        out_shape=jax.ShapeDtypeStruct((router.shape[0], tokens.shape[0]), F32),
        in_specs=whole(2),
        out_specs=whole(1)[0],
        compiler_params=params(),
        cost_estimate=COST,
    )(router, tokens)


def pack_kernel(experts, depth, k, code_ref, tokens_ref, *refs):
    sends = refs[:experts]
    held, staged, in_sems, out_sems = refs[experts:]
    start_all([tokens_ref], [held], in_sems)[0].wait()
    code_rows = [code_ref[pl.ds(shift, 1), :] for shift in range(experts)]
    pack(k, depth, code_rows, held, staged, sends, out_sems)


def later_batch(code, tokens, k, depth):
    rows, width = tokens.shape
    experts = code.shape[0]
    return pl.pallas_call(
        functools.partial(pack_kernel, experts, depth, k),
        out_shape=[jax.ShapeDtypeStruct((depth, width), BF16)] * experts,
        in_specs=whole(1) + apart(1),
        out_specs=apart(experts),
        scratch_shapes=[
            pltpu.VMEM((rows, width), BF16),
            pltpu.VMEM((experts, depth, width), BF16),
            pltpu.SemaphoreType.DMA((1,)),
            pltpu.SemaphoreType.DMA((experts,)),
        ],
        compiler_params=params(),
        cost_estimate=COST,
    )(code, tokens)


def compact_kernel(experts, k, offset_ref, count_ref, *refs):
    blocks, out_ref = refs[:experts], refs[experts]
    held, sems = refs[experts + 1 :]
    depth = blocks[0].shape[0]
    size = out_ref.shape[0]
    loads = start_all(blocks, [held.at[pl.ds(i * depth, depth)] for i in range(experts)], sems)
    row = lax.broadcasted_iota(I32, (size, depth), 0)
    lane = lax.broadcasted_iota(I32, (size, depth), 1)
    parts = [
        ((row - offset_ref[k, i] == lane) & (lane < count_ref[k, i])).astype(F32).astype(BF16)
        for i in range(experts)
    ]
    selector = jnp.concatenate(parts, axis=1)
    for load in loads:
        load.wait()
    out_ref[...] = dot(selector, held[...]).astype(BF16)


def compact(offsets, counts, k, blocks, size):
    experts = len(blocks)
    depth, width = blocks[0].shape
    return pl.pallas_call(
        functools.partial(compact_kernel, experts, k),
        out_shape=jax.ShapeDtypeStruct((size, width), BF16),
        in_specs=[smem(), smem()] + apart(experts),
        out_specs=whole(1)[0],
        scratch_shapes=[pltpu.VMEM((experts * depth, width), BF16), pltpu.SemaphoreType.DMA((experts,))],
        compiler_params=params(),
        cost_estimate=COST,
    )(offsets, counts, *blocks)


def gate_up_near_kernel(parts, near, far, order_ref, gate_ref, up_ref, *refs):
    xs, refs = refs[:parts], refs[parts:]
    gate_out, up_out, gate_far, up_far, gate_held, up_held, x_held, sems = refs
    width = xs[0].shape[1]

    def fetch(i, place, gate_to, up_to, base):
        first = pl.multiple_of(order_ref[place] * width, width)
        return start_all(
            [gate_ref.at[0, pl.ds(first, width), :], up_ref.at[0, pl.ds(first, width), :]],
            [gate_to.at[i], up_to.at[i]],
            sems.at[pl.ds(base, 2)],
        )

    x_loads = start_all(xs, [x_held.at[i] for i in range(parts)], sems.at[pl.ds(0, parts)])
    loads = [fetch(i, near[i], gate_held, up_held, parts + 2 * i) for i in range(parts)]
    late = [fetch(i, far[i], gate_far, up_far, 3 * parts + 2 * i) for i in range(len(far))]
    gate = up = None
    for i in range(parts):
        for copy in [x_loads[i]] + loads[i]:
            copy.wait()
        x = x_held[i]
        gate_term = dot(x, gate_held[i])
        up_term = dot(x, up_held[i])
        gate = gate_term if gate is None else gate + gate_term
        up = up_term if up is None else up + up_term
    gate_out[...] = gate
    up_out[...] = up
    for copies in late:
        for copy in copies:
            copy.wait()


def gate_up_near(order, near, far, gate_weight, up_weight, xs):
    parts = len(xs)
    size, width = xs[0].shape
    units = gate_weight.shape[2]
    held = jax.ShapeDtypeStruct((len(far), width, units), BF16)
    return pl.pallas_call(
        functools.partial(gate_up_near_kernel, parts, near, far),
        out_shape=[jax.ShapeDtypeStruct((size, units), F32)] * 2 + [held] * 2,
        in_specs=[smem()] + apart(2 + parts),
        out_specs=whole(4),
        scratch_shapes=[
            pltpu.VMEM((parts, width, units), BF16),
            pltpu.VMEM((parts, width, units), BF16),
            pltpu.VMEM((parts, size, width), BF16),
            pltpu.SemaphoreType.DMA((3 * parts + 2 * len(far),)),
        ],
        compiler_params=params(),
        cost_estimate=COST,
    )(order, gate_weight, up_weight, *xs)


def gate_up_far_kernel(parts, first, last, gate_before, up_before, gate_ref, up_ref, *refs):
    xs, outs = refs[:parts], refs[parts:]
    gate, up = gate_before[...], up_before[...]
    for i in range(parts):
        x = xs[i][...]
        gate = gate + dot(x, gate_ref[first + i])
        up = up + dot(x, up_ref[first + i])
    if last:
        outs[0][...] = (gate * jax.nn.sigmoid(gate) * up).astype(BF16)
    else:
        outs[0][...] = gate
        outs[1][...] = up


def gate_up_far(xs, before, first, last):
    shape = before[0].shape
    sums = [jax.ShapeDtypeStruct(shape, F32)] * 2
    return pl.pallas_call(
        functools.partial(gate_up_far_kernel, len(xs), first, last),
        out_shape=[jax.ShapeDtypeStruct(shape, BF16)] if last else sums,
        in_specs=whole(4 + len(xs)),
        out_specs=whole(1 if last else 2),
        compiler_params=params(),
        cost_estimate=COST,
    )(*before, *xs)


def down_first_kernel(parts, near, far, order_ref, down_ref, *refs):
    hs, (out_ref, far_ref, down_held, h_held, sems) = refs[:parts], refs[parts:]
    units = hs[0].shape[1]

    def fetch(i, place, target, sem):
        first = pl.multiple_of(order_ref[place] * units, units)
        copy = pltpu.make_async_copy(down_ref.at[0, pl.ds(first, units), :], target.at[i], sems.at[sem])
        copy.start()
        return copy

    h_loads = start_all(hs, [h_held.at[i] for i in range(parts)], sems.at[pl.ds(0, parts)])
    loads = [fetch(i, near[i], down_held, parts + i) for i in range(parts)]
    late = [fetch(i, far[i], far_ref, 2 * parts + i) for i in range(len(far))]
    total = None
    for i in range(parts):
        h_loads[i].wait()
        loads[i].wait()
        term = dot(h_held[i], down_held[i])
        total = term if total is None else total + term
    out_ref[...] = total
    for copy in late:
        copy.wait()


def down_first(order, near, far, down_weight, hs):
    parts = len(hs)
    size, units = hs[0].shape
    width = down_weight.shape[2]
    return pl.pallas_call(
        functools.partial(down_first_kernel, parts, near, far),
        out_shape=[
            jax.ShapeDtypeStruct((size, width), F32),
            jax.ShapeDtypeStruct((len(far), units, width), BF16),
        ],
        in_specs=[smem()] + apart(1 + parts),
        out_specs=whole(2),
        scratch_shapes=[
            pltpu.VMEM((parts, units, width), BF16),
            pltpu.VMEM((parts, size, units), BF16),
            pltpu.SemaphoreType.DMA((2 * parts + len(far),)),
        ],
        compiler_params=params(),
        cost_estimate=COST,
    )(order, down_weight, *hs)


def down_step_kernel(h_ref, before_ref, down_ref, out_ref):
    out_ref[...] = before_ref[...] + dot(h_ref[...], down_ref[0])


def down_step(h, before, down):
    return pl.pallas_call(
        down_step_kernel,
        out_shape=jax.ShapeDtypeStruct(before.shape, F32),
        in_specs=whole(3),
        out_specs=whole(1)[0],
        compiler_params=params(),
        cost_estimate=COST,
    )(h, before, down)


def down_last_kernel(parts, experts, k, direct, offset_ref, count_ref, before_ref, down_ref, *refs):
    hs, outs = refs[:parts], refs[parts : parts + experts]
    h_held, sems, *staged = refs[parts + experts :]
    loads = start_all(hs, [h_held.at[i] for i in range(parts)], sems)
    size = hs[0].shape[0]
    depth = outs[0].shape[0]
    row = lax.broadcasted_iota(I32, (depth, size), 0)
    lane = lax.broadcasted_iota(I32, (depth, size), 1)
    picks = [
        ((lane - offset_ref[k, i] == row) & (row < count_ref[k, i])).astype(F32).astype(BF16)
        for i in range(experts)
    ]
    total = before_ref[...]
    for i in range(parts):
        loads[i].wait()
        total = total + dot(h_held[i], down_ref[i + 1])
    result = total.astype(BF16)
    if direct:
        for i in range(experts):
            outs[i][...] = dot(picks[i], result).astype(BF16)
        return
    staged_ref, out_sems = staged
    copies = []
    for i in list(range(1, experts)) + [0]:
        staged_ref[i] = dot(picks[i], result).astype(BF16)
        copy = pltpu.make_async_copy(staged_ref.at[i], outs[i], out_sems.at[i])
        copy.start()
        copies.append(copy)
    for copy in copies:
        copy.wait()


def down_last(offsets, counts, k, hs, before, experts, depth, direct):
    parts = len(hs)
    size, units = hs[0].shape
    width = before[0].shape[1]
    return pl.pallas_call(
        functools.partial(down_last_kernel, parts, experts, k, direct),
        out_shape=[jax.ShapeDtypeStruct((depth, width), BF16)] * experts,
        in_specs=[smem()] * 2 + whole(2) + apart(parts),
        out_specs=whole(experts) if direct else apart(experts),
        scratch_shapes=[pltpu.VMEM((parts, size, units), BF16), pltpu.SemaphoreType.DMA((parts,))]
        + ([] if direct else [pltpu.VMEM((experts, depth, width), BF16), pltpu.SemaphoreType.DMA((experts,))]),
        compiler_params=params(),
        cost_estimate=COST,
    )(offsets, counts, *before, *hs)


def weight_kernel(experts, place_ref, own_ref, logits_ref, code_ref, out_ref, score_ref):
    me = place_ref[0]
    kernel = jnp.exp(logits_ref[...])
    row_scale = jnp.ones((kernel.shape[0], 1, kernel.shape[2]), F32)
    for sweep in range(3):
        column = jnp.sum(jnp.sum(kernel * row_scale, axis=0, keepdims=True), axis=2, keepdims=True)
        column_scale = 1.0 / column
        row_scale = 1.0 / jnp.sum(kernel * column_scale, axis=1, keepdims=True)
    own = jnp.exp(own_ref[...])
    column_scale = column_scale[0]
    own_scale = 1.0 / jnp.sum(own * column_scale, axis=0, keepdims=True)
    score_ref[...] = own_scale * own * column_scale
    picked = []
    for shift in range(experts):
        score = score_ref[pl.ds(jnp.bitwise_xor(me, partner(shift, experts)), 1), :]
        picked.append(jnp.where(code_ref[pl.ds(shift, 1), :] >= 0, score, 0.0))
    total = picked[0]
    for one in picked[1:]:
        total = total + one
    total = jnp.maximum(total, 1.0 / experts)
    for shift in range(experts):
        out_ref[pl.ds(shift, 1), :] = picked[shift] / total


def slot_weights(place, own, logits, code):
    experts, rows = own.shape
    return pl.pallas_call(
        functools.partial(weight_kernel, experts),
        out_shape=jax.ShapeDtypeStruct((experts, rows), F32),
        in_specs=[smem()] + whole(3),
        out_specs=whole(1)[0],
        scratch_shapes=[pltpu.VMEM((experts, rows), F32)],
        compiler_params=params(),
        cost_estimate=COST,
    )(place, own, logits, code)


def combine_kernel(places, k, more, code_ref, weight_ref, *refs):
    before, refs = refs[:more], refs[more:]
    count = len(places)
    blocks, (out_ref, held, sems) = refs[:count], refs[count:]
    depth = blocks[0].shape[0]
    rows = code_ref.shape[1]
    loads = start_all(blocks, [held.at[pl.ds(i * depth, depth)] for i in range(count)], sems)
    slot_ids = lax.broadcasted_iota(I32, (depth, rows), 0) + k * depth
    parts = [
        jnp.where(slot_ids == code_ref[pl.ds(i, 1), :], weight_ref[pl.ds(i, 1), :], 0.0).astype(BF16)
        for i in places
    ]
    spread = jnp.concatenate(parts, axis=0)
    for load in loads:
        load.wait()
    total = lax.dot_general(spread, held[...], (((0,), (0,)), ((), ())), preferred_element_type=F32)
    if more:
        total = total + before[0][...]
    out_ref[...] = total.astype(out_ref.dtype)


def combine(code, weights, k, places, blocks, so_far, last):
    count = len(places)
    depth, width = blocks[0].shape
    rows = code.shape[1]
    more = [] if so_far is None else [so_far]
    return pl.pallas_call(
        functools.partial(combine_kernel, places, k, len(more)),
        out_shape=jax.ShapeDtypeStruct((rows, width), BF16 if last else F32),
        in_specs=whole(2 + len(more)) + apart(count),
        out_specs=whole(1)[0],
        scratch_shapes=[pltpu.VMEM((count * depth, width), BF16), pltpu.SemaphoreType.DMA((count,))],
        compiler_params=params(),
        cost_estimate=COST,
    )(code, weights, *more, *[blocks[i] for i in places])


def after(value, *first):
    return lax.optimization_barrier((value, first))[0]


def shards(tokens, router_weight, gate_weight, up_weight, down_weight, picks):
    experts = lax.axis_size("expert")
    width_parts = lax.axis_size("dp")
    me = lax.axis_index("expert")
    part = lax.axis_index("dp")
    rows = tokens.shape[0]
    capacity = picks.shape[1]
    depth = 2 * capacity // experts // BATCHES
    size = capacity // BATCHES
    place = me.astype(I32).reshape(1)

    def along_expert(x, shift):
        return lax.ppermute(x, "expert", [(i, i ^ shift) for i in range(experts)])

    def swap(x, bit):
        return lax.ppermute(x, "dp", [(i, i ^ bit) for i in range(width_parts)])

    bits = []
    bit = width_parts // 2
    while bit:
        bits.append(bit)
        bit //= 2
    near = [0]
    for bit in bits[1:]:
        near = near + [m ^ bit for m in near]
    masks = near + [m ^ bits[0] for m in near]
    places = range(len(masks))
    near_places, far_places = places[: len(near)], places[len(near) :]
    order = jnp.stack([part ^ m for m in masks]).astype(I32)

    def exchange(blocks):
        return [blocks[0]] + [along_expert(blocks[i], partner(i, experts)) for i in range(1, experts)]

    expert_bits = [1 << i for i in range(experts.bit_length() - 1)]

    def spread(x):
        held = [x]
        for bit in bits[1:]:
            held = held + [swap(h, bit) for h in held]
        return held

    def both_parts(x):
        far = swap(x, bits[0])
        return spread(x), spread(far)

    code, first = first_batch(place, picks, tokens, depth)
    own_picks = lax.dynamic_slice_in_dim(picks, me, 1, axis=0)
    sources = jnp.bitwise_xor(me, jnp.array([partner(i, experts) for i in range(experts)], I32))
    start = jnp.sum((own_picks < (sources * rows)[:, None]).astype(I32), axis=1)
    stop = jnp.sum((own_picks < ((sources + 1) * rows)[:, None]).astype(I32), axis=1)
    ids = jnp.arange(BATCHES, dtype=I32)[:, None]
    offsets = (start[None, :] + (BATCHES - 1) - ids) // BATCHES
    counts = (stop[None, :] + (BATCHES - 1) - ids) // BATCHES - offsets

    present = [jnp.sum(counts[k]) > 0 for k in range(BATCHES)]

    def beside_first(router):
        logits = partial_logits(router, tokens)
        later = [tuple(later_batch(code, tokens, k, depth)) for k in range(1, BATCHES)]
        for bit in bits:
            logits = logits + swap(logits, bit)
        gathered = logits[None]
        for bit in expert_bits[:-1]:
            gathered = jnp.concatenate([gathered, along_expert(gathered, bit)])
        return later, logits, gathered

    def nothing_first(router):
        return jax.tree.map(lambda x: jnp.zeros(x.shape, x.dtype), jax.eval_shape(beside_first, router))

    arrived = [exchange(first)]
    later, logits, gathered = lax.cond(present[0], beside_first, nothing_first, router_weight.T)

    def far_half(far, sums):
        far = spread(far)
        gate, up, *weights = sums
        sums = gate_up_far(far[:1], (gate, up, *weights), 0, False)
        far, sums = lax.optimization_barrier((far[1:], sums))
        hidden = gate_up_far(far, (*sums, *weights), 1, True)[0]
        far = swap(hidden, bits[0])
        partial = down_first(order, near_places, far_places, down_weight, spread(hidden))
        far, partial = lax.optimization_barrier((far, partial))
        far = spread(far)
        total = down_step(far[0], *partial)
        far, total = lax.optimization_barrier((far[1:], total))
        return far, (total, partial[1])

    def settle(k, far, partial):
        return tuple(
            down_last(offsets, counts, k, far, partial, experts, depth, k == BATCHES - 1)
        )

    def fenced(k, run, *operands):
        def skip(*operands):
            return jax.tree.map(lambda x: jnp.zeros(x.shape, x.dtype), jax.eval_shape(run, *operands))

        return lax.cond(present[k], run, skip, *operands)

    waiting = []
    far = partial = None
    moved = gathered
    for k in range(BATCHES):
        blocks = after(arrived[k], moved)
        if k < BATCHES - 1:
            moving = after(later[k], blocks)
            arrived.append(exchange(moving))
        if k == 0:
            block = fenced(k, lambda *blocks: compact(offsets, counts, 0, blocks, size), *blocks)
        else:
            block = compact(offsets, counts, k, blocks, size)
        across = swap(block, bits[0])
        near = spread(block)
        if k > 0:
            far, partial = after((far, partial), block)
            results = settle(k - 1, far, partial)
            if k > 1:
                results, waiting[k - 2] = lax.optimization_barrier((results, waiting[k - 2]))
            waiting.append(exchange(results))
            near = after(near, results)
        sums = gate_up_near(order, near_places, far_places, gate_weight, up_weight, near)
        across, sums = lax.optimization_barrier((across, sums))
        if k == BATCHES - 1:
            gathered = after(gathered, sums)
            gathered = jnp.concatenate([gathered, along_expert(gathered, expert_bits[-1])])
        far, partial = fenced(k, far_half, across, sums)
        moved = partial
    results = settle(BATCHES - 1, far, partial)
    results, waiting[-1] = lax.optimization_barrier((list(results), waiting[-1]))
    results[-1], gathered = lax.optimization_barrier((results[-1], gathered))
    waiting.append(exchange(results))
    weights = slot_weights(place, logits, gathered, code)
    total = None
    for k in range(BATCHES - 1):
        total = combine(code, weights, k, range(experts), waiting[k], total, False)
    early = range(experts // 2)
    total = combine(code, weights, BATCHES - 1, early, waiting[-1], total, False)
    return combine(code, weights, BATCHES - 1, range(experts // 2, experts), waiting[-1], total, True)


def solution(mesh):
    return jax.shard_map(
        shards,
        mesh=mesh,
        in_specs=(
            P(("groups", "expert"), "dp"),
            P("dp", None),
            P("expert", None, "dp"),
            P("expert", None, "dp"),
            P("expert", None, "dp"),
            P("groups", None),
        ),
        out_specs=P(("groups", "expert"), "dp"),
        check_vma=False,
    )
```

```python
import functools

import jax
import jax.numpy as jnp
from jax import lax
from jax.experimental import pallas as pl
from jax.experimental.pallas import tpu as pltpu
from jax.sharding import PartitionSpec as P

BATCHES = 2
F32 = jnp.float32
BF16 = jnp.bfloat16
I32 = jnp.int32
VMEM_LIMIT = 16 * 1024 * 1024
COST = pl.CostEstimate(flops=1024, bytes_accessed=1024, transcendentals=0)


def whole(count):
    return [pl.BlockSpec(memory_space=pltpu.VMEM)] * count


def apart(count):
    return [pl.BlockSpec(memory_space=pl.ANY)] * count


def smem():
    return pl.BlockSpec(memory_space=pltpu.SMEM)


def params(limit=VMEM_LIMIT):
    return pltpu.CompilerParams(vmem_limit_bytes=limit)


def partner(place, experts):
    return -place % experts


def dot(a, b):
    return jnp.dot(a, b, preferred_element_type=F32)


def start_all(sources, targets, sems):
    copies = [pltpu.make_async_copy(a, b, sems.at[i]) for i, (a, b) in enumerate(zip(sources, targets))]
    for copy in copies:
        copy.start()
    return copies


def code_kernel(experts, depth, place_ref, picks_in, tokens_ref, code_ref, *refs):
    sends = refs[:experts]
    picks_ref, held, staged, in_sems, out_sems = refs[experts:]
    picks_load, load = start_all([picks_in, tokens_ref], [picks_ref, held], in_sems)
    me = place_ref[0]
    rows, width = held.shape
    capacity = picks_ref.shape[1]
    strips = rows // 128
    lanes = lax.broadcasted_iota(I32, (128, capacity), 0)
    strip_ids = lax.broadcasted_iota(I32, (8, capacity), 0)
    total = 8 * experts
    row_ids = lax.broadcasted_iota(I32, (total, total), 0)
    lane_ids = lax.broadcasted_iota(I32, (total, total), 1)
    same = lax.shift_right_logical(row_ids, 3) == lax.shift_right_logical(lane_ids, 3)
    before = (same & (lane_ids < row_ids)).astype(F32).astype(BF16)
    upper = (lax.broadcasted_iota(I32, (128, 128), 0) < lax.broadcasted_iota(I32, (128, 128), 1)).astype(BF16)
    ones = jnp.ones((128, 128), BF16)
    picks_load.wait()
    masks, starts = [], []
    for shift in range(experts):
        local = picks_ref[pl.ds(jnp.bitwise_xor(me, partner(shift, experts)), 1), :] - me * rows
        starts.append(jnp.broadcast_to(jnp.sum((local < 0).astype(F32), axis=1, keepdims=True), (8, 128)))
        strip = lax.shift_right_arithmetic(local, 7)
        place = jnp.bitwise_and(local, 127)
        high = ((strip == strip_ids) & (strip_ids < strips)).astype(F32).astype(BF16)
        low = (place == lanes).astype(F32).astype(BF16)
        masks.append(lax.dot_general(high, low, (((1,), (1,)), ((), ())), preferred_element_type=F32))
    mask = jnp.concatenate(masks, axis=0)
    start = jnp.concatenate(starts, axis=0).astype(I32)
    mask16 = mask.astype(BF16)
    totals = dot(mask16, ones)
    rank = (dot(mask16, upper) + dot(before, totals.astype(BF16))).astype(I32)
    slot = lax.rem(rank + start, BATCHES) * depth + lax.div(rank, BATCHES)
    code = jnp.where(mask > 0.5, slot, -1)
    code_rows = []
    for shift in range(experts):
        row = jnp.concatenate([code[8 * shift + i : 8 * shift + i + 1] for i in range(strips)], axis=1)
        code_ref[pl.ds(shift, 1), :] = row
        code_rows.append(row)
    load.wait()
    pack(0, depth, code_rows, held, staged, sends, out_sems)


def pack(k, depth, code_rows, held, staged, sends, sems):
    slot_ids = lax.broadcasted_iota(I32, (depth, held.shape[0]), 0) + k * depth
    copies = []
    for shift in list(range(1, len(sends))) + [0]:
        selector = (slot_ids == code_rows[shift]).astype(F32).astype(BF16)
        staged[shift] = dot(selector, held[...]).astype(BF16)
        copy = pltpu.make_async_copy(staged.at[shift], sends[shift], sems.at[shift])
        copy.start()
        copies.append(copy)
    for copy in copies:
        copy.wait()


def first_batch(place, picks, tokens, depth):
    rows, width = tokens.shape
    experts = picks.shape[0]
    out = pl.pallas_call(
        functools.partial(code_kernel, experts, depth),
        out_shape=[jax.ShapeDtypeStruct((experts, rows), I32)]
        + [jax.ShapeDtypeStruct((depth, width), BF16)] * experts,
        in_specs=[smem()] + apart(2),
        out_specs=whole(1) + apart(experts),
        scratch_shapes=[
            pltpu.VMEM(picks.shape, I32),
            pltpu.VMEM((rows, width), BF16),
            pltpu.VMEM((experts, depth, width), BF16),
            pltpu.SemaphoreType.DMA((2,)),
            pltpu.SemaphoreType.DMA((experts,)),
        ],
        compiler_params=params(60 * 1024 * 1024),
        cost_estimate=COST,
    )(place, picks, tokens)
    return out[0], out[1:]


def logits_kernel(router_ref, tokens_ref, out_ref):
    out_ref[...] = lax.dot_general(
        router_ref[...], tokens_ref[...], (((1,), (1,)), ((), ())), preferred_element_type=F32
    )


def partial_logits(router, tokens):
    return pl.pallas_call(
        logits_kernel,
        out_shape=jax.ShapeDtypeStruct((router.shape[0], tokens.shape[0]), F32),
        in_specs=whole(2),
        out_specs=whole(1)[0],
        compiler_params=params(),
        cost_estimate=COST,
    )(router, tokens)


def pack_kernel(experts, depth, k, code_ref, tokens_ref, *refs):
    sends = refs[:experts]
    held, staged, in_sems, out_sems = refs[experts:]
    start_all([tokens_ref], [held], in_sems)[0].wait()
    code_rows = [code_ref[pl.ds(shift, 1), :] for shift in range(experts)]
    pack(k, depth, code_rows, held, staged, sends, out_sems)


def later_batch(code, tokens, k, depth):
    rows, width = tokens.shape
    experts = code.shape[0]
    return pl.pallas_call(
        functools.partial(pack_kernel, experts, depth, k),
        out_shape=[jax.ShapeDtypeStruct((depth, width), BF16)] * experts,
        in_specs=whole(1) + apart(1),
        out_specs=apart(experts),
        scratch_shapes=[
            pltpu.VMEM((rows, width), BF16),
            pltpu.VMEM((experts, depth, width), BF16),
            pltpu.SemaphoreType.DMA((1,)),
            pltpu.SemaphoreType.DMA((experts,)),
        ],
        compiler_params=params(),
        cost_estimate=COST,
    )(code, tokens)


def compact_kernel(experts, k, offset_ref, count_ref, *refs):
    blocks, out_ref = refs[:experts], refs[experts]
    held, sems = refs[experts + 1 :]
    depth = blocks[0].shape[0]
    size = out_ref.shape[0]
    loads = start_all(blocks, [held.at[pl.ds(i * depth, depth)] for i in range(experts)], sems)
    row = lax.broadcasted_iota(I32, (size, depth), 0)
    lane = lax.broadcasted_iota(I32, (size, depth), 1)
    parts = [
        ((row - offset_ref[k, i] == lane) & (lane < count_ref[k, i])).astype(F32).astype(BF16)
        for i in range(experts)
    ]
    selector = jnp.concatenate(parts, axis=1)
    for load in loads:
        load.wait()
    out_ref[...] = dot(selector, held[...]).astype(BF16)


def compact(offsets, counts, k, blocks, size):
    experts = len(blocks)
    depth, width = blocks[0].shape
    return pl.pallas_call(
        functools.partial(compact_kernel, experts, k),
        out_shape=jax.ShapeDtypeStruct((size, width), BF16),
        in_specs=[smem(), smem()] + apart(experts),
        out_specs=whole(1)[0],
        scratch_shapes=[pltpu.VMEM((experts * depth, width), BF16), pltpu.SemaphoreType.DMA((experts,))],
        compiler_params=params(),
        cost_estimate=COST,
    )(offsets, counts, *blocks)


def gate_up_near_kernel(parts, near, far, order_ref, gate_ref, up_ref, *refs):
    xs, refs = refs[:parts], refs[parts:]
    gate_out, up_out, gate_far, up_far, gate_held, up_held, x_held, sems = refs
    width = xs[0].shape[1]

    def fetch(i, place, gate_to, up_to, base):
        first = pl.multiple_of(order_ref[place] * width, width)
        return start_all(
            [gate_ref.at[0, pl.ds(first, width), :], up_ref.at[0, pl.ds(first, width), :]],
            [gate_to.at[i], up_to.at[i]],
            sems.at[pl.ds(base, 2)],
        )

    x_loads = start_all(xs, [x_held.at[i] for i in range(parts)], sems.at[pl.ds(0, parts)])
    loads = [fetch(i, near[i], gate_held, up_held, parts + 2 * i) for i in range(parts)]
    late = [fetch(i, far[i], gate_far, up_far, 3 * parts + 2 * i) for i in range(len(far))]
    gate = up = None
    for i in range(parts):
        for copy in [x_loads[i]] + loads[i]:
            copy.wait()
        x = x_held[i]
        gate_term = dot(x, gate_held[i])
        up_term = dot(x, up_held[i])
        gate = gate_term if gate is None else gate + gate_term
        up = up_term if up is None else up + up_term
    gate_out[...] = gate
    up_out[...] = up
    for copies in late:
        for copy in copies:
            copy.wait()


def gate_up_near(order, near, far, gate_weight, up_weight, xs):
    parts = len(xs)
    size, width = xs[0].shape
    units = gate_weight.shape[2]
    held = jax.ShapeDtypeStruct((len(far), width, units), BF16)
    return pl.pallas_call(
        functools.partial(gate_up_near_kernel, parts, near, far),
        out_shape=[jax.ShapeDtypeStruct((size, units), F32)] * 2 + [held] * 2,
        in_specs=[smem()] + apart(2 + parts),
        out_specs=whole(4),
        scratch_shapes=[
            pltpu.VMEM((parts, width, units), BF16),
            pltpu.VMEM((parts, width, units), BF16),
            pltpu.VMEM((parts, size, width), BF16),
            pltpu.SemaphoreType.DMA((3 * parts + 2 * len(far),)),
        ],
        compiler_params=params(),
        cost_estimate=COST,
    )(order, gate_weight, up_weight, *xs)


def gate_up_far_kernel(parts, first, last, gate_before, up_before, gate_ref, up_ref, *refs):
    xs, outs = refs[:parts], refs[parts:]
    gate, up = gate_before[...], up_before[...]
    for i in range(parts):
        x = xs[i][...]
        gate = gate + dot(x, gate_ref[first + i])
        up = up + dot(x, up_ref[first + i])
    if last:
        outs[0][...] = (gate * jax.nn.sigmoid(gate) * up).astype(BF16)
    else:
        outs[0][...] = gate
        outs[1][...] = up


def gate_up_far(xs, before, first, last):
    shape = before[0].shape
    sums = [jax.ShapeDtypeStruct(shape, F32)] * 2
    return pl.pallas_call(
        functools.partial(gate_up_far_kernel, len(xs), first, last),
        out_shape=[jax.ShapeDtypeStruct(shape, BF16)] if last else sums,
        in_specs=whole(4 + len(xs)),
        out_specs=whole(1 if last else 2),
        compiler_params=params(),
        cost_estimate=COST,
    )(*before, *xs)


def down_first_kernel(parts, near, far, order_ref, down_ref, *refs):
    hs, (out_ref, far_ref, down_held, h_held, sems) = refs[:parts], refs[parts:]
    units = hs[0].shape[1]

    def fetch(i, place, target, sem):
        first = pl.multiple_of(order_ref[place] * units, units)
        copy = pltpu.make_async_copy(down_ref.at[0, pl.ds(first, units), :], target.at[i], sems.at[sem])
        copy.start()
        return copy

    h_loads = start_all(hs, [h_held.at[i] for i in range(parts)], sems.at[pl.ds(0, parts)])
    loads = [fetch(i, near[i], down_held, parts + i) for i in range(parts)]
    late = [fetch(i, far[i], far_ref, 2 * parts + i) for i in range(len(far))]
    total = None
    for i in range(parts):
        h_loads[i].wait()
        loads[i].wait()
        term = dot(h_held[i], down_held[i])
        total = term if total is None else total + term
    out_ref[...] = total
    for copy in late:
        copy.wait()


def down_first(order, near, far, down_weight, hs):
    parts = len(hs)
    size, units = hs[0].shape
    width = down_weight.shape[2]
    return pl.pallas_call(
        functools.partial(down_first_kernel, parts, near, far),
        out_shape=[
            jax.ShapeDtypeStruct((size, width), F32),
            jax.ShapeDtypeStruct((len(far), units, width), BF16),
        ],
        in_specs=[smem()] + apart(1 + parts),
        out_specs=whole(2),
        scratch_shapes=[
            pltpu.VMEM((parts, units, width), BF16),
            pltpu.VMEM((parts, size, units), BF16),
            pltpu.SemaphoreType.DMA((2 * parts + len(far),)),
        ],
        compiler_params=params(),
        cost_estimate=COST,
    )(order, down_weight, *hs)


def down_last_kernel(parts, experts, k, direct, offset_ref, count_ref, before_ref, down_ref, *refs):
    hs, outs = refs[:parts], refs[parts : parts + experts]
    h_held, sems, *staged = refs[parts + experts :]
    loads = start_all(hs, [h_held.at[i] for i in range(parts)], sems)
    size = hs[0].shape[0]
    depth = outs[0].shape[0]
    row = lax.broadcasted_iota(I32, (depth, size), 0)
    lane = lax.broadcasted_iota(I32, (depth, size), 1)
    picks = [
        ((lane - offset_ref[k, i] == row) & (row < count_ref[k, i])).astype(F32).astype(BF16)
        for i in range(experts)
    ]
    total = before_ref[...]
    for i in range(parts):
        loads[i].wait()
        total = total + dot(h_held[i], down_ref[i])
    result = total.astype(BF16)
    if direct:
        for i in range(experts):
            outs[i][...] = dot(picks[i], result).astype(BF16)
        return
    staged_ref, out_sems = staged
    copies = []
    for i in list(range(1, experts)) + [0]:
        staged_ref[i] = dot(picks[i], result).astype(BF16)
        copy = pltpu.make_async_copy(staged_ref.at[i], outs[i], out_sems.at[i])
        copy.start()
        copies.append(copy)
    for copy in copies:
        copy.wait()


def down_last(offsets, counts, k, hs, before, experts, depth, direct):
    parts = len(hs)
    size, units = hs[0].shape
    width = before[0].shape[1]
    return pl.pallas_call(
        functools.partial(down_last_kernel, parts, experts, k, direct),
        out_shape=[jax.ShapeDtypeStruct((depth, width), BF16)] * experts,
        in_specs=[smem()] * 2 + whole(2) + apart(parts),
        out_specs=whole(experts) if direct else apart(experts),
        scratch_shapes=[pltpu.VMEM((parts, size, units), BF16), pltpu.SemaphoreType.DMA((parts,))]
        + ([] if direct else [pltpu.VMEM((experts, depth, width), BF16), pltpu.SemaphoreType.DMA((experts,))]),
        compiler_params=params(),
        cost_estimate=COST,
    )(offsets, counts, *before, *hs)


def weight_kernel(experts, place_ref, own_ref, logits_ref, code_ref, out_ref, score_ref):
    me = place_ref[0]
    kernel = jnp.exp(logits_ref[...])
    row_scale = jnp.ones((kernel.shape[0], 1, kernel.shape[2]), F32)
    for sweep in range(3):
        column = jnp.sum(jnp.sum(kernel * row_scale, axis=0, keepdims=True), axis=2, keepdims=True)
        column_scale = 1.0 / column
        row_scale = 1.0 / jnp.sum(kernel * column_scale, axis=1, keepdims=True)
    own = jnp.exp(own_ref[...])
    column_scale = column_scale[0]
    own_scale = 1.0 / jnp.sum(own * column_scale, axis=0, keepdims=True)
    score_ref[...] = own_scale * own * column_scale
    picked = []
    for shift in range(experts):
        score = score_ref[pl.ds(jnp.bitwise_xor(me, partner(shift, experts)), 1), :]
        picked.append(jnp.where(code_ref[pl.ds(shift, 1), :] >= 0, score, 0.0))
    total = picked[0]
    for one in picked[1:]:
        total = total + one
    total = jnp.maximum(total, 1.0 / experts)
    for shift in range(experts):
        out_ref[pl.ds(shift, 1), :] = picked[shift] / total


def slot_weights(place, own, logits, code):
    experts, rows = own.shape
    return pl.pallas_call(
        functools.partial(weight_kernel, experts),
        out_shape=jax.ShapeDtypeStruct((experts, rows), F32),
        in_specs=[smem()] + whole(3),
        out_specs=whole(1)[0],
        scratch_shapes=[pltpu.VMEM((experts, rows), F32)],
        compiler_params=params(),
        cost_estimate=COST,
    )(place, own, logits, code)


def combine_kernel(places, k, more, code_ref, weight_ref, *refs):
    before, refs = refs[:more], refs[more:]
    count = len(places)
    blocks, (out_ref, held, sems) = refs[:count], refs[count:]
    depth = blocks[0].shape[0]
    rows = code_ref.shape[1]
    loads = start_all(blocks, [held.at[pl.ds(i * depth, depth)] for i in range(count)], sems)
    slot_ids = lax.broadcasted_iota(I32, (depth, rows), 0) + k * depth
    parts = [
        jnp.where(slot_ids == code_ref[pl.ds(i, 1), :], weight_ref[pl.ds(i, 1), :], 0.0).astype(BF16)
        for i in places
    ]
    spread = jnp.concatenate(parts, axis=0)
    for load in loads:
        load.wait()
    total = lax.dot_general(spread, held[...], (((0,), (0,)), ((), ())), preferred_element_type=F32)
    if more:
        total = total + before[0][...]
    out_ref[...] = total.astype(out_ref.dtype)


def combine(code, weights, k, places, blocks, so_far, last):
    count = len(places)
    depth, width = blocks[0].shape
    rows = code.shape[1]
    more = [] if so_far is None else [so_far]
    return pl.pallas_call(
        functools.partial(combine_kernel, places, k, len(more)),
        out_shape=jax.ShapeDtypeStruct((rows, width), BF16 if last else F32),
        in_specs=whole(2 + len(more)) + apart(count),
        out_specs=whole(1)[0],
        scratch_shapes=[pltpu.VMEM((count * depth, width), BF16), pltpu.SemaphoreType.DMA((count,))],
        compiler_params=params(),
        cost_estimate=COST,
    )(code, weights, *more, *[blocks[i] for i in places])


def after(value, *first):
    return lax.optimization_barrier((value, first))[0]


def shards(tokens, router_weight, gate_weight, up_weight, down_weight, picks):
    experts = lax.axis_size("expert")
    width_parts = lax.axis_size("dp")
    me = lax.axis_index("expert")
    part = lax.axis_index("dp")
    rows = tokens.shape[0]
    capacity = picks.shape[1]
    depth = 2 * capacity // experts // BATCHES
    size = capacity // BATCHES
    place = me.astype(I32).reshape(1)

    def along_expert(x, shift):
        return lax.ppermute(x, "expert", [(i, i ^ shift) for i in range(experts)])

    def swap(x, bit):
        return lax.ppermute(x, "dp", [(i, i ^ bit) for i in range(width_parts)])

    bits = []
    bit = width_parts // 2
    while bit:
        bits.append(bit)
        bit //= 2
    near = [0]
    for bit in bits[1:]:
        near = near + [m ^ bit for m in near]
    masks = near + [m ^ bits[0] for m in near]
    places = range(len(masks))
    near_places, far_places = places[: len(near)], places[len(near) :]
    order = jnp.stack([part ^ m for m in masks]).astype(I32)

    def exchange(blocks):
        return [blocks[0]] + [along_expert(blocks[i], partner(i, experts)) for i in range(1, experts)]

    expert_bits = [1 << i for i in range(experts.bit_length() - 1)]

    def spread(x):
        held = [x]
        for bit in bits[1:]:
            held = held + [swap(h, bit) for h in held]
        return held

    def both_parts(x):
        far = swap(x, bits[0])
        return spread(x), spread(far)

    code, first = first_batch(place, picks, tokens, depth)
    own_picks = lax.dynamic_slice_in_dim(picks, me, 1, axis=0)
    sources = jnp.bitwise_xor(me, jnp.array([partner(i, experts) for i in range(experts)], I32))
    start = jnp.sum((own_picks < (sources * rows)[:, None]).astype(I32), axis=1)
    stop = jnp.sum((own_picks < ((sources + 1) * rows)[:, None]).astype(I32), axis=1)
    ids = jnp.arange(BATCHES, dtype=I32)[:, None]
    offsets = (start[None, :] + (BATCHES - 1) - ids) // BATCHES
    counts = (stop[None, :] + (BATCHES - 1) - ids) // BATCHES - offsets

    present = [jnp.sum(counts[k]) > 0 for k in range(BATCHES)]

    def beside_first(router):
        logits = partial_logits(router, tokens)
        later = [tuple(later_batch(code, tokens, k, depth)) for k in range(1, BATCHES)]
        for bit in bits:
            logits = logits + swap(logits, bit)
        gathered = logits[None]
        for bit in expert_bits[:-1]:
            gathered = jnp.concatenate([gathered, along_expert(gathered, bit)])
        return later, logits, gathered

    def nothing_first(router):
        return jax.tree.map(lambda x: jnp.zeros(x.shape, x.dtype), jax.eval_shape(beside_first, router))

    arrived = [exchange(first)]
    later, logits, gathered = lax.cond(present[0], beside_first, nothing_first, router_weight.T)

    def far_half(far, sums):
        far = spread(far)
        gate, up, *weights = sums
        sums = gate_up_far(far[:1], (gate, up, *weights), 0, False)
        far, sums = lax.optimization_barrier((far[1:], sums))
        hidden = gate_up_far(far, (*sums, *weights), 1, True)[0]
        far = swap(hidden, bits[0])
        partial = down_first(order, near_places, far_places, down_weight, spread(hidden))
        far, partial = lax.optimization_barrier((far, partial))
        return spread(far), partial

    def settle(k, far, partial):
        return tuple(
            down_last(offsets, counts, k, far, partial, experts, depth, k == BATCHES - 1)
        )

    def fenced(k, run, *operands):
        def skip(*operands):
            return jax.tree.map(lambda x: jnp.zeros(x.shape, x.dtype), jax.eval_shape(run, *operands))

        return lax.cond(present[k], run, skip, *operands)

    waiting = []
    far = partial = None
    moved = gathered
    for k in range(BATCHES):
        blocks = after(arrived[k], moved)
        if k < BATCHES - 1:
            moving = after(later[k], blocks)
            arrived.append(exchange(moving))
        if k == 0:
            block = fenced(k, lambda *blocks: compact(offsets, counts, 0, blocks, size), *blocks)
        else:
            block = compact(offsets, counts, k, blocks, size)
        across = swap(block, bits[0])
        near = spread(block)
        if k > 0:
            far, partial = after((far, partial), block)
            results = settle(k - 1, far, partial)
            if k > 1:
                results, waiting[k - 2] = lax.optimization_barrier((results, waiting[k - 2]))
            waiting.append(exchange(results))
            near = after(near, results)
        sums = gate_up_near(order, near_places, far_places, gate_weight, up_weight, near)
        across, sums = lax.optimization_barrier((across, sums))
        if k == BATCHES - 1:
            gathered = after(gathered, sums)
            gathered = jnp.concatenate([gathered, along_expert(gathered, expert_bits[-1])])
        far, partial = fenced(k, far_half, across, sums)
        moved = partial
    results = settle(BATCHES - 1, far, partial)
    results, waiting[-1] = lax.optimization_barrier((list(results), waiting[-1]))
    results[-1], gathered = lax.optimization_barrier((results[-1], gathered))
    waiting.append(exchange(results))
    weights = slot_weights(place, logits, gathered, code)
    total = None
    for k in range(BATCHES - 1):
        total = combine(code, weights, k, range(experts), waiting[k], total, False)
    early = range(experts // 2)
    total = combine(code, weights, BATCHES - 1, early, waiting[-1], total, False)
    return combine(code, weights, BATCHES - 1, range(experts // 2, experts), waiting[-1], total, True)


def solution(mesh):
    return jax.shard_map(
        shards,
        mesh=mesh,
        in_specs=(
            P(("groups", "expert"), "dp"),
            P("dp", None),
            P("expert", None, "dp"),
            P("expert", None, "dp"),
            P("expert", None, "dp"),
            P("groups", None),
        ),
        out_specs=P(("groups", "expert"), "dp"),
        check_vma=False,
    )
```

```python
import functools

import jax
import jax.numpy as jnp
from jax import lax
from jax.experimental import pallas as pl
from jax.experimental.pallas import tpu as pltpu
from jax.sharding import PartitionSpec as P

BATCHES = 2
F32 = jnp.float32
BF16 = jnp.bfloat16
I32 = jnp.int32
VMEM_LIMIT = 16 * 1024 * 1024
COST = pl.CostEstimate(flops=1024, bytes_accessed=1024, transcendentals=0)


def whole(count):
    return [pl.BlockSpec(memory_space=pltpu.VMEM)] * count


def apart(count):
    return [pl.BlockSpec(memory_space=pl.ANY)] * count


def smem():
    return pl.BlockSpec(memory_space=pltpu.SMEM)


def params(limit=VMEM_LIMIT):
    return pltpu.CompilerParams(vmem_limit_bytes=limit)


def partner(place, experts):
    return -(3 - place if place in (1, 2) else place) % experts


def dot(a, b):
    return jnp.dot(a, b, preferred_element_type=F32)


def start_all(sources, targets, sems):
    copies = [pltpu.make_async_copy(a, b, sems.at[i]) for i, (a, b) in enumerate(zip(sources, targets))]
    for copy in copies:
        copy.start()
    return copies


def code_kernel(experts, depth, place_ref, picks_in, tokens_ref, code_ref, *refs):
    sends = refs[:experts]
    picks_ref, held, staged, in_sems, out_sems = refs[experts:]
    picks_load, load = start_all([picks_in, tokens_ref], [picks_ref, held], in_sems)
    me = place_ref[0]
    rows, width = held.shape
    capacity = picks_ref.shape[1]
    strips = rows // 128
    lanes = lax.broadcasted_iota(I32, (128, capacity), 0)
    strip_ids = lax.broadcasted_iota(I32, (8, capacity), 0)
    total = 8 * experts
    row_ids = lax.broadcasted_iota(I32, (total, total), 0)
    lane_ids = lax.broadcasted_iota(I32, (total, total), 1)
    same = lax.shift_right_logical(row_ids, 3) == lax.shift_right_logical(lane_ids, 3)
    before = (same & (lane_ids < row_ids)).astype(F32).astype(BF16)
    upper = (lax.broadcasted_iota(I32, (128, 128), 0) < lax.broadcasted_iota(I32, (128, 128), 1)).astype(BF16)
    ones = jnp.ones((128, 128), BF16)
    picks_load.wait()
    masks, starts = [], []
    for shift in range(experts):
        local = picks_ref[pl.ds(jnp.bitwise_xor(me, partner(shift, experts)), 1), :] - me * rows
        starts.append(jnp.broadcast_to(jnp.sum((local < 0).astype(F32), axis=1, keepdims=True), (8, 128)))
        strip = lax.shift_right_arithmetic(local, 7)
        place = jnp.bitwise_and(local, 127)
        high = ((strip == strip_ids) & (strip_ids < strips)).astype(F32).astype(BF16)
        low = (place == lanes).astype(F32).astype(BF16)
        masks.append(lax.dot_general(high, low, (((1,), (1,)), ((), ())), preferred_element_type=F32))
    mask = jnp.concatenate(masks, axis=0)
    start = jnp.concatenate(starts, axis=0).astype(I32)
    mask16 = mask.astype(BF16)
    totals = dot(mask16, ones)
    rank = (dot(mask16, upper) + dot(before, totals.astype(BF16))).astype(I32)
    slot = lax.rem(rank + start, BATCHES) * depth + lax.div(rank, BATCHES)
    code = jnp.where(mask > 0.5, slot, -1)
    code_rows = []
    for shift in range(experts):
        row = jnp.concatenate([code[8 * shift + i : 8 * shift + i + 1] for i in range(strips)], axis=1)
        code_ref[pl.ds(shift, 1), :] = row
        code_rows.append(row)
    load.wait()
    pack(0, depth, code_rows, held, staged, sends, out_sems)


def pack(k, depth, code_rows, held, staged, sends, sems):
    slot_ids = lax.broadcasted_iota(I32, (depth, held.shape[0]), 0) + k * depth
    copies = []
    for shift in list(range(1, len(sends))) + [0]:
        selector = (slot_ids == code_rows[shift]).astype(F32).astype(BF16)
        staged[shift] = dot(selector, held[...]).astype(BF16)
        copy = pltpu.make_async_copy(staged.at[shift], sends[shift], sems.at[shift])
        copy.start()
        copies.append(copy)
    for copy in copies:
        copy.wait()


def first_batch(place, picks, tokens, depth):
    rows, width = tokens.shape
    experts = picks.shape[0]
    out = pl.pallas_call(
        functools.partial(code_kernel, experts, depth),
        out_shape=[jax.ShapeDtypeStruct((experts, rows), I32)]
        + [jax.ShapeDtypeStruct((depth, width), BF16)] * experts,
        in_specs=[smem()] + apart(2),
        out_specs=whole(1) + apart(experts),
        scratch_shapes=[
            pltpu.VMEM(picks.shape, I32),
            pltpu.VMEM((rows, width), BF16),
            pltpu.VMEM((experts, depth, width), BF16),
            pltpu.SemaphoreType.DMA((2,)),
            pltpu.SemaphoreType.DMA((experts,)),
        ],
        compiler_params=params(60 * 1024 * 1024),
        cost_estimate=COST,
    )(place, picks, tokens)
    return out[0], out[1:]


def logits_kernel(router_ref, tokens_ref, out_ref):
    out_ref[...] = lax.dot_general(
        router_ref[...], tokens_ref[...], (((1,), (1,)), ((), ())), preferred_element_type=F32
    )


def partial_logits(router, tokens):
    return pl.pallas_call(
        logits_kernel,
        out_shape=jax.ShapeDtypeStruct((router.shape[0], tokens.shape[0]), F32),
        in_specs=whole(2),
        out_specs=whole(1)[0],
        compiler_params=params(),
        cost_estimate=COST,
    )(router, tokens)


def pack_kernel(experts, depth, k, code_ref, tokens_ref, *refs):
    sends = refs[:experts]
    held, staged, in_sems, out_sems = refs[experts:]
    start_all([tokens_ref], [held], in_sems)[0].wait()
    code_rows = [code_ref[pl.ds(shift, 1), :] for shift in range(experts)]
    pack(k, depth, code_rows, held, staged, sends, out_sems)


def later_batch(code, tokens, k, depth):
    rows, width = tokens.shape
    experts = code.shape[0]
    return pl.pallas_call(
        functools.partial(pack_kernel, experts, depth, k),
        out_shape=[jax.ShapeDtypeStruct((depth, width), BF16)] * experts,
        in_specs=whole(1) + apart(1),
        out_specs=apart(experts),
        scratch_shapes=[
            pltpu.VMEM((rows, width), BF16),
            pltpu.VMEM((experts, depth, width), BF16),
            pltpu.SemaphoreType.DMA((1,)),
            pltpu.SemaphoreType.DMA((experts,)),
        ],
        compiler_params=params(),
        cost_estimate=COST,
    )(code, tokens)


def compact_kernel(experts, k, offset_ref, count_ref, *refs):
    blocks, out_ref = refs[:experts], refs[experts]
    held, sems = refs[experts + 1 :]
    depth = blocks[0].shape[0]
    size = out_ref.shape[0]
    loads = start_all(blocks, [held.at[pl.ds(i * depth, depth)] for i in range(experts)], sems)
    row = lax.broadcasted_iota(I32, (size, depth), 0)
    lane = lax.broadcasted_iota(I32, (size, depth), 1)
    parts = [
        ((row - offset_ref[k, i] == lane) & (lane < count_ref[k, i])).astype(F32).astype(BF16)
        for i in range(experts)
    ]
    selector = jnp.concatenate(parts, axis=1)
    for load in loads:
        load.wait()
    out_ref[...] = dot(selector, held[...]).astype(BF16)


def compact(offsets, counts, k, blocks, size):
    experts = len(blocks)
    depth, width = blocks[0].shape
    return pl.pallas_call(
        functools.partial(compact_kernel, experts, k),
        out_shape=jax.ShapeDtypeStruct((size, width), BF16),
        in_specs=[smem(), smem()] + apart(experts),
        out_specs=whole(1)[0],
        scratch_shapes=[pltpu.VMEM((experts * depth, width), BF16), pltpu.SemaphoreType.DMA((experts,))],
        compiler_params=params(),
        cost_estimate=COST,
    )(offsets, counts, *blocks)


def gate_up_near_kernel(parts, near, far, order_ref, gate_ref, up_ref, *refs):
    xs, refs = refs[:parts], refs[parts:]
    gate_out, up_out, gate_far, up_far, gate_held, up_held, x_held, sems = refs
    width = xs[0].shape[1]

    def fetch(i, place, gate_to, up_to, base):
        first = pl.multiple_of(order_ref[place] * width, width)
        return start_all(
            [gate_ref.at[0, pl.ds(first, width), :], up_ref.at[0, pl.ds(first, width), :]],
            [gate_to.at[i], up_to.at[i]],
            sems.at[pl.ds(base, 2)],
        )

    x_loads = start_all(xs, [x_held.at[i] for i in range(parts)], sems.at[pl.ds(0, parts)])
    loads = [fetch(i, near[i], gate_held, up_held, parts + 2 * i) for i in range(parts)]
    late = [fetch(i, far[i], gate_far, up_far, 3 * parts + 2 * i) for i in range(len(far))]
    gate = up = None
    for i in range(parts):
        for copy in [x_loads[i]] + loads[i]:
            copy.wait()
        x = x_held[i]
        gate_term = dot(x, gate_held[i])
        up_term = dot(x, up_held[i])
        gate = gate_term if gate is None else gate + gate_term
        up = up_term if up is None else up + up_term
    gate_out[...] = gate
    up_out[...] = up
    for copies in late:
        for copy in copies:
            copy.wait()


def gate_up_near(order, near, far, gate_weight, up_weight, xs):
    parts = len(xs)
    size, width = xs[0].shape
    units = gate_weight.shape[2]
    held = jax.ShapeDtypeStruct((len(far), width, units), BF16)
    return pl.pallas_call(
        functools.partial(gate_up_near_kernel, parts, near, far),
        out_shape=[jax.ShapeDtypeStruct((size, units), F32)] * 2 + [held] * 2,
        in_specs=[smem()] + apart(2 + parts),
        out_specs=whole(4),
        scratch_shapes=[
            pltpu.VMEM((parts, width, units), BF16),
            pltpu.VMEM((parts, width, units), BF16),
            pltpu.VMEM((parts, size, width), BF16),
            pltpu.SemaphoreType.DMA((3 * parts + 2 * len(far),)),
        ],
        compiler_params=params(),
        cost_estimate=COST,
    )(order, gate_weight, up_weight, *xs)


def gate_up_far_kernel(parts, first, last, gate_before, up_before, gate_ref, up_ref, *refs):
    xs, outs = refs[:parts], refs[parts:]
    gate, up = gate_before[...], up_before[...]
    for i in range(parts):
        x = xs[i][...]
        gate = gate + dot(x, gate_ref[first + i])
        up = up + dot(x, up_ref[first + i])
    if last:
        outs[0][...] = (gate * jax.nn.sigmoid(gate) * up).astype(BF16)
    else:
        outs[0][...] = gate
        outs[1][...] = up


def gate_up_far(xs, before, first, last):
    shape = before[0].shape
    sums = [jax.ShapeDtypeStruct(shape, F32)] * 2
    return pl.pallas_call(
        functools.partial(gate_up_far_kernel, len(xs), first, last),
        out_shape=[jax.ShapeDtypeStruct(shape, BF16)] if last else sums,
        in_specs=whole(4 + len(xs)),
        out_specs=whole(1 if last else 2),
        compiler_params=params(),
        cost_estimate=COST,
    )(*before, *xs)


def down_first_kernel(parts, near, far, order_ref, down_ref, *refs):
    hs, (out_ref, far_ref, down_held, h_held, sems) = refs[:parts], refs[parts:]
    units = hs[0].shape[1]

    def fetch(i, place, target, sem):
        first = pl.multiple_of(order_ref[place] * units, units)
        copy = pltpu.make_async_copy(down_ref.at[0, pl.ds(first, units), :], target.at[i], sems.at[sem])
        copy.start()
        return copy

    h_loads = start_all(hs, [h_held.at[i] for i in range(parts)], sems.at[pl.ds(0, parts)])
    loads = [fetch(i, near[i], down_held, parts + i) for i in range(parts)]
    late = [fetch(i, far[i], far_ref, 2 * parts + i) for i in range(len(far))]
    total = None
    for i in range(parts):
        h_loads[i].wait()
        loads[i].wait()
        term = dot(h_held[i], down_held[i])
        total = term if total is None else total + term
    out_ref[...] = total
    for copy in late:
        copy.wait()


def down_first(order, near, far, down_weight, hs):
    parts = len(hs)
    size, units = hs[0].shape
    width = down_weight.shape[2]
    return pl.pallas_call(
        functools.partial(down_first_kernel, parts, near, far),
        out_shape=[
            jax.ShapeDtypeStruct((size, width), F32),
            jax.ShapeDtypeStruct((len(far), units, width), BF16),
        ],
        in_specs=[smem()] + apart(1 + parts),
        out_specs=whole(2),
        scratch_shapes=[
            pltpu.VMEM((parts, units, width), BF16),
            pltpu.VMEM((parts, size, units), BF16),
            pltpu.SemaphoreType.DMA((2 * parts + len(far),)),
        ],
        compiler_params=params(),
        cost_estimate=COST,
    )(order, down_weight, *hs)


def down_last_kernel(parts, experts, k, direct, offset_ref, count_ref, before_ref, down_ref, *refs):
    hs, outs = refs[:parts], refs[parts : parts + experts]
    h_held, sems, *staged = refs[parts + experts :]
    loads = start_all(hs, [h_held.at[i] for i in range(parts)], sems)
    size = hs[0].shape[0]
    depth = outs[0].shape[0]
    row = lax.broadcasted_iota(I32, (depth, size), 0)
    lane = lax.broadcasted_iota(I32, (depth, size), 1)
    picks = [
        ((lane - offset_ref[k, i] == row) & (row < count_ref[k, i])).astype(F32).astype(BF16)
        for i in range(experts)
    ]
    total = before_ref[...]
    for i in range(parts):
        loads[i].wait()
        total = total + dot(h_held[i], down_ref[i])
    result = total.astype(BF16)
    if direct:
        for i in range(experts):
            outs[i][...] = dot(picks[i], result).astype(BF16)
        return
    staged_ref, out_sems = staged
    copies = []
    for i in list(range(1, experts)) + [0]:
        staged_ref[i] = dot(picks[i], result).astype(BF16)
        copy = pltpu.make_async_copy(staged_ref.at[i], outs[i], out_sems.at[i])
        copy.start()
        copies.append(copy)
    for copy in copies:
        copy.wait()


def down_last(offsets, counts, k, hs, before, experts, depth, direct):
    parts = len(hs)
    size, units = hs[0].shape
    width = before[0].shape[1]
    return pl.pallas_call(
        functools.partial(down_last_kernel, parts, experts, k, direct),
        out_shape=[jax.ShapeDtypeStruct((depth, width), BF16)] * experts,
        in_specs=[smem()] * 2 + whole(2) + apart(parts),
        out_specs=whole(experts) if direct else apart(experts),
        scratch_shapes=[pltpu.VMEM((parts, size, units), BF16), pltpu.SemaphoreType.DMA((parts,))]
        + ([] if direct else [pltpu.VMEM((experts, depth, width), BF16), pltpu.SemaphoreType.DMA((experts,))]),
        compiler_params=params(),
        cost_estimate=COST,
    )(offsets, counts, *before, *hs)


def weight_kernel(experts, place_ref, own_ref, logits_ref, code_ref, out_ref, score_ref):
    me = place_ref[0]
    kernel = jnp.exp(logits_ref[...])
    row_scale = jnp.ones((kernel.shape[0], 1, kernel.shape[2]), F32)
    for sweep in range(3):
        column = jnp.sum(jnp.sum(kernel * row_scale, axis=0, keepdims=True), axis=2, keepdims=True)
        column_scale = 1.0 / column
        row_scale = 1.0 / jnp.sum(kernel * column_scale, axis=1, keepdims=True)
    own = jnp.exp(own_ref[...])
    column_scale = column_scale[0]
    own_scale = 1.0 / jnp.sum(own * column_scale, axis=0, keepdims=True)
    score_ref[...] = own_scale * own * column_scale
    picked = []
    for shift in range(experts):
        score = score_ref[pl.ds(jnp.bitwise_xor(me, partner(shift, experts)), 1), :]
        picked.append(jnp.where(code_ref[pl.ds(shift, 1), :] >= 0, score, 0.0))
    total = picked[0]
    for one in picked[1:]:
        total = total + one
    total = jnp.maximum(total, 1.0 / experts)
    for shift in range(experts):
        out_ref[pl.ds(shift, 1), :] = picked[shift] / total


def slot_weights(place, own, logits, code):
    experts, rows = own.shape
    return pl.pallas_call(
        functools.partial(weight_kernel, experts),
        out_shape=jax.ShapeDtypeStruct((experts, rows), F32),
        in_specs=[smem()] + whole(3),
        out_specs=whole(1)[0],
        scratch_shapes=[pltpu.VMEM((experts, rows), F32)],
        compiler_params=params(),
        cost_estimate=COST,
    )(place, own, logits, code)


def combine_kernel(places, k, more, code_ref, weight_ref, *refs):
    before, refs = refs[:more], refs[more:]
    count = len(places)
    blocks, (out_ref, held, sems) = refs[:count], refs[count:]
    depth = blocks[0].shape[0]
    rows = code_ref.shape[1]
    loads = start_all(blocks, [held.at[pl.ds(i * depth, depth)] for i in range(count)], sems)
    slot_ids = lax.broadcasted_iota(I32, (depth, rows), 0) + k * depth
    parts = [
        jnp.where(slot_ids == code_ref[pl.ds(i, 1), :], weight_ref[pl.ds(i, 1), :], 0.0).astype(BF16)
        for i in places
    ]
    spread = jnp.concatenate(parts, axis=0)
    for load in loads:
        load.wait()
    total = lax.dot_general(spread, held[...], (((0,), (0,)), ((), ())), preferred_element_type=F32)
    if more:
        total = total + before[0][...]
    out_ref[...] = total.astype(out_ref.dtype)


def combine(code, weights, k, places, blocks, so_far, last):
    count = len(places)
    depth, width = blocks[0].shape
    rows = code.shape[1]
    more = [] if so_far is None else [so_far]
    return pl.pallas_call(
        functools.partial(combine_kernel, places, k, len(more)),
        out_shape=jax.ShapeDtypeStruct((rows, width), BF16 if last else F32),
        in_specs=whole(2 + len(more)) + apart(count),
        out_specs=whole(1)[0],
        scratch_shapes=[pltpu.VMEM((count * depth, width), BF16), pltpu.SemaphoreType.DMA((count,))],
        compiler_params=params(),
        cost_estimate=COST,
    )(code, weights, *more, *[blocks[i] for i in places])


def after(value, *first):
    return lax.optimization_barrier((value, first))[0]


def shards(tokens, router_weight, gate_weight, up_weight, down_weight, picks):
    experts = lax.axis_size("expert")
    width_parts = lax.axis_size("dp")
    me = lax.axis_index("expert")
    part = lax.axis_index("dp")
    rows = tokens.shape[0]
    capacity = picks.shape[1]
    depth = 2 * capacity // experts // BATCHES
    size = capacity // BATCHES
    place = me.astype(I32).reshape(1)

    def along_expert(x, shift):
        return lax.ppermute(x, "expert", [(i, i ^ shift) for i in range(experts)])

    def swap(x, bit):
        return lax.ppermute(x, "dp", [(i, i ^ bit) for i in range(width_parts)])

    bits = []
    bit = width_parts // 2
    while bit:
        bits.append(bit)
        bit //= 2
    near = [0]
    for bit in bits[1:]:
        near = near + [m ^ bit for m in near]
    masks = near + [m ^ bits[0] for m in near]
    places = range(len(masks))
    near_places, far_places = places[: len(near)], places[len(near) :]
    order = jnp.stack([part ^ m for m in masks]).astype(I32)

    def exchange(blocks):
        return [blocks[0]] + [along_expert(blocks[i], partner(i, experts)) for i in range(1, experts)]

    expert_bits = [1 << i for i in range(experts.bit_length() - 1)]

    def spread(x):
        held = [x]
        for bit in bits[1:]:
            held = held + [swap(h, bit) for h in held]
        return held

    def both_parts(x):
        far = swap(x, bits[0])
        return spread(x), spread(far)

    code, first = first_batch(place, picks, tokens, depth)
    own_picks = lax.dynamic_slice_in_dim(picks, me, 1, axis=0)
    sources = jnp.bitwise_xor(me, jnp.array([partner(i, experts) for i in range(experts)], I32))
    start = jnp.sum((own_picks < (sources * rows)[:, None]).astype(I32), axis=1)
    stop = jnp.sum((own_picks < ((sources + 1) * rows)[:, None]).astype(I32), axis=1)
    ids = jnp.arange(BATCHES, dtype=I32)[:, None]
    offsets = (start[None, :] + (BATCHES - 1) - ids) // BATCHES
    counts = (stop[None, :] + (BATCHES - 1) - ids) // BATCHES - offsets

    present = [jnp.sum(counts[k]) > 0 for k in range(BATCHES)]

    def beside_first(router):
        logits = partial_logits(router, tokens)
        later = [tuple(later_batch(code, tokens, k, depth)) for k in range(1, BATCHES)]
        for bit in bits:
            logits = logits + swap(logits, bit)
        gathered = logits[None]
        for bit in expert_bits[:-1]:
            gathered = jnp.concatenate([gathered, along_expert(gathered, bit)])
        return later, logits, gathered

    def nothing_first(router):
        return jax.tree.map(lambda x: jnp.zeros(x.shape, x.dtype), jax.eval_shape(beside_first, router))

    arrived = [exchange(first)]
    later, logits, gathered = lax.cond(present[0], beside_first, nothing_first, router_weight.T)

    def far_half(far, sums):
        far = spread(far)
        gate, up, *weights = sums
        sums = gate_up_far(far[:1], (gate, up, *weights), 0, False)
        far, sums = lax.optimization_barrier((far[1:], sums))
        hidden = gate_up_far(far, (*sums, *weights), 1, True)[0]
        far = swap(hidden, bits[0])
        partial = down_first(order, near_places, far_places, down_weight, spread(hidden))
        far, partial = lax.optimization_barrier((far, partial))
        return spread(far), partial

    def settle(k, far, partial):
        return tuple(
            down_last(offsets, counts, k, far, partial, experts, depth, k == BATCHES - 1)
        )

    def fenced(k, run, *operands):
        def skip(*operands):
            return jax.tree.map(lambda x: jnp.zeros(x.shape, x.dtype), jax.eval_shape(run, *operands))

        return lax.cond(present[k], run, skip, *operands)

    waiting = []
    far = partial = None
    moved = gathered
    for k in range(BATCHES):
        blocks = after(arrived[k], moved)
        if k < BATCHES - 1:
            moving = after(later[k], blocks)
            arrived.append(exchange(moving))
        if k == 0:
            block = fenced(k, lambda *blocks: compact(offsets, counts, 0, blocks, size), *blocks)
        else:
            block = compact(offsets, counts, k, blocks, size)
        across = swap(block, bits[0])
        near = spread(block)
        if k > 0:
            far, partial = after((far, partial), block)
            results = settle(k - 1, far, partial)
            if k > 1:
                results, waiting[k - 2] = lax.optimization_barrier((results, waiting[k - 2]))
            waiting.append(exchange(results))
            near = after(near, results)
        sums = gate_up_near(order, near_places, far_places, gate_weight, up_weight, near)
        across, sums = lax.optimization_barrier((across, sums))
        if k == BATCHES - 1:
            gathered = after(gathered, sums)
            gathered = jnp.concatenate([gathered, along_expert(gathered, expert_bits[-1])])
        far, partial = fenced(k, far_half, across, sums)
        moved = partial
    results = settle(BATCHES - 1, far, partial)
    results, waiting[-1] = lax.optimization_barrier((list(results), waiting[-1]))
    results[-1], gathered = lax.optimization_barrier((results[-1], gathered))
    waiting.append(exchange(results))
    weights = slot_weights(place, logits, gathered, code)
    total = None
    for k in range(BATCHES - 1):
        total = combine(code, weights, k, range(experts), waiting[k], total, False)
    early = range(experts // 2)
    total = combine(code, weights, BATCHES - 1, early, waiting[-1], total, False)
    return combine(code, weights, BATCHES - 1, range(experts // 2, experts), waiting[-1], total, True)


def solution(mesh):
    return jax.shard_map(
        shards,
        mesh=mesh,
        in_specs=(
            P(("groups", "expert"), "dp"),
            P("dp", None),
            P("expert", None, "dp"),
            P("expert", None, "dp"),
            P("expert", None, "dp"),
            P("groups", None),
        ),
        out_specs=P(("groups", "expert"), "dp"),
        check_vma=False,
    )
```

```python
import functools

import jax
import jax.numpy as jnp
from jax import lax
from jax.experimental import pallas as pl
from jax.experimental.pallas import tpu as pltpu
from jax.sharding import PartitionSpec as P

BATCHES = 2
F32 = jnp.float32
BF16 = jnp.bfloat16
I32 = jnp.int32
VMEM_LIMIT = 16 * 1024 * 1024
COST = pl.CostEstimate(flops=1024, bytes_accessed=1024, transcendentals=0)


def whole(count):
    return [pl.BlockSpec(memory_space=pltpu.VMEM)] * count


def apart(count):
    return [pl.BlockSpec(memory_space=pl.ANY)] * count


def smem():
    return pl.BlockSpec(memory_space=pltpu.SMEM)


def params(limit=VMEM_LIMIT):
    return pltpu.CompilerParams(vmem_limit_bytes=limit)


def partner(place, experts):
    return -(3 - place if place in (1, 2) else place) % experts


def dot(a, b):
    return jnp.dot(a, b, preferred_element_type=F32)


def start_all(sources, targets, sems):
    copies = [pltpu.make_async_copy(a, b, sems.at[i]) for i, (a, b) in enumerate(zip(sources, targets))]
    for copy in copies:
        copy.start()
    return copies


def code_kernel(experts, depth, place_ref, picks_in, tokens_ref, code_ref, *refs):
    sends = refs[:experts]
    picks_ref, held, staged, in_sems, out_sems = refs[experts:]
    picks_load, load = start_all([picks_in, tokens_ref], [picks_ref, held], in_sems)
    me = place_ref[0]
    rows, width = held.shape
    capacity = picks_ref.shape[1]
    strips = rows // 128
    lanes = lax.broadcasted_iota(I32, (128, capacity), 0)
    strip_ids = lax.broadcasted_iota(I32, (8, capacity), 0)
    total = 8 * experts
    row_ids = lax.broadcasted_iota(I32, (total, total), 0)
    lane_ids = lax.broadcasted_iota(I32, (total, total), 1)
    same = lax.shift_right_logical(row_ids, 3) == lax.shift_right_logical(lane_ids, 3)
    before = (same & (lane_ids < row_ids)).astype(F32).astype(BF16)
    upper = (lax.broadcasted_iota(I32, (128, 128), 0) < lax.broadcasted_iota(I32, (128, 128), 1)).astype(BF16)
    ones = jnp.ones((128, 128), BF16)
    picks_load.wait()
    masks, starts = [], []
    for shift in range(experts):
        local = picks_ref[pl.ds(jnp.bitwise_xor(me, partner(shift, experts)), 1), :] - me * rows
        starts.append(jnp.broadcast_to(jnp.sum((local < 0).astype(F32), axis=1, keepdims=True), (8, 128)))
        strip = lax.shift_right_arithmetic(local, 7)
        place = jnp.bitwise_and(local, 127)
        high = ((strip == strip_ids) & (strip_ids < strips)).astype(F32).astype(BF16)
        low = (place == lanes).astype(F32).astype(BF16)
        masks.append(lax.dot_general(high, low, (((1,), (1,)), ((), ())), preferred_element_type=F32))
    mask = jnp.concatenate(masks, axis=0)
    start = jnp.concatenate(starts, axis=0).astype(I32)
    mask16 = mask.astype(BF16)
    totals = dot(mask16, ones)
    rank = (dot(mask16, upper) + dot(before, totals.astype(BF16))).astype(I32)
    slot = lax.rem(rank + start, BATCHES) * depth + lax.div(rank, BATCHES)
    code = jnp.where(mask > 0.5, slot, -1)
    code_rows = []
    for shift in range(experts):
        row = jnp.concatenate([code[8 * shift + i : 8 * shift + i + 1] for i in range(strips)], axis=1)
        code_ref[pl.ds(shift, 1), :] = row
        code_rows.append(row)
    load.wait()
    pack(0, depth, code_rows, held, staged, sends, out_sems)


def pack(k, depth, code_rows, held, staged, sends, sems):
    slot_ids = lax.broadcasted_iota(I32, (depth, held.shape[0]), 0) + k * depth
    copies = []
    for shift in list(range(1, len(sends))) + [0]:
        selector = (slot_ids == code_rows[shift]).astype(F32).astype(BF16)
        staged[shift] = dot(selector, held[...]).astype(BF16)
        copy = pltpu.make_async_copy(staged.at[shift], sends[shift], sems.at[shift])
        copy.start()
        copies.append(copy)
    for copy in copies:
        copy.wait()


def first_batch(place, picks, tokens, depth):
    rows, width = tokens.shape
    experts = picks.shape[0]
    out = pl.pallas_call(
        functools.partial(code_kernel, experts, depth),
        out_shape=[jax.ShapeDtypeStruct((experts, rows), I32)]
        + [jax.ShapeDtypeStruct((depth, width), BF16)] * experts,
        in_specs=[smem()] + apart(2),
        out_specs=whole(1) + apart(experts),
        scratch_shapes=[
            pltpu.VMEM(picks.shape, I32),
            pltpu.VMEM((rows, width), BF16),
            pltpu.VMEM((experts, depth, width), BF16),
            pltpu.SemaphoreType.DMA((2,)),
            pltpu.SemaphoreType.DMA((experts,)),
        ],
        compiler_params=params(60 * 1024 * 1024),
        cost_estimate=COST,
    )(place, picks, tokens)
    return out[0], out[1:]


def logits_kernel(router_ref, tokens_ref, out_ref):
    out_ref[...] = lax.dot_general(
        router_ref[...], tokens_ref[...], (((1,), (1,)), ((), ())), preferred_element_type=F32
    )


def partial_logits(router, tokens):
    return pl.pallas_call(
        logits_kernel,
        out_shape=jax.ShapeDtypeStruct((router.shape[0], tokens.shape[0]), F32),
        in_specs=whole(2),
        out_specs=whole(1)[0],
        compiler_params=params(),
        cost_estimate=COST,
    )(router, tokens)


def pack_kernel(experts, depth, k, code_ref, tokens_ref, *refs):
    sends = refs[:experts]
    held, staged, in_sems, out_sems = refs[experts:]
    start_all([tokens_ref], [held], in_sems)[0].wait()
    code_rows = [code_ref[pl.ds(shift, 1), :] for shift in range(experts)]
    pack(k, depth, code_rows, held, staged, sends, out_sems)


def later_batch(code, tokens, k, depth):
    rows, width = tokens.shape
    experts = code.shape[0]
    return pl.pallas_call(
        functools.partial(pack_kernel, experts, depth, k),
        out_shape=[jax.ShapeDtypeStruct((depth, width), BF16)] * experts,
        in_specs=whole(1) + apart(1),
        out_specs=apart(experts),
        scratch_shapes=[
            pltpu.VMEM((rows, width), BF16),
            pltpu.VMEM((experts, depth, width), BF16),
            pltpu.SemaphoreType.DMA((1,)),
            pltpu.SemaphoreType.DMA((experts,)),
        ],
        compiler_params=params(),
        cost_estimate=COST,
    )(code, tokens)


def compact_kernel(experts, k, offset_ref, count_ref, *refs):
    blocks, out_ref = refs[:experts], refs[experts]
    held, sems = refs[experts + 1 :]
    depth = blocks[0].shape[0]
    size = out_ref.shape[0]
    loads = start_all(blocks, [held.at[pl.ds(i * depth, depth)] for i in range(experts)], sems)
    row = lax.broadcasted_iota(I32, (size, depth), 0)
    lane = lax.broadcasted_iota(I32, (size, depth), 1)
    parts = [
        ((row - offset_ref[k, i] == lane) & (lane < count_ref[k, i])).astype(F32).astype(BF16)
        for i in range(experts)
    ]
    selector = jnp.concatenate(parts, axis=1)
    for load in loads:
        load.wait()
    out_ref[...] = dot(selector, held[...]).astype(BF16)


def compact(offsets, counts, k, blocks, size):
    experts = len(blocks)
    depth, width = blocks[0].shape
    return pl.pallas_call(
        functools.partial(compact_kernel, experts, k),
        out_shape=jax.ShapeDtypeStruct((size, width), BF16),
        in_specs=[smem(), smem()] + apart(experts),
        out_specs=whole(1)[0],
        scratch_shapes=[pltpu.VMEM((experts * depth, width), BF16), pltpu.SemaphoreType.DMA((experts,))],
        compiler_params=params(),
        cost_estimate=COST,
    )(offsets, counts, *blocks)


def gate_up_near_kernel(parts, near, far, order_ref, gate_ref, up_ref, *refs):
    xs, refs = refs[:parts], refs[parts:]
    gate_out, up_out, gate_far, up_far, gate_held, up_held, x_held, sems = refs
    width = xs[0].shape[1]

    def fetch(i, place, gate_to, up_to, base):
        first = pl.multiple_of(order_ref[place] * width, width)
        return start_all(
            [gate_ref.at[0, pl.ds(first, width), :], up_ref.at[0, pl.ds(first, width), :]],
            [gate_to.at[i], up_to.at[i]],
            sems.at[pl.ds(base, 2)],
        )

    x_loads = start_all(xs, [x_held.at[i] for i in range(parts)], sems.at[pl.ds(0, parts)])
    loads = [fetch(i, near[i], gate_held, up_held, parts + 2 * i) for i in range(parts)]
    late = [fetch(i, far[i], gate_far, up_far, 3 * parts + 2 * i) for i in range(len(far))]
    gate = up = None
    for i in range(parts):
        for copy in [x_loads[i]] + loads[i]:
            copy.wait()
        x = x_held[i]
        gate_term = dot(x, gate_held[i])
        up_term = dot(x, up_held[i])
        gate = gate_term if gate is None else gate + gate_term
        up = up_term if up is None else up + up_term
    gate_out[...] = gate
    up_out[...] = up
    for copies in late:
        for copy in copies:
            copy.wait()


def gate_up_near(order, near, far, gate_weight, up_weight, xs):
    parts = len(xs)
    size, width = xs[0].shape
    units = gate_weight.shape[2]
    held = jax.ShapeDtypeStruct((len(far), width, units), BF16)
    return pl.pallas_call(
        functools.partial(gate_up_near_kernel, parts, near, far),
        out_shape=[jax.ShapeDtypeStruct((size, units), F32)] * 2 + [held] * 2,
        in_specs=[smem()] + apart(2 + parts),
        out_specs=whole(4),
        scratch_shapes=[
            pltpu.VMEM((parts, width, units), BF16),
            pltpu.VMEM((parts, width, units), BF16),
            pltpu.VMEM((parts, size, width), BF16),
            pltpu.SemaphoreType.DMA((3 * parts + 2 * len(far),)),
        ],
        compiler_params=params(),
        cost_estimate=COST,
    )(order, gate_weight, up_weight, *xs)


def gate_up_far_kernel(parts, first, last, gate_before, up_before, gate_ref, up_ref, *refs):
    xs, outs = refs[:parts], refs[parts:]
    gate, up = gate_before[...], up_before[...]
    for i in range(parts):
        x = xs[i][...]
        gate = gate + dot(x, gate_ref[first + i])
        up = up + dot(x, up_ref[first + i])
    if last:
        outs[0][...] = (gate * jax.nn.sigmoid(gate) * up).astype(BF16)
    else:
        outs[0][...] = gate
        outs[1][...] = up


def gate_up_far(xs, before, first, last):
    shape = before[0].shape
    sums = [jax.ShapeDtypeStruct(shape, F32)] * 2
    return pl.pallas_call(
        functools.partial(gate_up_far_kernel, len(xs), first, last),
        out_shape=[jax.ShapeDtypeStruct(shape, BF16)] if last else sums,
        in_specs=whole(4 + len(xs)),
        out_specs=whole(1 if last else 2),
        compiler_params=params(),
        cost_estimate=COST,
    )(*before, *xs)


def down_first_kernel(parts, near, far, order_ref, down_ref, *refs):
    hs, (out_ref, far_ref, down_held, h_held, sems) = refs[:parts], refs[parts:]
    units = hs[0].shape[1]

    def fetch(i, place, target, sem):
        first = pl.multiple_of(order_ref[place] * units, units)
        copy = pltpu.make_async_copy(down_ref.at[0, pl.ds(first, units), :], target.at[i], sems.at[sem])
        copy.start()
        return copy

    h_loads = start_all(hs, [h_held.at[i] for i in range(parts)], sems.at[pl.ds(0, parts)])
    loads = [fetch(i, near[i], down_held, parts + i) for i in range(parts)]
    late = [fetch(i, far[i], far_ref, 2 * parts + i) for i in range(len(far))]
    total = None
    for i in range(parts):
        h_loads[i].wait()
        loads[i].wait()
        term = dot(h_held[i], down_held[i])
        total = term if total is None else total + term
    out_ref[...] = total
    for copy in late:
        copy.wait()


def down_first(order, near, far, down_weight, hs):
    parts = len(hs)
    size, units = hs[0].shape
    width = down_weight.shape[2]
    return pl.pallas_call(
        functools.partial(down_first_kernel, parts, near, far),
        out_shape=[
            jax.ShapeDtypeStruct((size, width), F32),
            jax.ShapeDtypeStruct((len(far), units, width), BF16),
        ],
        in_specs=[smem()] + apart(1 + parts),
        out_specs=whole(2),
        scratch_shapes=[
            pltpu.VMEM((parts, units, width), BF16),
            pltpu.VMEM((parts, size, units), BF16),
            pltpu.SemaphoreType.DMA((2 * parts + len(far),)),
        ],
        compiler_params=params(),
        cost_estimate=COST,
    )(order, down_weight, *hs)


def down_last_kernel(parts, experts, k, direct, offset_ref, count_ref, before_ref, down_ref, *refs):
    hs, outs = refs[:parts], refs[parts : parts + experts]
    h_held, sems, *staged = refs[parts + experts :]
    loads = start_all(hs, [h_held.at[i] for i in range(parts)], sems)
    size = hs[0].shape[0]
    depth = outs[0].shape[0]
    row = lax.broadcasted_iota(I32, (depth, size), 0)
    lane = lax.broadcasted_iota(I32, (depth, size), 1)
    picks = [
        ((lane - offset_ref[k, i] == row) & (row < count_ref[k, i])).astype(F32).astype(BF16)
        for i in range(experts)
    ]
    total = before_ref[...]
    for i in range(parts):
        loads[i].wait()
        total = total + dot(h_held[i], down_ref[i])
    result = total.astype(BF16)
    if direct:
        for i in range(experts):
            outs[i][...] = dot(picks[i], result).astype(BF16)
        return
    staged_ref, out_sems = staged
    copies = []
    for i in list(range(1, experts)) + [0]:
        staged_ref[i] = dot(picks[i], result).astype(BF16)
        copy = pltpu.make_async_copy(staged_ref.at[i], outs[i], out_sems.at[i])
        copy.start()
        copies.append(copy)
    for copy in copies:
        copy.wait()


def down_last(offsets, counts, k, hs, before, experts, depth, direct):
    parts = len(hs)
    size, units = hs[0].shape
    width = before[0].shape[1]
    return pl.pallas_call(
        functools.partial(down_last_kernel, parts, experts, k, direct),
        out_shape=[jax.ShapeDtypeStruct((depth, width), BF16)] * experts,
        in_specs=[smem()] * 2 + whole(2) + apart(parts),
        out_specs=whole(experts) if direct else apart(experts),
        scratch_shapes=[pltpu.VMEM((parts, size, units), BF16), pltpu.SemaphoreType.DMA((parts,))]
        + ([] if direct else [pltpu.VMEM((experts, depth, width), BF16), pltpu.SemaphoreType.DMA((experts,))]),
        compiler_params=params(),
        cost_estimate=COST,
    )(offsets, counts, *before, *hs)


def weight_kernel(experts, place_ref, own_ref, logits_ref, code_ref, out_ref, score_ref):
    me = place_ref[0]
    kernel = jnp.exp(logits_ref[...])
    row_scale = jnp.ones((kernel.shape[0], 1, kernel.shape[2]), F32)
    for sweep in range(3):
        column = jnp.sum(jnp.sum(kernel * row_scale, axis=0, keepdims=True), axis=2, keepdims=True)
        column_scale = 1.0 / column
        row_scale = 1.0 / jnp.sum(kernel * column_scale, axis=1, keepdims=True)
    own = jnp.exp(own_ref[...])
    column_scale = column_scale[0]
    own_scale = 1.0 / jnp.sum(own * column_scale, axis=0, keepdims=True)
    score_ref[...] = own_scale * own * column_scale
    picked = []
    for shift in range(experts):
        score = score_ref[pl.ds(jnp.bitwise_xor(me, partner(shift, experts)), 1), :]
        picked.append(jnp.where(code_ref[pl.ds(shift, 1), :] >= 0, score, 0.0))
    total = picked[0]
    for one in picked[1:]:
        total = total + one
    total = jnp.maximum(total, 1.0 / experts)
    for shift in range(experts):
        out_ref[pl.ds(shift, 1), :] = picked[shift] / total


def slot_weights(place, own, logits, code):
    experts, rows = own.shape
    return pl.pallas_call(
        functools.partial(weight_kernel, experts),
        out_shape=jax.ShapeDtypeStruct((experts, rows), F32),
        in_specs=[smem()] + whole(3),
        out_specs=whole(1)[0],
        scratch_shapes=[pltpu.VMEM((experts, rows), F32)],
        compiler_params=params(),
        cost_estimate=COST,
    )(place, own, logits, code)


def combine_kernel(places, k, more, code_ref, weight_ref, *refs):
    before, refs = refs[:more], refs[more:]
    count = len(places)
    blocks, (out_ref, held, sems) = refs[:count], refs[count:]
    depth = blocks[0].shape[0]
    rows = code_ref.shape[1]
    loads = start_all(blocks, [held.at[pl.ds(i * depth, depth)] for i in range(count)], sems)
    slot_ids = lax.broadcasted_iota(I32, (depth, rows), 0) + k * depth
    parts = [
        jnp.where(slot_ids == code_ref[pl.ds(i, 1), :], weight_ref[pl.ds(i, 1), :], 0.0).astype(BF16)
        for i in places
    ]
    spread = jnp.concatenate(parts, axis=0)
    for load in loads:
        load.wait()
    total = lax.dot_general(spread, held[...], (((0,), (0,)), ((), ())), preferred_element_type=F32)
    if more:
        total = total + before[0][...]
    out_ref[...] = total.astype(out_ref.dtype)


def combine(code, weights, k, places, blocks, so_far, last):
    count = len(places)
    depth, width = blocks[0].shape
    rows = code.shape[1]
    more = [] if so_far is None else [so_far]
    return pl.pallas_call(
        functools.partial(combine_kernel, places, k, len(more)),
        out_shape=jax.ShapeDtypeStruct((rows, width), BF16 if last else F32),
        in_specs=whole(2 + len(more)) + apart(count),
        out_specs=whole(1)[0],
        scratch_shapes=[pltpu.VMEM((count * depth, width), BF16), pltpu.SemaphoreType.DMA((count,))],
        compiler_params=params(),
        cost_estimate=COST,
    )(code, weights, *more, *[blocks[i] for i in places])


def after(value, *first):
    return lax.optimization_barrier((value, first))[0]


def shards(tokens, router_weight, gate_weight, up_weight, down_weight, picks):
    experts = lax.axis_size("expert")
    width_parts = lax.axis_size("dp")
    me = lax.axis_index("expert")
    part = lax.axis_index("dp")
    rows = tokens.shape[0]
    capacity = picks.shape[1]
    depth = 2 * capacity // experts // BATCHES
    size = capacity // BATCHES
    place = me.astype(I32).reshape(1)

    def along_expert(x, shift):
        return lax.ppermute(x, "expert", [(i, i ^ shift) for i in range(experts)])

    def swap(x, bit):
        return lax.ppermute(x, "dp", [(i, i ^ bit) for i in range(width_parts)])

    bits = []
    bit = width_parts // 2
    while bit:
        bits.append(bit)
        bit //= 2
    near = [0]
    for bit in bits[1:]:
        near = near + [m ^ bit for m in near]
    masks = near + [m ^ bits[0] for m in near]
    places = range(len(masks))
    near_places, far_places = places[: len(near)], places[len(near) :]
    order = jnp.stack([part ^ m for m in masks]).astype(I32)

    def exchange(blocks):
        return [blocks[0]] + [along_expert(blocks[i], partner(i, experts)) for i in range(1, experts)]

    expert_bits = [1 << i for i in range(experts.bit_length() - 1)]

    def spread(x):
        held = [x]
        for bit in bits[1:]:
            held = held + [swap(h, bit) for h in held]
        return held

    def both_parts(x):
        far = swap(x, bits[0])
        return spread(x), spread(far)

    code, first = first_batch(place, picks, tokens, depth)
    own_picks = lax.dynamic_slice_in_dim(picks, me, 1, axis=0)
    sources = jnp.bitwise_xor(me, jnp.array([partner(i, experts) for i in range(experts)], I32))
    start = jnp.sum((own_picks < (sources * rows)[:, None]).astype(I32), axis=1)
    stop = jnp.sum((own_picks < ((sources + 1) * rows)[:, None]).astype(I32), axis=1)
    ids = jnp.arange(BATCHES, dtype=I32)[:, None]
    offsets = (start[None, :] + (BATCHES - 1) - ids) // BATCHES
    counts = (stop[None, :] + (BATCHES - 1) - ids) // BATCHES - offsets

    present = [jnp.sum(counts[k]) > 0 for k in range(BATCHES)]

    def beside_first(router):
        logits = partial_logits(router, tokens)
        later = [tuple(later_batch(code, tokens, k, depth)) for k in range(1, BATCHES)]
        for bit in bits:
            logits = logits + swap(logits, bit)
        gathered = logits[None]
        for bit in expert_bits[:-1]:
            gathered = jnp.concatenate([gathered, along_expert(gathered, bit)])
        return later, logits, gathered

    def nothing_first(router):
        return jax.tree.map(lambda x: jnp.zeros(x.shape, x.dtype), jax.eval_shape(beside_first, router))

    arrived = [exchange(first)]
    later, logits, gathered = lax.cond(present[0], beside_first, nothing_first, router_weight.T)

    def far_half(far, sums):
        far = spread(far)
        gate, up, *weights = sums
        sums = gate_up_far(far[:1], (gate, up, *weights), 0, False)
        far, sums = lax.optimization_barrier((far[1:], sums))
        hidden = gate_up_far(far, (*sums, *weights), 1, True)[0]
        far = swap(hidden, bits[0])
        partial = down_first(order, near_places, far_places, down_weight, spread(hidden))
        far, partial = lax.optimization_barrier((far, partial))
        return spread(far), partial

    def settle(k, far, partial):
        return tuple(
            down_last(offsets, counts, k, far, partial, experts, depth, k == BATCHES - 1)
        )

    def fenced(k, run, *operands):
        def skip(*operands):
            return jax.tree.map(lambda x: jnp.zeros(x.shape, x.dtype), jax.eval_shape(run, *operands))

        return lax.cond(present[k], run, skip, *operands)

    waiting = []
    far = partial = None
    moved = gathered
    for k in range(BATCHES):
        blocks = after(arrived[k], moved)
        if k < BATCHES - 1:
            moving = after(later[k], blocks)
            arrived.append(exchange(moving))
        if k == 0:
            block = fenced(k, lambda *blocks: compact(offsets, counts, 0, blocks, size), *blocks)
        else:
            block = compact(offsets, counts, k, blocks, size)
        across = swap(block, bits[0])
        near = spread(block)
        if k > 0:
            far, partial = after((far, partial), block)
            results = settle(k - 1, far, partial)
            if k > 1:
                results, waiting[k - 2] = lax.optimization_barrier((results, waiting[k - 2]))
            waiting.append(exchange(results))
            near = after(near, results)
        sums = gate_up_near(order, near_places, far_places, gate_weight, up_weight, near)
        across, sums = lax.optimization_barrier((across, sums))
        if k == BATCHES - 1:
            gathered = after(gathered, sums)
            gathered = jnp.concatenate([gathered, along_expert(gathered, expert_bits[-1])])
        far, partial = fenced(k, far_half, across, sums)
        moved = partial
    results = settle(BATCHES - 1, far, partial)
    results, waiting[-1] = lax.optimization_barrier((list(results), waiting[-1]))
    results[-1], gathered = lax.optimization_barrier((results[-1], gathered))
    waiting.append(exchange(results))
    weights = slot_weights(place, logits, gathered, code)
    total = None
    for k in range(BATCHES - 1):
        total = combine(code, weights, k, range(experts), waiting[k], total, False)
    late = (min(2, experts - 1),)
    early = [i for i in range(experts) if i not in late]
    total = combine(code, weights, BATCHES - 1, early, waiting[-1], total, False)
    return combine(code, weights, BATCHES - 1, late, waiting[-1], total, True)


def solution(mesh):
    return jax.shard_map(
        shards,
        mesh=mesh,
        in_specs=(
            P(("groups", "expert"), "dp"),
            P("dp", None),
            P("expert", None, "dp"),
            P("expert", None, "dp"),
            P("expert", None, "dp"),
            P("groups", None),
        ),
        out_specs=P(("groups", "expert"), "dp"),
        check_vma=False,
    )
```

```python
import functools

import jax
import jax.numpy as jnp
from jax import lax
from jax.experimental import pallas as pl
from jax.experimental.pallas import tpu as pltpu
from jax.sharding import PartitionSpec as P

BATCHES = 2
F32 = jnp.float32
BF16 = jnp.bfloat16
I32 = jnp.int32
VMEM_LIMIT = 16 * 1024 * 1024
COST = pl.CostEstimate(flops=1024, bytes_accessed=1024, transcendentals=0)


def whole(count):
    return [pl.BlockSpec(memory_space=pltpu.VMEM)] * count


def apart(count):
    return [pl.BlockSpec(memory_space=pl.ANY)] * count


def smem():
    return pl.BlockSpec(memory_space=pltpu.SMEM)


def params(limit=VMEM_LIMIT):
    return pltpu.CompilerParams(vmem_limit_bytes=limit)


def partner(place, experts):
    return -(3 - place if place in (1, 2) else place) % experts


def dot(a, b):
    return jnp.dot(a, b, preferred_element_type=F32)


def start_all(sources, targets, sems):
    copies = [pltpu.make_async_copy(a, b, sems.at[i]) for i, (a, b) in enumerate(zip(sources, targets))]
    for copy in copies:
        copy.start()
    return copies


def code_kernel(experts, depth, place_ref, picks_in, tokens_ref, code_ref, *refs):
    sends = refs[:experts]
    picks_ref, held, staged, in_sems, out_sems = refs[experts:]
    picks_load, load = start_all([picks_in, tokens_ref], [picks_ref, held], in_sems)
    me = place_ref[0]
    rows, width = held.shape
    capacity = picks_ref.shape[1]
    strips = rows // 128
    lanes = lax.broadcasted_iota(I32, (128, capacity), 0)
    strip_ids = lax.broadcasted_iota(I32, (8, capacity), 0)
    total = 8 * experts
    row_ids = lax.broadcasted_iota(I32, (total, total), 0)
    lane_ids = lax.broadcasted_iota(I32, (total, total), 1)
    same = lax.shift_right_logical(row_ids, 3) == lax.shift_right_logical(lane_ids, 3)
    before = (same & (lane_ids < row_ids)).astype(F32).astype(BF16)
    upper = (lax.broadcasted_iota(I32, (128, 128), 0) < lax.broadcasted_iota(I32, (128, 128), 1)).astype(BF16)
    ones = jnp.ones((128, 128), BF16)
    picks_load.wait()
    masks, starts = [], []
    for shift in range(experts):
        local = picks_ref[pl.ds(jnp.bitwise_xor(me, partner(shift, experts)), 1), :] - me * rows
        starts.append(jnp.broadcast_to(jnp.sum((local < 0).astype(F32), axis=1, keepdims=True), (8, 128)))
        strip = lax.shift_right_arithmetic(local, 7)
        place = jnp.bitwise_and(local, 127)
        high = ((strip == strip_ids) & (strip_ids < strips)).astype(F32).astype(BF16)
        low = (place == lanes).astype(F32).astype(BF16)
        masks.append(lax.dot_general(high, low, (((1,), (1,)), ((), ())), preferred_element_type=F32))
    mask = jnp.concatenate(masks, axis=0)
    start = jnp.concatenate(starts, axis=0).astype(I32)
    mask16 = mask.astype(BF16)
    totals = dot(mask16, ones)
    rank = (dot(mask16, upper) + dot(before, totals.astype(BF16))).astype(I32)
    slot = lax.rem(rank + start, BATCHES) * depth + lax.div(rank, BATCHES)
    code = jnp.where(mask > 0.5, slot, -1)
    code_rows = []
    for shift in range(experts):
        row = jnp.concatenate([code[8 * shift + i : 8 * shift + i + 1] for i in range(strips)], axis=1)
        code_ref[pl.ds(shift, 1), :] = row
        code_rows.append(row)
    load.wait()
    pack(0, depth, code_rows, held, staged, sends, out_sems)


def pack(k, depth, code_rows, held, staged, sends, sems):
    slot_ids = lax.broadcasted_iota(I32, (depth, held.shape[0]), 0) + k * depth
    copies = []
    for shift in list(range(1, len(sends))) + [0]:
        selector = (slot_ids == code_rows[shift]).astype(F32).astype(BF16)
        staged[shift] = dot(selector, held[...]).astype(BF16)
        copy = pltpu.make_async_copy(staged.at[shift], sends[shift], sems.at[shift])
        copy.start()
        copies.append(copy)
    for copy in copies:
        copy.wait()


def first_batch(place, picks, tokens, depth):
    rows, width = tokens.shape
    experts = picks.shape[0]
    out = pl.pallas_call(
        functools.partial(code_kernel, experts, depth),
        out_shape=[jax.ShapeDtypeStruct((experts, rows), I32)]
        + [jax.ShapeDtypeStruct((depth, width), BF16)] * experts,
        in_specs=[smem()] + apart(2),
        out_specs=whole(1) + apart(experts),
        scratch_shapes=[
            pltpu.VMEM(picks.shape, I32),
            pltpu.VMEM((rows, width), BF16),
            pltpu.VMEM((experts, depth, width), BF16),
            pltpu.SemaphoreType.DMA((2,)),
            pltpu.SemaphoreType.DMA((experts,)),
        ],
        compiler_params=params(60 * 1024 * 1024),
        cost_estimate=COST,
    )(place, picks, tokens)
    return out[0], out[1:]


def logits_kernel(router_ref, tokens_ref, out_ref):
    out_ref[...] = lax.dot_general(
        router_ref[...], tokens_ref[...], (((1,), (1,)), ((), ())), preferred_element_type=F32
    )


def partial_logits(router, tokens):
    return pl.pallas_call(
        logits_kernel,
        out_shape=jax.ShapeDtypeStruct((router.shape[0], tokens.shape[0]), F32),
        in_specs=whole(2),
        out_specs=whole(1)[0],
        compiler_params=params(),
        cost_estimate=COST,
    )(router, tokens)


def pack_kernel(experts, depth, k, code_ref, tokens_ref, *refs):
    sends = refs[:experts]
    held, staged, in_sems, out_sems = refs[experts:]
    start_all([tokens_ref], [held], in_sems)[0].wait()
    code_rows = [code_ref[pl.ds(shift, 1), :] for shift in range(experts)]
    pack(k, depth, code_rows, held, staged, sends, out_sems)


def later_batch(code, tokens, k, depth):
    rows, width = tokens.shape
    experts = code.shape[0]
    return pl.pallas_call(
        functools.partial(pack_kernel, experts, depth, k),
        out_shape=[jax.ShapeDtypeStruct((depth, width), BF16)] * experts,
        in_specs=whole(1) + apart(1),
        out_specs=apart(experts),
        scratch_shapes=[
            pltpu.VMEM((rows, width), BF16),
            pltpu.VMEM((experts, depth, width), BF16),
            pltpu.SemaphoreType.DMA((1,)),
            pltpu.SemaphoreType.DMA((experts,)),
        ],
        compiler_params=params(),
        cost_estimate=COST,
    )(code, tokens)


def compact_kernel(experts, k, offset_ref, count_ref, *refs):
    blocks, out_ref = refs[:experts], refs[experts]
    held, sems = refs[experts + 1 :]
    depth = blocks[0].shape[0]
    size = out_ref.shape[0]
    loads = start_all(blocks, [held.at[pl.ds(i * depth, depth)] for i in range(experts)], sems)
    row = lax.broadcasted_iota(I32, (size, depth), 0)
    lane = lax.broadcasted_iota(I32, (size, depth), 1)
    parts = [
        ((row - offset_ref[k, i] == lane) & (lane < count_ref[k, i])).astype(F32).astype(BF16)
        for i in range(experts)
    ]
    selector = jnp.concatenate(parts, axis=1)
    for load in loads:
        load.wait()
    out_ref[...] = dot(selector, held[...]).astype(BF16)


def compact(offsets, counts, k, blocks, size):
    experts = len(blocks)
    depth, width = blocks[0].shape
    return pl.pallas_call(
        functools.partial(compact_kernel, experts, k),
        out_shape=jax.ShapeDtypeStruct((size, width), BF16),
        in_specs=[smem(), smem()] + apart(experts),
        out_specs=whole(1)[0],
        scratch_shapes=[pltpu.VMEM((experts * depth, width), BF16), pltpu.SemaphoreType.DMA((experts,))],
        compiler_params=params(),
        cost_estimate=COST,
    )(offsets, counts, *blocks)


def gate_up_near_kernel(parts, near, far, order_ref, gate_ref, up_ref, *refs):
    xs, refs = refs[:parts], refs[parts:]
    gate_out, up_out, gate_far, up_far, gate_held, up_held, x_held, sems = refs
    width = xs[0].shape[1]

    def fetch(i, place, gate_to, up_to, base):
        first = pl.multiple_of(order_ref[place] * width, width)
        return start_all(
            [gate_ref.at[0, pl.ds(first, width), :], up_ref.at[0, pl.ds(first, width), :]],
            [gate_to.at[i], up_to.at[i]],
            sems.at[pl.ds(base, 2)],
        )

    x_loads = start_all(xs, [x_held.at[i] for i in range(parts)], sems.at[pl.ds(0, parts)])
    loads = [fetch(i, near[i], gate_held, up_held, parts + 2 * i) for i in range(parts)]
    late = [fetch(i, far[i], gate_far, up_far, 3 * parts + 2 * i) for i in range(len(far))]
    gate = up = None
    for i in range(parts):
        for copy in [x_loads[i]] + loads[i]:
            copy.wait()
        x = x_held[i]
        gate_term = dot(x, gate_held[i])
        up_term = dot(x, up_held[i])
        gate = gate_term if gate is None else gate + gate_term
        up = up_term if up is None else up + up_term
    gate_out[...] = gate
    up_out[...] = up
    for copies in late:
        for copy in copies:
            copy.wait()


def gate_up_near(order, near, far, gate_weight, up_weight, xs):
    parts = len(xs)
    size, width = xs[0].shape
    units = gate_weight.shape[2]
    held = jax.ShapeDtypeStruct((len(far), width, units), BF16)
    return pl.pallas_call(
        functools.partial(gate_up_near_kernel, parts, near, far),
        out_shape=[jax.ShapeDtypeStruct((size, units), F32)] * 2 + [held] * 2,
        in_specs=[smem()] + apart(2 + parts),
        out_specs=whole(4),
        scratch_shapes=[
            pltpu.VMEM((parts, width, units), BF16),
            pltpu.VMEM((parts, width, units), BF16),
            pltpu.VMEM((parts, size, width), BF16),
            pltpu.SemaphoreType.DMA((3 * parts + 2 * len(far),)),
        ],
        compiler_params=params(),
        cost_estimate=COST,
    )(order, gate_weight, up_weight, *xs)


def gate_up_far_kernel(parts, first, last, gate_before, up_before, gate_ref, up_ref, *refs):
    xs, outs = refs[:parts], refs[parts:]
    gate, up = gate_before[...], up_before[...]
    for i in range(parts):
        x = xs[i][...]
        gate = gate + dot(x, gate_ref[first + i])
        up = up + dot(x, up_ref[first + i])
    if last:
        outs[0][...] = (gate * jax.nn.sigmoid(gate) * up).astype(BF16)
    else:
        outs[0][...] = gate
        outs[1][...] = up


def gate_up_far(xs, before, first, last):
    shape = before[0].shape
    sums = [jax.ShapeDtypeStruct(shape, F32)] * 2
    return pl.pallas_call(
        functools.partial(gate_up_far_kernel, len(xs), first, last),
        out_shape=[jax.ShapeDtypeStruct(shape, BF16)] if last else sums,
        in_specs=whole(4 + len(xs)),
        out_specs=whole(1 if last else 2),
        compiler_params=params(),
        cost_estimate=COST,
    )(*before, *xs)


def down_first_kernel(parts, near, far, order_ref, down_ref, *refs):
    hs, (out_ref, far_ref, down_held, h_held, sems) = refs[:parts], refs[parts:]
    units = hs[0].shape[1]

    def fetch(i, place, target, sem):
        first = pl.multiple_of(order_ref[place] * units, units)
        copy = pltpu.make_async_copy(down_ref.at[0, pl.ds(first, units), :], target.at[i], sems.at[sem])
        copy.start()
        return copy

    h_loads = start_all(hs, [h_held.at[i] for i in range(parts)], sems.at[pl.ds(0, parts)])
    loads = [fetch(i, near[i], down_held, parts + i) for i in range(parts)]
    late = [fetch(i, far[i], far_ref, 2 * parts + i) for i in range(len(far))]
    total = None
    for i in range(parts):
        h_loads[i].wait()
        loads[i].wait()
        term = dot(h_held[i], down_held[i])
        total = term if total is None else total + term
    out_ref[...] = total
    for copy in late:
        copy.wait()


def down_first(order, near, far, down_weight, hs):
    parts = len(hs)
    size, units = hs[0].shape
    width = down_weight.shape[2]
    return pl.pallas_call(
        functools.partial(down_first_kernel, parts, near, far),
        out_shape=[
            jax.ShapeDtypeStruct((size, width), F32),
            jax.ShapeDtypeStruct((len(far), units, width), BF16),
        ],
        in_specs=[smem()] + apart(1 + parts),
        out_specs=whole(2),
        scratch_shapes=[
            pltpu.VMEM((parts, units, width), BF16),
            pltpu.VMEM((parts, size, units), BF16),
            pltpu.SemaphoreType.DMA((2 * parts + len(far),)),
        ],
        compiler_params=params(),
        cost_estimate=COST,
    )(order, down_weight, *hs)


def down_last_kernel(parts, experts, k, direct, offset_ref, count_ref, before_ref, down_ref, *refs):
    hs, outs = refs[:parts], refs[parts : parts + experts]
    h_held, sems, *staged = refs[parts + experts :]
    loads = start_all(hs, [h_held.at[i] for i in range(parts)], sems)
    size = hs[0].shape[0]
    depth = outs[0].shape[0]
    row = lax.broadcasted_iota(I32, (depth, size), 0)
    lane = lax.broadcasted_iota(I32, (depth, size), 1)
    picks = [
        ((lane - offset_ref[k, i] == row) & (row < count_ref[k, i])).astype(F32).astype(BF16)
        for i in range(experts)
    ]
    total = before_ref[...]
    for i in range(parts):
        loads[i].wait()
        total = total + dot(h_held[i], down_ref[i])
    result = total.astype(BF16)
    if direct:
        for i in range(experts):
            outs[i][...] = dot(picks[i], result).astype(BF16)
        return
    staged_ref, out_sems = staged
    copies = []
    for i in list(range(1, experts)) + [0]:
        staged_ref[i] = dot(picks[i], result).astype(BF16)
        copy = pltpu.make_async_copy(staged_ref.at[i], outs[i], out_sems.at[i])
        copy.start()
        copies.append(copy)
    for copy in copies:
        copy.wait()


def down_last(offsets, counts, k, hs, before, experts, depth, direct):
    parts = len(hs)
    size, units = hs[0].shape
    width = before[0].shape[1]
    return pl.pallas_call(
        functools.partial(down_last_kernel, parts, experts, k, direct),
        out_shape=[jax.ShapeDtypeStruct((depth, width), BF16)] * experts,
        in_specs=[smem()] * 2 + whole(2) + apart(parts),
        out_specs=whole(experts) if direct else apart(experts),
        scratch_shapes=[pltpu.VMEM((parts, size, units), BF16), pltpu.SemaphoreType.DMA((parts,))]
        + ([] if direct else [pltpu.VMEM((experts, depth, width), BF16), pltpu.SemaphoreType.DMA((experts,))]),
        compiler_params=params(),
        cost_estimate=COST,
    )(offsets, counts, *before, *hs)


def weight_kernel(experts, place_ref, own_ref, logits_ref, code_ref, out_ref, score_ref):
    me = place_ref[0]
    kernel = jnp.exp(logits_ref[...])
    row_scale = jnp.ones((kernel.shape[0], 1, kernel.shape[2]), F32)
    for sweep in range(3):
        column = jnp.sum(jnp.sum(kernel * row_scale, axis=0, keepdims=True), axis=2, keepdims=True)
        column_scale = 1.0 / column
        row_scale = 1.0 / jnp.sum(kernel * column_scale, axis=1, keepdims=True)
    own = jnp.exp(own_ref[...])
    column_scale = column_scale[0]
    own_scale = 1.0 / jnp.sum(own * column_scale, axis=0, keepdims=True)
    score_ref[...] = own_scale * own * column_scale
    picked = []
    for shift in range(experts):
        score = score_ref[pl.ds(jnp.bitwise_xor(me, partner(shift, experts)), 1), :]
        picked.append(jnp.where(code_ref[pl.ds(shift, 1), :] >= 0, score, 0.0))
    total = picked[0]
    for one in picked[1:]:
        total = total + one
    total = jnp.maximum(total, 1.0 / experts)
    for shift in range(experts):
        out_ref[pl.ds(shift, 1), :] = picked[shift] / total


def slot_weights(place, own, logits, code):
    experts, rows = own.shape
    return pl.pallas_call(
        functools.partial(weight_kernel, experts),
        out_shape=jax.ShapeDtypeStruct((experts, rows), F32),
        in_specs=[smem()] + whole(3),
        out_specs=whole(1)[0],
        scratch_shapes=[pltpu.VMEM((experts, rows), F32)],
        compiler_params=params(),
        cost_estimate=COST,
    )(place, own, logits, code)


def combine_kernel(places, k, more, code_ref, weight_ref, *refs):
    before, refs = refs[:more], refs[more:]
    count = len(places)
    blocks, (out_ref, held, sems) = refs[:count], refs[count:]
    depth = blocks[0].shape[0]
    rows = code_ref.shape[1]
    loads = start_all(blocks, [held.at[pl.ds(i * depth, depth)] for i in range(count)], sems)
    slot_ids = lax.broadcasted_iota(I32, (depth, rows), 0) + k * depth
    parts = [
        jnp.where(slot_ids == code_ref[pl.ds(i, 1), :], weight_ref[pl.ds(i, 1), :], 0.0).astype(BF16)
        for i in places
    ]
    spread = jnp.concatenate(parts, axis=0)
    for load in loads:
        load.wait()
    total = lax.dot_general(spread, held[...], (((0,), (0,)), ((), ())), preferred_element_type=F32)
    if more:
        total = total + before[0][...]
    out_ref[...] = total.astype(out_ref.dtype)


def combine(code, weights, k, places, blocks, so_far, last):
    count = len(places)
    depth, width = blocks[0].shape
    rows = code.shape[1]
    more = [] if so_far is None else [so_far]
    return pl.pallas_call(
        functools.partial(combine_kernel, places, k, len(more)),
        out_shape=jax.ShapeDtypeStruct((rows, width), BF16 if last else F32),
        in_specs=whole(2 + len(more)) + apart(count),
        out_specs=whole(1)[0],
        scratch_shapes=[pltpu.VMEM((count * depth, width), BF16), pltpu.SemaphoreType.DMA((count,))],
        compiler_params=params(),
        cost_estimate=COST,
    )(code, weights, *more, *[blocks[i] for i in places])


def after(value, *first):
    return lax.optimization_barrier((value, first))[0]


def shards(tokens, router_weight, gate_weight, up_weight, down_weight, picks):
    experts = lax.axis_size("expert")
    width_parts = lax.axis_size("dp")
    me = lax.axis_index("expert")
    part = lax.axis_index("dp")
    rows = tokens.shape[0]
    capacity = picks.shape[1]
    depth = 2 * capacity // experts // BATCHES
    size = capacity // BATCHES
    place = me.astype(I32).reshape(1)

    def along_expert(x, shift):
        return lax.ppermute(x, "expert", [(i, i ^ shift) for i in range(experts)])

    def swap(x, bit):
        return lax.ppermute(x, "dp", [(i, i ^ bit) for i in range(width_parts)])

    bits = []
    bit = width_parts // 2
    while bit:
        bits.append(bit)
        bit //= 2
    near = [0]
    for bit in bits[1:]:
        near = near + [m ^ bit for m in near]
    masks = near + [m ^ bits[0] for m in near]
    places = range(len(masks))
    near_places, far_places = places[: len(near)], places[len(near) :]
    order = jnp.stack([part ^ m for m in masks]).astype(I32)

    def exchange(blocks):
        return [blocks[0]] + [along_expert(blocks[i], partner(i, experts)) for i in range(1, experts)]

    expert_bits = [1 << i for i in range(experts.bit_length() - 1)]

    def spread(x):
        held = [x]
        for bit in bits[1:]:
            held = held + [swap(h, bit) for h in held]
        return held

    def both_parts(x):
        far = swap(x, bits[0])
        return spread(x), spread(far)

    code, first = first_batch(place, picks, tokens, depth)
    own_picks = lax.dynamic_slice_in_dim(picks, me, 1, axis=0)
    sources = jnp.bitwise_xor(me, jnp.array([partner(i, experts) for i in range(experts)], I32))
    start = jnp.sum((own_picks < (sources * rows)[:, None]).astype(I32), axis=1)
    stop = jnp.sum((own_picks < ((sources + 1) * rows)[:, None]).astype(I32), axis=1)
    ids = jnp.arange(BATCHES, dtype=I32)[:, None]
    offsets = (start[None, :] + (BATCHES - 1) - ids) // BATCHES
    counts = (stop[None, :] + (BATCHES - 1) - ids) // BATCHES - offsets

    present = [jnp.sum(counts[k]) > 0 for k in range(BATCHES)]

    def beside_first(router):
        logits = partial_logits(router, tokens)
        later = [tuple(later_batch(code, tokens, k, depth)) for k in range(1, BATCHES)]
        for bit in bits:
            logits = logits + swap(logits, bit)
        gathered = logits[None]
        for bit in expert_bits[:-1]:
            gathered = jnp.concatenate([gathered, along_expert(gathered, bit)])
        return later, logits, gathered

    def nothing_first(router):
        return jax.tree.map(lambda x: jnp.zeros(x.shape, x.dtype), jax.eval_shape(beside_first, router))

    arrived = [exchange(first)]
    later, logits, gathered = lax.cond(present[0], beside_first, nothing_first, router_weight.T)

    def far_half(far, sums):
        far = spread(far)
        gate, up, *weights = sums
        sums = gate_up_far(far[:1], (gate, up, *weights), 0, False)
        far, sums = lax.optimization_barrier((far[1:], sums))
        hidden = gate_up_far(far, (*sums, *weights), 1, True)[0]
        far = swap(hidden, bits[0])
        partial = down_first(order, near_places, far_places, down_weight, spread(hidden))
        far, partial = lax.optimization_barrier((far, partial))
        return spread(far), partial

    def settle(k, far, partial):
        return tuple(
            down_last(offsets, counts, k, far, partial, experts, depth, k == BATCHES - 1)
        )

    def fenced(k, run, *operands):
        def skip(*operands):
            return jax.tree.map(lambda x: jnp.zeros(x.shape, x.dtype), jax.eval_shape(run, *operands))

        return lax.cond(present[k], run, skip, *operands)

    waiting = []
    far = partial = None
    moved = gathered
    for k in range(BATCHES):
        blocks = after(arrived[k], moved)
        if k < BATCHES - 1:
            moving = after(later[k], blocks)
            arrived.append(exchange(moving))
        if k == 0:
            block = fenced(k, lambda *blocks: compact(offsets, counts, 0, blocks, size), *blocks)
        else:
            block = compact(offsets, counts, k, blocks, size)
        across = swap(block, bits[0])
        near = spread(block)
        if k > 0:
            far, partial = after((far, partial), block)
            results = settle(k - 1, far, partial)
            if k > 1:
                results, waiting[k - 2] = lax.optimization_barrier((results, waiting[k - 2]))
            waiting.append(exchange(results))
            near = after(near, results)
        sums = gate_up_near(order, near_places, far_places, gate_weight, up_weight, near)
        across, sums = lax.optimization_barrier((across, sums))
        if k == BATCHES - 1:
            gathered = after(gathered, sums)
            gathered = jnp.concatenate([gathered, along_expert(gathered, expert_bits[-1])])
        far, partial = fenced(k, far_half, across, sums)
        moved = partial
    results = settle(BATCHES - 1, far, partial)
    results, waiting[-1] = lax.optimization_barrier((list(results), waiting[-1]))
    results[-1], gathered = lax.optimization_barrier((results[-1], gathered))
    waiting.append(exchange(results))
    weights = slot_weights(place, logits, gathered, code)
    total = None
    for k in range(BATCHES - 1):
        total = combine(code, weights, k, sorted(range(experts), key=lambda i: (0, 2, 1)[i] if i < 3 else i), waiting[k], total, False)
    late = (min(1, experts - 1),)
    early = [i for i in range(experts) if i not in late]
    total = combine(code, weights, BATCHES - 1, early, waiting[-1], total, False)
    return combine(code, weights, BATCHES - 1, late, waiting[-1], total, True)


def solution(mesh):
    return jax.shard_map(
        shards,
        mesh=mesh,
        in_specs=(
            P(("groups", "expert"), "dp"),
            P("dp", None),
            P("expert", None, "dp"),
            P("expert", None, "dp"),
            P("expert", None, "dp"),
            P("groups", None),
        ),
        out_specs=P(("groups", "expert"), "dp"),
        check_vma=False,
    )
```
